32 devices in a mesh: seq: 4 (over y, x), exp: 8 (over z, core).
Axes of the slice: x: 2, y: 2, z: 4, core: 2. Of those that a mesh axis runs over, the one named last changes fastest.
Arguments:
- tokens: bfloat16 [8, 1024, 1024], P('exp', 'seq'), may hold values from -6 to 6
- lengths: int32 [8, 3], P('exp'), may hold values from 32 to 960, as said below
- expert_ids: int32 [8, 1024, 1], P('exp', 'seq'), may hold values from 0 to 7; in each aligned block of 256 rows (0 to 255, 256 to 511, ..., all dimensions but the last counted through in order) at most 64 rows name the same one
- ln1_gain: bfloat16 [1024], replicated, may hold values from 0.5 to 1.5
- ln1_bias: bfloat16 [1024], replicated, may hold values from -1.25 to 1.25
- w_query: bfloat16 [1024, 1024], replicated, may hold values from -0.25 to 0.25
- b_query: bfloat16 [1024], replicated, may hold values from -1.25 to 1.25
- w_key: bfloat16 [1024, 1024], replicated, may hold values from -0.1875 to 0.1875
- w_value: bfloat16 [1024, 1024], replicated, may hold values from -0.1875 to 0.1875
- b_value: bfloat16 [1024], replicated, may hold values from -1.25 to 1.25
- w_out: bfloat16 [1024, 1024], replicated, may hold values from -1 to 1
- b_out: bfloat16 [1024], replicated, may hold values from -1.25 to 1.25
- ln2_gain: bfloat16 [1024], replicated, may hold values from 0.5 to 1.5
- ln2_bias: bfloat16 [1024], replicated, may hold values from -1.25 to 1.25
- w_up: bfloat16 [8, 1024, 4096], P('exp', None, 'seq'), may hold values from -0.1875 to 0.1875
- b_up: bfloat16 [8, 4096], P('exp', 'seq'), may hold values from -1.25 to 1.25
- w_down: bfloat16 [8, 4096, 1024], P('exp', 'seq'), may hold values from -0.09375 to 0.09375
- b_down: bfloat16 [8, 1024], P('exp'), may hold values from -1.25 to 1.25
- cotangent: bfloat16 [8, 1024, 1024], P('exp', 'seq'), may hold values from -6 to 6
Outputs:
- output: bfloat16 [8, 1024, 1024], P('exp', 'seq')
- input_grad: float32 [8, 1024, 1024], P('exp', 'seq')
- grad_ln1_gain: float32 [1024], replicated
- grad_ln1_bias: float32 [1024], replicated
- grad_w_query: float32 [1024, 1024], replicated
- grad_b_query: float32 [1024], replicated
- grad_w_key: float32 [1024, 1024], replicated
- grad_w_value: float32 [1024, 1024], replicated
- grad_b_value: float32 [1024], replicated
- grad_w_out: float32 [1024, 1024], replicated
- grad_b_out: float32 [1024], replicated
- grad_ln2_gain: float32 [1024], replicated
- grad_ln2_bias: float32 [1024], replicated
- grad_w_up: float32 [8, 1024, 4096], P('exp', None, 'seq')
- grad_b_up: float32 [8, 4096], P('exp', 'seq')
- grad_w_down: float32 [8, 4096, 1024], P('exp', 'seq')
- grad_b_down: float32 [8, 1024], P('exp', 'seq')
The draws below stay inside these ranges and needn't reach their ends.
Inputs may be any that keep to these rules, and one draw needn't show every extreme that they name: Each group's 3 lengths sum to 1024. `expert_ids`: among the 256 tokens of one device (aligned blocks along the token dimensions), no expert is named more than 64 times; in some blocks an expert is named exactly 64 times.
All inputs are finite; a program needn't handle non-finite values.
Results may differ from the reference program's by a relative error of at most 0.017.
Values may be sent and summed in bfloat16 or wider, within the bound.
A program may use at most 192 MiB of HBM per device.

```python
import math
import jax
import jax.numpy as jnp
import numpy as np
from jax import lax

D = 1024
HEADS = 16
HEAD_DIM = 64
FF = 4096
TOK_DEV = 256
GROUP_TOK = 1024
GROUPS = 8
EXPERTS = 8
CAP = 64
N_SEQ = 4


def draw_lengths(key, part):
    key = jax.random.fold_in(key, 7)
    short_key, place_key = jax.random.split(key)
    shorts = jax.random.randint(short_key, (GROUPS, 2), TOK_DEV // 8, TOK_DEV // 2)
    before = jax.random.randint(place_key, (GROUPS,), 0, 3)
    longest = GROUP_TOK - jnp.sum(shorts, axis=1)
    first_len = jnp.where(before == 0, longest, shorts[:, 0])
    second = jnp.where(before == 0, shorts[:, 0], jnp.where(before == 1, longest, shorts[:, 1]))
    third_len = jnp.where(before == 2, longest, shorts[:, 1])
    return jnp.stack([first_len, second, third_len], axis=1).astype(jnp.int32)


def steps_of(own_key, shape, shards, low, largest):
    loudness = 1.0
    for axis_at, parts in shards:
        heights = jax.random.uniform(jax.random.fold_in(jax.random.fold_in(own_key, 6), axis_at), (parts,), jnp.float32, low / len(shards), largest / len(shards))
        loudness = loudness * jnp.repeat(jnp.exp(heights), shape[axis_at] // parts).reshape((-1,) + (1,) * (len(shape) - 1 - axis_at))
    return loudness


def deal_out(stream_key, own, number, rows, number_of, top, limit, lean):
    order = jax.random.permutation(stream_key, number_of)
    heavy_load, common = load_shares(number_of, rows * top, limit, lean, True), load_shares(number_of, rows * top, limit, lean, False)
    places = jnp.arange(number_of)

    def named(sizes, rotation):
        used = int((sizes > 0).sum())
        fixed = max(1, used // 4)
        moved = fixed + (places - fixed + rotation * (used - fixed)) % max(1, number_of - fixed)
        return jnp.zeros((number_of,), jnp.int32).at[order[jnp.where(places < fixed, places, moved)]].set(jnp.asarray(sizes, jnp.int32))

    sizes = jnp.where(number % 4 == 0, named(heavy_load, number // 4), named(common, number - number // 4 - 1))
    mixed = jax.random.permutation(jax.random.fold_in(own, 3), number_of)
    source_of, receiver = mixed[0:number_of // 2 * 2:2], mixed[1:number_of // 2 * 2:2]
    slack = jnp.minimum(sizes[source_of] - 1, limit - sizes[receiver]) // 2
    slack = jnp.where((source_of == order[0]) | (receiver == order[0]) | (sizes[receiver] == 0), 0, jnp.maximum(slack, 0))
    moved = jax.random.randint(jax.random.fold_in(own, 4), (number_of // 2,), 0, 1 << 20) % (slack + 1)
    sizes = sizes.at[source_of].add(-moved).at[receiver].add(moved)
    items = jnp.searchsorted(jnp.cumsum(sizes), jnp.arange(rows * top), side="right").astype(jnp.int32)
    table = items.reshape(top, rows).T
    table = table[jax.random.permutation(jax.random.fold_in(own, 1), rows)]
    rotation = jax.random.randint(jax.random.fold_in(own, 2), (rows, 1), 0, top)
    return jnp.take_along_axis(table, (jnp.arange(top)[None, :] + rotation) % top, axis=1)


def load_shares(count, total, reach, lean, full):
    loads = [(1 << 20) // math.isqrt(grade ** lean) + 1 for grade in range(1, count + 1)]
    largest = reach if full else min(reach, max(-(-total // count), total * loads[0] // sum(loads)))
    least = 1 if total - largest >= count - 1 else 0
    counts, spare = [largest] + [least] * (count - 1), total - largest - least * (count - 1)
    while spare > 0:
        candidates = [i for i in range(1, count) if counts[i] < largest] or [i for i in range(1, count) if counts[i] < reach]
        whole, remaining = sum([loads[i] for i in candidates]), spare
        for i in candidates:
            addition = min(reach - counts[i], max(1, remaining * loads[i] // whole), spare)
            counts[i] = counts[i] + addition
            spare = spare - addition
    return np.array(counts)


def normal_values(key, dims, scale, bound, pieces=(), held_as=jnp.bfloat16):
    entries = jax.random.normal(key, dims, jnp.float32) * scale
    if len(pieces) > 0:
        entries = steps_of(key, dims, pieces, -0.22, 0.18) * entries
    return jnp.clip(entries, min=-bound, max=bound).astype(held_as)


def setup_inputs(seed: int = 0) -> dict:
    seeds = jax.random.split(jax.random.key(seed), 20)
    tokens = normal_values(seeds[0], (GROUPS, GROUP_TOK, D), 1.0, 6.0, ((0, 8), (1, 4)))
    lengths = draw_lengths(jax.random.fold_in(seeds[19], 71), 0)
    expert_ids_keys = jax.random.split(jax.random.fold_in(seeds[2], 1), GROUPS * GROUP_TOK // TOK_DEV)
    expert_ids_turns = jax.random.permutation(jax.random.fold_in(seeds[2], 3), GROUPS * GROUP_TOK // TOK_DEV)
    expert_ids = jax.vmap(lambda own, number: deal_out(jax.random.fold_in(seeds[2], 2), own, number, TOK_DEV, EXPERTS, 1, CAP, 2))(expert_ids_keys, expert_ids_turns).reshape((GROUPS, GROUP_TOK, 1))
    ln1_gain = jnp.clip(1.0 + 0.1 * jax.random.normal(seeds[3], (D,), jnp.float32), 0.5, 1.5).astype(jnp.bfloat16)
    ln1_bias = normal_values(seeds[4], (D,), 0.2, 1.25)
    w_query = normal_values(seeds[5], (D, D), (D // 2) ** -0.5, 0.25)
    b_query = normal_values(seeds[6], (D,), 0.2, 1.25)
    w_key = normal_values(seeds[7], (D, D), D ** -0.5, 0.1875)
    w_value = normal_values(seeds[8], (D, D), D ** -0.5, 0.1875)
    b_value = normal_values(seeds[9], (D,), 0.2, 1.25)
    w_out = normal_values(seeds[10], (D, D), (D // 32) ** -0.5, 1.0)
    b_out = normal_values(seeds[11], (D,), 0.2, 1.25)
    ln2_gain = jnp.clip(1.0 + 0.1 * jax.random.normal(seeds[12], (D,), jnp.float32), 0.5, 1.5).astype(jnp.bfloat16)
    ln2_bias = normal_values(seeds[13], (D,), 0.2, 1.25)
    w_up = normal_values(seeds[14], (EXPERTS, D, FF), D ** -0.5, 0.1875, ((0, 8), (2, 4)))
    b_up = normal_values(seeds[15], (EXPERTS, FF), 0.2, 1.25, ((0, 8), (1, 4)))
    w_down = normal_values(seeds[16], (EXPERTS, FF, D), FF ** -0.5, 0.09375, ((0, 8), (1, 4)))
    b_down = normal_values(seeds[17], (EXPERTS, D), 0.2, 1.25, ((0, 8),))
    cotangent = normal_values(seeds[18], (GROUPS, GROUP_TOK, D), 1.0, 6.0, ((0, 8), (1, 4)))
    return dict(tokens=tokens, lengths=lengths, expert_ids=expert_ids, ln1_gain=ln1_gain, ln1_bias=ln1_bias, w_query=w_query, b_query=b_query, w_key=w_key, w_value=w_value, b_value=b_value, w_out=w_out, b_out=b_out, ln2_gain=ln2_gain, ln2_bias=ln2_bias, w_up=w_up, b_up=b_up, w_down=w_down, b_down=b_down, cotangent=cotangent)


@jax.custom_vjp
def low(v):
    return lax.optimization_barrier(v.astype(jnp.bfloat16)).astype(jnp.float32)

@jax.custom_vjp
def low_back(v):
    return v

def low_keep(v):
    return (low(v), None)

def low_pass(kept, grad):
    return (grad,)

def back_keep(v):
    return (v, None)

def back_low(kept, grad):
    return (low(grad),)
low.defvjp(low_keep, low_pass)
low_back.defvjp(back_keep, back_low)
EPSILON = 1e-05
SCORE_SCALE = 0.125
MASKED_SCORE = -1e+30

def norm_layer(values_in, gain_vec, shift_vec):
    center = values_in - lax.optimization_barrier(jnp.mean(values_in, axis=-1, keepdims=True))
    inv_std = lax.rsqrt(lax.optimization_barrier(jnp.mean(center * center, axis=-1, keepdims=True)) + EPSILON)
    return center * inv_std * gain_vec + shift_vec

def matmul(left_op, right_op):
    return jnp.dot(left_op, right_op, precision=lax.Precision.HIGHEST, preferred_element_type=jnp.float32)

def segment_ids(positions, seq_ends):
    return lax.optimization_barrier(jnp.sum((positions[:, None] >= seq_ends[None, :]).astype(jnp.int32), axis=1))

def attend_group(queries, keys_h, values_h, seq_ends):
    total_len = queries.shape[0]
    block_len = math.gcd(total_len, 512)
    positions = jnp.arange(total_len, dtype=jnp.int32)
    segments = segment_ids(positions, seq_ends)
    q_blocks = queries.reshape(total_len // block_len, block_len, HEADS, HEAD_DIM)
    pos_blocks = positions.reshape(total_len // block_len, block_len)
    seg_blocks = segments.reshape(total_len // block_len, block_len)

    @jax.checkpoint
    def one_block(packed):
        q_blk, q_pos, q_seg = packed
        scores = low_back(jnp.einsum('qhd,khd->hqk', q_blk, keys_h, precision=lax.Precision.HIGHEST) * SCORE_SCALE)
        allowed = ((q_seg[:, None] == segments[None, :]) & (positions[None, :] <= q_pos[:, None]))[None]
        masked = jnp.where(allowed, scores, MASKED_SCORE)
        row_max = lax.optimization_barrier(jnp.max(masked, axis=-1, keepdims=True))
        weights = jnp.where(allowed, jnp.exp(masked - row_max), 0.0)
        probabilities = low(weights / lax.optimization_barrier(jnp.sum(weights, axis=-1, keepdims=True)))
        return jnp.einsum('hqk,khd->qhd', probabilities, values_h, precision=lax.Precision.HIGHEST)
    attended = lax.map(one_block, (q_blocks, pos_blocks, seg_blocks))
    return attended.reshape(total_len, HEADS * HEAD_DIM)

def reference(tokens, lengths, expert_ids, ln1_gain, ln1_bias, w_query, b_query, w_key, w_value, b_value, w_out, b_out, ln2_gain, ln2_bias, w_up, b_up, w_down, b_down, cotangent):
    groups = tokens.shape[0]
    group_len = tokens.shape[1]
    width = tokens.shape[2]
    seq_ends = jnp.cumsum(lengths, axis=1).astype(jnp.int32)
    devices = groups * N_SEQ
    expert_of = expert_ids.reshape(devices, TOK_DEV).astype(jnp.int32)
    onehot = (expert_of[:, :, None] == jnp.arange(EXPERTS, dtype=jnp.int32)[None, None, :]).astype(jnp.int32)
    slot_of = lax.optimization_barrier(jnp.sum(onehot * (jnp.cumsum(onehot, axis=1) - onehot), axis=2))
    row_of = (jnp.arange(devices, dtype=jnp.int32)[:, None] * CAP + slot_of).astype(jnp.int32)
    head_shape = (groups, group_len, HEADS, HEAD_DIM)

    def group_attend(packed):
        return attend_group(packed[0], packed[1], packed[2], packed[3])

    @jax.checkpoint
    def expert_apply(packed):
        rows_in, up_mat, up_vec, down_mat, down_vec = packed
        preact = low_back(matmul(rows_in, up_mat) + up_vec)
        act_low = low(jax.nn.gelu(preact))
        return low(low_back(matmul(act_low, down_mat) + down_vec))

    def forward(inputs, gain_one, bias_one, wq_mat, bq_vec, wk_mat, wv_mat, bv_vec, wo_mat, bo_vec, gain_two, bias_two, wu_all, bu_all, wd_all, bd_all):
        flat = inputs.reshape(-1, width)
        normed_one = low(low_back(norm_layer(flat, gain_one, bias_one)))
        queries = low(low_back(matmul(normed_one, wq_mat) + bq_vec))
        keys_all = low(low_back(matmul(normed_one, wk_mat)))
        values_all = low(low_back(matmul(normed_one, wv_mat) + bv_vec))
        attended = lax.map(group_attend, (queries.reshape(head_shape), keys_all.reshape(head_shape), values_all.reshape(head_shape), seq_ends))
        attn_low = low(low_back(attended.reshape(-1, width)))
        resid = flat + low_back(matmul(attn_low, wo_mat) + bo_vec)
        normed_two = low(low_back(norm_layer(resid, gain_two, bias_two)))
        buffer = jnp.zeros((EXPERTS, devices * CAP, width), jnp.float32).at[expert_of, row_of].set(normed_two.reshape(devices, TOK_DEV, width))
        produced = lax.map(expert_apply, (buffer, wu_all, bu_all, wd_all, bd_all))
        ffn_rows = produced[expert_of, row_of].reshape(-1, width)
        return (resid + ffn_rows).reshape(groups, group_len, width)
    floats = [tokens.astype(jnp.float32), ln1_gain.astype(jnp.float32), ln1_bias.astype(jnp.float32), w_query.astype(jnp.float32), b_query.astype(jnp.float32), w_key.astype(jnp.float32), w_value.astype(jnp.float32), b_value.astype(jnp.float32), w_out.astype(jnp.float32), b_out.astype(jnp.float32), ln2_gain.astype(jnp.float32), ln2_bias.astype(jnp.float32), w_up.astype(jnp.float32), b_up.astype(jnp.float32), w_down.astype(jnp.float32), b_down.astype(jnp.float32)]
    output, pullback = jax.vjp(forward, floats[0], floats[1], floats[2], floats[3], floats[4], floats[5], floats[6], floats[7], floats[8], floats[9], floats[10], floats[11], floats[12], floats[13], floats[14], floats[15])
    gradients = pullback(cotangent.astype(jnp.float32))
    return (output.astype(jnp.bfloat16), gradients[0], gradients[1], gradients[2], gradients[3], gradients[4], gradients[5], gradients[6], gradients[7], gradients[8], gradients[9], gradients[10], gradients[11], gradients[12], gradients[13], gradients[14], gradients[15])
```

```python
import functools
import math

import jax
import jax.numpy as jnp
from jax import lax
from jax.experimental import pallas as pl
from jax.experimental.pallas import tpu as pltpu
from jax.sharding import PartitionSpec as P


HEADS = 16
HEAD_DIM = 64


EPSILON = 1e-05
SCORE_SCALE = 0.125
MASKED_SCORE = -1e30


def norm_layer(values_in, gain_vec, shift_vec):
    center = values_in - jnp.mean(values_in, axis=-1, keepdims=True)
    inv_std = lax.rsqrt(jnp.mean(center * center, axis=-1, keepdims=True) + EPSILON)
    return center * inv_std * gain_vec + shift_vec


def segment_ids(positions, seq_ends):
    return jnp.sum((positions[:, None] >= seq_ends[None, :]).astype(jnp.int32), axis=1)


def visible_pairs(query_pos, query_seg, key_pos, key_seg):
    return ((query_seg[:, None] == key_seg[None, :]) & (key_pos[None, :] <= query_pos[:, None]))[
        None
    ]


def project(left_op, right_op):
    return jnp.dot(left_op, right_op, preferred_element_type=jnp.float32)


MESH = pl.DeviceIdType.MESH
F32 = jnp.float32
BF16 = jnp.bfloat16
VMEM_LIMIT = 60 * 2**20


def dot(a, b, dims=((1,), (0,))):
    return lax.dot_general(a, b, (dims, ((), ())), preferred_element_type=F32)


class Place:
    def __init__(self, n_exp):
        self.n_exp = n_exp
        self.s = lax.axis_index("seq")
        self.e = lax.axis_index("exp")
        low = lax.rem(self.s, 2)
        high = lax.div(self.s, 2)
        self.near = high * 2 + (1 - low)
        self.far = (1 - high) * 2 + low
        self.diag = (1 - high) * 2 + (1 - low)
        self.core = lax.rem(self.e, 2)
        self.chip = lax.div(self.e, 2)

    def peer(self, step, way):
        chips = self.n_exp // 2
        hop = lax.div(step, 2)
        if chips == 4:
            hop = hop + lax.div(hop, 2) * (5 - 2 * hop)
        chip = lax.rem(self.chip + way * hop + chips, chips)
        return chip * 2 + lax.rem(self.core + step, 2)

    def greet(self, seq=True, exp=True):
        barrier = pltpu.get_barrier_semaphore()
        count = 0
        if seq:
            for other in (self.near, self.far):
                pl.semaphore_signal(barrier, inc=1, device_id=(other, self.e), device_id_type=MESH)
            count += 2
        if exp:

            def tell(step, carry):
                pl.semaphore_signal(
                    barrier, inc=1, device_id=(self.s, self.peer(step, 1)), device_id_type=MESH
                )
                return carry

            lax.fori_loop(1, self.n_exp, tell, 0)
            count += self.n_exp - 1
        pl.semaphore_wait(barrier, count)

    def to_seq(self, src, dst, send_sem, recv_sem, other):
        return pltpu.make_async_remote_copy(
            src_ref=src, dst_ref=dst, send_sem=send_sem, recv_sem=recv_sem,
            device_id=(other, self.e), device_id_type=MESH,
        )

    def to_exp(self, src, dst, send_sem, recv_sem, other):
        return pltpu.make_async_remote_copy(
            src_ref=src, dst_ref=dst, send_sem=send_sem, recv_sem=recv_sem,
            device_id=(self.s, other), device_id_type=MESH,
        )


class Dispatch:
    def __init__(self, place, send, held, exp_sems, seq_sems):
        self.place, self.send, self.held = place, send, held
        self.exp_send, self.exp_recv = exp_sems
        self.seq_send, self.seq_recv = seq_sems
        self.cap = send.shape[1]

    @staticmethod
    def scratch(n_exp):
        return [
            pltpu.SemaphoreType.DMA((n_exp,)),
            pltpu.SemaphoreType.DMA((n_exp,)),
            pltpu.SemaphoreType.DMA((n_exp, 6)),
            pltpu.SemaphoreType.DMA((n_exp, 6)),
        ]

    def _exp(self, step):
        p = self.place
        other = p.peer(step, -1)
        return p.to_exp(
            self.send.at[other], self.held.at[step, p.s], self.exp_send.at[step], self.exp_recv.at[step], other
        )

    def _seq(self, step, owner, half, lane, other):
        p = self.place
        rows = pl.ds(half * (self.cap // 2), self.cap // 2)
        part = self.held.at[step, owner, rows]
        return p.to_seq(part, part, self.seq_send.at[step, lane], self.seq_recv.at[step, lane], other)

    def copies(self, step, lanes=range(6)):
        p = self.place
        spec = (
            (p.s, 0, p.near),
            (p.s, 1, p.far),
            (p.s, 1, p.near),
            (p.s, 0, p.far),
            (p.near, 0, p.far),
            (p.far, 1, p.near),
        )
        return [self._seq(step, spec[n][0], spec[n][1], n, spec[n][2]) for n in lanes]

    def start_exp(self, step):
        self._exp(step).start()

    def own(self):
        p = self.place
        self.held[0, p.s] = self.send[p.e]

    def start_seq(self, step):
        @pl.when(step > 0)
        def _():
            self._exp(step).wait_recv()

        for c in self.copies(step, range(4)):
            c.start()

    def relay(self, step):
        for c, out in zip(self.copies(step, (0, 1)), self.copies(step, (4, 5))):
            c.wait_recv()
            out.start()

    def arrived(self, step):
        for c in self.copies(step, range(2, 6)):
            c.wait_recv()

    def drain(self):
        def body(step, carry):
            for c in self.copies(step):
                c.wait_send()

            @pl.when(step > 0)
            def _():
                self._exp(step).wait_send()

            return carry

        lax.fori_loop(0, self.place.n_exp, body, 0)


class Combine:
    def __init__(self, place, part, passing, landing, total, back, seq_sems, exp_sems, slots):
        self.place, self.part, self.passing, self.landing = place, part, passing, landing
        self.total, self.back, self.slots = total, back, slots
        self.seq_send, self.seq_recv = seq_sems
        self.exp_send, self.exp_recv = exp_sems
        self.cap = back.shape[1]
        self.half = self.cap // 2

    @staticmethod
    def scratch(n_exp, cap, width):
        return [
            pltpu.VMEM((n_exp, 2, cap // 2, width), BF16),
            pltpu.VMEM((n_exp, 4, cap // 2, width), BF16),
            pltpu.VMEM((n_exp, cap, width), BF16),
            pltpu.SemaphoreType.DMA((n_exp, 6)),
            pltpu.SemaphoreType.DMA((n_exp, 6)),
            pltpu.SemaphoreType.DMA((n_exp,)),
            pltpu.SemaphoreType.DMA((n_exp,)),
        ]

    def _slot(self, step):
        return lax.rem(step, self.slots)

    def _piece(self, step, owner, half):
        return self.part.at[self._slot(step), owner, pl.ds(half * self.half, self.half)]

    def _seq(self, src, dst, step, lane, other):
        return self.place.to_seq(
            src, dst, self.seq_send.at[step, lane], self.seq_recv.at[step, lane], other
        )

    def copies(self, step, lanes=range(6)):
        p = self.place
        spec = (
            (p.diag, 0, self.passing, 0, p.near),
            (p.diag, 1, self.passing, 1, p.far),
            (p.near, 0, self.landing, 0, p.near),
            (p.far, 1, self.landing, 3, p.far),
            (p.far, 0, self.landing, 2, p.far),
            (p.near, 1, self.landing, 1, p.near),
        )
        made = []
        for n in lanes:
            owner, half, buffer, at, other = spec[n]
            made.append(self._seq(self._piece(step, owner, half), buffer.at[step, at], step, n, other))
        return made

    def start(self, step):
        for c in self.copies(step, range(4)):
            c.start()

    def pass_on(self, step):
        p = self.place
        slot = self._slot(step)
        came, out = self.copies(step, (0, 1)), self.copies(step, (4, 5))
        for n, owner in enumerate((p.far, p.near)):
            rows = pl.ds(n * self.half, self.half)
            came[n].wait_recv()
            self.part[slot, owner, rows] = (
                self.part[slot, owner, rows].astype(F32) + self.passing[step, n].astype(F32)
            ).astype(BF16)
            out[n].start()

    def _exp(self, step):
        p = self.place
        other = p.peer(step, 1)
        return p.to_exp(
            self.total.at[step], self.back.at[p.e], self.exp_send.at[step], self.exp_recv.at[step], other
        )

    def finish(self, step, bias=None):
        p = self.place
        slot = self._slot(step)
        copies = self.copies(step)
        for c in copies[2:]:
            c.wait_recv()
        for half in range(2):
            rows = pl.ds(half * self.half, self.half)
            value = (
                self.part[slot, p.s, rows].astype(F32)
                + self.landing[step, half].astype(F32)
                + self.landing[step, 2 + half].astype(F32)
            )
            if bias is not None:
                value = value + bias
            self.total[step, rows] = value.astype(BF16)
        for c in copies:
            c.wait_send()

        @pl.when(step > 0)
        def _():
            self._exp(step).start()

        @pl.when(step == 0)
        def _():
            self.back[p.e] = self.total[0]

    def drain(self):
        p = self.place

        def body(step, carry):
            c = self._exp(step)
            c.wait_send()
            c.wait_recv()
            return carry

        lax.fori_loop(1, p.n_exp, body, 0)


def dispatch_rows(send, collective_id):
    n_exp, cap, width = send.shape

    def kernel(send, held, *sems):
        p = Place(n_exp)
        p.greet()
        d = Dispatch(p, send, held, sems[0:2], sems[2:4])
        d.own()

        d.start_seq(0)
        for step in range(1, n_exp):
            d.start_exp(step)

        def loop(t, carry):
            @pl.when(t < n_exp)
            def _():
                d.start_seq(t)

            d.relay(t - 1)

            @pl.when(t >= 2)
            def _():
                d.arrived(t - 2)

            return carry

        lax.fori_loop(1, n_exp + 1, loop, 0)
        d.arrived(n_exp - 1)
        d.drain()

    return pl.pallas_call(
        kernel,
        out_shape=jax.ShapeDtypeStruct((n_exp, 4, cap, width), BF16),
        in_specs=[pl.BlockSpec(memory_space=pltpu.VMEM)],
        out_specs=pl.BlockSpec(memory_space=pltpu.VMEM),
        scratch_shapes=Dispatch.scratch(n_exp),
        compiler_params=pltpu.CompilerParams(
            collective_id=collective_id, has_side_effects=True, vmem_limit_bytes=VMEM_LIMIT
        ),
        name="dispatch_rows",
    )(send)


def combine_rows(part, bias, collective_id):
    n_exp, _, cap, width = part.shape

    def kernel(part_in, bias_ref, back, part, load_sem, passing, landing, total, *sems):
        p = Place(n_exp)

        def load(step):
            return pltpu.make_async_copy(part_in.at[step], part.at[step], load_sem.at[step])

        for step in range(n_exp):
            load(step).start()
        p.greet()
        c = Combine(p, part, passing, landing, total, back, sems[0:2], sems[2:4], n_exp)
        bias_row = bias_ref[...].astype(F32)

        def loop(t, carry):
            @pl.when(t < n_exp)
            def _():
                load(t).wait()
                c.start(t)

            @pl.when((t >= 2) & (t < n_exp + 2))
            def _():
                c.pass_on(t - 2)

            @pl.when(t >= 4)
            def _():
                c.finish(t - 4, bias_row)

            return carry

        lax.fori_loop(0, n_exp + 4, loop, 0)
        c.drain()

    return pl.pallas_call(
        kernel,
        out_shape=jax.ShapeDtypeStruct((n_exp, cap, width), BF16),
        in_specs=[pl.BlockSpec(memory_space=pl.ANY), pl.BlockSpec(memory_space=pltpu.VMEM)],
        out_specs=pl.BlockSpec(memory_space=pltpu.VMEM),
        scratch_shapes=[
            pltpu.VMEM((n_exp, 4, cap, width), BF16),
            pltpu.SemaphoreType.DMA((n_exp,)),
        ]
        + Combine.scratch(n_exp, cap, width),
        compiler_params=pltpu.CompilerParams(
            collective_id=collective_id, has_side_effects=True, vmem_limit_bytes=VMEM_LIMIT
        ),
        name="combine_rows",
    )(part, bias)


GELU_A = math.sqrt(2.0 / math.pi)
GELU_B = 0.044715


def ffn_both(send, cot_rows, w_up, b_up, w_down, collective_id):
    n_exp, cap, width = send.shape
    hidden = w_up.shape[1]
    rows = 4 * cap
    block = min(512, hidden)
    slots = 4

    def kernel(send, cot_in, wu_in, bu_ref, wd_in, back, dwu_out, dwd_out, dbu_out, gsum_out, ffn_out,
               held, cot, wu, wd, part, ffn, dwu, dwd, local_sems, ffn_sems, out_sems, *rest):
        p = Place(n_exp)
        loads = [
            pltpu.make_async_copy(wu_in, wu, local_sems.at[0]),
            pltpu.make_async_copy(wd_in, wd, local_sems.at[1]),
            pltpu.make_async_copy(cot_in, cot, local_sems.at[2]),
        ]
        for c in loads:
            c.start()
        p.greet()
        d = Dispatch(p, send, held, rest[0:2], rest[2:4])
        passing, landing, total = rest[4:7]
        c = Combine(p, part, passing, landing, total, back, rest[7:9], rest[9:11], slots)
        d.own()
        d.start_seq(0)
        for step in range(1, n_exp):
            d.start_exp(step)
        dwu[...] = jnp.zeros_like(dwu)
        dwd[...] = jnp.zeros_like(dwd)
        dbu_out[...] = jnp.zeros_like(dbu_out)
        gsum_out[...] = jnp.zeros_like(gsum_out)

        def store(step):
            slot = lax.rem(step, 2)
            return pltpu.make_async_copy(ffn.at[slot], ffn_out.at[step], ffn_sems.at[slot])

        def compute(step):
            x = held[step].reshape(rows, width)
            g = cot[step].reshape(rows, width)
            gsum_out[...] += jnp.sum(g.astype(F32), axis=0, keepdims=True)
            y = jnp.zeros((rows, width), F32)
            gx = jnp.zeros((rows, width), F32)
            for k in range(hidden // block):
                cols = pl.ds(k * block, block)
                wu_k, wd_k = wu[:, cols], wd[cols, :]
                pre = dot(x, wu_k) + bu_ref[:, cols].astype(F32)
                g_act = dot(g, wd_k, ((1,), (1,)))
                sq = pre * pre
                th = jnp.tanh(GELU_A * pre * (1.0 + GELU_B * sq))
                half = 0.5 * (1.0 + th)
                act = (pre * half).astype(BF16)
                slope = half + 0.5 * pre * (1.0 - th * th) * (GELU_A * (1.0 + 3.0 * GELU_B * sq))
                g_pre32 = g_act * slope
                g_pre = g_pre32.astype(BF16)
                dbu_out[:, cols] += jnp.sum(g_pre.astype(F32), axis=0, keepdims=True)
                y = y + dot(act, wd_k)
                gx = gx + dot(g_pre, wu_k, ((1,), (1,)))
                dwu[:, cols] += dot(x, g_pre, ((0,), (0,)))
                dwd[cols, :] += dot(act, g, ((0,), (0,)))
            part[lax.rem(step, slots)] = gx.astype(BF16).reshape(4, cap, width)

            @pl.when(step >= 2)
            def _():
                store(step - 2).wait()

            ffn[lax.rem(step, 2)] = y.astype(BF16).reshape(4, cap, width)
            store(step).start()

        def loop(t, carry):
            @pl.when(t < n_exp)
            def _():
                d.start_seq(t)

            @pl.when(t <= n_exp)
            def _():
                d.relay(t - 1)

            @pl.when((t >= 3) & (t <= n_exp + 2))
            def _():
                c.pass_on(t - 3)

            @pl.when(t >= 4)
            def _():
                c.finish(t - 4)

            @pl.when(t == 2)
            def _():
                for load in loads:
                    load.wait()

            @pl.when((t >= 2) & (t <= n_exp + 1))
            def _():
                d.arrived(t - 2)
                compute(t - 2)
                c.start(t - 2)

            @pl.when(t == n_exp + 1)
            def _():
                pltpu.make_async_copy(dwu, dwu_out, out_sems.at[0]).start()
                pltpu.make_async_copy(dwd, dwd_out, out_sems.at[1]).start()

            return carry

        lax.fori_loop(1, n_exp + 4, loop, 0)
        d.drain()
        c.drain()
        store(n_exp - 2).wait()
        store(n_exp - 1).wait()
        pltpu.make_async_copy(dwu, dwu_out, out_sems.at[0]).wait()
        pltpu.make_async_copy(dwd, dwd_out, out_sems.at[1]).wait()

    vmem = pl.BlockSpec(memory_space=pltpu.VMEM)
    hbm = pl.BlockSpec(memory_space=pl.ANY)
    return pl.pallas_call(
        kernel,
        out_shape=[
            jax.ShapeDtypeStruct((n_exp, cap, width), BF16),
            jax.ShapeDtypeStruct((width, hidden), F32),
            jax.ShapeDtypeStruct((hidden, width), F32),
            jax.ShapeDtypeStruct((1, hidden), F32),
            jax.ShapeDtypeStruct((1, width), F32),
            jax.ShapeDtypeStruct((n_exp, 4, cap, width), BF16),
        ],
        in_specs=[vmem, hbm, hbm, vmem, hbm],
        out_specs=[vmem, hbm, hbm, vmem, vmem, hbm],
        scratch_shapes=[
            pltpu.VMEM((n_exp, 4, cap, width), BF16),
            pltpu.VMEM((n_exp, 4, cap, width), BF16),
            pltpu.VMEM((width, hidden), BF16),
            pltpu.VMEM((hidden, width), BF16),
            pltpu.VMEM((slots, 4, cap, width), BF16),
            pltpu.VMEM((2, 4, cap, width), BF16),
            pltpu.VMEM((width, hidden), F32),
            pltpu.VMEM((hidden, width), F32),
            pltpu.SemaphoreType.DMA((3,)),
            pltpu.SemaphoreType.DMA((2,)),
            pltpu.SemaphoreType.DMA((2,)),
        ]
        + Dispatch.scratch(n_exp)
        + Combine.scratch(n_exp, cap, width),
        compiler_params=pltpu.CompilerParams(
            collective_id=collective_id, has_side_effects=True, vmem_limit_bytes=VMEM_LIMIT
        ),
        name="ffn_both",
    )(send, cot_rows, w_up, b_up, w_down)


def shards(
    tokens,
    lengths,
    expert_ids,
    ln1_gain,
    ln1_bias,
    w_query,
    b_query,
    w_key,
    w_value,
    b_value,
    w_out,
    b_out,
    ln2_gain,
    ln2_bias,
    w_up,
    b_up,
    w_down,
    b_down,
    cotangent,
):
    tok_rows = tokens.shape[1]
    width = tokens.shape[2]
    seq_size = lax.axis_size("seq")
    exp_size = lax.axis_size("exp")
    seq_rank = lax.axis_index("seq")
    seq_ends = jnp.cumsum(lengths[0])
    own_pos = seq_rank * tok_rows + jnp.arange(tok_rows, dtype=jnp.int32)
    own_seg = segment_ids(own_pos, seq_ends)
    inputs = tokens[0].astype(jnp.float32)
    gain_one = ln1_gain.astype(jnp.float32)
    bias_one = ln1_bias.astype(jnp.float32)
    gain_two = ln2_gain.astype(jnp.float32)
    bias_two = ln2_bias.astype(jnp.float32)
    normed_one_low = norm_layer(inputs, gain_one, bias_one).astype(jnp.bfloat16)
    query_low = (project(normed_one_low, w_query) + b_query.astype(jnp.float32)).astype(
        jnp.bfloat16
    )
    keys_low = project(normed_one_low, w_key).astype(jnp.bfloat16)
    values_low = (project(normed_one_low, w_value) + b_value.astype(jnp.float32)).astype(
        jnp.bfloat16
    )
    query_heads = query_low.reshape(tok_rows, HEADS, HEAD_DIM)
    initial = (
        jnp.full((HEADS, tok_rows), MASKED_SCORE, jnp.float32),
        jnp.zeros((HEADS, tok_rows), jnp.float32),
        jnp.zeros((HEADS, tok_rows, HEAD_DIM), jnp.float32),
    )
    key_piece = lax.all_gather(keys_low, "seq", axis=0, tiled=True)
    value_piece = lax.all_gather(values_low, "seq", axis=0, tiled=True)
    piece_len = key_piece.shape[0]
    fold_block_len = math.gcd(piece_len, 512)
    block_count = piece_len // fold_block_len
    key_blocks = key_piece.reshape(block_count, fold_block_len, HEADS, HEAD_DIM)
    value_blocks = value_piece.reshape(block_count, fold_block_len, HEADS, HEAD_DIM)
    offsets = jnp.arange(block_count, dtype=jnp.int32) * fold_block_len

    def block_step(state_now, packed):
        row_max, row_total, accumulated = state_now
        key_blk, value_blk, offset = packed
        key_pos = offset + jnp.arange(fold_block_len, dtype=jnp.int32)
        allowed = visible_pairs(own_pos, own_seg, key_pos, segment_ids(key_pos, seq_ends))
        scores = (
            jnp.einsum("qhd,khd->hqk", query_heads, key_blk, preferred_element_type=jnp.float32)
            * SCORE_SCALE
        )
        masked = jnp.where(allowed, scores, MASKED_SCORE)
        new_max = jnp.maximum(row_max, jnp.max(masked, axis=-1))
        weights = jnp.where(allowed, jnp.exp(masked - new_max[..., None]), 0.0)
        factor = jnp.exp(row_max - new_max)
        row_total = row_total * factor + jnp.sum(weights, axis=-1)
        accumulated = accumulated * factor[..., None] + jnp.einsum(
            "hqk,khd->hqd",
            weights.astype(jnp.bfloat16),
            value_blk,
            preferred_element_type=jnp.float32,
        )
        return ((new_max, row_total, accumulated), None)

    result, _ = lax.scan(block_step, initial, (key_blocks, value_blocks, offsets))
    row_max, row_total, accumulated = result
    attn_heads = accumulated / row_total[..., None]
    attn_low = jnp.transpose(attn_heads, (1, 0, 2)).reshape(tok_rows, width).astype(jnp.bfloat16)
    resid = inputs + project(attn_low, w_out) + b_out.astype(jnp.float32)
    normed_two_low = norm_layer(resid, gain_two, bias_two).astype(jnp.bfloat16)
    experts = exp_size * w_up.shape[0]
    capacity = 2 * tok_rows // experts
    expert_of = expert_ids[0, :, 0]
    onehot = (expert_of[:, None] == jnp.arange(experts, dtype=jnp.int32)[None, :]).astype(jnp.int32)
    slot_of = jnp.sum(onehot * (jnp.cumsum(onehot, axis=0) - onehot), axis=1)
    place_of = expert_of * capacity + slot_of
    pick = (
        place_of[:, None] == jnp.arange(experts * capacity, dtype=jnp.int32)[None, :]
    ).astype(jnp.bfloat16)

    def scatter_rows(rows):
        laid = jnp.einsum("ts,td->sd", pick, rows, preferred_element_type=jnp.float32)
        return laid.astype(jnp.bfloat16).reshape(experts, capacity, width)

    def collect_rows(laid):
        return project(pick, laid.reshape(experts * capacity, width))

    cot_rows = dispatch_rows(scatter_rows(cotangent[0]), 0)
    grad_back, grad_w_up, grad_w_down, grad_b_up, bias_full, ffn_part = ffn_both(
        scatter_rows(normed_two_low), cot_rows, w_up[0], b_up, w_down[0], 1
    )
    returned = combine_rows(ffn_part, b_down, 2)
    piece_width = width // seq_size
    grad_b_up = grad_b_up[0]
    grad_b_down = lax.dynamic_slice_in_dim(bias_full[0], seq_rank * piece_width, piece_width, 0)
    ffn_rows = collect_rows(returned)
    output = (resid + ffn_rows).astype(jnp.bfloat16)
    grad_normed_two = collect_rows(grad_back)
    _, norm_two_back = jax.vjp(norm_layer, resid, gain_two, bias_two)
    grad_resid_norm, grad_gain_two, grad_bias_two = norm_two_back(grad_normed_two)
    grad_resid = cotangent[0].astype(jnp.float32) + grad_resid_norm
    grad_out_low = grad_resid.astype(jnp.bfloat16)
    grad_w_out = jnp.einsum("qa,qd->ad", attn_low, grad_out_low, preferred_element_type=jnp.float32)
    grad_b_out = jnp.sum(grad_out_low.astype(jnp.float32), axis=0)
    grad_attn_low = jnp.einsum(
        "qd,ad->qa", grad_out_low, w_out, preferred_element_type=jnp.float32
    ).astype(jnp.bfloat16)
    grad_attn_heads = grad_attn_low.reshape(tok_rows, HEADS, HEAD_DIM)
    delta = jnp.sum(
        jnp.transpose(grad_attn_heads.astype(jnp.float32), (1, 0, 2)) * attn_heads, axis=-1
    )
    whole_keys, whole_values = (
        lax.all_gather(keys_low, "seq", axis=0, tiled=True),
        lax.all_gather(values_low, "seq", axis=0, tiled=True),
    )
    group_len = whole_keys.shape[0]
    block_len = math.gcd(group_len, 512)
    block_count = group_len // block_len

    def back_step(grad_query, packed):
        key_blk, value_blk, offset = packed
        key_pos = offset + jnp.arange(block_len, dtype=jnp.int32)
        allowed = visible_pairs(own_pos, own_seg, key_pos, segment_ids(key_pos, seq_ends))
        scores = (
            jnp.einsum("qhd,khd->hqk", query_heads, key_blk, preferred_element_type=jnp.float32)
            * SCORE_SCALE
        )
        masked = jnp.where(allowed, scores, MASKED_SCORE)
        probabilities = (
            jnp.where(allowed, jnp.exp(masked - row_max[..., None]), 0.0) / row_total[..., None]
        )
        probs_low = probabilities.astype(jnp.bfloat16)
        grad_probs = jnp.einsum(
            "qhd,khd->hqk", grad_attn_heads, value_blk, preferred_element_type=jnp.float32
        )
        grad_scores = (probabilities * (grad_probs - delta[..., None])).astype(jnp.bfloat16)
        grad_query = (
            grad_query
            + jnp.einsum("hqk,khd->qhd", grad_scores, key_blk, preferred_element_type=jnp.float32)
            * SCORE_SCALE
        )
        grad_key_blk = (
            jnp.einsum("hqk,qhd->khd", grad_scores, query_heads, preferred_element_type=jnp.float32)
            * SCORE_SCALE
        )
        grad_value_blk = jnp.einsum(
            "hqk,qhd->khd", probs_low, grad_attn_heads, preferred_element_type=jnp.float32
        )
        return (grad_query, (grad_key_blk, grad_value_blk))

    block_offsets = jnp.arange(block_count, dtype=jnp.int32) * block_len
    grad_query, key_value_parts = lax.scan(
        back_step,
        jnp.zeros((tok_rows, HEADS, HEAD_DIM), jnp.float32),
        (
            whole_keys.reshape(block_count, block_len, HEADS, HEAD_DIM),
            whole_values.reshape(block_count, block_len, HEADS, HEAD_DIM),
            block_offsets,
        ),
    )
    grad_keys, grad_values = (
        lax.psum_scatter(
            key_value_parts[0].reshape(group_len, width).astype(jnp.bfloat16),
            "seq",
            scatter_dimension=0,
            tiled=True,
        ).astype(jnp.float32),
        lax.psum_scatter(
            key_value_parts[1].reshape(group_len, width).astype(jnp.bfloat16),
            "seq",
            scatter_dimension=0,
            tiled=True,
        ).astype(jnp.float32),
    )
    grad_query_low = grad_query.reshape(tok_rows, width).astype(jnp.bfloat16)
    grad_keys_low = grad_keys.astype(jnp.bfloat16)
    grad_values_low = grad_values.astype(jnp.bfloat16)
    grad_w_query = jnp.einsum(
        "qa,qd->ad", normed_one_low, grad_query_low, preferred_element_type=jnp.float32
    )
    grad_b_query = jnp.sum(grad_query_low.astype(jnp.float32), axis=0)
    grad_w_key = jnp.einsum(
        "qa,qd->ad", normed_one_low, grad_keys_low, preferred_element_type=jnp.float32
    )
    grad_w_value = jnp.einsum(
        "qa,qd->ad", normed_one_low, grad_values_low, preferred_element_type=jnp.float32
    )
    grad_b_value = jnp.sum(grad_values_low.astype(jnp.float32), axis=0)
    grad_normed_one = (
        (
            jnp.einsum("qd,ad->qa", grad_query_low, w_query, preferred_element_type=jnp.float32)
            + jnp.einsum("qd,ad->qa", grad_keys_low, w_key, preferred_element_type=jnp.float32)
            + jnp.einsum("qd,ad->qa", grad_values_low, w_value, preferred_element_type=jnp.float32)
        )
        .astype(jnp.bfloat16)
        .astype(jnp.float32)
    )
    _, norm_one_back = jax.vjp(norm_layer, inputs, gain_one, bias_one)
    grad_in_norm, grad_gain_one, grad_bias_one = norm_one_back(grad_normed_one)
    input_grad = grad_resid + grad_in_norm
    summed = lax.psum(
        (
            grad_gain_one,
            grad_bias_one,
            grad_w_query,
            grad_b_query,
            grad_w_key,
            grad_w_value,
            grad_b_value,
            grad_w_out,
            grad_b_out,
            grad_gain_two,
            grad_bias_two,
        ),
        ("seq", "exp"),
    )
    return (
        output[None],
        input_grad[None],
        summed[0],
        summed[1],
        summed[2],
        summed[3],
        summed[4],
        summed[5],
        summed[6],
        summed[7],
        summed[8],
        summed[9],
        summed[10],
        grad_w_up[None],
        grad_b_up[None],
        grad_w_down[None],
        grad_b_down[None],
    )


def solution(mesh):
    placed = (
        P("exp", "seq", None),
        P("exp", None),
        P("exp", "seq", None),
        P(),
        P(),
        P(),
        P(),
        P(),
        P(),
        P(),
        P(),
        P(),
        P(),
        P(),
        P("exp", None, "seq"),
        P("exp", "seq"),
        P("exp", "seq", None),
        P("exp", None),
        P("exp", "seq", None),
    )
    return jax.shard_map(
        shards,
        mesh=mesh,
        in_specs=placed,
        out_specs=(
            P("exp", "seq", None),
            P("exp", "seq", None),
            P(),
            P(),
            P(),
            P(),
            P(),
            P(),
            P(),
            P(),
            P(),
            P(),
            P(),
            P("exp", None, "seq"),
            P("exp", "seq"),
            P("exp", "seq", None),
            P("exp", "seq"),
        ),
        check_vma=False,
    )
```

```python
import functools
import math

import jax
import jax.numpy as jnp
from jax import lax
from jax.experimental import pallas as pl
from jax.experimental.pallas import tpu as pltpu
from jax.sharding import PartitionSpec as P

MESH = pl.DeviceIdType.MESH
F32 = jnp.float32
BF16 = jnp.bfloat16
VMEM_LIMIT = 60 * 2**20


def dot(a, b, dims=((1,), (0,))):
    return lax.dot_general(a, b, (dims, ((), ())), preferred_element_type=F32)


class Place:
    def __init__(self, n_exp):
        self.n_exp = n_exp
        self.s = lax.axis_index("seq")
        self.e = lax.axis_index("exp")
        low = lax.rem(self.s, 2)
        high = lax.div(self.s, 2)
        self.near = high * 2 + (1 - low)
        self.far = (1 - high) * 2 + low
        self.diag = (1 - high) * 2 + (1 - low)
        self.core = lax.rem(self.e, 2)
        self.chip = lax.div(self.e, 2)

    def peer(self, step, way):
        chips = self.n_exp // 2
        hop = lax.div(step, 2)
        if chips == 4:
            hop = hop + lax.div(hop, 2) * (5 - 2 * hop)
        chip = lax.rem(self.chip + way * hop + chips, chips)
        return chip * 2 + lax.rem(self.core + step, 2)

    def greet(self, diag=False):
        barrier = pltpu.get_barrier_semaphore()
        others = (self.near, self.far, self.diag) if diag else (self.near, self.far)
        for other in others:
            pl.semaphore_signal(barrier, inc=1, device_id=(other, self.e), device_id_type=MESH)

        def tell(step, carry):
            pl.semaphore_signal(
                barrier, inc=1, device_id=(self.s, self.peer(step, 1)), device_id_type=MESH
            )
            return carry

        lax.fori_loop(1, self.n_exp, tell, 0)
        pl.semaphore_wait(barrier, len(others) + self.n_exp - 1)

    def to_seq(self, src, dst, send_sem, recv_sem, other):
        return pltpu.make_async_remote_copy(
            src_ref=src, dst_ref=dst, send_sem=send_sem, recv_sem=recv_sem,
            device_id=(other, self.e), device_id_type=MESH,
        )

    def to_exp(self, src, dst, send_sem, recv_sem, other):
        return pltpu.make_async_remote_copy(
            src_ref=src, dst_ref=dst, send_sem=send_sem, recv_sem=recv_sem,
            device_id=(self.s, other), device_id_type=MESH,
        )


class Dispatch:
    def __init__(self, place, send, held, exp_sems, seq_sems):
        self.place, self.send, self.held = place, send, held
        self.exp_send, self.exp_recv = exp_sems
        self.seq_send, self.seq_recv = seq_sems
        self.cap = send.shape[1]

    @staticmethod
    def scratch(n_exp):
        return [
            pltpu.SemaphoreType.DMA((n_exp,)),
            pltpu.SemaphoreType.DMA((n_exp,)),
            pltpu.SemaphoreType.DMA((n_exp, 6)),
            pltpu.SemaphoreType.DMA((n_exp, 6)),
        ]

    def _exp(self, step):
        p = self.place
        other = p.peer(step, -1)
        return p.to_exp(
            self.send.at[other], self.held.at[step, p.s], self.exp_send.at[step], self.exp_recv.at[step], other
        )

    def _seq(self, step, owner, half, lane, other):
        p = self.place
        rows = pl.ds(half * (self.cap // 2), self.cap // 2)
        part = self.held.at[step, owner, rows]
        return p.to_seq(part, part, self.seq_send.at[step, lane], self.seq_recv.at[step, lane], other)

    def copies(self, step, lanes=range(6)):
        p = self.place
        spec = (
            (p.s, 0, p.near),
            (p.s, 1, p.far),
            (p.s, 1, p.near),
            (p.s, 0, p.far),
            (p.near, 0, p.far),
            (p.far, 1, p.near),
        )
        return [self._seq(step, spec[n][0], spec[n][1], n, spec[n][2]) for n in lanes]

    def start_exp(self, step):
        self._exp(step).start()

    def own(self):
        p = self.place
        self.held[0, p.s] = self.send[p.e]

    def start_seq(self, step):
        @pl.when(step > 0)
        def _():
            self._exp(step).wait_recv()

        for c in self.copies(step, range(4)):
            c.start()

    def relay(self, step):
        for c, out in zip(self.copies(step, (0, 1)), self.copies(step, (4, 5))):
            c.wait_recv()
            out.start()

    def arrived(self, step):
        for c in self.copies(step, range(2, 6)):
            c.wait_recv()

    def drain(self):
        def body(step, carry):
            for c in self.copies(step):
                c.wait_send()

            @pl.when(step > 0)
            def _():
                self._exp(step).wait_send()

            return carry

        lax.fori_loop(0, self.place.n_exp, body, 0)


class Combine:
    def __init__(self, place, part, passing, landing, total, back, seq_sems, exp_sems, slots):
        self.place, self.part, self.passing, self.landing = place, part, passing, landing
        self.total, self.back, self.slots = total, back, slots
        self.seq_send, self.seq_recv = seq_sems
        self.exp_send, self.exp_recv = exp_sems
        self.half = part.shape[2] // 2

    @staticmethod
    def scratch(n_exp, cap, width):
        return [
            pltpu.VMEM((n_exp, 2, cap // 2, width), BF16),
            pltpu.VMEM((n_exp, 4, cap // 2, width), BF16),
            pltpu.VMEM((n_exp, cap, width), BF16),
            pltpu.SemaphoreType.DMA((n_exp, 6)),
            pltpu.SemaphoreType.DMA((n_exp, 6)),
            pltpu.SemaphoreType.DMA((n_exp,)),
            pltpu.SemaphoreType.DMA((n_exp,)),
        ]

    def _slot(self, step):
        return lax.rem(step, self.slots)

    def _piece(self, step, owner, half):
        return self.part.at[self._slot(step), owner, pl.ds(half * self.half, self.half)]

    def _seq(self, src, dst, step, lane, other):
        return self.place.to_seq(
            src, dst, self.seq_send.at[step, lane], self.seq_recv.at[step, lane], other
        )

    def copies(self, step, lanes=range(6)):
        p = self.place
        spec = (
            (p.diag, 0, self.passing, 0, p.near),
            (p.diag, 1, self.passing, 1, p.far),
            (p.near, 0, self.landing, 0, p.near),
            (p.far, 1, self.landing, 3, p.far),
            (p.far, 0, self.landing, 2, p.far),
            (p.near, 1, self.landing, 1, p.near),
        )
        made = []
        for n in lanes:
            owner, half, buffer, at, other = spec[n]
            made.append(self._seq(self._piece(step, owner, half), buffer.at[step, at], step, n, other))
        return made

    def start(self, step):
        for c in self.copies(step, range(4)):
            c.start()

    def pass_on(self, step):
        p = self.place
        slot = self._slot(step)
        came, out = self.copies(step, (0, 1)), self.copies(step, (4, 5))
        for n, owner in enumerate((p.far, p.near)):
            rows = pl.ds(n * self.half, self.half)
            came[n].wait_recv()
            self.part[slot, owner, rows] = (
                self.part[slot, owner, rows].astype(F32) + self.passing[step, n].astype(F32)
            ).astype(BF16)
            out[n].start()

    def _exp(self, step):
        p = self.place
        other = p.peer(step, 1)
        return p.to_exp(
            self.total.at[step], self.back.at[p.e], self.exp_send.at[step], self.exp_recv.at[step], other
        )

    def arrived(self, step):
        copies = self.copies(step)
        for c in copies[2:]:
            c.wait_recv()
        for c in copies:
            c.wait_send()

    def summed(self, step, half):
        rows = pl.ds(half * self.half, self.half)
        return (
            self.part[self._slot(step), self.place.s, rows].astype(F32)
            + self.landing[step, half].astype(F32)
            + self.landing[step, 2 + half].astype(F32)
        )

    def finish(self, step, bias=None):
        p = self.place
        self.arrived(step)
        for half in range(2):
            value = self.summed(step, half)
            if bias is not None:
                value = value + bias
            self.total[step, pl.ds(half * self.half, self.half)] = value.astype(BF16)

        @pl.when(step > 0)
        def _():
            self._exp(step).start()

        @pl.when(step == 0)
        def _():
            self.back[p.e] = self.total[0]

    def drain(self):
        p = self.place

        def body(step, carry):
            c = self._exp(step)
            c.wait_send()
            c.wait_recv()
            return carry

        lax.fori_loop(1, p.n_exp, body, 0)


GELU_A = math.sqrt(2.0 / math.pi)
GELU_B = 0.044715


def ffn_both(send, cot_rows, w_up, b_up, w_down, collective_id):
    n_exp, cap, width = send.shape
    hidden = w_up.shape[1]
    rows = 4 * cap
    block = min(512, hidden)
    slots = 4

    def kernel(send, cot_in, wu_in, bu_ref, wd_in, back, dwu_out, dwd_out, dbu_out, gsum_out, ffn_out,
               held, cot, wu, wd, part, ffn, dwu, dwd, local_sems, ffn_sems, out_sems, *rest):
        p = Place(n_exp)
        loads = [
            pltpu.make_async_copy(wu_in, wu, local_sems.at[0]),
            pltpu.make_async_copy(wd_in, wd, local_sems.at[1]),
            pltpu.make_async_copy(cot_in, cot, local_sems.at[2]),
        ]
        for c in loads:
            c.start()
        p.greet()
        d = Dispatch(p, send, held, rest[0:2], rest[2:4])
        passing, landing, total = rest[4:7]
        c = Combine(p, part, passing, landing, total, back, rest[7:9], rest[9:11], slots)
        d.own()
        d.start_seq(0)
        for step in range(1, n_exp):
            d.start_exp(step)
        dwu[...] = jnp.zeros_like(dwu)
        dwd[...] = jnp.zeros_like(dwd)
        dbu_out[...] = jnp.zeros_like(dbu_out)
        gsum_out[...] = jnp.zeros_like(gsum_out)

        def store(step):
            slot = lax.rem(step, 2)
            return pltpu.make_async_copy(ffn.at[slot], ffn_out.at[step], ffn_sems.at[slot])

        def compute(step):
            x = held[step].reshape(rows, width)
            g = cot[step].reshape(rows, width)
            gsum_out[...] += jnp.sum(g.astype(F32), axis=0, keepdims=True)
            y = jnp.zeros((rows, width), F32)
            gx = jnp.zeros((rows, width), F32)
            for k in range(hidden // block):
                cols = pl.ds(k * block, block)
                wu_k, wd_k = wu[:, cols], wd[cols, :]
                pre = dot(x, wu_k) + bu_ref[:, cols].astype(F32)
                g_act = dot(g, wd_k, ((1,), (1,)))
                sq = pre * pre
                th = jnp.tanh(GELU_A * pre * (1.0 + GELU_B * sq))
                half = 0.5 * (1.0 + th)
                act = (pre * half).astype(BF16)
                slope = half + 0.5 * pre * (1.0 - th * th) * (GELU_A * (1.0 + 3.0 * GELU_B * sq))
                g_pre32 = g_act * slope
                g_pre = g_pre32.astype(BF16)
                dbu_out[:, cols] += jnp.sum(g_pre.astype(F32), axis=0, keepdims=True)
                y = y + dot(act, wd_k)
                gx = gx + dot(g_pre, wu_k, ((1,), (1,)))
                dwu[:, cols] += dot(x, g_pre, ((0,), (0,)))
                dwd[cols, :] += dot(act, g, ((0,), (0,)))
            part[lax.rem(step, slots)] = gx.astype(BF16).reshape(4, cap, width)

            @pl.when(step >= 2)
            def _():
                store(step - 2).wait()

            ffn[lax.rem(step, 2)] = y.astype(BF16).reshape(4, cap, width)
            store(step).start()

        def loop(t, carry):
            @pl.when(t < n_exp)
            def _():
                d.start_seq(t)

            @pl.when(t <= n_exp)
            def _():
                d.relay(t - 1)

            @pl.when((t >= 3) & (t <= n_exp + 2))
            def _():
                c.pass_on(t - 3)

            @pl.when(t >= 4)
            def _():
                c.finish(t - 4)

            @pl.when(t == 2)
            def _():
                for load in loads:
                    load.wait()

            @pl.when((t >= 2) & (t <= n_exp + 1))
            def _():
                d.arrived(t - 2)
                compute(t - 2)
                c.start(t - 2)

            @pl.when(t == n_exp + 1)
            def _():
                pltpu.make_async_copy(dwu, dwu_out, out_sems.at[0]).start()
                pltpu.make_async_copy(dwd, dwd_out, out_sems.at[1]).start()

            return carry

        lax.fori_loop(1, n_exp + 4, loop, 0)
        d.drain()
        c.drain()
        store(n_exp - 2).wait()
        store(n_exp - 1).wait()
        pltpu.make_async_copy(dwu, dwu_out, out_sems.at[0]).wait()
        pltpu.make_async_copy(dwd, dwd_out, out_sems.at[1]).wait()

    vmem = pl.BlockSpec(memory_space=pltpu.VMEM)
    hbm = pl.BlockSpec(memory_space=pl.ANY)
    return pl.pallas_call(
        kernel,
        out_shape=[
            jax.ShapeDtypeStruct((n_exp, cap, width), BF16),
            jax.ShapeDtypeStruct((width, hidden), F32),
            jax.ShapeDtypeStruct((hidden, width), F32),
            jax.ShapeDtypeStruct((1, hidden), F32),
            jax.ShapeDtypeStruct((1, width), F32),
            jax.ShapeDtypeStruct((n_exp, 4, cap, width), BF16),
        ],
        in_specs=[vmem, hbm, hbm, vmem, hbm],
        out_specs=[vmem, hbm, hbm, vmem, vmem, hbm],
        scratch_shapes=[
            pltpu.VMEM((n_exp, 4, cap, width), BF16),
            pltpu.VMEM((n_exp, 4, cap, width), BF16),
            pltpu.VMEM((width, hidden), BF16),
            pltpu.VMEM((hidden, width), BF16),
            pltpu.VMEM((slots, 4, cap, width), BF16),
            pltpu.VMEM((2, 4, cap, width), BF16),
            pltpu.VMEM((width, hidden), F32),
            pltpu.VMEM((hidden, width), F32),
            pltpu.SemaphoreType.DMA((3,)),
            pltpu.SemaphoreType.DMA((2,)),
            pltpu.SemaphoreType.DMA((2,)),
        ]
        + Dispatch.scratch(n_exp)
        + Combine.scratch(n_exp, cap, width),
        compiler_params=pltpu.CompilerParams(
            collective_id=collective_id, has_side_effects=True, vmem_limit_bytes=VMEM_LIMIT
        ),
        name="ffn_both",
    )(send, cot_rows, w_up, b_up, w_down)


EPSILON = 1e-05
SCORE_SCALE = 0.125
MASKED_SCORE = -1e30
HEAD_DIM = 64
HEADS = 16


class Gather:
    def __init__(self, place, held, send_sems, recv_sems):
        self.place, self.held = place, held
        self.send_sems, self.recv_sems = send_sems, recv_sems
        self.half = held.shape[1] // 2

    @staticmethod
    def scratch():
        return [pltpu.SemaphoreType.DMA((6,)), pltpu.SemaphoreType.DMA((6,))]

    def copies(self, lanes=range(6)):
        p = self.place
        spec = (
            (p.s, 0, p.near),
            (p.s, 1, p.far),
            (p.s, 1, p.near),
            (p.s, 0, p.far),
            (p.near, 0, p.far),
            (p.far, 1, p.near),
        )
        made = []
        for n in lanes:
            owner, half, other = spec[n]
            part = self.held.at[owner, pl.ds(half * self.half, self.half)]
            made.append(p.to_seq(part, part, self.send_sems.at[n], self.recv_sems.at[n], other))
        return made

    def start(self):
        for c in self.copies(range(4)):
            c.start()

    def relay(self):
        for c, out in zip(self.copies((0, 1)), self.copies((4, 5))):
            c.wait_recv()
            out.start()

    def wait(self, lanes):
        for c in self.copies(lanes):
            c.wait_recv()

    def drain(self):
        for c in self.copies():
            c.wait_send()


def layer_norm(values, gain, shift):
    center = values - jnp.mean(values, axis=-1, keepdims=True)
    inv_std = lax.rsqrt(jnp.mean(center * center, axis=-1, keepdims=True) + EPSILON)
    xhat = center * inv_std
    return xhat * gain + shift, xhat, inv_std


def norm_back(grad, xhat, inv_std, gain):
    d = grad * gain
    return (
        d - jnp.mean(d, axis=-1, keepdims=True) - xhat * jnp.mean(d * xhat, axis=-1, keepdims=True)
    ) * inv_std


def row_choice(ids, n_exp, cap):
    tokens = ids.shape[0]
    named = (ids == lax.broadcasted_iota(jnp.int32, (tokens, 128), 1)).astype(BF16)
    before = (
        lax.broadcasted_iota(jnp.int32, (tokens, tokens), 1)
        < lax.broadcasted_iota(jnp.int32, (tokens, tokens), 0)
    ).astype(BF16)
    earlier = dot(before, named) * named.astype(F32)
    slot = jnp.sum(earlier, axis=1, keepdims=True).astype(jnp.int32) + ids * cap
    return (slot == lax.broadcasted_iota(jnp.int32, (tokens, n_exp * cap), 1)).astype(BF16)


def segment_of(position, lengths):
    end = jnp.int32(0)
    count = jnp.zeros_like(position)
    for n in range(lengths.shape[1]):
        end = end + lengths[0, n]
        count = count + (position >= end).astype(jnp.int32)
    return count


def head_mask(rows, width, head):
    lane = lax.broadcasted_iota(jnp.int32, (rows, width), 1)
    return (lane >= head * HEAD_DIM) & (lane < (head + 1) * HEAD_DIM)


def front_part(
    tokens, lengths, ids, ln1, w_qkv, b_qkv, w_out, b_out, ln2, cotangent, n_exp, collective_id
):
    tok, width = tokens.shape
    n_seq = 4
    total = n_seq * tok
    cols = width // n_seq
    heads = cols // HEAD_DIM
    cap = 2 * tok // n_exp
    q_block = 256

    def kernel(tok_ref, len_ref, ids_ref, ln1_ref, wq_in, wk_in, wv_in, bqkv_ref, wo_in, bo_ref, ln2_ref, cot_ref,
               n1_ref, q_ref, k_ref, v_ref, attn_ref, lse_ref, resid_ref, pick_ref, sendn_ref, cotall_ref,
               xall, w_qkv, w_o, sendc, attn_out, attn_in, local_sems, a2a_send, a2a_recv, *rest):
        p = Place(n_exp)
        mine = pl.ds(pl.multiple_of(p.s * cols, cols), cols)
        loads = [
            pltpu.make_async_copy(src.at[:, mine], w_qkv.at[:, pl.ds(n * cols, cols)], local_sems.at[n])
            for n, src in enumerate((wq_in, wk_in, wv_in))
        ]
        load_out = pltpu.make_async_copy(wo_in, w_o, local_sems.at[3])
        for c in loads:
            c.start()
        load_out.start()
        xall[p.s] = tok_ref[...]
        p.greet(diag=True)
        gather = Gather(p, xall, rest[0], rest[1])
        gather.start()
        pick = row_choice(ids_ref[...], n_exp, cap)
        pick_ref[...] = pick
        sendc[...] = dot(pick, cot_ref[...], ((0,), (0,))).astype(BF16).reshape(n_exp, cap, width)
        d = Dispatch(p, sendc, cotall_ref, rest[2:4], rest[4:6])
        for step in range(1, n_exp):
            d.start_exp(step)
        d.own()
        gain1 = ln1_ref[0:1, :].astype(F32)
        bias1 = ln1_ref[1:2, :].astype(F32)
        bq = bqkv_ref[0:1, mine].astype(F32)
        bv = bqkv_ref[1:2, mine].astype(F32)

        def project(owner):
            x = xall[owner].astype(F32)
            normed = layer_norm(x, gain1, bias1)[0].astype(BF16)
            rows = pl.ds(pl.multiple_of(owner * tok, tok), tok)
            n1_ref[rows, :] = normed
            out = dot(normed, w_qkv[...])
            q = (out[:, 0:cols] + bq).astype(BF16)
            q_ref[rows, :] = (q.astype(F32) * SCORE_SCALE).astype(BF16)
            k_ref[rows, :] = out[:, cols : 2 * cols].astype(BF16)
            v_ref[rows, :] = (out[:, 2 * cols :] + bv).astype(BF16)

        for c in loads:
            c.wait()
        project(p.s)
        gather.relay()
        gather.wait((2, 3))
        project(p.near)
        project(p.far)
        gather.wait((4, 5))
        d.start_seq(0)
        project(p.diag)

        background = []
        for t in range(1, n_exp + 2):
            def some(t=t):
                if t < n_exp:
                    d.start_seq(t)
                if t <= n_exp:
                    d.relay(t - 1)
                if t >= 2:
                    d.arrived(t - 2)
            background.append(some)

        def a2a(owner):
            return p.to_seq(
                attn_out.at[owner], attn_in.at[p.s], a2a_send.at[owner], a2a_recv.at[p.s], owner
            )

        def a2a_from(owner):
            return p.to_seq(
                attn_out.at[owner], attn_in.at[owner], a2a_send.at[owner], a2a_recv.at[owner], owner
            )

        for n in reversed(range(total // q_block)):
            seen = (n + 1) * q_block
            rows = pl.ds(n * q_block, q_block)
            q_pos = lax.broadcasted_iota(jnp.int32, (q_block, 1), 0) + n * q_block
            k_pos = lax.broadcasted_iota(jnp.int32, (1, seen), 1)
            allowed = (segment_of(q_pos, len_ref) == segment_of(k_pos, len_ref)) & (k_pos <= q_pos)
            q_rows = q_ref[rows, :]
            acc = jnp.zeros((q_block, cols), F32)
            lse = jnp.zeros((q_block, 128), F32)
            lane = lax.broadcasted_iota(jnp.int32, (q_block, 128), 1)
            for head in range(heads):
                own = head_mask(q_block, cols, head)
                scores = dot(jnp.where(own, q_rows, jnp.zeros_like(q_rows)), k_ref[0:seen, :], ((1,), (1,)))
                scores = jnp.where(allowed, scores, MASKED_SCORE)
                top = jnp.max(scores, axis=1, keepdims=True)
                weights = jnp.exp(scores - top)
                sums = jnp.sum(weights, axis=1, keepdims=True)
                out = dot(weights.astype(BF16), v_ref[0:seen, :]) / sums
                acc = jnp.where(own, out, acc)
                lse = jnp.where(lane == head, top + jnp.log(sums), lse)
            attn_ref[rows, :] = acc
            lse_ref[:, rows] = jnp.transpose(lse)[0:8, :]
            owner, at = (n * q_block) // tok, (n * q_block) % tok
            attn_out[owner, pl.ds(at, q_block)] = acc.astype(BF16)
            if at == 0:

                @pl.when(p.s != owner)
                def _(owner=owner):
                    a2a(owner).start()

                @pl.when(p.s == owner)
                def _(owner=owner):
                    attn_in[owner] = attn_out[owner]

            if background and n % 2 == 1:
                background.pop(0)()
        load_out.wait()
        sums = tok_ref[...].astype(F32) + bo_ref[...].astype(F32)
        for owner in range(n_seq):

            @pl.when(p.s != owner)
            def _(owner=owner):
                a2a_from(owner).wait_recv()

            sums = sums + dot(attn_in[owner], w_o[pl.ds(owner * cols, cols), :])
        resid_ref[...] = sums
        normed_two = layer_norm(sums, ln2_ref[0:1, :].astype(F32), ln2_ref[1:2, :].astype(F32))[0].astype(BF16)
        sendn_ref[...] = dot(pick_ref[...], normed_two, ((0,), (0,))).astype(BF16).reshape(n_exp, cap, width)
        while background:
            background.pop(0)()
        for owner in range(n_seq):

            @pl.when(p.s != owner)
            def _(owner=owner):
                a2a(owner).wait_send()

        gather.drain()
        d.drain()

    vmem = pl.BlockSpec(memory_space=pltpu.VMEM)
    hbm = pl.BlockSpec(memory_space=pl.ANY)
    smem = pl.BlockSpec(memory_space=pltpu.SMEM)
    shape = jax.ShapeDtypeStruct
    return pl.pallas_call(
        kernel,
        out_shape=[
            shape((total, width), BF16),
            shape((total, cols), BF16),
            shape((total, cols), BF16),
            shape((total, cols), BF16),
            shape((total, cols), F32),
            shape((8, total), F32),
            shape((tok, width), F32),
            shape((tok, n_exp * cap), BF16),
            shape((n_exp, cap, width), BF16),
            shape((n_exp, n_seq, cap, width), BF16),
        ],
        in_specs=[vmem, smem, vmem, vmem, hbm, hbm, hbm, vmem, hbm, vmem, vmem, vmem],
        out_specs=[vmem] * 10,
        scratch_shapes=[
            pltpu.VMEM((n_seq, tok, width), BF16),
            pltpu.VMEM((width, 3 * cols), BF16),
            pltpu.VMEM((width, width), BF16),
            pltpu.VMEM((n_exp, cap, width), BF16),
            pltpu.VMEM((n_seq, tok, cols), BF16),
            pltpu.VMEM((n_seq, tok, cols), BF16),
            pltpu.SemaphoreType.DMA((4,)),
            pltpu.SemaphoreType.DMA((n_seq,)),
            pltpu.SemaphoreType.DMA((n_seq,)),
        ]
        + Gather.scratch()
        + Dispatch.scratch(n_exp),
        compiler_params=pltpu.CompilerParams(
            collective_id=collective_id, has_side_effects=True, vmem_limit_bytes=VMEM_LIMIT
        ),
        name="front_part",
    )(tokens, lengths, ids, ln1, *w_qkv, b_qkv, w_out, b_out, ln2, cotangent)


class SumAll:
    def __init__(self, place, src, core_in, mine, chip_in, res, result, local_sem, sems, by_rows):
        self.place, self.src, self.core_in, self.mine = place, src, core_in, mine
        self.chip_in, self.res, self.result, self.local_sem = chip_in, res, result, local_sem
        (self.core_sems, self.rs_send, self.rs_recv, self.ag_send, self.ag_recv,
         self.seq_send, self.seq_recv, self.pair_send, self.pair_recv) = sems
        self.chips = place.n_exp // 2
        self.by_rows = by_rows
        p = place
        self.sibling = p.chip * 2 + (1 - p.core)

    @staticmethod
    def scratch(n_exp, rows, width):
        chips = n_exp // 2
        dma = pltpu.SemaphoreType.DMA
        return [
            pltpu.VMEM((2, chips, rows, width), BF16),
            pltpu.VMEM((chips, rows, width), BF16),
            pltpu.VMEM((chips, rows, width), BF16),
            pltpu.VMEM((chips, rows, width), BF16),
            pltpu.VMEM((rows, width), BF16),
            dma((1,)),
            dma((2,)),
            dma((chips,)),
            dma((chips,)),
            dma((chips,)),
            dma((chips,)),
            dma((chips, 6)),
            dma((chips, 6)),
            dma((chips, 4)),
            dma((chips, 4)),
        ]

    def chip(self, hop):
        return lax.rem(self.place.chip + hop, self.chips)

    def exp(self, hop):
        return self.chip(hop) * 2 + self.place.core

    def _core(self):
        p = self.place
        return p.to_exp(
            self.src.at[1 - p.core], self.core_in, self.core_sems.at[0], self.core_sems.at[1], self.sibling
        )

    def start(self):
        self._core().start()

    def _spread(self, hop):
        p = self.place
        to = self.chip(hop)
        return p.to_exp(
            self.mine.at[to], self.chip_in.at[p.chip], self.rs_send.at[to], self.rs_recv.at[p.chip], self.exp(hop)
        )

    def _spread_from(self, hop):
        p = self.place
        at = self.chip(hop)
        return p.to_exp(
            self.mine.at[at], self.chip_in.at[at], self.rs_send.at[at], self.rs_recv.at[at], self.exp(hop)
        )

    def spread(self):
        p = self.place
        self._core().wait_recv()
        for n in range(self.chips):
            self.mine[n] = (self.src[p.core, n].astype(F32) + self.core_in[n].astype(F32)).astype(BF16)
        for hop in range(1, self.chips):
            self._spread(hop).start()

    def _local(self):
        p = self.place
        return pltpu.make_async_copy(self.res, self.result.at[p.s, p.e], self.local_sem.at[0])

    def _share(self, hop):
        p = self.place
        to = self.chip(hop)
        return p.to_exp(
            self.res, self.result.at[p.s, p.e], self.ag_send.at[to], self.ag_recv.at[p.chip], self.exp(hop)
        )

    def _share_from(self, hop):
        p = self.place
        at = self.chip(hop)
        return p.to_exp(
            self.res, self.result.at[p.s, self.exp(hop)], self.ag_send.at[at], self.ag_recv.at[at], self.exp(hop)
        )

    def _part(self, hop, owner, half):
        where = self.result.at[owner, self.exp(hop)]
        rows, width = where.shape
        if self.by_rows:
            return where.at[pl.ds(half * (rows // 2), rows // 2)]
        return where.at[:, pl.ds(half * (width // 2), width // 2)]

    def copies(self, hop, lanes=range(6)):
        p = self.place
        spec = (
            (p.s, 0, p.near),
            (p.s, 1, p.far),
            (p.s, 1, p.near),
            (p.s, 0, p.far),
            (p.near, 0, p.far),
            (p.far, 1, p.near),
        )
        made = []
        for n in lanes:
            owner, half, other = spec[n]
            part = self._part(hop, owner, half)
            made.append(p.to_seq(part, part, self.seq_send.at[hop, n], self.seq_recv.at[hop, n], other))
        return made

    def _pair(self, hop, n):
        p = self.place
        part = self.result.at[(p.s, p.near, p.far, p.diag)[n], self.exp(hop)]
        return p.to_exp(part, part, self.pair_send.at[hop, n], self.pair_recv.at[hop, n], self.sibling)

    def _pair_from(self, hop, n):
        p = self.place
        owner = (p.s, p.near, p.far, p.diag)[n]
        part = self.result.at[owner, self.chip(hop) * 2 + (1 - p.core)]
        return p.to_exp(part, part, self.pair_send.at[hop, n], self.pair_recv.at[hop, n], self.sibling)

    def reduce(self):
        p = self.place
        for hop in range(1, self.chips):
            self._spread_from(hop).wait_recv()
        total = self.mine[p.chip].astype(F32)
        for hop in range(1, self.chips):
            total = total + self.chip_in[self.chip(hop)].astype(F32)
        self.res[...] = total.astype(BF16)
        self._local().start()
        for hop in range(1, self.chips):
            self._share(hop).start()
        self._local().wait()

    def forward(self, hop):
        if hop > 0:
            self._share_from(hop).wait_recv()
        for c in self.copies(hop, range(4)):
            c.start()
        self._pair(hop, 0).start()

    def relay(self, hop):
        for c, out in zip(self.copies(hop, (0, 1)), self.copies(hop, (4, 5))):
            c.wait_recv()
            out.start()

    def arrived(self, hop):
        for c in self.copies(hop, (2, 3)):
            c.wait_recv()
        self._pair(hop, 1).start()
        self._pair(hop, 2).start()
        for c in self.copies(hop, (4, 5)):
            c.wait_recv()
        self._pair(hop, 3).start()

    def drain(self):
        self._core().wait_send()
        for hop in range(1, self.chips):
            self._spread(hop).wait_send()
            self._share(hop).wait_send()
        for hop in range(self.chips):
            for c in self.copies(hop):
                c.wait_send()
            for n in range(4):
                self._pair(hop, n).wait_send()
                self._pair_from(hop, n).wait_recv()


def back_part(
    grad_back, pick, resid, ln2, cotangent, w_out, q, k, v, attn, lse, n1, w_qkv, tokens, ln1, ffn_part, b_down,
    lengths, collective_id
):
    tok, width = tokens.shape
    n_exp, n_seq, cap, _ = ffn_part.shape
    total = n_seq * tok
    cols = width // n_seq
    heads = cols // HEAD_DIM
    q_block = 256
    rows_w, rows_o = width // n_exp, cols // n_exp
    n_sum = len(SumAll.scratch(n_exp, 16, 128))
    n_comb = len(Combine.scratch(n_exp, cap, width))

    def kernel(gback_ref, pick_ref, resid_ref, ln2_ref, cot_ref, wo_in, q_ref, k_ref, v_ref, attn_ref, lse_ref,
               n1_in, wq_in, wk_in, wv_in, tok_ref, ln1_ref, ffn_in, bd_ref, len_ref,
               out_ref, gin_ref, vec_ref, gw_ref, go_ref,
               gout, gattn, dqkv, dk, dv, n1, w_all, w_o, part, red_part, ret, vec_own, vec_seq, vec_exp,
               local_sems, load_sems, vs_send, vs_recv, ve_send, ve_recv, *rest):
        p = Place(n_exp)
        mine = pl.ds(pl.multiple_of(p.s * cols, cols), cols)
        load_o = pltpu.make_async_copy(wo_in.at[mine, :], w_o, local_sems.at[3])
        loads = [
            pltpu.make_async_copy(src.at[:, mine], w_all.at[:, pl.ds(n * cols, cols)], local_sems.at[n])
            for n, src in enumerate((wq_in, wk_in, wv_in))
        ] + [pltpu.make_async_copy(n1_in, n1, local_sems.at[4])]
        load_o.start()
        for c in loads:
            c.start()

        def load(step):
            return pltpu.make_async_copy(ffn_in.at[step], part.at[step], load_sems.at[step])

        for step in range(n_exp):
            load(step).start()
        p.greet(diag=True)
        at = 0
        gather = Gather(p, gout, rest[0], rest[1])
        at = 2
        comb = Combine(p, part, *rest[at : at + 3], ret, rest[at + 3 : at + 5], rest[at + 5 : at + 7], n_exp)
        at += n_comb
        red = Combine(p, red_part, rest[at], rest[at + 1], None, None, rest[at + 2 : at + 4], (None, None), 1)
        at += 4
        sum_o = SumAll(p, *rest[at : at + 5], go_ref, rest[at + 5], rest[at + 6 : at + n_sum], False)
        at += n_sum
        sum_w = SumAll(p, *rest[at : at + 5], gw_ref, rest[at + 5], rest[at + 6 : at + n_sum], True)
        src_o, src_w = sum_o.src, sum_w.src

        g_two = dot(pick_ref[...], gback_ref[...].reshape(n_exp * cap, width))
        gain2 = ln2_ref[0:1, :].astype(F32)
        _, xhat, inv_std = layer_norm(resid_ref[...], gain2, 0.0)
        g_resid = cot_ref[...].astype(F32) + norm_back(g_two, xhat, inv_std, gain2)
        gin_ref[...] = g_resid
        g_low = g_resid.astype(BF16)
        gout[p.s] = g_low
        gather.start()
        vec_own[...] = jnp.zeros_like(vec_own)
        vec_own[4:5, :] = jnp.sum(g_low.astype(F32), axis=0, keepdims=True)
        vec_own[5:6, :] = jnp.sum(g_two * xhat, axis=0, keepdims=True)
        vec_own[6:7, :] = jnp.sum(g_two, axis=0, keepdims=True)
        load_o.wait()

        def grad_attn(owner):
            rows = pl.ds(pl.multiple_of(owner * tok, tok), tok)
            gattn[rows, :] = dot(gout[owner], w_o[...], ((1,), (1,))).astype(BF16)

        grad_attn(p.s)
        dk[...] = jnp.zeros_like(dk)
        dv[...] = jnp.zeros_like(dv)
        gather.relay()
        gather.wait((2, 3))
        grad_attn(p.near)
        grad_attn(p.far)
        gather.wait((4, 5))
        grad_attn(p.diag)

        g_all = gout[...].reshape(total, width)
        for b in range(cols // 128):
            a_low = attn_ref[:, b * 128 : (b + 1) * 128].astype(BF16)
            got = dot(a_low, g_all, ((0,), (0,))).astype(BF16)
            for n in range(128 // rows_o):
                e = b * (128 // rows_o) + n
                src_o[e % 2, e // 2] = got[n * rows_o : (n + 1) * rows_o]
        sum_o.start()

        bias_row = bd_ref[...].astype(F32)
        background = []
        for t in range(n_exp + 3):

            def some(t=t):
                if t < n_exp:
                    load(t).wait()
                    comb.start(t)
                if 2 <= t < n_exp + 2:
                    comb.pass_on(t - 2)
                if t >= 3:
                    comb.finish(t - 3, bias_row)

            background.append(some)

        def turn(count=1):
            for _ in range(count):
                if background:
                    background.pop(0)()

        blocks = total // q_block
        head_rows = lax.broadcasted_iota(jnp.int32, (8, cols), 0)
        head_lane = lax.broadcasted_iota(jnp.int32, (8, cols), 1)
        per_head = (lax.div(head_lane, HEAD_DIM) == head_rows).astype(F32)
        for n in reversed(range(blocks)):
            turn(1)
            seen = (n + 1) * q_block
            rows = pl.ds(n * q_block, q_block)
            q_pos = lax.broadcasted_iota(jnp.int32, (1, q_block), 1) + n * q_block
            k_pos = lax.broadcasted_iota(jnp.int32, (seen, 1), 0)
            allowed = (segment_of(q_pos, len_ref) == segment_of(k_pos, len_ref)) & (k_pos <= q_pos)
            q_rows, g_rows = q_ref[rows, :], gattn[rows, :]
            delta = lax.dot_general(
                per_head, g_rows.astype(F32) * attn_ref[rows, :], (((1,), (1,)), ((), ())),
                precision=lax.Precision.HIGHEST, preferred_element_type=F32,
            )
            k_seen, v_seen = k_ref[0:seen, :], v_ref[0:seen, :]
            dq = jnp.zeros((q_block, cols), F32)
            dk_new = jnp.zeros((seen, cols), F32)
            dv_new = jnp.zeros((seen, cols), F32)
            for head in range(heads):
                own = head_mask(q_block, cols, head)
                q_own = jnp.where(own, q_rows, jnp.zeros_like(q_rows))
                g_own = jnp.where(own, g_rows, jnp.zeros_like(g_rows))
                scores = dot(k_seen, q_own, ((1,), (1,)))
                probs = jnp.where(allowed, jnp.exp(scores - lse_ref[head : head + 1, rows]), 0.0)
                g_probs = dot(v_seen, g_own, ((1,), (1,)))
                g_scores = (probs * (g_probs - delta[head : head + 1, :])).astype(BF16)
                dk_new = dk_new + dot(g_scores, q_own)
                dv_new = dv_new + dot(probs.astype(BF16), g_own)
                dq = jnp.where(own, dot(g_scores, k_seen, ((0,), (0,))), dq)
            dqkv[rows, 0:cols] = (dq * SCORE_SCALE).astype(BF16)
            dk[0:seen, :] += dk_new
            dv[0:seen, :] += dv_new
            if n == blocks - 2:
                sum_o.spread()
        sum_o.reduce()
        sum_o.forward(0)
        dqkv[:, cols : 2 * cols] = dk[...].astype(BF16)
        dqkv[:, 2 * cols :] = dv[...].astype(BF16)
        for c in loads:
            c.wait()
        d_all = dqkv[...]
        for b in range(width // 128):
            got = dot(n1[:, b * 128 : (b + 1) * 128], d_all, ((0,), (0,))).astype(BF16)
            for n in range(128 // rows_w):
                e = b * (128 // rows_w) + n
                src_w[e % 2, e // 2] = got[n * rows_w : (n + 1) * rows_w]
        sum_w.start()
        for owner in range(n_seq):
            piece = dqkv[pl.ds(owner * tok, tok), :]
            red_part[0, owner] = dot(piece, w_all[...], ((1,), (1,))).astype(BF16)
        red.start(0)
        sum_w.spread()
        vec_own[2:3, mine] = jnp.sum(dqkv[:, 0:cols].astype(F32), axis=0, keepdims=True)
        vec_own[3:4, mine] = jnp.sum(dqkv[:, 2 * cols :].astype(F32), axis=0, keepdims=True)
        chips = n_exp // 2
        turn(1)
        sum_o.relay(0)
        for hop in range(1, chips):
            sum_o.forward(hop)
        turn(1)
        red.pass_on(0)
        turn(1)
        for hop in range(1, chips):
            sum_o.relay(hop)
        turn(1)
        sum_w.reduce()
        sum_w.forward(0)
        red.arrived(0)
        gain1 = ln1_ref[0:1, :].astype(F32)
        half = tok // 2
        for n in range(2):
            rows = pl.ds(n * half, half)
            g_one = red.summed(0, n).astype(BF16).astype(F32)
            _, xhat, inv_std = layer_norm(tok_ref[rows, :].astype(F32), gain1, 0.0)
            gin_ref[rows, :] += norm_back(g_one, xhat, inv_std, gain1)
            vec_own[0:1, :] += jnp.sum(g_one * xhat, axis=0, keepdims=True)
            vec_own[1:2, :] += jnp.sum(g_one, axis=0, keepdims=True)
        vec_seq[p.s] = vec_own[...]

        def tell(other):
            return p.to_seq(vec_own, vec_seq.at[p.s], vs_send.at[other], vs_recv.at[p.s], other)

        def told(other):
            return p.to_seq(vec_own, vec_seq.at[other], vs_send.at[other], vs_recv.at[other], other)

        others = (p.near, p.far, p.diag)
        for other in others:
            tell(other).start()
        turn(2)
        for hop in range(1, chips):
            sum_w.forward(hop)
            sum_w.relay(hop - 1)
            turn(1)
        for other in others:
            told(other).wait_recv()
        for other in others:
            tell(other).wait_send()
        vec = vec_seq[0]
        for n in range(1, n_seq):
            vec = vec + vec_seq[n]
        vec_own[...] = vec
        vec_exp[p.e] = vec

        def show(step):
            other = p.peer(step, -1)
            return p.to_exp(vec_own, vec_exp.at[p.e], ve_send.at[step], ve_recv.at[step], other)

        def shown(step):
            other = p.peer(step, 1)
            return p.to_exp(vec_own, vec_exp.at[other], ve_send.at[step], ve_recv.at[step], other)

        for step in range(1, n_exp):
            show(step).start()
        sum_w.relay(chips - 1)
        turn(n_exp)
        comb.drain()
        out_ref[...] = (
            resid_ref[...] + dot(pick_ref[...], ret[...].reshape(n_exp * cap, width))
        ).astype(BF16)
        for hop in range(chips):
            sum_o.arrived(hop)
        for hop in range(chips):
            sum_w.arrived(hop)
        for step in range(1, n_exp):
            shown(step).wait_recv()
            show(step).wait_send()
        vec = vec_exp[0]
        for n in range(1, n_exp):
            vec = vec + vec_exp[n]
        vec_ref[...] = vec
        gather.drain()
        sum_o.drain()
        sum_w.drain()

    vmem = pl.BlockSpec(memory_space=pltpu.VMEM)
    hbm = pl.BlockSpec(memory_space=pl.ANY)
    smem = pl.BlockSpec(memory_space=pltpu.SMEM)
    shape = jax.ShapeDtypeStruct
    dma = pltpu.SemaphoreType.DMA
    return pl.pallas_call(
        kernel,
        out_shape=[
            shape((tok, width), BF16),
            shape((tok, width), F32),
            shape((8, width), F32),
            shape((n_seq, n_exp, rows_w, 3 * cols), BF16),
            shape((n_seq, n_exp, rows_o, width), BF16),
        ],
        in_specs=[vmem] * 5 + [hbm] + [vmem] * 5 + [hbm] * 4 + [vmem, vmem, hbm, vmem, smem],
        out_specs=[vmem, vmem, vmem, hbm, hbm],
        scratch_shapes=[
            pltpu.VMEM((n_seq, tok, width), BF16),
            pltpu.VMEM((total, cols), BF16),
            pltpu.VMEM((total, 3 * cols), BF16),
            pltpu.VMEM((total, cols), F32),
            pltpu.VMEM((total, cols), F32),
            pltpu.VMEM((total, width), BF16),
            pltpu.VMEM((width, 3 * cols), BF16),
            pltpu.VMEM((cols, width), BF16),
            pltpu.VMEM((n_exp, n_seq, cap, width), BF16),
            pltpu.VMEM((1, n_seq, tok, width), BF16),
            pltpu.VMEM((n_exp, cap, width), BF16),
            pltpu.VMEM((8, width), F32),
            pltpu.VMEM((n_seq, 8, width), F32),
            pltpu.VMEM((n_exp, 8, width), F32),
            dma((5,)),
            dma((n_exp,)),
            dma((n_seq,)),
            dma((n_seq,)),
            dma((n_exp,)),
            dma((n_exp,)),
        ]
        + Gather.scratch()
        + Combine.scratch(n_exp, cap, width)
        + [
            pltpu.VMEM((1, 2, tok // 2, width), BF16),
            pltpu.VMEM((1, 4, tok // 2, width), BF16),
            dma((1, 6)),
            dma((1, 6)),
        ]
        + SumAll.scratch(n_exp, rows_o, width)
        + SumAll.scratch(n_exp, rows_w, 3 * cols),
        compiler_params=pltpu.CompilerParams(
            collective_id=collective_id, has_side_effects=True, vmem_limit_bytes=VMEM_LIMIT
        ),
        name="back_part",
    )(grad_back, pick, resid, ln2, cotangent, w_out, q, k, v, attn, lse, n1, *w_qkv, tokens, ln1, ffn_part,
      b_down, lengths)


def shards(
    tokens, lengths, expert_ids, ln1_gain, ln1_bias, w_query, b_query, w_key, w_value, b_value, w_out, b_out,
    ln2_gain, ln2_bias, w_up, b_up, w_down, b_down, cotangent,
):
    n_exp = lax.axis_size("exp")
    n_seq = lax.axis_size("seq")
    seq_rank = lax.axis_index("seq")
    width = tokens.shape[2]
    cols = width // n_seq
    ln1 = jnp.stack([ln1_gain, ln1_bias])
    ln2 = jnp.stack([ln2_gain, ln2_bias])
    w_qkv = (w_query, w_key, w_value)
    n1, q, k, v, attn, lse, resid, pick, send, cot_rows = front_part(
        tokens[0], lengths, expert_ids[0], ln1, w_qkv, jnp.stack([b_query, b_value]), w_out, b_out[None], ln2,
        cotangent[0], n_exp, 0,
    )
    grad_back, grad_w_up, grad_w_down, grad_b_up, cot_sum, ffn_part = ffn_both(
        send, cot_rows, w_up[0], b_up, w_down[0], 1
    )
    grad_b_down = lax.dynamic_slice_in_dim(cot_sum, seq_rank * cols, cols, 1)
    output, input_grad, vec, grad_qkv, grad_out = back_part(
        grad_back, pick, resid, ln2, cotangent[0], w_out, q, k, v, attn, lse, n1, w_qkv, tokens[0], ln1, ffn_part,
        b_down, lengths, 2,
    )

    def whole(at):
        piece = grad_qkv[:, :, :, at * cols : (at + 1) * cols]
        return jnp.transpose(piece, (1, 2, 0, 3)).reshape(width, width).astype(F32)

    return (
        output[None], input_grad[None], vec[0], vec[1], whole(0), vec[2], whole(1), whole(2), vec[3],
        grad_out.reshape(width, width).astype(F32), vec[4], vec[5], vec[6],
        grad_w_up[None], grad_b_up, grad_w_down[None], grad_b_down,
    )


def norm_layer(values_in, gain_vec, shift_vec):
    center = values_in - jnp.mean(values_in, axis=-1, keepdims=True)
    inv_std = lax.rsqrt(jnp.mean(center * center, axis=-1, keepdims=True) + EPSILON)
    return center * inv_std * gain_vec + shift_vec


def segment_ids(positions, seq_ends):
    return jnp.sum((positions[:, None] >= seq_ends[None, :]).astype(jnp.int32), axis=1)


def visible_pairs(query_pos, query_seg, key_pos, key_seg):
    return ((query_seg[:, None] == key_seg[None, :]) & (key_pos[None, :] <= query_pos[:, None]))[
        None
    ]


def project(left_op, right_op):
    return jnp.dot(left_op, right_op, preferred_element_type=jnp.float32)


def shards_any(
    tokens,
    lengths,
    expert_ids,
    ln1_gain,
    ln1_bias,
    w_query,
    b_query,
    w_key,
    w_value,
    b_value,
    w_out,
    b_out,
    ln2_gain,
    ln2_bias,
    w_up,
    b_up,
    w_down,
    b_down,
    cotangent,
):
    tok_rows = tokens.shape[1]
    width = tokens.shape[2]
    seq_size = lax.axis_size("seq")
    exp_size = lax.axis_size("exp")
    seq_rank = lax.axis_index("seq")
    seq_ends = jnp.cumsum(lengths[0])
    own_pos = seq_rank * tok_rows + jnp.arange(tok_rows, dtype=jnp.int32)
    own_seg = segment_ids(own_pos, seq_ends)
    inputs = tokens[0].astype(jnp.float32)
    gain_one = ln1_gain.astype(jnp.float32)
    bias_one = ln1_bias.astype(jnp.float32)
    gain_two = ln2_gain.astype(jnp.float32)
    bias_two = ln2_bias.astype(jnp.float32)
    normed_one_low = norm_layer(inputs, gain_one, bias_one).astype(jnp.bfloat16)
    query_low = (project(normed_one_low, w_query) + b_query.astype(jnp.float32)).astype(
        jnp.bfloat16
    )
    keys_low = project(normed_one_low, w_key).astype(jnp.bfloat16)
    values_low = (project(normed_one_low, w_value) + b_value.astype(jnp.float32)).astype(
        jnp.bfloat16
    )
    query_heads = query_low.reshape(tok_rows, HEADS, HEAD_DIM)
    initial = (
        jnp.full((HEADS, tok_rows), MASKED_SCORE, jnp.float32),
        jnp.zeros((HEADS, tok_rows), jnp.float32),
        jnp.zeros((HEADS, tok_rows, HEAD_DIM), jnp.float32),
    )
    key_piece = lax.all_gather(keys_low, "seq", axis=0, tiled=True)
    value_piece = lax.all_gather(values_low, "seq", axis=0, tiled=True)
    piece_len = key_piece.shape[0]
    fold_block_len = math.gcd(piece_len, 512)
    block_count = piece_len // fold_block_len
    key_blocks = key_piece.reshape(block_count, fold_block_len, HEADS, HEAD_DIM)
    value_blocks = value_piece.reshape(block_count, fold_block_len, HEADS, HEAD_DIM)
    offsets = jnp.arange(block_count, dtype=jnp.int32) * fold_block_len

    def block_step(state_now, packed):
        row_max, row_total, accumulated = state_now
        key_blk, value_blk, offset = packed
        key_pos = offset + jnp.arange(fold_block_len, dtype=jnp.int32)
        allowed = visible_pairs(own_pos, own_seg, key_pos, segment_ids(key_pos, seq_ends))
        scores = (
            jnp.einsum("qhd,khd->hqk", query_heads, key_blk, preferred_element_type=jnp.float32)
            * SCORE_SCALE
        )
        masked = jnp.where(allowed, scores, MASKED_SCORE)
        new_max = jnp.maximum(row_max, jnp.max(masked, axis=-1))
        weights = jnp.where(allowed, jnp.exp(masked - new_max[..., None]), 0.0)
        factor = jnp.exp(row_max - new_max)
        row_total = row_total * factor + jnp.sum(weights, axis=-1)
        accumulated = accumulated * factor[..., None] + jnp.einsum(
            "hqk,khd->hqd",
            weights.astype(jnp.bfloat16),
            value_blk,
            preferred_element_type=jnp.float32,
        )
        return ((new_max, row_total, accumulated), None)

    result, _ = lax.scan(block_step, initial, (key_blocks, value_blocks, offsets))
    row_max, row_total, accumulated = result
    attn_heads = accumulated / row_total[..., None]
    attn_low = jnp.transpose(attn_heads, (1, 0, 2)).reshape(tok_rows, width).astype(jnp.bfloat16)
    resid = inputs + project(attn_low, w_out) + b_out.astype(jnp.float32)
    normed_two_low = norm_layer(resid, gain_two, bias_two).astype(jnp.bfloat16)
    experts = exp_size * w_up.shape[0]
    capacity = 2 * tok_rows // experts
    expert_of = expert_ids[0, :, 0]
    onehot = (expert_of[:, None] == jnp.arange(experts, dtype=jnp.int32)[None, :]).astype(jnp.int32)
    slot_of = jnp.sum(onehot * (jnp.cumsum(onehot, axis=0) - onehot), axis=1)
    send_rows = (
        jnp.zeros((experts, capacity, width), jnp.bfloat16)
        .at[expert_of, slot_of]
        .set(normed_two_low)
    )
    received = lax.all_to_all(send_rows, "exp", split_axis=0, concat_axis=0, tiled=True)
    recv_count = experts * capacity
    recv_rows = received.reshape(recv_count, width)
    up_weight = w_up[0]
    up_bias = b_up[0]
    down_weight = w_down[0]
    down_bias = b_down[0].astype(jnp.float32)
    piece_width = width // seq_size
    grad_send = (
        jnp.zeros((experts, capacity, width), jnp.bfloat16).at[expert_of, slot_of].set(cotangent[0])
    )
    gathered = lax.all_gather(recv_rows, "seq", axis=0, tiled=True)
    preact = project(gathered, up_weight) + up_bias.astype(jnp.float32)
    act_low = jax.nn.gelu(preact).astype(jnp.bfloat16)
    part = act_low
    expert_out = (
        lax.psum_scatter(
            project(part, down_weight).astype(jnp.bfloat16), "seq", scatter_dimension=0, tiled=True
        ).astype(jnp.float32)
        + down_bias
    )
    returned = lax.all_to_all(
        expert_out.astype(jnp.bfloat16).reshape(experts, capacity, width),
        "exp",
        split_axis=0,
        concat_axis=0,
        tiled=True,
    )
    grad_recv = lax.all_to_all(grad_send, "exp", split_axis=0, concat_axis=0, tiled=True).reshape(
        recv_count, width
    )
    grad_all = lax.all_gather(grad_recv, "seq", axis=0, tiled=True)
    bias_full = jnp.sum(grad_all.astype(jnp.float32), axis=0)
    grad_b_down = lax.dynamic_slice_in_dim(bias_full, seq_rank * piece_width, piece_width, 0)
    grad_act = jnp.einsum("rd,fd->rf", grad_all, down_weight, preferred_element_type=jnp.float32)
    grad_pre = jax.vjp(jax.nn.gelu, preact)[1](grad_act)[0].astype(jnp.bfloat16)
    grad_w_down = jnp.einsum("rf,rd->fd", act_low, grad_all, preferred_element_type=jnp.float32)
    grad_w_up = jnp.einsum("rd,rf->df", gathered, grad_pre, preferred_element_type=jnp.float32)
    grad_b_up = jnp.sum(grad_pre.astype(jnp.float32), axis=0)
    part = grad_pre
    grad_home = lax.psum_scatter(
        jnp.einsum("rf,df->rd", part, up_weight, preferred_element_type=jnp.float32).astype(
            jnp.bfloat16
        ),
        "seq",
        scatter_dimension=0,
        tiled=True,
    )
    ffn_rows = returned[expert_of, slot_of].astype(jnp.float32)
    output = (resid + ffn_rows).astype(jnp.bfloat16)
    grad_back = lax.all_to_all(
        grad_home.reshape(experts, capacity, width), "exp", split_axis=0, concat_axis=0, tiled=True
    )
    grad_normed_two = grad_back[expert_of, slot_of].astype(jnp.float32)
    _, norm_two_back = jax.vjp(norm_layer, resid, gain_two, bias_two)
    grad_resid_norm, grad_gain_two, grad_bias_two = norm_two_back(grad_normed_two)
    grad_resid = cotangent[0].astype(jnp.float32) + grad_resid_norm
    grad_out_low = grad_resid.astype(jnp.bfloat16)
    grad_w_out = jnp.einsum("qa,qd->ad", attn_low, grad_out_low, preferred_element_type=jnp.float32)
    grad_b_out = jnp.sum(grad_out_low.astype(jnp.float32), axis=0)
    grad_attn_low = jnp.einsum(
        "qd,ad->qa", grad_out_low, w_out, preferred_element_type=jnp.float32
    ).astype(jnp.bfloat16)
    grad_attn_heads = grad_attn_low.reshape(tok_rows, HEADS, HEAD_DIM)
    delta = jnp.sum(
        jnp.transpose(grad_attn_heads.astype(jnp.float32), (1, 0, 2)) * attn_heads, axis=-1
    )
    whole_keys, whole_values = (
        lax.all_gather(keys_low, "seq", axis=0, tiled=True),
        lax.all_gather(values_low, "seq", axis=0, tiled=True),
    )
    group_len = whole_keys.shape[0]
    block_len = math.gcd(group_len, 512)
    block_count = group_len // block_len

    def back_step(grad_query, packed):
        key_blk, value_blk, offset = packed
        key_pos = offset + jnp.arange(block_len, dtype=jnp.int32)
        allowed = visible_pairs(own_pos, own_seg, key_pos, segment_ids(key_pos, seq_ends))
        scores = (
            jnp.einsum("qhd,khd->hqk", query_heads, key_blk, preferred_element_type=jnp.float32)
            * SCORE_SCALE
        )
        masked = jnp.where(allowed, scores, MASKED_SCORE)
        probabilities = (
            jnp.where(allowed, jnp.exp(masked - row_max[..., None]), 0.0) / row_total[..., None]
        )
        probs_low = probabilities.astype(jnp.bfloat16)
        grad_probs = jnp.einsum(
            "qhd,khd->hqk", grad_attn_heads, value_blk, preferred_element_type=jnp.float32
        )
        grad_scores = (probabilities * (grad_probs - delta[..., None])).astype(jnp.bfloat16)
        grad_query = (
            grad_query
            + jnp.einsum("hqk,khd->qhd", grad_scores, key_blk, preferred_element_type=jnp.float32)
            * SCORE_SCALE
        )
        grad_key_blk = (
            jnp.einsum("hqk,qhd->khd", grad_scores, query_heads, preferred_element_type=jnp.float32)
            * SCORE_SCALE
        )
        grad_value_blk = jnp.einsum(
            "hqk,qhd->khd", probs_low, grad_attn_heads, preferred_element_type=jnp.float32
        )
        return (grad_query, (grad_key_blk, grad_value_blk))

    block_offsets = jnp.arange(block_count, dtype=jnp.int32) * block_len
    grad_query, key_value_parts = lax.scan(
        back_step,
        jnp.zeros((tok_rows, HEADS, HEAD_DIM), jnp.float32),
        (
            whole_keys.reshape(block_count, block_len, HEADS, HEAD_DIM),
            whole_values.reshape(block_count, block_len, HEADS, HEAD_DIM),
            block_offsets,
        ),
    )
    grad_keys, grad_values = (
        lax.psum_scatter(
            key_value_parts[0].reshape(group_len, width).astype(jnp.bfloat16),
            "seq",
            scatter_dimension=0,
            tiled=True,
        ).astype(jnp.float32),
        lax.psum_scatter(
            key_value_parts[1].reshape(group_len, width).astype(jnp.bfloat16),
            "seq",
            scatter_dimension=0,
            tiled=True,
        ).astype(jnp.float32),
    )
    grad_query_low = grad_query.reshape(tok_rows, width).astype(jnp.bfloat16)
    grad_keys_low = grad_keys.astype(jnp.bfloat16)
    grad_values_low = grad_values.astype(jnp.bfloat16)
    grad_w_query = jnp.einsum(
        "qa,qd->ad", normed_one_low, grad_query_low, preferred_element_type=jnp.float32
    )
    grad_b_query = jnp.sum(grad_query_low.astype(jnp.float32), axis=0)
    grad_w_key = jnp.einsum(
        "qa,qd->ad", normed_one_low, grad_keys_low, preferred_element_type=jnp.float32
    )
    grad_w_value = jnp.einsum(
        "qa,qd->ad", normed_one_low, grad_values_low, preferred_element_type=jnp.float32
    )
    grad_b_value = jnp.sum(grad_values_low.astype(jnp.float32), axis=0)
    grad_normed_one = (
        (
            jnp.einsum("qd,ad->qa", grad_query_low, w_query, preferred_element_type=jnp.float32)
            + jnp.einsum("qd,ad->qa", grad_keys_low, w_key, preferred_element_type=jnp.float32)
            + jnp.einsum("qd,ad->qa", grad_values_low, w_value, preferred_element_type=jnp.float32)
        )
        .astype(jnp.bfloat16)
        .astype(jnp.float32)
    )
    _, norm_one_back = jax.vjp(norm_layer, inputs, gain_one, bias_one)
    grad_in_norm, grad_gain_one, grad_bias_one = norm_one_back(grad_normed_one)
    input_grad = grad_resid + grad_in_norm
    summed = lax.psum(
        (
            grad_gain_one,
            grad_bias_one,
            grad_w_query,
            grad_b_query,
            grad_w_key,
            grad_w_value,
            grad_b_value,
            grad_w_out,
            grad_b_out,
            grad_gain_two,
            grad_bias_two,
        ),
        ("seq", "exp"),
    )
    return (
        output[None],
        input_grad[None],
        summed[0],
        summed[1],
        summed[2],
        summed[3],
        summed[4],
        summed[5],
        summed[6],
        summed[7],
        summed[8],
        summed[9],
        summed[10],
        grad_w_up[None],
        grad_b_up[None],
        grad_w_down[None],
        grad_b_down[None],
    )


def solution(mesh):
    placed = (
        P("exp", "seq", None),
        P("exp", None),
        P("exp", "seq", None),
        P(),
        P(),
        P(),
        P(),
        P(),
        P(),
        P(),
        P(),
        P(),
        P(),
        P(),
        P("exp", None, "seq"),
        P("exp", "seq"),
        P("exp", "seq", None),
        P("exp", None),
        P("exp", "seq", None),
    )
    plane = mesh.shape["seq"] == 4 and mesh.shape["exp"] % 2 == 0
    return jax.shard_map(
        shards if plane else shards_any,
        mesh=mesh,
        in_specs=placed,
        out_specs=(
            P("exp", "seq", None),
            P("exp", "seq", None),
            P(),
            P(),
            P(),
            P(),
            P(),
            P(),
            P(),
            P(),
            P(),
            P(),
            P(),
            P("exp", None, "seq"),
            P("exp", "seq"),
            P("exp", "seq", None),
            P("exp", "seq"),
        ),
        check_vma=False,
    )
```

```python
import functools
import math

import jax
import jax.numpy as jnp
from jax import lax
from jax.experimental import pallas as pl
from jax.experimental.pallas import tpu as pltpu
from jax.sharding import PartitionSpec as P

MESH = pl.DeviceIdType.MESH
F32 = jnp.float32
BF16 = jnp.bfloat16
VMEM_LIMIT = 63 * 2**20


def dot(a, b, dims=((1,), (0,))):
    return lax.dot_general(a, b, (dims, ((), ())), preferred_element_type=F32)


class Place:
    def __init__(self, n_exp):
        self.n_exp = n_exp
        self.s = lax.axis_index("seq")
        self.e = lax.axis_index("exp")
        low = lax.rem(self.s, 2)
        high = lax.div(self.s, 2)
        self.near = high * 2 + (1 - low)
        self.far = (1 - high) * 2 + low
        self.diag = (1 - high) * 2 + (1 - low)
        self.core = lax.rem(self.e, 2)
        self.chip = lax.div(self.e, 2)

    def peer(self, step, way):
        chips = self.n_exp // 2
        hop = lax.div(step, 2)
        if chips == 4:
            hop = hop + lax.div(hop, 2) * (5 - 2 * hop)
        chip = lax.rem(self.chip + way * hop + chips, chips)
        return chip * 2 + lax.rem(self.core + step, 2)

    def greet(self, diag=False):
        barrier = pltpu.get_barrier_semaphore()
        others = (self.near, self.far, self.diag) if diag else (self.near, self.far)
        for other in others:
            pl.semaphore_signal(barrier, inc=1, device_id=(other, self.e), device_id_type=MESH)

        def tell(step, carry):
            pl.semaphore_signal(
                barrier, inc=1, device_id=(self.s, self.peer(step, 1)), device_id_type=MESH
            )
            return carry

        lax.fori_loop(1, self.n_exp, tell, 0)
        pl.semaphore_wait(barrier, len(others) + self.n_exp - 1)

    def to_seq(self, src, dst, send_sem, recv_sem, other):
        return pltpu.make_async_remote_copy(
            src_ref=src, dst_ref=dst, send_sem=send_sem, recv_sem=recv_sem,
            device_id=(other, self.e), device_id_type=MESH,
        )

    def to_exp(self, src, dst, send_sem, recv_sem, other):
        return pltpu.make_async_remote_copy(
            src_ref=src, dst_ref=dst, send_sem=send_sem, recv_sem=recv_sem,
            device_id=(self.s, other), device_id_type=MESH,
        )


class Dispatch:
    def __init__(self, place, send, held, exp_sems, seq_sems):
        self.place, self.send, self.held = place, send, held
        self.exp_send, self.exp_recv = exp_sems
        self.seq_send, self.seq_recv = seq_sems
        self.cap = send.shape[1]

    @staticmethod
    def scratch(n_exp):
        return [
            pltpu.SemaphoreType.DMA((n_exp,)),
            pltpu.SemaphoreType.DMA((n_exp,)),
            pltpu.SemaphoreType.DMA((n_exp, 6)),
            pltpu.SemaphoreType.DMA((n_exp, 6)),
        ]

    def _exp(self, step):
        p = self.place
        other = p.peer(step, -1)
        return p.to_exp(
            self.send.at[other], self.held.at[step, p.s], self.exp_send.at[step], self.exp_recv.at[step], other
        )

    def _seq(self, step, owner, half, lane, other):
        p = self.place
        rows = pl.ds(half * (self.cap // 2), self.cap // 2)
        part = self.held.at[step, owner, rows]
        return p.to_seq(part, part, self.seq_send.at[step, lane], self.seq_recv.at[step, lane], other)

    def copies(self, step, lanes=range(6)):
        p = self.place
        spec = (
            (p.s, 0, p.near),
            (p.s, 1, p.far),
            (p.s, 1, p.near),
            (p.s, 0, p.far),
            (p.near, 0, p.far),
            (p.far, 1, p.near),
        )
        return [self._seq(step, spec[n][0], spec[n][1], n, spec[n][2]) for n in lanes]

    def start_exp(self, step):
        self._exp(step).start()

    def own(self):
        p = self.place
        self.held[0, p.s] = self.send[p.e]

    def start_seq(self, step):
        @pl.when(step > 0)
        def _():
            self._exp(step).wait_recv()

        for c in self.copies(step, range(4)):
            c.start()

    def relay(self, step):
        for c, out in zip(self.copies(step, (0, 1)), self.copies(step, (4, 5))):
            c.wait_recv()
            out.start()

    def arrived(self, step):
        for c in self.copies(step, range(2, 6)):
            c.wait_recv()

    def sent(self, step):
        for c in self.copies(step):
            c.wait_send()

    def drain(self, seq=True):
        def body(step, carry):
            if seq:
                self.sent(step)

            @pl.when(step > 0)
            def _():
                self._exp(step).wait_send()

            return carry

        lax.fori_loop(0, self.place.n_exp, body, 0)


class Combine:
    def __init__(self, place, part, passing, landing, total, back, seq_sems, exp_sems, slots):
        self.place, self.part, self.passing, self.landing = place, part, passing, landing
        self.total, self.back, self.slots = total, back, slots
        self.seq_send, self.seq_recv = seq_sems
        self.exp_send, self.exp_recv = exp_sems
        self.half = part.shape[2] // 2

    @staticmethod
    def scratch(n_exp, cap, width):
        return [
            pltpu.VMEM((n_exp, 2, cap // 2, width), BF16),
            pltpu.VMEM((n_exp, 4, cap // 2, width), BF16),
            pltpu.VMEM((n_exp, cap, width), BF16),
            pltpu.SemaphoreType.DMA((n_exp, 6)),
            pltpu.SemaphoreType.DMA((n_exp, 6)),
            pltpu.SemaphoreType.DMA((n_exp,)),
            pltpu.SemaphoreType.DMA((n_exp,)),
        ]

    def _slot(self, step):
        return lax.rem(step, self.slots)

    def _piece(self, step, owner, half):
        return self.part.at[self._slot(step), owner, pl.ds(half * self.half, self.half)]

    def _seq(self, src, dst, step, lane, other):
        return self.place.to_seq(
            src, dst, self.seq_send.at[step, lane], self.seq_recv.at[step, lane], other
        )

    def copies(self, step, lanes=range(6)):
        p = self.place
        spec = (
            (p.diag, 0, self.passing, 0, p.near),
            (p.diag, 1, self.passing, 1, p.far),
            (p.near, 0, self.landing, 0, p.near),
            (p.far, 1, self.landing, 3, p.far),
            (p.far, 0, self.landing, 2, p.far),
            (p.near, 1, self.landing, 1, p.near),
        )
        made = []
        for n in lanes:
            owner, half, buffer, at, other = spec[n]
            made.append(self._seq(self._piece(step, owner, half), buffer.at[step, at], step, n, other))
        return made

    def start(self, step):
        for c in self.copies(step, range(4)):
            c.start()

    def pass_on(self, step):
        p = self.place
        slot = self._slot(step)
        came, out = self.copies(step, (0, 1)), self.copies(step, (4, 5))
        for n, owner in enumerate((p.far, p.near)):
            rows = pl.ds(n * self.half, self.half)
            came[n].wait_recv()
            self.part[slot, owner, rows] = (
                self.part[slot, owner, rows].astype(F32) + self.passing[step, n].astype(F32)
            ).astype(BF16)
            out[n].start()

    def _whole(self, step):
        if self.total is None:
            return self.part.at[self._slot(step), self.place.s]
        return self.total.at[step]

    def _exp(self, step):
        p = self.place
        other = p.peer(step, 1)
        return p.to_exp(
            self._whole(step), self.back.at[p.e], self.exp_send.at[step], self.exp_recv.at[step], other
        )

    def arrived(self, step):
        copies = self.copies(step)
        for c in copies[2:]:
            c.wait_recv()
        for c in copies:
            c.wait_send()

    def summed(self, step, half):
        rows = pl.ds(half * self.half, self.half)
        return (
            self.part[self._slot(step), self.place.s, rows].astype(F32)
            + self.landing[step, half].astype(F32)
            + self.landing[step, 2 + half].astype(F32)
        )

    def finish(self, step, bias=None):
        p = self.place
        self.arrived(step)
        for half in range(2):
            value = self.summed(step, half)
            if bias is not None:
                value = value + bias
            rows = pl.ds(half * self.half, self.half)
            if self.total is None:
                self.part[self._slot(step), p.s, rows] = value.astype(BF16)
            else:
                self.total[step, rows] = value.astype(BF16)

        @pl.when(step > 0)
        def _():
            self._exp(step).start()

        @pl.when(step == 0)
        def _():
            self.back[p.e] = self._whole(0)[...]

    def drain(self):
        p = self.place

        def body(step, carry):
            c = self._exp(step)
            c.wait_send()
            c.wait_recv()
            return carry

        lax.fori_loop(1, p.n_exp, body, 0)


GELU_A = math.sqrt(2.0 / math.pi)
GELU_B = 0.044715


EPSILON = 1e-05
SCORE_SCALE = 0.125
MASKED_SCORE = -1e30
HEAD_DIM = 64
HEADS = 16


class Gather:
    def __init__(self, place, held, send_sems, recv_sems):
        self.place, self.held = place, held
        self.send_sems, self.recv_sems = send_sems, recv_sems
        self.half = held.shape[1] // 2

    @staticmethod
    def scratch():
        return [pltpu.SemaphoreType.DMA((6,)), pltpu.SemaphoreType.DMA((6,))]

    def copies(self, lanes=range(6)):
        p = self.place
        spec = (
            (p.s, 0, p.near),
            (p.s, 1, p.far),
            (p.s, 1, p.near),
            (p.s, 0, p.far),
            (p.near, 0, p.far),
            (p.far, 1, p.near),
        )
        made = []
        for n in lanes:
            owner, half, other = spec[n]
            part = self.held.at[owner, pl.ds(half * self.half, self.half)]
            made.append(p.to_seq(part, part, self.send_sems.at[n], self.recv_sems.at[n], other))
        return made

    def start(self):
        for c in self.copies(range(4)):
            c.start()

    def relay(self):
        for c, out in zip(self.copies((0, 1)), self.copies((4, 5))):
            c.wait_recv()
            out.start()

    def wait(self, lanes):
        for c in self.copies(lanes):
            c.wait_recv()

    def drain(self):
        for c in self.copies():
            c.wait_send()


def layer_norm(values, gain, shift):
    center = values - jnp.mean(values, axis=-1, keepdims=True)
    inv_std = lax.rsqrt(jnp.mean(center * center, axis=-1, keepdims=True) + EPSILON)
    xhat = center * inv_std
    return xhat * gain + shift, xhat, inv_std


def norm_back(grad, xhat, inv_std, gain):
    d = grad * gain
    return (
        d - jnp.mean(d, axis=-1, keepdims=True) - xhat * jnp.mean(d * xhat, axis=-1, keepdims=True)
    ) * inv_std


def row_choice(ids, n_exp, cap):
    tokens = ids.shape[1]
    named = (ids == lax.broadcasted_iota(jnp.int32, (128, tokens), 0)).astype(BF16)
    before = (
        lax.broadcasted_iota(jnp.int32, (tokens, tokens), 0)
        < lax.broadcasted_iota(jnp.int32, (tokens, tokens), 1)
    ).astype(BF16)
    earlier = dot(named, before) * named.astype(F32)
    slot = jnp.sum(earlier, axis=0, keepdims=True).astype(jnp.int32) + ids * cap
    return (slot == lax.broadcasted_iota(jnp.int32, (n_exp * cap, tokens), 0)).astype(BF16)


def segment_of(position, lengths):
    end = jnp.int32(0)
    count = jnp.zeros_like(position)
    for n in range(lengths.shape[1]):
        end = end + lengths[0, n]
        count = count + (position >= end).astype(jnp.int32)
    return count


def head_mask(rows, width, head):
    lane = lax.broadcasted_iota(jnp.int32, (rows, width), 1)
    return (lane >= head * HEAD_DIM) & (lane < (head + 1) * HEAD_DIM)


class SumAll:
    def __init__(self, place, src, core_in, mine, chip_in, res, where, local_sem, sems):
        self.place, self.src, self.core_in, self.mine = place, src, core_in, mine
        self.chip_in, self.res, self.where, self.local_sem = chip_in, res, where, local_sem
        (self.core_sems, self.rs_send, self.rs_recv, self.ag_send, self.ag_recv,
         self.seq_send, self.seq_recv, self.pair_send, self.pair_recv) = sems
        self.chips = place.n_exp // 2
        p = place
        self.sibling = p.chip * 2 + (1 - p.core)

    @staticmethod
    def scratch(n_exp, *piece):
        chips = n_exp // 2
        dma = pltpu.SemaphoreType.DMA
        return [
            pltpu.VMEM((2, chips, *piece), BF16),
            pltpu.VMEM((chips, *piece), BF16),
            pltpu.VMEM((chips, *piece), BF16),
            pltpu.VMEM((chips, *piece), BF16),
            pltpu.VMEM(piece, BF16),
            dma((1,)),
            dma((2,)),
            dma((chips,)),
            dma((chips,)),
            dma((chips,)),
            dma((chips,)),
            dma((chips, 6)),
            dma((chips, 6)),
            dma((chips, 4)),
            dma((chips, 4)),
        ]

    def chip(self, hop):
        return lax.rem(self.place.chip + hop, self.chips)

    def exp(self, hop):
        return self.chip(hop) * 2 + self.place.core

    def _core(self):
        p = self.place
        return p.to_exp(
            self.src.at[1 - p.core], self.core_in, self.core_sems.at[0], self.core_sems.at[1], self.sibling
        )

    def start(self):
        self._core().start()

    def _spread(self, hop):
        p = self.place
        to = self.chip(hop)
        return p.to_exp(
            self.mine.at[to], self.chip_in.at[p.chip], self.rs_send.at[to], self.rs_recv.at[p.chip], self.exp(hop)
        )

    def _spread_from(self, hop):
        p = self.place
        at = self.chip(hop)
        return p.to_exp(
            self.mine.at[at], self.chip_in.at[at], self.rs_send.at[at], self.rs_recv.at[at], self.exp(hop)
        )

    def spread(self):
        p = self.place
        self._core().wait_recv()
        for n in range(self.chips):
            self.mine[n] = (self.src[p.core, n].astype(F32) + self.core_in[n].astype(F32)).astype(BF16)
        for hop in range(1, self.chips):
            self._spread(hop).start()

    def _local(self):
        p = self.place
        return pltpu.make_async_copy(self.res, self.where(p.s, p.e), self.local_sem.at[0])

    def _share(self, hop):
        p = self.place
        to = self.chip(hop)
        return p.to_exp(
            self.res, self.where(p.s, p.e), self.ag_send.at[to], self.ag_recv.at[p.chip], self.exp(hop)
        )

    def _share_from(self, hop):
        p = self.place
        at = self.chip(hop)
        return p.to_exp(
            self.res, self.where(p.s, self.exp(hop)), self.ag_send.at[at], self.ag_recv.at[at], self.exp(hop)
        )

    def copies(self, hop, lanes=range(6)):
        p = self.place
        spec = (
            (p.s, 0, p.near),
            (p.s, 1, p.far),
            (p.s, 1, p.near),
            (p.s, 0, p.far),
            (p.near, 0, p.far),
            (p.far, 1, p.near),
        )
        made = []
        for n in lanes:
            owner, half, other = spec[n]
            part = self.where(owner, self.exp(hop), half)
            made.append(p.to_seq(part, part, self.seq_send.at[hop, n], self.seq_recv.at[hop, n], other))
        return made

    def _pair(self, hop, n):
        p = self.place
        part = self.where((p.s, p.near, p.far, p.diag)[n], self.exp(hop))
        return p.to_exp(part, part, self.pair_send.at[hop, n], self.pair_recv.at[hop, n], self.sibling)

    def _pair_from(self, hop, n):
        p = self.place
        owner = (p.s, p.near, p.far, p.diag)[n]
        part = self.where(owner, self.chip(hop) * 2 + (1 - p.core))
        return p.to_exp(part, part, self.pair_send.at[hop, n], self.pair_recv.at[hop, n], self.sibling)

    def reduce(self):
        p = self.place
        for hop in range(1, self.chips):
            self._spread_from(hop).wait_recv()
        total = self.mine[p.chip].astype(F32)
        for hop in range(1, self.chips):
            total = total + self.chip_in[self.chip(hop)].astype(F32)
        self.res[...] = total.astype(BF16)
        self._local().start()
        for hop in range(1, self.chips):
            self._share(hop).start()
        self._local().wait()

    def forward(self, hop):
        if hop > 0:
            self._share_from(hop).wait_recv()
        for c in self.copies(hop, range(4)):
            c.start()
        self._pair(hop, 0).start()

    def relay(self, hop):
        for c, out in zip(self.copies(hop, (0, 1)), self.copies(hop, (4, 5))):
            c.wait_recv()
            out.start()

    def arrived(self, hop):
        for c in self.copies(hop, (2, 3)):
            c.wait_recv()
        self._pair(hop, 1).start()
        self._pair(hop, 2).start()
        for c in self.copies(hop, (4, 5)):
            c.wait_recv()
        self._pair(hop, 3).start()

    def drain(self):
        self._core().wait_send()
        for hop in range(1, self.chips):
            self._spread(hop).wait_send()
            self._share(hop).wait_send()
        for hop in range(self.chips):
            for c in self.copies(hop):
                c.wait_send()
            for n in range(4):
                self._pair(hop, n).wait_send()
                self._pair_from(hop, n).wait_recv()


def layer(
    tokens, ids, cotangent, lengths, ln1, w_qkv, b_query, b_value, w_out, b_out, ln2, w_up, b_up, w_down, b_down,
    n_exp, collective_id,
):
    tok, width = tokens.shape
    hidden = w_up.shape[1]
    n_seq = 4
    total = n_seq * tok
    cols = width // n_seq
    heads = cols // HEAD_DIM
    cap = 2 * tok // n_exp
    q_block = 256
    chips = n_exp // 2
    rows_w, rows_o = width // n_exp, cols // n_exp
    routed = n_seq * cap
    block = min(256, hidden)
    slots = 2
    ahead = 4

    vm = pltpu.VMEM
    dma = pltpu.SemaphoreType.DMA
    table = dict(
        xall=vm((1, n_seq, tok, width), BF16),
        n1=vm((total, width), BF16),
        q=vm((total, cols), BF16),
        k=vm((total, cols), BF16),
        v=vm((total, cols), BF16),
        attn=vm((total, cols), F32),
        lse=vm((8, total), F32),
        resid=vm((tok, width), F32),
        pick=vm((n_exp * cap, tok), BF16),
        w_all=vm((width, 3 * cols), BF16),
        w_o=vm((width, width), BF16),
        send_c=vm((n_exp, cap, width), BF16),
        send_n=vm((n_exp, cap, width), BF16),
        back=vm((n_exp, cap, width), BF16),
        ret=vm((n_exp, cap, width), BF16),
        attn_out=vm((n_seq, tok, cols), BF16),
        attn_in=vm((n_seq, tok, cols), BF16),
        cot=vm((n_exp, n_seq, cap, width), BF16),
        held=vm((n_exp, n_seq, cap, width), BF16),
        wu=vm((width, hidden), BF16),
        wd=vm((hidden, width), BF16),
        part=vm((slots, n_seq, cap, width), BF16),
        dwu=vm((width, hidden), F32),
        dwd=vm((hidden, width), F32),
        gattn=vm((total, cols), BF16),
        dqkv=vm((total, 3 * cols), BF16),
        vec_own=vm((8, width), F32),
        vec_seq=vm((n_seq, 8, width), F32),
        vec_exp=vm((n_exp, 8, width), F32),
        local_sems=dma((8,)),
        a2a_send=dma((n_seq,)),
        a2a_recv=dma((n_seq,)),
        vs_send=dma((n_seq,)),
        vs_recv=dma((n_seq,)),
        ve_send=dma((n_exp,)),
        ve_recv=dma((n_exp,)),
    )
    groups = dict(
        gather1=Gather.scratch(),
        gather2=Gather.scratch(),
        disp_c=Dispatch.scratch(n_exp),
        disp_n=Dispatch.scratch(n_exp),
        comb_g=Combine.scratch(n_exp, cap, width),
        comb_f=Combine.scratch(n_exp, cap, width)[:2] + Combine.scratch(n_exp, cap, width)[3:],
        red=[
            vm((1, 2, tok // 2, width), BF16),
            vm((1, 4, tok // 2, width), BF16),
            dma((1, 6)),
            dma((1, 6)),
        ],
        sum_o=SumAll.scratch(n_exp, rows_o, width),
        sum_w=SumAll.scratch(n_exp, 3, rows_w, cols),
    )
    scratch = list(table.values()) + [ref for group in groups.values() for ref in group]

    def kernel(tok_ref, ids_ref, cot_ref, len_ref, g1_ref, c1_ref, wq_in, wk_in, wv_in, bq_ref, bv_ref, wo_in, bo_ref,
               g2_ref, c2_ref, wu_in, bu_ref, wd_in, bd_ref,
               out_ref, gin_ref, vec_ref, dbu_ref, csum_ref, dwu_out, dwd_out, gw_out, go_out, *refs):
        r = dict(zip(table, refs))
        at = len(table)
        g = {}
        for name, group in groups.items():
            g[name] = refs[at : at + len(group)]
            at += len(group)
        xall, n1, q_all, k_all, v_all = r["xall"], r["n1"], r["q"], r["k"], r["v"]
        attn, lse_all, resid, pick = r["attn"], r["lse"], r["resid"], r["pick"]
        w_all, w_o, wu, wd = r["w_all"], r["w_o"], r["wu"], r["wd"]
        send_c, send_n, back, ret = r["send_c"], r["send_n"], r["back"], r["ret"]
        attn_out, attn_in, cot, held, part = r["attn_out"], r["attn_in"], r["cot"], r["held"], r["part"]
        dwu, dwd, gattn, dqkv = r["dwu"], r["dwd"], r["gattn"], r["dqkv"]
        dk, dv = dwu.at[0:total, 0:cols], dwu.at[0:total, cols : 2 * cols]
        vec_own, vec_seq, vec_exp = r["vec_own"], r["vec_seq"], r["vec_exp"]
        local_sems = r["local_sems"]

        p = Place(n_exp)
        mine = pl.ds(pl.multiple_of(p.s * cols, cols), cols)

        tile = 32

        def tile_rows(n):
            return pl.ds(pl.multiple_of(n * tile, tile), tile)

        def row_of(ref):
            return ref[...].astype(F32).reshape(1, ref.shape[-1])

        loads = [
            pltpu.make_async_copy(src.at[:, mine], w_all.at[:, pl.ds(n * cols, cols)], local_sems.at[n])
            for n, src in enumerate((wq_in, wk_in, wv_in))
        ]
        load_o = pltpu.make_async_copy(wo_in, w_o, local_sems.at[3])
        load_ffn = [
            pltpu.make_async_copy(wu_in, wu, local_sems.at[4]),
            pltpu.make_async_copy(wd_in, wd, local_sems.at[5]),
        ]
        for c in loads + [load_o] + load_ffn:
            c.start()

        xall[0, p.s] = tok_ref[...]
        p.greet(diag=True)
        gather1 = Gather(p, xall.at[0], *g["gather1"])
        gather1.start()
        pick[...] = row_choice(ids_ref[...], n_exp, cap)

        def lay_out(send, rows_ref):
            for e in range(0, n_exp, 2):
                laid = dot(pick[e * cap : (e + 2) * cap, :], rows_ref[...])
                send[e : e + 2] = laid.astype(BF16).reshape(2, cap, width)

        lay_out(send_c, cot_ref)
        disp_c = Dispatch(p, send_c, cot, g["disp_c"][0:2], g["disp_c"][2:4])
        for step in range(1, n_exp):
            disp_c.start_exp(step)
        disp_c.own()
        gain1, bias1 = row_of(g1_ref), row_of(c1_ref)
        gain2, bias2 = row_of(g2_ref), row_of(c2_ref)
        bq = bq_ref[mine].astype(F32).reshape(1, cols)
        bv = bv_ref[mine].astype(F32).reshape(1, cols)

        def project(owner):
            rows = pl.ds(pl.multiple_of(owner * tok, tok), tok)

            def norm_tile(n, carry):
                x = xall[0, owner, tile_rows(n), :].astype(F32)
                n1[pl.ds(pl.multiple_of(owner * tok + n * tile, tile), tile), :] = layer_norm(
                    x, gain1, bias1
                )[0].astype(BF16)
                return carry

            lax.fori_loop(0, tok // tile, norm_tile, 0)
            out = dot(n1[rows, :], w_all[...])
            q = (out[:, 0:cols] + bq).astype(BF16)
            q_all[rows, :] = (q.astype(F32) * SCORE_SCALE).astype(BF16)
            k_all[rows, :] = out[:, cols : 2 * cols].astype(BF16)
            v_all[rows, :] = (out[:, 2 * cols :] + bv).astype(BF16)

        for c in loads:
            c.wait()
        project(p.s)
        gather1.relay()
        gather1.wait((2, 3))
        project(p.near)
        project(p.far)
        gather1.wait((4, 5))
        disp_c.start_seq(0)
        disp_c.start_seq(1)
        project(p.diag)

        def a2a(owner):
            return p.to_seq(
                attn_out.at[owner], attn_in.at[p.s], r["a2a_send"].at[owner], r["a2a_recv"].at[p.s], owner
            )

        def a2a_from(owner):
            return p.to_seq(
                attn_out.at[owner], attn_in.at[owner], r["a2a_send"].at[owner], r["a2a_recv"].at[owner], owner
            )

        blocks = total // q_block
        for n in reversed(range(blocks)):
            seen = (n + 1) * q_block
            rows = pl.ds(n * q_block, q_block)
            q_pos = lax.broadcasted_iota(jnp.int32, (q_block, 1), 0) + n * q_block
            k_pos = lax.broadcasted_iota(jnp.int32, (1, seen), 1)
            allowed = (segment_of(q_pos, len_ref) == segment_of(k_pos, len_ref)) & (k_pos <= q_pos)
            q_rows = q_all[rows, :]
            acc = jnp.zeros((q_block, cols), F32)
            lse = jnp.zeros((q_block, 128), F32)
            lane = lax.broadcasted_iota(jnp.int32, (q_block, 128), 1)
            for head in range(heads):
                own = head_mask(q_block, cols, head)
                scores = dot(jnp.where(own, q_rows, jnp.zeros_like(q_rows)), k_all[0:seen, :], ((1,), (1,)))
                scores = jnp.where(allowed, scores, MASKED_SCORE)
                top = jnp.max(scores, axis=1, keepdims=True)
                weights = jnp.exp(scores - top)
                sums = jnp.sum(weights, axis=1, keepdims=True)
                out = dot(weights.astype(BF16), v_all[0:seen, :]) / sums
                acc = jnp.where(own, out, acc)
                lse = jnp.where(lane == head, top + jnp.log(sums), lse)
            attn[rows, :] = acc
            lse_all[:, rows] = jnp.transpose(lse)[0:8, :]
            owner, first = (n * q_block) // tok, (n * q_block) % tok
            attn_out[owner, pl.ds(first, q_block)] = acc.astype(BF16)
            if first == 0:

                @pl.when(p.s != owner)
                def _(owner=owner):
                    a2a(owner).start()

                @pl.when(p.s == owner)
                def _(owner=owner):
                    attn_in[owner] = attn_out[owner]

        disp_c.relay(0)
        disp_c.relay(1)
        disp_c.start_seq(2)
        load_o.wait()
        sums = tok_ref[...].astype(F32) + row_of(bo_ref)
        for owner in range(n_seq):

            @pl.when(p.s != owner)
            def _(owner=owner):
                a2a_from(owner).wait_recv()

            sums = sums + dot(attn_in[owner], w_o[pl.ds(owner * cols, cols), :])
        resid[...] = sums
        disp_c.relay(2)
        disp_c.start_seq(3)

        gather1.drain()
        gout = xall.at[0]
        low = gout.at[p.s]

        def norm_two_tile(n, carry):
            low[tile_rows(n), :] = layer_norm(resid[tile_rows(n), :], gain2, bias2)[0].astype(BF16)
            return carry

        lax.fori_loop(0, tok // tile, norm_two_tile, 0)
        lay_out(send_n, low)

        disp_n = Dispatch(p, send_n, held, g["disp_n"][0:2], g["disp_n"][2:4])
        comb_g = Combine(p, part, *g["comb_g"][0:3], back, g["comb_g"][3:5], g["comb_g"][5:7], slots)
        comb_f = Combine(p, held, *g["comb_f"][0:2], None, ret, g["comb_f"][2:4], g["comb_f"][4:6], n_exp)
        disp_n.own()
        disp_n.start_seq(0)
        for step in range(1, n_exp):
            disp_n.start_exp(step)
        dwu[...] = jnp.zeros_like(dwu)
        dwd[...] = jnp.zeros_like(dwd)
        dbu_ref[...] = jnp.zeros_like(dbu_ref)
        csum_ref[...] = jnp.zeros_like(csum_ref)
        bias_down = bd_ref[...].astype(F32)
        for c in load_ffn:
            c.wait()

        def forward_rows(t):
            if t < n_exp:
                comb_f.start(t)
            if 2 <= t < n_exp + 2:
                comb_f.pass_on(t - 2)
            if t >= 3:
                comb_f.finish(t - 3, bias_down)

        def compute(step):
            x = held[step].reshape(routed, width)
            gr = cot[step].reshape(routed, width)
            ones = jnp.ones((8, routed), BF16)
            csum_ref[...] += dot(ones, gr)[0:1, :]
            y = jnp.zeros((routed, width), F32)
            gx = jnp.zeros((routed, width), F32)
            for b in range(hidden // block):
                at = pl.ds(b * block, block)
                wu_b, wd_b = wu[:, at], wd[at, :]
                pre = dot(x, wu_b) + bu_ref[:, at].astype(F32)
                g_act = dot(gr, wd_b, ((1,), (1,)))
                sq = pre * pre
                th = jnp.tanh(GELU_A * pre * (1.0 + GELU_B * sq))
                half = 0.5 * (1.0 + th)
                act = (pre * half).astype(BF16)
                slope = half + 0.5 * pre * (1.0 - th * th) * (GELU_A * (1.0 + 3.0 * GELU_B * sq))
                g_pre = (g_act * slope).astype(BF16)
                dbu_ref[:, at] += dot(ones, g_pre)[0:1, :]
                y = y + dot(act, wd_b)
                gx = gx + dot(g_pre, wu_b, ((1,), (1,)))
                dwu[:, at] += dot(x, g_pre, ((0,), (0,)))
                dwd[at, :] += dot(act, gr, ((0,), (0,)))
            part[lax.rem(step, slots)] = gx.astype(BF16).reshape(n_seq, cap, width)
            disp_n.sent(step)
            held[step] = y.astype(BF16).reshape(n_seq, cap, width)

        stores = [
            pltpu.make_async_copy(dwu, dwu_out, local_sems.at[6]),
            pltpu.make_async_copy(dwd, dwd_out, local_sems.at[7]),
        ]

        def loop(t, carry):
            @pl.when(t < n_exp)
            def _():
                disp_n.start_seq(t)

            @pl.when(t + ahead - 1 < n_exp)
            def _():
                disp_c.start_seq(t + ahead - 1)

            @pl.when(t <= n_exp)
            def _():
                disp_n.relay(t - 1)

            @pl.when(t + ahead - 2 < n_exp)
            def _():
                disp_c.relay(t + ahead - 2)

            @pl.when((t >= 3) & (t <= n_exp + 2))
            def _():
                comb_g.pass_on(t - 3)

            @pl.when(t >= 4)
            def _():
                comb_g.finish(t - 4)

            @pl.when(t == n_exp + 1)
            def _():
                forward_rows(0)

            @pl.when((t >= 2) & (t <= n_exp + 1))
            def _():
                disp_c.arrived(t - 2)
                disp_n.arrived(t - 2)
                compute(t - 2)
                comb_g.start(t - 2)

            @pl.when(t == n_exp + 1)
            def _():
                for c in stores:
                    c.start()

            @pl.when(t == n_exp + 2)
            def _():
                forward_rows(1)

            @pl.when(t == n_exp + 3)
            def _():
                forward_rows(2)

            return carry

        lax.fori_loop(1, n_exp + 4, loop, 0)
        background = [functools.partial(forward_rows, t) for t in range(3, n_exp + 3)]

        def turn(count=1):
            for _ in range(count):
                if background:
                    background.pop(0)()

        turn(1)
        comb_g.drain()

        gin_ref[...] = dot(pick[...], back[...].reshape(n_exp * cap, width), ((0,), (0,)))

        def norm_two_back(n, carry):
            at = tile_rows(n)
            g_two = gin_ref[at, :]
            _, xhat, inv_std = layer_norm(resid[at, :], gain2, 0.0)
            g_resid = cot_ref[at, :].astype(F32) + norm_back(g_two, xhat, inv_std, gain2)
            gin_ref[at, :] = g_resid
            g_low = g_resid.astype(BF16)
            gout[p.s, at, :] = g_low
            new = (g_low.astype(F32), g_two * xhat, g_two)
            return tuple(old + jnp.sum(v, axis=0, keepdims=True) for old, v in zip(carry, new))

        zero_row = jnp.zeros((1, width), F32)
        sums2 = lax.fori_loop(0, tok // tile, norm_two_back, (zero_row,) * 3)
        gather2 = Gather(p, gout, *g["gather2"])
        gather2.start()
        vec_own[...] = jnp.zeros_like(vec_own)
        for n in range(3):
            vec_own[4 + n : 5 + n, :] = sums2[n]
        wo_mine = w_o.at[mine, :]

        def grad_attn(owner):
            rows = pl.ds(pl.multiple_of(owner * tok, tok), tok)
            gattn[rows, :] = dot(gout[owner], wo_mine[...], ((1,), (1,))).astype(BF16)

        grad_attn(p.s)
        for c in stores:
            c.wait()
        dwu[0:total, 0 : 2 * cols] = jnp.zeros((total, 2 * cols), F32)
        gather2.relay()
        gather2.wait((2, 3))
        grad_attn(p.near)
        grad_attn(p.far)
        gather2.wait((4, 5))
        turn(1)
        grad_attn(p.diag)

        def place_w(owner, e, half=None):
            rows = rows_w if half is None else rows_w // 2
            first = e * rows_w + (0 if half is None else half * rows)
            return gw_out.at[
                :, pl.ds(pl.multiple_of(first, rows), rows), pl.ds(pl.multiple_of(owner * cols, cols), cols)
            ]

        def place_o(owner, e, half=None):
            rows = pl.ds(pl.multiple_of(owner * cols + e * rows_o, rows_o), rows_o)
            if half is None:
                return go_out.at[rows, :]
            return go_out.at[rows, pl.ds(half * (width // 2), width // 2)]

        sum_o = SumAll(p, *g["sum_o"][0:5], place_o, g["sum_o"][5], g["sum_o"][6:])
        sum_w = SumAll(p, *g["sum_w"][0:5], place_w, g["sum_w"][5], g["sum_w"][6:])
        src_o, src_w = sum_o.src, sum_w.src
        for b in range(cols // 128):
            a_low = attn[:, b * 128 : (b + 1) * 128].astype(BF16)
            got = dot(a_low, gout[...].reshape(total, width), ((0,), (0,))).astype(BF16)
            for n in range(128 // rows_o):
                e = b * (128 // rows_o) + n
                src_o[e % 2, e // 2] = got[n * rows_o : (n + 1) * rows_o]
        sum_o.start()

        head_rows = lax.broadcasted_iota(jnp.int32, (8, cols), 0)
        head_lane = lax.broadcasted_iota(jnp.int32, (8, cols), 1)
        per_head = (lax.div(head_lane, HEAD_DIM) == head_rows).astype(F32)
        for n in reversed(range(blocks)):
            turn(1)
            seen = (n + 1) * q_block
            rows = pl.ds(n * q_block, q_block)
            q_pos = lax.broadcasted_iota(jnp.int32, (1, q_block), 1) + n * q_block
            q_rows, g_rows = q_all[rows, :], gattn[rows, :]
            delta = lax.dot_general(
                per_head, g_rows.astype(F32) * attn[rows, :], (((1,), (1,)), ((), ())),
                precision=lax.Precision.HIGHEST, preferred_element_type=F32,
            )
            dq = jnp.zeros((q_block, cols), F32)
            for first in range(0, seen, 512):
                size = min(512, seen - first)
                keys = pl.ds(first, size)
                k_pos = lax.broadcasted_iota(jnp.int32, (size, 1), 0) + first
                allowed = (segment_of(q_pos, len_ref) == segment_of(k_pos, len_ref)) & (k_pos <= q_pos)
                k_seen, v_seen = k_all[keys, :], v_all[keys, :]
                dk_new = jnp.zeros((size, cols), F32)
                dv_new = jnp.zeros((size, cols), F32)
                for head in range(heads):
                    own = head_mask(q_block, cols, head)
                    q_own = jnp.where(own, q_rows, jnp.zeros_like(q_rows))
                    g_own = jnp.where(own, g_rows, jnp.zeros_like(g_rows))
                    scores = dot(k_seen, q_own, ((1,), (1,)))
                    probs = jnp.where(allowed, jnp.exp(scores - lse_all[head : head + 1, rows]), 0.0)
                    g_probs = dot(v_seen, g_own, ((1,), (1,)))
                    g_scores = (probs * (g_probs - delta[head : head + 1, :])).astype(BF16)
                    dk_new = dk_new + dot(g_scores, q_own)
                    dv_new = dv_new + dot(probs.astype(BF16), g_own)
                    dq = dq + jnp.where(own, dot(g_scores, k_seen, ((0,), (0,))), 0.0)
                dk[keys, :] += dk_new
                dv[keys, :] += dv_new
            dqkv[rows, 0:cols] = (dq * SCORE_SCALE).astype(BF16)
            if n == blocks - 2:
                sum_o.spread()
        sum_o.reduce()
        sum_o.forward(0)
        dqkv[:, cols : 2 * cols] = dk[...].astype(BF16)
        dqkv[:, 2 * cols :] = dv[...].astype(BF16)

        for b in range(width // 128):
            got = dot(n1[:, b * 128 : (b + 1) * 128], dqkv[...], ((0,), (0,))).astype(BF16)
            for n in range(128 // rows_w):
                e = b * (128 // rows_w) + n
                for m in range(3):
                    src_w[e % 2, e // 2, m] = got[n * rows_w : (n + 1) * rows_w, m * cols : (m + 1) * cols]
        sum_w.start()
        gather2.drain()
        red = Combine(p, xall, *g["red"][0:2], None, None, g["red"][2:4], (None, None), 1)
        for owner in range(n_seq):
            piece = dqkv[pl.ds(owner * tok, tok), :]
            xall[0, owner] = dot(piece, w_all[...], ((1,), (1,))).astype(BF16)
        red.start(0)
        sum_w.spread()
        d_sums = dot(jnp.ones((8, total), BF16), dqkv[...])
        vec_own[2:3, mine] = d_sums[0:1, 0:cols]
        vec_own[3:4, mine] = d_sums[0:1, 2 * cols :]
        turn(1)
        sum_o.relay(0)
        for hop in range(1, chips):
            sum_o.forward(hop)
        turn(1)
        red.pass_on(0)
        turn(1)
        for hop in range(1, chips):
            sum_o.relay(hop)
        turn(1)
        sum_w.reduce()
        sum_w.forward(0)
        red.arrived(0)
        half_tok = tok // 2
        for n in range(2):
            gout[p.s, pl.ds(n * half_tok, half_tok), :] = red.summed(0, n).astype(BF16)

        def norm_one_back(n, carry):
            at = tile_rows(n)
            g_one = gout[p.s, at, :].astype(F32)
            _, xhat, inv_std = layer_norm(tok_ref[at, :].astype(F32), gain1, 0.0)
            gin_ref[at, :] += norm_back(g_one, xhat, inv_std, gain1)
            new = (g_one * xhat, g_one)
            return tuple(old + jnp.sum(v, axis=0, keepdims=True) for old, v in zip(carry, new))

        sums1 = lax.fori_loop(0, tok // tile, norm_one_back, (zero_row,) * 2)
        for n in range(2):
            vec_own[n : n + 1, :] = sums1[n]
        vec_seq[p.s] = vec_own[...]

        def tell(other):
            return p.to_seq(vec_own, vec_seq.at[p.s], r["vs_send"].at[other], r["vs_recv"].at[p.s], other)

        def told(other):
            return p.to_seq(vec_own, vec_seq.at[other], r["vs_send"].at[other], r["vs_recv"].at[other], other)

        others = (p.near, p.far, p.diag)
        for other in others:
            tell(other).start()
        turn(2)
        for hop in range(1, chips):
            sum_w.forward(hop)
            sum_w.relay(hop - 1)
            turn(1)
        for other in others:
            told(other).wait_recv()
        for other in others:
            tell(other).wait_send()
        vec = vec_seq[0]
        for n in range(1, n_seq):
            vec = vec + vec_seq[n]
        vec_own[...] = vec
        vec_exp[p.e] = vec

        def show(step):
            other = p.peer(step, -1)
            return p.to_exp(vec_own, vec_exp.at[p.e], r["ve_send"].at[step], r["ve_recv"].at[step], other)

        def shown(step):
            other = p.peer(step, 1)
            return p.to_exp(vec_own, vec_exp.at[other], r["ve_send"].at[step], r["ve_recv"].at[step], other)

        for step in range(1, n_exp):
            show(step).start()
        sum_w.relay(chips - 1)
        turn(n_exp)
        comb_f.drain()
        for n in range(tok // 128):
            at = slice(n * 128, (n + 1) * 128)
            rows_back = dot(pick[:, at], ret[...].reshape(n_exp * cap, width), ((0,), (0,)))
            out_ref[at, :] = (resid[at, :] + rows_back).astype(BF16)
        for hop in range(chips):
            sum_o.arrived(hop)
        for hop in range(chips):
            sum_w.arrived(hop)
        for step in range(1, n_exp):
            shown(step).wait_recv()
            show(step).wait_send()
        vec = vec_exp[0]
        for n in range(1, n_exp):
            vec = vec + vec_exp[n]
        vec_ref[...] = vec
        for owner in range(n_seq):

            @pl.when(p.s != owner)
            def _(owner=owner):
                a2a(owner).wait_send()

        disp_c.drain()
        disp_n.drain(seq=False)
        sum_o.drain()
        sum_w.drain()

    vmem = pl.BlockSpec(memory_space=pltpu.VMEM)
    hbm = pl.BlockSpec(memory_space=pl.ANY)
    smem = pl.BlockSpec(memory_space=pltpu.SMEM)
    shape = jax.ShapeDtypeStruct
    return pl.pallas_call(
        kernel,
        out_shape=[
            shape((tok, width), BF16),
            shape((tok, width), F32),
            shape((8, width), F32),
            shape((1, hidden), F32),
            shape((1, width), F32),
            shape((width, hidden), F32),
            shape((hidden, width), F32),
            shape((3, width, width), BF16),
            shape((width, width), BF16),
        ],
        in_specs=[vmem] * 3 + [smem] + [vmem] * 2 + [hbm] * 3 + [vmem] * 2 + [hbm] + [vmem] * 3
        + [hbm, vmem, hbm, vmem],
        out_specs=[vmem] * 5 + [hbm] * 4,
        scratch_shapes=scratch,
        compiler_params=pltpu.CompilerParams(
            collective_id=collective_id, has_side_effects=True, vmem_limit_bytes=VMEM_LIMIT
        ),
        name="layer",
    )(tokens, ids, cotangent, lengths, *ln1, *w_qkv, b_query, b_value, w_out, b_out, *ln2, w_up, b_up, w_down, b_down)


def finish(output, input_grad, vec, dbu, csum, dwu, dwd, gw, go):
    tok, width = output.shape
    hidden = dwu.shape[1]
    cols = width // 4
    piece = 256

    def kernel(out_in, gin_in, vec_ref, dbu_in, csum_ref, dwu_in, dwd_in, gw_in, go_in, *refs):
        (out_o, gin_o, l1g, l1b, wq_o, bq_o, wk_o, wv_o, bv_o, wo_o, bo_o, l2g, l2b, dwu_o, dbu_o, dwd_o, dbd_o) = refs[:17]
        small, wide, same_b, same_f, sems = refs[17:22]
        count = 0

        def pair(src, mid_in, mid_out, dst):
            nonlocal count
            load = pltpu.make_async_copy(src, mid_in, sems.at[count])
            store = pltpu.make_async_copy(mid_out, dst, sems.at[count + 1])
            count += 2
            return load, store

        widen, plain = [], []
        for m, (src, dst) in enumerate(
            ((gw_in.at[0], wq_o), (gw_in.at[1], wk_o), (gw_in.at[2], wv_o), (go_in, wo_o))
        ):
            for n in range(width // piece):
                rows = pl.ds(n * piece, piece)
                at = m * (width // piece) + n
                widen.append((pair(src.at[rows], small.at[at], wide.at[at], dst.at[rows]), at))
        at = 0
        for src, dst, total in ((dwu_in, dwu_o.at[0], width), (dwd_in, dwd_o.at[0], hidden), (gin_in, gin_o.at[0], tok)):
            for n in range(total // piece):
                rows = pl.ds(n * piece, piece)
                plain.append(pair(src.at[rows], same_f.at[at], same_f.at[at], dst.at[rows]))
                at += 1
        plain.append(pair(out_in, same_b, same_b, out_o.at[0]))
        order = []
        for n in range(max(len(widen), len(plain))):
            order += widen[n : n + 1] + [(c, None) for c in plain[n : n + 1]]
        for (load, _), _ in order:
            load.start()
        for n, ref in enumerate((l1g, l1b, bq_o, bv_o, bo_o, l2g, l2b)):
            ref[...] = vec_ref[n : n + 1, :].reshape(width)
        dbu_o[...] = dbu_in[...]
        first = pl.multiple_of(lax.axis_index("seq") * cols, cols)
        dbd_o[...] = csum_ref[:, pl.ds(first, cols)]
        for (load, store), at in order:
            load.wait()
            if at is not None:
                wide[at] = small[at].astype(F32)
            store.start()
        for (_, store), _ in order:
            store.wait()

    vmem = pl.BlockSpec(memory_space=pltpu.VMEM)
    hbm = pl.BlockSpec(memory_space=pl.ANY)
    shape = jax.ShapeDtypeStruct
    row, square = shape((width,), F32), shape((width, width), F32)
    n_widen = 4 * (width // piece)
    n_plain = (width + hidden + tok) // piece
    return pl.pallas_call(
        kernel,
        out_shape=[
            shape((1, tok, width), BF16), shape((1, tok, width), F32), row, row, square, row, square, square, row,
            square, row, row, row, shape((1, width, hidden), F32), shape((1, hidden), F32),
            shape((1, hidden, width), F32), shape((1, cols), F32),
        ],
        in_specs=[hbm, hbm, vmem, vmem, vmem, hbm, hbm, hbm, hbm],
        out_specs=[hbm, hbm, vmem, vmem, hbm, vmem, hbm, hbm, vmem, hbm, vmem, vmem, vmem, hbm, vmem, hbm, vmem],
        scratch_shapes=[
            pltpu.VMEM((n_widen, piece, width), BF16),
            pltpu.VMEM((n_widen, piece, width), F32),
            pltpu.VMEM((tok, width), BF16),
            pltpu.VMEM((n_plain, piece, width), F32),
            pltpu.SemaphoreType.DMA((2 * (n_widen + n_plain + 1),)),
        ],
        compiler_params=pltpu.CompilerParams(vmem_limit_bytes=VMEM_LIMIT),
        name="finish",
    )(output, input_grad, vec, dbu, csum, dwu, dwd, gw, go)


def shards(
    tokens, lengths, expert_ids, ln1_gain, ln1_bias, w_query, b_query, w_key, w_value, b_value, w_out, b_out,
    ln2_gain, ln2_bias, w_up, b_up, w_down, b_down, cotangent,
):
    parts = layer(
        tokens[0], expert_ids[0, :, 0][None], cotangent[0], lengths, (ln1_gain, ln1_bias),
        (w_query, w_key, w_value), b_query, b_value, w_out, b_out, (ln2_gain, ln2_bias), w_up[0], b_up, w_down[0],
        b_down, lax.axis_size("exp"), 0,
    )
    return tuple(finish(*parts))


def norm_layer(values_in, gain_vec, shift_vec):
    center = values_in - jnp.mean(values_in, axis=-1, keepdims=True)
    inv_std = lax.rsqrt(jnp.mean(center * center, axis=-1, keepdims=True) + EPSILON)
    return center * inv_std * gain_vec + shift_vec


def segment_ids(positions, seq_ends):
    return jnp.sum((positions[:, None] >= seq_ends[None, :]).astype(jnp.int32), axis=1)


def visible_pairs(query_pos, query_seg, key_pos, key_seg):
    return ((query_seg[:, None] == key_seg[None, :]) & (key_pos[None, :] <= query_pos[:, None]))[
        None
    ]


def project(left_op, right_op):
    return jnp.dot(left_op, right_op, preferred_element_type=jnp.float32)


def shards_any(
    tokens,
    lengths,
    expert_ids,
    ln1_gain,
    ln1_bias,
    w_query,
    b_query,
    w_key,
    w_value,
    b_value,
    w_out,
    b_out,
    ln2_gain,
    ln2_bias,
    w_up,
    b_up,
    w_down,
    b_down,
    cotangent,
):
    tok_rows = tokens.shape[1]
    width = tokens.shape[2]
    seq_size = lax.axis_size("seq")
    exp_size = lax.axis_size("exp")
    seq_rank = lax.axis_index("seq")
    seq_ends = jnp.cumsum(lengths[0])
    own_pos = seq_rank * tok_rows + jnp.arange(tok_rows, dtype=jnp.int32)
    own_seg = segment_ids(own_pos, seq_ends)
    inputs = tokens[0].astype(jnp.float32)
    gain_one = ln1_gain.astype(jnp.float32)
    bias_one = ln1_bias.astype(jnp.float32)
    gain_two = ln2_gain.astype(jnp.float32)
    bias_two = ln2_bias.astype(jnp.float32)
    normed_one_low = norm_layer(inputs, gain_one, bias_one).astype(jnp.bfloat16)
    query_low = (project(normed_one_low, w_query) + b_query.astype(jnp.float32)).astype(
        jnp.bfloat16
    )
    keys_low = project(normed_one_low, w_key).astype(jnp.bfloat16)
    values_low = (project(normed_one_low, w_value) + b_value.astype(jnp.float32)).astype(
        jnp.bfloat16
    )
    query_heads = query_low.reshape(tok_rows, HEADS, HEAD_DIM)
    initial = (
        jnp.full((HEADS, tok_rows), MASKED_SCORE, jnp.float32),
        jnp.zeros((HEADS, tok_rows), jnp.float32),
        jnp.zeros((HEADS, tok_rows, HEAD_DIM), jnp.float32),
    )
    key_piece = lax.all_gather(keys_low, "seq", axis=0, tiled=True)
    value_piece = lax.all_gather(values_low, "seq", axis=0, tiled=True)
    piece_len = key_piece.shape[0]
    fold_block_len = math.gcd(piece_len, 512)
    block_count = piece_len // fold_block_len
    key_blocks = key_piece.reshape(block_count, fold_block_len, HEADS, HEAD_DIM)
    value_blocks = value_piece.reshape(block_count, fold_block_len, HEADS, HEAD_DIM)
    offsets = jnp.arange(block_count, dtype=jnp.int32) * fold_block_len

    def block_step(state_now, packed):
        row_max, row_total, accumulated = state_now
        key_blk, value_blk, offset = packed
        key_pos = offset + jnp.arange(fold_block_len, dtype=jnp.int32)
        allowed = visible_pairs(own_pos, own_seg, key_pos, segment_ids(key_pos, seq_ends))
        scores = (
            jnp.einsum("qhd,khd->hqk", query_heads, key_blk, preferred_element_type=jnp.float32)
            * SCORE_SCALE
        )
        masked = jnp.where(allowed, scores, MASKED_SCORE)
        new_max = jnp.maximum(row_max, jnp.max(masked, axis=-1))
        weights = jnp.where(allowed, jnp.exp(masked - new_max[..., None]), 0.0)
        factor = jnp.exp(row_max - new_max)
        row_total = row_total * factor + jnp.sum(weights, axis=-1)
        accumulated = accumulated * factor[..., None] + jnp.einsum(
            "hqk,khd->hqd",
            weights.astype(jnp.bfloat16),
            value_blk,
            preferred_element_type=jnp.float32,
        )
        return ((new_max, row_total, accumulated), None)

    result, _ = lax.scan(block_step, initial, (key_blocks, value_blocks, offsets))
    row_max, row_total, accumulated = result
    attn_heads = accumulated / row_total[..., None]
    attn_low = jnp.transpose(attn_heads, (1, 0, 2)).reshape(tok_rows, width).astype(jnp.bfloat16)
    resid = inputs + project(attn_low, w_out) + b_out.astype(jnp.float32)
    normed_two_low = norm_layer(resid, gain_two, bias_two).astype(jnp.bfloat16)
    experts = exp_size * w_up.shape[0]
    capacity = 2 * tok_rows // experts
    expert_of = expert_ids[0, :, 0]
    onehot = (expert_of[:, None] == jnp.arange(experts, dtype=jnp.int32)[None, :]).astype(jnp.int32)
    slot_of = jnp.sum(onehot * (jnp.cumsum(onehot, axis=0) - onehot), axis=1)
    send_rows = (
        jnp.zeros((experts, capacity, width), jnp.bfloat16)
        .at[expert_of, slot_of]
        .set(normed_two_low)
    )
    received = lax.all_to_all(send_rows, "exp", split_axis=0, concat_axis=0, tiled=True)
    recv_count = experts * capacity
    recv_rows = received.reshape(recv_count, width)
    up_weight = w_up[0]
    up_bias = b_up[0]
    down_weight = w_down[0]
    down_bias = b_down[0].astype(jnp.float32)
    piece_width = width // seq_size
    grad_send = (
        jnp.zeros((experts, capacity, width), jnp.bfloat16).at[expert_of, slot_of].set(cotangent[0])
    )
    gathered = lax.all_gather(recv_rows, "seq", axis=0, tiled=True)
    preact = project(gathered, up_weight) + up_bias.astype(jnp.float32)
    act_low = jax.nn.gelu(preact).astype(jnp.bfloat16)
    part = act_low
    expert_out = (
        lax.psum_scatter(
            project(part, down_weight).astype(jnp.bfloat16), "seq", scatter_dimension=0, tiled=True
        ).astype(jnp.float32)
        + down_bias
    )
    returned = lax.all_to_all(
        expert_out.astype(jnp.bfloat16).reshape(experts, capacity, width),
        "exp",
        split_axis=0,
        concat_axis=0,
        tiled=True,
    )
    grad_recv = lax.all_to_all(grad_send, "exp", split_axis=0, concat_axis=0, tiled=True).reshape(
        recv_count, width
    )
    grad_all = lax.all_gather(grad_recv, "seq", axis=0, tiled=True)
    bias_full = jnp.sum(grad_all.astype(jnp.float32), axis=0)
    grad_b_down = lax.dynamic_slice_in_dim(bias_full, seq_rank * piece_width, piece_width, 0)
    grad_act = jnp.einsum("rd,fd->rf", grad_all, down_weight, preferred_element_type=jnp.float32)
    grad_pre = jax.vjp(jax.nn.gelu, preact)[1](grad_act)[0].astype(jnp.bfloat16)
    grad_w_down = jnp.einsum("rf,rd->fd", act_low, grad_all, preferred_element_type=jnp.float32)
    grad_w_up = jnp.einsum("rd,rf->df", gathered, grad_pre, preferred_element_type=jnp.float32)
    grad_b_up = jnp.sum(grad_pre.astype(jnp.float32), axis=0)
    part = grad_pre
    grad_home = lax.psum_scatter(
        jnp.einsum("rf,df->rd", part, up_weight, preferred_element_type=jnp.float32).astype(
            jnp.bfloat16
        ),
        "seq",
        scatter_dimension=0,
        tiled=True,
    )
    ffn_rows = returned[expert_of, slot_of].astype(jnp.float32)
    output = (resid + ffn_rows).astype(jnp.bfloat16)
    grad_back = lax.all_to_all(
        grad_home.reshape(experts, capacity, width), "exp", split_axis=0, concat_axis=0, tiled=True
    )
    grad_normed_two = grad_back[expert_of, slot_of].astype(jnp.float32)
    _, norm_two_back = jax.vjp(norm_layer, resid, gain_two, bias_two)
    grad_resid_norm, grad_gain_two, grad_bias_two = norm_two_back(grad_normed_two)
    grad_resid = cotangent[0].astype(jnp.float32) + grad_resid_norm
    grad_out_low = grad_resid.astype(jnp.bfloat16)
    grad_w_out = jnp.einsum("qa,qd->ad", attn_low, grad_out_low, preferred_element_type=jnp.float32)
    grad_b_out = jnp.sum(grad_out_low.astype(jnp.float32), axis=0)
    grad_attn_low = jnp.einsum(
        "qd,ad->qa", grad_out_low, w_out, preferred_element_type=jnp.float32
    ).astype(jnp.bfloat16)
    grad_attn_heads = grad_attn_low.reshape(tok_rows, HEADS, HEAD_DIM)
    delta = jnp.sum(
        jnp.transpose(grad_attn_heads.astype(jnp.float32), (1, 0, 2)) * attn_heads, axis=-1
    )
    whole_keys, whole_values = (
        lax.all_gather(keys_low, "seq", axis=0, tiled=True),
        lax.all_gather(values_low, "seq", axis=0, tiled=True),
    )
    group_len = whole_keys.shape[0]
    block_len = math.gcd(group_len, 512)
    block_count = group_len // block_len

    def back_step(grad_query, packed):
        key_blk, value_blk, offset = packed
        key_pos = offset + jnp.arange(block_len, dtype=jnp.int32)
        allowed = visible_pairs(own_pos, own_seg, key_pos, segment_ids(key_pos, seq_ends))
        scores = (
            jnp.einsum("qhd,khd->hqk", query_heads, key_blk, preferred_element_type=jnp.float32)
            * SCORE_SCALE
        )
        masked = jnp.where(allowed, scores, MASKED_SCORE)
        probabilities = (
            jnp.where(allowed, jnp.exp(masked - row_max[..., None]), 0.0) / row_total[..., None]
        )
        probs_low = probabilities.astype(jnp.bfloat16)
        grad_probs = jnp.einsum(
            "qhd,khd->hqk", grad_attn_heads, value_blk, preferred_element_type=jnp.float32
        )
        grad_scores = (probabilities * (grad_probs - delta[..., None])).astype(jnp.bfloat16)
        grad_query = (
            grad_query
            + jnp.einsum("hqk,khd->qhd", grad_scores, key_blk, preferred_element_type=jnp.float32)
            * SCORE_SCALE
        )
        grad_key_blk = (
            jnp.einsum("hqk,qhd->khd", grad_scores, query_heads, preferred_element_type=jnp.float32)
            * SCORE_SCALE
        )
        grad_value_blk = jnp.einsum(
            "hqk,qhd->khd", probs_low, grad_attn_heads, preferred_element_type=jnp.float32
        )
        return (grad_query, (grad_key_blk, grad_value_blk))

    block_offsets = jnp.arange(block_count, dtype=jnp.int32) * block_len
    grad_query, key_value_parts = lax.scan(
        back_step,
        jnp.zeros((tok_rows, HEADS, HEAD_DIM), jnp.float32),
        (
            whole_keys.reshape(block_count, block_len, HEADS, HEAD_DIM),
            whole_values.reshape(block_count, block_len, HEADS, HEAD_DIM),
            block_offsets,
        ),
    )
    grad_keys, grad_values = (
        lax.psum_scatter(
            key_value_parts[0].reshape(group_len, width).astype(jnp.bfloat16),
            "seq",
            scatter_dimension=0,
            tiled=True,
        ).astype(jnp.float32),
        lax.psum_scatter(
            key_value_parts[1].reshape(group_len, width).astype(jnp.bfloat16),
            "seq",
            scatter_dimension=0,
            tiled=True,
        ).astype(jnp.float32),
    )
    grad_query_low = grad_query.reshape(tok_rows, width).astype(jnp.bfloat16)
    grad_keys_low = grad_keys.astype(jnp.bfloat16)
    grad_values_low = grad_values.astype(jnp.bfloat16)
    grad_w_query = jnp.einsum(
        "qa,qd->ad", normed_one_low, grad_query_low, preferred_element_type=jnp.float32
    )
    grad_b_query = jnp.sum(grad_query_low.astype(jnp.float32), axis=0)
    grad_w_key = jnp.einsum(
        "qa,qd->ad", normed_one_low, grad_keys_low, preferred_element_type=jnp.float32
    )
    grad_w_value = jnp.einsum(
        "qa,qd->ad", normed_one_low, grad_values_low, preferred_element_type=jnp.float32
    )
    grad_b_value = jnp.sum(grad_values_low.astype(jnp.float32), axis=0)
    grad_normed_one = (
        (
            jnp.einsum("qd,ad->qa", grad_query_low, w_query, preferred_element_type=jnp.float32)
            + jnp.einsum("qd,ad->qa", grad_keys_low, w_key, preferred_element_type=jnp.float32)
            + jnp.einsum("qd,ad->qa", grad_values_low, w_value, preferred_element_type=jnp.float32)
        )
        .astype(jnp.bfloat16)
        .astype(jnp.float32)
    )
    _, norm_one_back = jax.vjp(norm_layer, inputs, gain_one, bias_one)
    grad_in_norm, grad_gain_one, grad_bias_one = norm_one_back(grad_normed_one)
    input_grad = grad_resid + grad_in_norm
    summed = lax.psum(
        (
            grad_gain_one,
            grad_bias_one,
            grad_w_query,
            grad_b_query,
            grad_w_key,
            grad_w_value,
            grad_b_value,
            grad_w_out,
            grad_b_out,
            grad_gain_two,
            grad_bias_two,
        ),
        ("seq", "exp"),
    )
    return (
        output[None],
        input_grad[None],
        summed[0],
        summed[1],
        summed[2],
        summed[3],
        summed[4],
        summed[5],
        summed[6],
        summed[7],
        summed[8],
        summed[9],
        summed[10],
        grad_w_up[None],
        grad_b_up[None],
        grad_w_down[None],
        grad_b_down[None],
    )


def solution(mesh):
    placed = (
        P("exp", "seq", None),
        P("exp", None),
        P("exp", "seq", None),
        P(),
        P(),
        P(),
        P(),
        P(),
        P(),
        P(),
        P(),
        P(),
        P(),
        P(),
        P("exp", None, "seq"),
        P("exp", "seq"),
        P("exp", "seq", None),
        P("exp", None),
        P("exp", "seq", None),
    )
    plane = mesh.shape["seq"] == 4 and mesh.shape["exp"] % 2 == 0
    return jax.shard_map(
        shards if plane else shards_any,
        mesh=mesh,
        in_specs=placed,
        out_specs=(
            P("exp", "seq", None),
            P("exp", "seq", None),
            P(),
            P(),
            P(),
            P(),
            P(),
            P(),
            P(),
            P(),
            P(),
            P(),
            P(),
            P("exp", None, "seq"),
            P("exp", "seq"),
            P("exp", "seq", None),
            P("exp", "seq"),
        ),
        check_vma=False,
    )
```

```python
import functools
import math

import jax
import jax.numpy as jnp
from jax import lax
from jax.experimental import pallas as pl
from jax.experimental.pallas import tpu as pltpu
from jax.sharding import PartitionSpec as P

MESH = pl.DeviceIdType.MESH
F32 = jnp.float32
BF16 = jnp.bfloat16
VMEM_LIMIT = 63 * 2**20


def dot(a, b, dims=((1,), (0,))):
    return lax.dot_general(a, b, (dims, ((), ())), preferred_element_type=F32)


class Place:
    def __init__(self, n_exp):
        self.n_exp = n_exp
        self.s = lax.axis_index("seq")
        self.e = lax.axis_index("exp")
        low = lax.rem(self.s, 2)
        high = lax.div(self.s, 2)
        self.near = high * 2 + (1 - low)
        self.far = (1 - high) * 2 + low
        self.diag = (1 - high) * 2 + (1 - low)
        self.core = lax.rem(self.e, 2)
        self.chip = lax.div(self.e, 2)

    def peer(self, step, way):
        chips = self.n_exp // 2
        hop = lax.div(step, 2)
        if chips == 4:
            hop = hop + lax.div(hop, 2) * (5 - 2 * hop)
        chip = lax.rem(self.chip + way * hop + chips, chips)
        return chip * 2 + lax.rem(self.core + step, 2)

    def greet(self, diag=False):
        barrier = pltpu.get_barrier_semaphore()
        others = (self.near, self.far, self.diag) if diag else (self.near, self.far)
        for other in others:
            pl.semaphore_signal(barrier, inc=1, device_id=(other, self.e), device_id_type=MESH)

        def tell(step, carry):
            pl.semaphore_signal(
                barrier, inc=1, device_id=(self.s, self.peer(step, 1)), device_id_type=MESH
            )
            return carry

        lax.fori_loop(1, self.n_exp, tell, 0)
        pl.semaphore_wait(barrier, len(others) + self.n_exp - 1)

    def to_seq(self, src, dst, send_sem, recv_sem, other):
        return pltpu.make_async_remote_copy(
            src_ref=src, dst_ref=dst, send_sem=send_sem, recv_sem=recv_sem,
            device_id=(other, self.e), device_id_type=MESH,
        )

    def to_exp(self, src, dst, send_sem, recv_sem, other):
        return pltpu.make_async_remote_copy(
            src_ref=src, dst_ref=dst, send_sem=send_sem, recv_sem=recv_sem,
            device_id=(self.s, other), device_id_type=MESH,
        )


class Dispatch:
    def __init__(self, place, send, held, exp_sems, seq_sems):
        self.place, self.send, self.held = place, send, held
        self.exp_send, self.exp_recv = exp_sems
        self.seq_send, self.seq_recv = seq_sems
        self.cap = send.shape[1]

    @staticmethod
    def scratch(n_exp):
        return [
            pltpu.SemaphoreType.DMA((n_exp,)),
            pltpu.SemaphoreType.DMA((n_exp,)),
            pltpu.SemaphoreType.DMA((n_exp, 6)),
            pltpu.SemaphoreType.DMA((n_exp, 6)),
        ]

    def _exp(self, step):
        p = self.place
        other = p.peer(step, -1)
        return p.to_exp(
            self.send.at[other], self.held.at[step, p.s], self.exp_send.at[step], self.exp_recv.at[step], other
        )

    def _seq(self, step, owner, half, lane, other):
        p = self.place
        rows = pl.ds(half * (self.cap // 2), self.cap // 2)
        part = self.held.at[step, owner, rows]
        return p.to_seq(part, part, self.seq_send.at[step, lane], self.seq_recv.at[step, lane], other)

    def copies(self, step, lanes=range(6)):
        p = self.place
        spec = (
            (p.s, 0, p.near),
            (p.s, 1, p.far),
            (p.s, 1, p.near),
            (p.s, 0, p.far),
            (p.near, 0, p.far),
            (p.far, 1, p.near),
        )
        return [self._seq(step, spec[n][0], spec[n][1], n, spec[n][2]) for n in lanes]

    def start_exp(self, step):
        self._exp(step).start()

    def own(self):
        p = self.place
        self.held[0, p.s] = self.send[p.e]

    def start_seq(self, step):
        @pl.when(step > 0)
        def _():
            self._exp(step).wait_recv()

        for c in self.copies(step, range(4)):
            c.start()

    def relay(self, step):
        for c, out in zip(self.copies(step, (0, 1)), self.copies(step, (4, 5))):
            c.wait_recv()
            out.start()

    def arrived(self, step):
        for c in self.copies(step, range(2, 6)):
            c.wait_recv()

    def sent(self, step):
        for c in self.copies(step):
            c.wait_send()

    def drain(self, seq=True):
        def body(step, carry):
            if seq:
                self.sent(step)

            @pl.when(step > 0)
            def _():
                self._exp(step).wait_send()

            return carry

        lax.fori_loop(0, self.place.n_exp, body, 0)


class Combine:
    def __init__(self, place, part, passing, landing, total, back, seq_sems, exp_sems, slots):
        self.place, self.part, self.passing, self.landing = place, part, passing, landing
        self.total, self.back, self.slots = total, back, slots
        self.seq_send, self.seq_recv = seq_sems
        self.exp_send, self.exp_recv = exp_sems
        self.half = part.shape[2] // 2

    @staticmethod
    def scratch(n_exp, cap, width):
        return [
            pltpu.VMEM((n_exp, 2, cap // 2, width), BF16),
            pltpu.VMEM((n_exp, 4, cap // 2, width), BF16),
            pltpu.VMEM((n_exp, cap, width), BF16),
            pltpu.SemaphoreType.DMA((n_exp, 6)),
            pltpu.SemaphoreType.DMA((n_exp, 6)),
            pltpu.SemaphoreType.DMA((n_exp,)),
            pltpu.SemaphoreType.DMA((n_exp,)),
        ]

    def _slot(self, step):
        return lax.rem(step, self.slots)

    def _piece(self, step, owner, half):
        return self.part.at[self._slot(step), owner, pl.ds(half * self.half, self.half)]

    def _seq(self, src, dst, step, lane, other):
        return self.place.to_seq(
            src, dst, self.seq_send.at[step, lane], self.seq_recv.at[step, lane], other
        )

    def copies(self, step, lanes=range(6)):
        p = self.place
        spec = (
            (p.diag, 0, self.passing, 0, p.near),
            (p.diag, 1, self.passing, 1, p.far),
            (p.near, 0, self.landing, 0, p.near),
            (p.far, 1, self.landing, 3, p.far),
            (p.far, 0, self.landing, 2, p.far),
            (p.near, 1, self.landing, 1, p.near),
        )
        made = []
        for n in lanes:
            owner, half, buffer, at, other = spec[n]
            made.append(self._seq(self._piece(step, owner, half), buffer.at[step, at], step, n, other))
        return made

    def start(self, step):
        for c in self.copies(step, range(4)):
            c.start()

    def pass_on(self, step):
        p = self.place
        slot = self._slot(step)
        came, out = self.copies(step, (0, 1)), self.copies(step, (4, 5))
        for n, owner in enumerate((p.far, p.near)):
            rows = pl.ds(n * self.half, self.half)
            came[n].wait_recv()
            self.part[slot, owner, rows] = (
                self.part[slot, owner, rows].astype(F32) + self.passing[step, n].astype(F32)
            ).astype(BF16)
            out[n].start()

    def _whole(self, step):
        if self.total is None:
            return self.part.at[self._slot(step), self.place.s]
        return self.total.at[step]

    def _exp(self, step):
        p = self.place
        other = p.peer(step, 1)
        return p.to_exp(
            self._whole(step), self.back.at[p.e], self.exp_send.at[step], self.exp_recv.at[step], other
        )

    def arrived(self, step):
        copies = self.copies(step)
        for c in copies[2:]:
            c.wait_recv()
        for c in copies:
            c.wait_send()

    def summed(self, step, half):
        rows = pl.ds(half * self.half, self.half)
        return (
            self.part[self._slot(step), self.place.s, rows].astype(F32)
            + self.landing[step, half].astype(F32)
            + self.landing[step, 2 + half].astype(F32)
        )

    def finish(self, step, bias=None):
        p = self.place
        self.arrived(step)
        for half in range(2):
            value = self.summed(step, half)
            if bias is not None:
                value = value + bias
            rows = pl.ds(half * self.half, self.half)
            if self.total is None:
                self.part[self._slot(step), p.s, rows] = value.astype(BF16)
            else:
                self.total[step, rows] = value.astype(BF16)

        @pl.when(step > 0)
        def _():
            self._exp(step).start()

        @pl.when(step == 0)
        def _():
            self.back[p.e] = self._whole(0)[...]

    def drain(self):
        p = self.place

        def body(step, carry):
            c = self._exp(step)
            c.wait_send()
            c.wait_recv()
            return carry

        lax.fori_loop(1, p.n_exp, body, 0)


GELU_A = math.sqrt(2.0 / math.pi)
GELU_B = 0.044715


EPSILON = 1e-05
SCORE_SCALE = 0.125
MASKED_SCORE = -1e30
HEAD_DIM = 64
HEADS = 16


class Gather:
    def __init__(self, place, held, send_sems, recv_sems):
        self.place, self.held = place, held
        self.send_sems, self.recv_sems = send_sems, recv_sems
        self.half = held.shape[1] // 2

    @staticmethod
    def scratch():
        return [pltpu.SemaphoreType.DMA((6,)), pltpu.SemaphoreType.DMA((6,))]

    def copies(self, lanes=range(6)):
        p = self.place
        spec = (
            (p.s, 0, p.near),
            (p.s, 1, p.far),
            (p.s, 1, p.near),
            (p.s, 0, p.far),
            (p.near, 0, p.far),
            (p.far, 1, p.near),
        )
        made = []
        for n in lanes:
            owner, half, other = spec[n]
            part = self.held.at[owner, pl.ds(half * self.half, self.half)]
            made.append(p.to_seq(part, part, self.send_sems.at[n], self.recv_sems.at[n], other))
        return made

    def start(self):
        for c in self.copies(range(4)):
            c.start()

    def relay(self):
        for c, out in zip(self.copies((0, 1)), self.copies((4, 5))):
            c.wait_recv()
            out.start()

    def wait(self, lanes):
        for c in self.copies(lanes):
            c.wait_recv()

    def drain(self):
        for c in self.copies():
            c.wait_send()


def layer_norm(values, gain, shift):
    center = values - jnp.mean(values, axis=-1, keepdims=True)
    inv_std = lax.rsqrt(jnp.mean(center * center, axis=-1, keepdims=True) + EPSILON)
    xhat = center * inv_std
    return xhat * gain + shift, xhat, inv_std


def norm_back(grad, xhat, inv_std, gain):
    d = grad * gain
    return (
        d - jnp.mean(d, axis=-1, keepdims=True) - xhat * jnp.mean(d * xhat, axis=-1, keepdims=True)
    ) * inv_std


def row_choice(ids, n_exp, cap):
    tokens = ids.shape[1]
    named = (ids == lax.broadcasted_iota(jnp.int32, (128, tokens), 0)).astype(BF16)
    before = (
        lax.broadcasted_iota(jnp.int32, (tokens, tokens), 0)
        < lax.broadcasted_iota(jnp.int32, (tokens, tokens), 1)
    ).astype(BF16)
    earlier = dot(named, before) * named.astype(F32)
    slot = jnp.sum(earlier, axis=0, keepdims=True).astype(jnp.int32) + ids * cap
    return (slot == lax.broadcasted_iota(jnp.int32, (n_exp * cap, tokens), 0)).astype(BF16)


def segment_of(position, lengths):
    end = jnp.int32(0)
    count = jnp.zeros_like(position)
    for n in range(lengths.shape[1]):
        end = end + lengths[0, n]
        count = count + (position >= end).astype(jnp.int32)
    return count


def head_mask(rows, width, head):
    lane = lax.broadcasted_iota(jnp.int32, (rows, width), 1)
    return (lane >= head * HEAD_DIM) & (lane < (head + 1) * HEAD_DIM)


class SumAll:
    def __init__(self, place, src, core_in, mine, chip_in, res, where, local_sem, sems):
        self.place, self.src, self.core_in, self.mine = place, src, core_in, mine
        self.chip_in, self.res, self.where, self.local_sem = chip_in, res, where, local_sem
        (self.core_sems, self.rs_send, self.rs_recv, self.ag_send, self.ag_recv,
         self.seq_send, self.seq_recv, self.pair_send, self.pair_recv) = sems
        self.chips = place.n_exp // 2
        p = place
        self.sibling = p.chip * 2 + (1 - p.core)

    @staticmethod
    def scratch(n_exp, *piece):
        chips = n_exp // 2
        dma = pltpu.SemaphoreType.DMA
        return [
            pltpu.VMEM((2, chips, *piece), BF16),
            pltpu.VMEM((chips, *piece), BF16),
            pltpu.VMEM((chips, *piece), BF16),
            pltpu.VMEM((chips, *piece), BF16),
            pltpu.VMEM(piece, BF16),
            dma((1,)),
            dma((2,)),
            dma((chips,)),
            dma((chips,)),
            dma((chips,)),
            dma((chips,)),
            dma((chips, 6)),
            dma((chips, 6)),
            dma((chips, 4)),
            dma((chips, 4)),
        ]

    def chip(self, hop):
        return lax.rem(self.place.chip + hop, self.chips)

    def exp(self, hop):
        return self.chip(hop) * 2 + self.place.core

    def _core(self):
        p = self.place
        return p.to_exp(
            self.src.at[1 - p.core], self.core_in, self.core_sems.at[0], self.core_sems.at[1], self.sibling
        )

    def start(self):
        self._core().start()

    def _spread(self, hop):
        p = self.place
        to = self.chip(hop)
        return p.to_exp(
            self.mine.at[to], self.chip_in.at[p.chip], self.rs_send.at[to], self.rs_recv.at[p.chip], self.exp(hop)
        )

    def _spread_from(self, hop):
        p = self.place
        at = self.chip(hop)
        return p.to_exp(
            self.mine.at[at], self.chip_in.at[at], self.rs_send.at[at], self.rs_recv.at[at], self.exp(hop)
        )

    def spread(self):
        p = self.place
        self._core().wait_recv()
        for n in range(self.chips):
            self.mine[n] = (self.src[p.core, n].astype(F32) + self.core_in[n].astype(F32)).astype(BF16)
        for hop in range(1, self.chips):
            self._spread(hop).start()

    def _local(self):
        p = self.place
        return pltpu.make_async_copy(self.res, self.where(p.s, p.e), self.local_sem.at[0])

    def _share(self, hop):
        p = self.place
        to = self.chip(hop)
        return p.to_exp(
            self.res, self.where(p.s, p.e), self.ag_send.at[to], self.ag_recv.at[p.chip], self.exp(hop)
        )

    def _share_from(self, hop):
        p = self.place
        at = self.chip(hop)
        return p.to_exp(
            self.res, self.where(p.s, self.exp(hop)), self.ag_send.at[at], self.ag_recv.at[at], self.exp(hop)
        )

    def copies(self, hop, lanes=range(6)):
        p = self.place
        spec = (
            (p.s, 0, p.near),
            (p.s, 1, p.far),
            (p.s, 1, p.near),
            (p.s, 0, p.far),
            (p.near, 0, p.far),
            (p.far, 1, p.near),
        )
        made = []
        for n in lanes:
            owner, half, other = spec[n]
            part = self.where(owner, self.exp(hop), half)
            made.append(p.to_seq(part, part, self.seq_send.at[hop, n], self.seq_recv.at[hop, n], other))
        return made

    def _pair(self, hop, n):
        p = self.place
        part = self.where((p.s, p.near, p.far, p.diag)[n], self.exp(hop))
        return p.to_exp(part, part, self.pair_send.at[hop, n], self.pair_recv.at[hop, n], self.sibling)

    def _pair_from(self, hop, n):
        p = self.place
        owner = (p.s, p.near, p.far, p.diag)[n]
        part = self.where(owner, self.chip(hop) * 2 + (1 - p.core))
        return p.to_exp(part, part, self.pair_send.at[hop, n], self.pair_recv.at[hop, n], self.sibling)

    def reduce(self):
        p = self.place
        for hop in range(1, self.chips):
            self._spread_from(hop).wait_recv()
        total = self.mine[p.chip].astype(F32)
        for hop in range(1, self.chips):
            total = total + self.chip_in[self.chip(hop)].astype(F32)
        self.res[...] = total.astype(BF16)
        self._local().start()
        for hop in range(1, self.chips):
            self._share(hop).start()
        self._local().wait()

    def forward(self, hop):
        if hop > 0:
            self._share_from(hop).wait_recv()
        for c in self.copies(hop, range(4)):
            c.start()
        self._pair(hop, 0).start()

    def relay(self, hop):
        for c, out in zip(self.copies(hop, (0, 1)), self.copies(hop, (4, 5))):
            c.wait_recv()
            out.start()

    def arrived(self, hop):
        for c in self.copies(hop, (2, 3)):
            c.wait_recv()
        self._pair(hop, 1).start()
        self._pair(hop, 2).start()
        for c in self.copies(hop, (4, 5)):
            c.wait_recv()
        self._pair(hop, 3).start()

    def drain(self):
        self._core().wait_send()
        for hop in range(1, self.chips):
            self._spread(hop).wait_send()
            self._share(hop).wait_send()
        for hop in range(self.chips):
            for c in self.copies(hop):
                c.wait_send()
            for n in range(4):
                self._pair(hop, n).wait_send()
                self._pair_from(hop, n).wait_recv()


def layer(
    tokens, ids, cotangent, lengths, ln1, w_qkv, b_query, b_value, w_out, b_out, ln2, w_up, b_up, w_down, b_down,
    n_exp, collective_id,
):
    tok, width = tokens.shape
    hidden = w_up.shape[1]
    n_seq = 4
    total = n_seq * tok
    cols = width // n_seq
    heads = cols // HEAD_DIM
    cap = 2 * tok // n_exp
    q_block = 256
    chips = n_exp // 2
    rows_w, rows_o = width // n_exp, cols // n_exp
    pairs = cols // 128
    per_pair = 128 // HEAD_DIM
    routed = n_seq * cap
    block = min(256, hidden)
    slots = 2
    ahead = 5

    vm = pltpu.VMEM
    dma = pltpu.SemaphoreType.DMA
    table = dict(
        xall=vm((1, n_seq, tok, width), BF16),
        n1=vm((width, total), BF16),
        q=vm((total, cols), BF16),
        k=vm((total, cols), BF16),
        v=vm((total, cols), BF16),
        attn=vm((total, cols), F32),
        lse=vm((8, total), F32),
        resid=vm((tok, width), F32),
        pick=vm((n_exp * cap, tok), BF16),
        w_all=vm((width, 3 * cols), BF16),
        w_o=vm((width, width), BF16),
        send_c=vm((n_exp, cap, width), BF16),
        send_n=vm((n_exp, cap, width), BF16),
        back=vm((n_exp, cap, width), BF16),
        ret=vm((n_exp, cap, width), BF16),
        attn_out=vm((n_seq, tok, cols), BF16),
        attn_in=vm((n_seq, tok, cols), BF16),
        cot=vm((n_exp, n_seq, cap, width), BF16),
        held=vm((n_exp, n_seq, cap, width), BF16),
        wu=vm((width, hidden), BF16),
        wd=vm((hidden, width), BF16),
        part=vm((slots, n_seq, cap, width), BF16),
        dwu=vm((width, hidden), F32),
        dwd=vm((hidden, width), F32),
        dqkv=vm((total, 3 * cols), BF16),
        vec_own=vm((8, width), F32),
        vec_seq=vm((n_seq, 8, width), F32),
        vec_exp=vm((n_exp, 8, width), F32),
        local_sems=dma((8,)),
        load_sems=dma((3 * pairs,)),
        dq=vm((tok, cols), F32),
        a2a_send=dma((n_seq,)),
        a2a_recv=dma((n_seq,)),
        vs_send=dma((n_seq,)),
        vs_recv=dma((n_seq,)),
        ve_send=dma((n_exp,)),
        ve_recv=dma((n_exp,)),
    )
    groups = dict(
        gather1=Gather.scratch(),
        gather2=Gather.scratch(),
        disp_c=Dispatch.scratch(n_exp),
        disp_n=Dispatch.scratch(n_exp),
        comb_g=Combine.scratch(n_exp, cap, width),
        comb_f=Combine.scratch(n_exp, cap, width)[:2] + Combine.scratch(n_exp, cap, width)[3:],
        red=[
            vm((1, 2, tok // 2, width), BF16),
            vm((1, 4, tok // 2, width), BF16),
            dma((1, 6)),
            dma((1, 6)),
        ],
        sum_o=SumAll.scratch(n_exp, rows_o, width),
        **{f"sum_{j}": SumAll.scratch(n_exp, 3, rows_w, 128) for j in range(pairs)},
    )
    scratch = list(table.values()) + [ref for group in groups.values() for ref in group]

    def kernel(tok_ref, ids_ref, cot_ref, len_ref, g1_ref, c1_ref, wq_in, wk_in, wv_in, bq_ref, bv_ref, wo_in, bo_ref,
               g2_ref, c2_ref, wu_in, bu_ref, wd_in, bd_ref,
               out_out, gin_out, vec_ref, dbu_ref, csum_ref, dwu_out, dwd_out, gw_out, go_out, *refs):
        r = dict(zip(table, refs))
        at = len(table)
        g = {}
        for name, group in groups.items():
            g[name] = refs[at : at + len(group)]
            at += len(group)
        xall, n1, q_all, k_all, v_all = r["xall"], r["n1"], r["q"], r["k"], r["v"]
        attn, lse_all, resid, pick = r["attn"], r["lse"], r["resid"], r["pick"]
        w_all, w_o, wu, wd = r["w_all"], r["w_o"], r["wu"], r["wd"]
        send_c, send_n, back, ret = r["send_c"], r["send_n"], r["back"], r["ret"]
        attn_out, attn_in, cot, held, part = r["attn_out"], r["attn_in"], r["cot"], r["held"], r["part"]
        dwu, dwd, dqkv = r["dwu"], r["dwd"], r["dqkv"]
        gattn = attn_out
        gin_ref = dwd.at[0:tok, :]
        dk, dv = dwu.at[0:total, 0:cols], dwu.at[0:total, cols : 2 * cols]
        vec_own, vec_seq, vec_exp = r["vec_own"], r["vec_seq"], r["vec_exp"]
        local_sems, load_sems, dq = r["local_sems"], r["load_sems"], r["dq"]

        p = Place(n_exp)
        mine = pl.ds(pl.multiple_of(p.s * cols, cols), cols)

        tile = 32

        def tile_rows(n):
            return pl.ds(pl.multiple_of(n * tile, tile), tile)

        def row_of(ref):
            return ref[...].astype(F32).reshape(1, ref.shape[-1])

        loads = [
            pltpu.make_async_copy(
                src.at[:, pl.ds(pl.multiple_of(p.s * cols + j * 128, 128), 128)],
                w_all.at[:, pl.ds((3 * j + m) * 128, 128)],
                load_sems.at[3 * j + m],
            )
            for m, src in enumerate((wq_in, wk_in, wv_in))
            for j in range(pairs)
        ]
        load_o = pltpu.make_async_copy(wo_in, w_o, local_sems.at[3])
        load_ffn = [
            pltpu.make_async_copy(wu_in, wu, local_sems.at[4]),
            pltpu.make_async_copy(wd_in, wd, local_sems.at[5]),
        ]
        for c in loads + [load_o] + load_ffn:
            c.start()

        xall[0, p.s] = tok_ref[...]
        p.greet(diag=True)
        gather1 = Gather(p, xall.at[0], *g["gather1"])
        gather1.start()
        pick[...] = row_choice(ids_ref[...], n_exp, cap)

        def lay_out(send, rows_ref):
            for e in range(0, n_exp, 2):
                laid = dot(pick[e * cap : (e + 2) * cap, :], rows_ref[...])
                send[e : e + 2] = laid.astype(BF16).reshape(2, cap, width)

        lay_out(send_c, cot_ref)
        disp_c = Dispatch(p, send_c, cot, g["disp_c"][0:2], g["disp_c"][2:4])
        for step in range(1, n_exp):
            disp_c.start_exp(step)
        disp_c.own()
        gain1, bias1 = row_of(g1_ref), row_of(c1_ref)
        gain2, bias2 = row_of(g2_ref), row_of(c2_ref)
        bq = bq_ref[mine].astype(F32).reshape(1, cols)
        bv = bv_ref[mine].astype(F32).reshape(1, cols)

        def project(owner):
            rows = pl.ds(pl.multiple_of(owner * tok, tok), tok)

            def norm_tile(n, carry):
                x = xall[0, owner, tile_rows(n), :].astype(F32)
                per = cap // tile
                rows = pl.ds(pl.multiple_of(lax.rem(n, per) * tile, tile), tile)
                part[0, lax.div(n, per), rows, :] = layer_norm(x, gain1, bias1)[0].astype(BF16)
                return carry

            lax.fori_loop(0, tok // tile, norm_tile, 0)
            normed = part[0].reshape(tok, width)
            n1[:, rows] = jnp.transpose(normed)
            out = dot(normed, w_all[...])
            for j in range(pairs):
                at, first = slice(j * 128, (j + 1) * 128), 3 * j * 128
                q = (out[:, first : first + 128] + bq[:, at]).astype(BF16)
                q_all[rows, at] = (q.astype(F32) * SCORE_SCALE).astype(BF16)
                k_all[rows, at] = out[:, first + 128 : first + 256].astype(BF16)
                v_all[rows, at] = (out[:, first + 256 : first + 384] + bv[:, at]).astype(BF16)

        for c in loads:
            c.wait()
        project(p.s)
        gather1.relay()
        gather1.wait((2, 3))
        project(p.near)
        project(p.far)
        gather1.wait((4, 5))
        disp_c.start_seq(0)
        disp_c.start_seq(1)
        project(p.diag)

        def a2a(owner):
            return p.to_seq(
                attn_out.at[owner], attn_in.at[p.s], r["a2a_send"].at[owner], r["a2a_recv"].at[p.s], owner
            )

        def a2a_from(owner):
            return p.to_seq(
                attn_out.at[owner], attn_in.at[owner], r["a2a_send"].at[owner], r["a2a_recv"].at[owner], owner
            )

        blocks = total // q_block
        for n in reversed(range(blocks)):
            seen = (n + 1) * q_block
            rows = pl.ds(n * q_block, q_block)
            q_pos = lax.broadcasted_iota(jnp.int32, (q_block, 1), 0) + n * q_block
            k_pos = lax.broadcasted_iota(jnp.int32, (1, seen), 1)
            allowed = (segment_of(q_pos, len_ref) == segment_of(k_pos, len_ref)) & (k_pos <= q_pos)
            q_rows = q_all[rows, :]
            acc = jnp.zeros((q_block, cols), F32)
            lse = jnp.zeros((q_block, 128), F32)
            lane = lax.broadcasted_iota(jnp.int32, (q_block, 128), 1)
            for head in range(heads):
                own = head_mask(q_block, cols, head)
                scores = dot(jnp.where(own, q_rows, jnp.zeros_like(q_rows)), k_all[0:seen, :], ((1,), (1,)))
                scores = jnp.where(allowed, scores, MASKED_SCORE)
                top = jnp.max(scores, axis=1, keepdims=True)
                weights = jnp.exp(scores - top)
                sums = jnp.sum(weights, axis=1, keepdims=True)
                out = dot(weights.astype(BF16), v_all[0:seen, :]) / sums
                acc = jnp.where(own, out, acc)
                lse = jnp.where(lane == head, top + jnp.log(sums), lse)
            attn[rows, :] = acc
            lse_all[:, rows] = jnp.transpose(lse)[0:8, :]
            owner, first = (n * q_block) // tok, (n * q_block) % tok
            attn_out[owner, pl.ds(first, q_block)] = acc.astype(BF16)
            if first == 0:

                @pl.when(p.s != owner)
                def _(owner=owner):
                    a2a(owner).start()

                @pl.when(p.s == owner)
                def _(owner=owner):
                    attn_in[owner] = attn_out[owner]

        disp_c.start_seq(2)
        disp_c.relay(0)
        disp_c.relay(1)
        load_o.wait()
        sums = tok_ref[...].astype(F32) + row_of(bo_ref)
        for owner in range(n_seq):

            @pl.when(p.s != owner)
            def _(owner=owner):
                a2a_from(owner).wait_recv()

            sums = sums + dot(attn_in[owner], w_o[pl.ds(owner * cols, cols), :])
        resid[...] = sums
        disp_c.start_seq(3)
        disp_c.relay(2)

        gather1.drain()
        for owner in range(n_seq):

            @pl.when(p.s != owner)
            def _(owner=owner):
                a2a(owner).wait_send()

        gout = xall.at[0]
        low = gout.at[p.s]

        def norm_two_tile(n, carry):
            low[tile_rows(n), :] = layer_norm(resid[tile_rows(n), :], gain2, bias2)[0].astype(BF16)
            return carry

        lax.fori_loop(0, tok // tile, norm_two_tile, 0)
        lay_out(send_n, low)

        disp_n = Dispatch(p, send_n, held, g["disp_n"][0:2], g["disp_n"][2:4])
        comb_g = Combine(p, part, *g["comb_g"][0:3], back, g["comb_g"][3:5], g["comb_g"][5:7], slots)
        comb_f = Combine(p, held, *g["comb_f"][0:2], None, ret, g["comb_f"][2:4], g["comb_f"][4:6], n_exp)
        disp_n.own()
        disp_n.start_seq(0)
        for step in range(1, n_exp):
            disp_n.start_exp(step)
        disp_c.start_seq(4)
        disp_c.relay(3)
        dwu[...] = jnp.zeros_like(dwu)
        dwd[...] = jnp.zeros_like(dwd)
        dbu_ref[...] = jnp.zeros_like(dbu_ref)
        csum_ref[...] = jnp.zeros_like(csum_ref)
        bias_down = bd_ref[...].astype(F32)
        for c in load_ffn:
            c.wait()

        def ffn_start(*steps):
            for step in steps:
                comb_f.start(step)

        def ffn_pass(*steps):
            for step in steps:
                comb_f.pass_on(step)

        def ffn_finish(*steps):
            for step in steps:
                comb_f.finish(step, bias_down)

        def compute(step):
            x = held[step].reshape(routed, width)
            gr = cot[step].reshape(routed, width)
            ones = jnp.ones((8, routed), BF16)
            csum_ref[...] += dot(ones, gr)[0:1, :]
            y = jnp.zeros((routed, width), F32)
            gx = jnp.zeros((routed, width), F32)
            for b in range(hidden // block):
                at = pl.ds(b * block, block)
                wu_b, wd_b = wu[:, at], wd[at, :]
                pre = dot(x, wu_b) + bu_ref[:, at].astype(F32)
                g_act = dot(gr, wd_b, ((1,), (1,)))
                sq = pre * pre
                th = jnp.tanh(GELU_A * pre * (1.0 + GELU_B * sq))
                half = 0.5 * (1.0 + th)
                act = (pre * half).astype(BF16)
                slope = half + 0.5 * pre * (1.0 - th * th) * (GELU_A * (1.0 + 3.0 * GELU_B * sq))
                g_pre = (g_act * slope).astype(BF16)
                dbu_ref[:, at] += dot(ones, g_pre)[0:1, :]
                y = y + dot(act, wd_b)
                gx = gx + dot(g_pre, wu_b, ((1,), (1,)))
                dwu[:, at] += dot(x, g_pre, ((0,), (0,)))
                dwd[at, :] += dot(act, gr, ((0,), (0,)))
            part[lax.rem(step, slots)] = gx.astype(BF16).reshape(n_seq, cap, width)
            disp_n.sent(step)
            held[step] = y.astype(BF16).reshape(n_seq, cap, width)

        stores = [
            pltpu.make_async_copy(dwu, dwu_out, local_sems.at[6]),
            pltpu.make_async_copy(dwd, dwd_out, local_sems.at[7]),
        ]

        def loop(t, carry):
            @pl.when(t + ahead - 1 < n_exp)
            def _():
                disp_c.start_seq(t + ahead - 1)

            @pl.when(t + ahead - 2 < n_exp)
            def _():
                disp_c.relay(t + ahead - 2)

            @pl.when(t <= n_exp)
            def _():
                disp_n.relay(t - 1)

            @pl.when(t < n_exp)
            def _():
                disp_n.start_seq(t)

            @pl.when((t >= 3) & (t <= n_exp + 2))
            def _():
                comb_g.pass_on(t - 3)

            @pl.when(t >= 4)
            def _():
                comb_g.finish(t - 4)

            @pl.when(t == n_exp + 1)
            def _():
                ffn_start(0)

            @pl.when((t >= 2) & (t <= n_exp + 1))
            def _():
                disp_c.arrived(t - 2)
                disp_n.arrived(t - 2)
                compute(t - 2)
                comb_g.start(t - 2)

            @pl.when(t == n_exp + 1)
            def _():
                for c in stores:
                    c.start()
                ffn_start(1)

            @pl.when(t == n_exp + 2)
            def _():
                ffn_start(2)

            @pl.when(t == n_exp + 3)
            def _():
                ffn_start(3)

            return carry

        lax.fori_loop(1, n_exp + 4, loop, 0)
        ffn_pass(0, 1)
        comb_g.drain()
        ffn_pass(2, 3)

        for c in stores:
            c.wait()
        gin_ref[...] = dot(pick[...], back[...].reshape(n_exp * cap, width), ((0,), (0,)))

        def norm_two_back(n, carry):
            at = tile_rows(n)
            g_two = gin_ref[at, :]
            _, xhat, inv_std = layer_norm(resid[at, :], gain2, 0.0)
            g_resid = cot_ref[at, :].astype(F32) + norm_back(g_two, xhat, inv_std, gain2)
            gin_ref[at, :] = g_resid
            g_low = g_resid.astype(BF16)
            gout[p.s, at, :] = g_low
            new = (g_low.astype(F32), g_two * xhat, g_two)
            return tuple(old + jnp.sum(v, axis=0, keepdims=True) for old, v in zip(carry, new))

        zero_row = jnp.zeros((1, width), F32)
        sums2 = lax.fori_loop(0, tok // tile, norm_two_back, (zero_row,) * 3)
        gather2 = Gather(p, gout, *g["gather2"])
        gather2.start()
        vec_own[...] = jnp.zeros_like(vec_own)
        for n in range(3):
            vec_own[4 + n : 5 + n, :] = sums2[n]
        wo_mine = w_o.at[mine, :]

        def grad_attn(owner):
            gattn[owner] = dot(gout[owner], wo_mine[...], ((1,), (1,))).astype(BF16)

        dwu[0:total, 0 : 2 * cols] = jnp.zeros((total, 2 * cols), F32)

        head_rows = lax.broadcasted_iota(jnp.int32, (8, cols), 0)
        head_lane = lax.broadcasted_iota(jnp.int32, (8, cols), 1)
        per_head = (lax.div(head_lane, HEAD_DIM) == head_rows).astype(F32)

        def attn_back(owner, some_heads):
            rows = pl.ds(pl.multiple_of(owner * tok, tok), tok)
            q_pos = lax.broadcasted_iota(jnp.int32, (1, tok), 1) + owner * tok
            q_seg = segment_of(q_pos, len_ref)
            q_rows, g_rows = q_all[rows, :], gattn[owner]
            delta = lax.dot_general(
                per_head, g_rows.astype(F32) * attn[rows, :], (((1,), (1,)), ((), ())),
                precision=lax.Precision.HIGHEST, preferred_element_type=F32,
            )
            dq[...] = jnp.zeros_like(dq)

            def key_block(n, carry):
                keys = pl.ds(pl.multiple_of(n * tok, tok), tok)
                k_pos = lax.broadcasted_iota(jnp.int32, (tok, 1), 0) + n * tok
                allowed = (q_seg == segment_of(k_pos, len_ref)) & (k_pos <= q_pos)
                k_rows, v_rows = k_all[keys, :], v_all[keys, :]
                dq_new = jnp.zeros((tok, cols), F32)
                dk_new = jnp.zeros((tok, cols), F32)
                dv_new = jnp.zeros((tok, cols), F32)
                for head in some_heads:
                    own = head_mask(tok, cols, head)
                    q_own = jnp.where(own, q_rows, jnp.zeros_like(q_rows))
                    g_own = jnp.where(own, g_rows, jnp.zeros_like(g_rows))
                    scores = dot(k_rows, q_own, ((1,), (1,)))
                    probs = jnp.where(allowed, jnp.exp(scores - lse_all[head : head + 1, rows]), 0.0)
                    g_probs = dot(v_rows, g_own, ((1,), (1,)))
                    g_scores = (probs * (g_probs - delta[head : head + 1, :])).astype(BF16)
                    dk_new = dk_new + dot(g_scores, q_own)
                    dv_new = dv_new + dot(probs.astype(BF16), g_own)
                    dq_new = dq_new + jnp.where(own, dot(g_scores, k_rows, ((0,), (0,))), 0.0)
                dk[keys, :] += dk_new
                dv[keys, :] += dv_new
                dq[...] += dq_new
                return carry

            lax.fori_loop(0, owner + 1, key_block, 0)
            low_dq = (dq[...] * SCORE_SCALE).astype(BF16)
            for j in sorted({head // per_pair for head in some_heads}):
                dqkv[rows, pl.ds(3 * j * 128, 128)] = low_dq[:, j * 128 : (j + 1) * 128]

        every = range(heads)
        grad_attn(p.s)
        gather2.relay()
        attn_back(p.s, every)
        ffn_finish(0, 1, 2, 3)
        gather2.wait((2, 3))
        grad_attn(p.near)
        attn_back(p.near, every)
        grad_attn(p.far)
        attn_back(p.far, every)
        gather2.wait((4, 5))
        ffn_start(4, 5, 6, 7)
        grad_attn(p.diag)

        def place_w(j, owner, e, half=None):
            rows = rows_w if half is None else rows_w // 2
            first = e * rows_w + (0 if half is None else half * rows)
            return gw_out.at[
                :, pl.ds(pl.multiple_of(first, rows), rows), pl.ds(pl.multiple_of(owner * cols + j * 128, 128), 128)
            ]

        def place_o(owner, e, half=None):
            rows = pl.ds(pl.multiple_of(owner * cols + e * rows_o, rows_o), rows_o)
            if half is None:
                return go_out.at[rows, :]
            return go_out.at[rows, pl.ds(half * (width // 2), width // 2)]

        def summing(name, place):
            return SumAll(p, *g[name][0:5], place, g[name][5], g[name][6:])

        sum_w = [summing(f"sum_{j}", functools.partial(place_w, j)) for j in range(pairs)]
        sum_o = summing("sum_o", place_o)

        for b in range(cols // 128):
            a_low = attn[:, b * 128 : (b + 1) * 128].astype(BF16)
            got = dot(a_low, gout[...].reshape(total, width), ((0,), (0,))).astype(BF16)
            for n in range(128 // rows_o):
                e = b * (128 // rows_o) + n
                sum_o.src[e % 2, e // 2] = got[n * rows_o : (n + 1) * rows_o]
        for j in range(pairs):
            attn_back(p.diag, range(j * per_pair, (j + 1) * per_pair))
            first = 3 * j * 128
            at = slice(j * 128, (j + 1) * 128)
            dqkv[:, first + 128 : first + 256] = dk[:, at].astype(BF16)
            dqkv[:, first + 256 : first + 384] = dv[:, at].astype(BF16)
            src = sum_w[j].src
            for b in range(width // 256):
                got = dot(n1[b * 256 : (b + 1) * 256, :], dqkv[:, first : first + 384]).astype(BF16)
                for n in range(256 // rows_w):
                    e = b * (256 // rows_w) + n
                    for m in range(3):
                        src[e % 2, e // 2, m] = got[n * rows_w : (n + 1) * rows_w, m * 128 : (m + 1) * 128]
            sum_w[j].start()
            if j > 0:
                sum_w[j - 1].spread()
        sum_w[pairs - 1].spread()
        sum_o.start()
        gather2.drain()
        red = Combine(p, xall, *g["red"][0:2], None, None, g["red"][2:4], (None, None), 1)
        for owner in range(n_seq):
            piece = dqkv[pl.ds(owner * tok, tok), :]
            xall[0, owner] = dot(piece, w_all[...], ((1,), (1,))).astype(BF16)
        red.start(0)
        sum_o.spread()
        d_sums = dot(jnp.ones((8, total), BF16), dqkv[...])
        for j in range(pairs):
            at = pl.ds(pl.multiple_of(p.s * cols + j * 128, 128), 128)
            first = 3 * j * 128
            vec_own[2:3, at] = d_sums[0:1, first : first + 128]
            vec_own[3:4, at] = d_sums[0:1, first + 256 : first + 384]
        sums = sum_w + [sum_o]
        ffn_pass(4, 5, 6, 7)
        sums[0].reduce()
        sums[0].forward(0)
        red.pass_on(0)
        for n in range(1, len(sums)):
            sums[n].reduce()
            sums[n].forward(0)
            sums[n - 1].relay(0)
        ffn_finish(4, 5, 6, 7)
        red.arrived(0)
        half_tok = tok // 2
        for n in range(2):
            gout[p.s, pl.ds(n * half_tok, half_tok), :] = red.summed(0, n).astype(BF16)

        def norm_one_back(n, carry):
            at = tile_rows(n)
            g_one = gout[p.s, at, :].astype(F32)
            _, xhat, inv_std = layer_norm(tok_ref[at, :].astype(F32), gain1, 0.0)
            gin_ref[at, :] += norm_back(g_one, xhat, inv_std, gain1)
            new = (g_one * xhat, g_one)
            return tuple(old + jnp.sum(v, axis=0, keepdims=True) for old, v in zip(carry, new))

        sums1 = lax.fori_loop(0, tok // tile, norm_one_back, (zero_row,) * 2)
        store_gin = pltpu.make_async_copy(gin_ref, gin_out, local_sems.at[0])
        store_gin.start()
        for n in range(2):
            vec_own[n : n + 1, :] = sums1[n]
        vec_seq[p.s] = vec_own[...]

        def tell(other):
            return p.to_seq(vec_own, vec_seq.at[p.s], r["vs_send"].at[other], r["vs_recv"].at[p.s], other)

        def told(other):
            return p.to_seq(vec_own, vec_seq.at[other], r["vs_send"].at[other], r["vs_recv"].at[other], other)

        others = (p.near, p.far, p.diag)
        for other in others:
            tell(other).start()
        for hop in range(1, chips):
            for one in sums:
                one.forward(hop)
                if hop > 1 or one is sums[-1]:
                    one.relay(hop - 1)
        for other in others:
            told(other).wait_recv()
        for other in others:
            tell(other).wait_send()
        vec = vec_seq[0]
        for n in range(1, n_seq):
            vec = vec + vec_seq[n]
        vec_own[...] = vec
        vec_exp[p.e] = vec

        def show(step):
            other = p.peer(step, -1)
            return p.to_exp(vec_own, vec_exp.at[p.e], r["ve_send"].at[step], r["ve_recv"].at[step], other)

        def shown(step):
            other = p.peer(step, 1)
            return p.to_exp(vec_own, vec_exp.at[other], r["ve_send"].at[step], r["ve_recv"].at[step], other)

        for step in range(1, n_exp):
            show(step).start()
        for one in sums:
            one.relay(chips - 1)
        comb_f.drain()
        out_ref = part.at[0]
        for n in range(tok // 128):
            at = slice(n * 128, (n + 1) * 128)
            rows_back = dot(pick[:, at], ret[...].reshape(n_exp * cap, width), ((0,), (0,)))
            out_ref[n * 128 // cap : (n + 1) * 128 // cap] = (
                (resid[at, :] + rows_back).astype(BF16).reshape(128 // cap, cap, width)
            )
        store_out = pltpu.make_async_copy(out_ref, out_out, local_sems.at[1])
        store_out.start()
        for hop in range(chips):
            for one in sums:
                one.arrived(hop)
        for step in range(1, n_exp):
            shown(step).wait_recv()
            show(step).wait_send()
        vec = vec_exp[0]
        for n in range(1, n_exp):
            vec = vec + vec_exp[n]
        vec_ref[...] = vec
        disp_c.drain()
        disp_n.drain(seq=False)
        for one in sums:
            one.drain()
        store_gin.wait()
        store_out.wait()

    vmem = pl.BlockSpec(memory_space=pltpu.VMEM)
    hbm = pl.BlockSpec(memory_space=pl.ANY)
    smem = pl.BlockSpec(memory_space=pltpu.SMEM)
    shape = jax.ShapeDtypeStruct
    return pl.pallas_call(
        kernel,
        out_shape=[
            shape((n_seq, cap, width), BF16),
            shape((tok, width), F32),
            shape((8, width), F32),
            shape((1, hidden), F32),
            shape((1, width), F32),
            shape((width, hidden), F32),
            shape((hidden, width), F32),
            shape((3, width, width), BF16),
            shape((width, width), BF16),
        ],
        in_specs=[vmem] * 3 + [smem] + [vmem] * 2 + [hbm] * 3 + [vmem] * 2 + [hbm] + [vmem] * 3
        + [hbm, vmem, hbm, vmem],
        out_specs=[hbm, hbm] + [vmem] * 3 + [hbm] * 4,
        scratch_shapes=scratch,
        compiler_params=pltpu.CompilerParams(
            collective_id=collective_id, has_side_effects=True, vmem_limit_bytes=VMEM_LIMIT
        ),
        name="layer",
    )(tokens, ids, cotangent, lengths, *ln1, *w_qkv, b_query, b_value, w_out, b_out, *ln2, w_up, b_up, w_down, b_down)


def finish(output, input_grad, vec, dbu, csum, dwu, dwd, gw, go):
    tok, width = output.shape
    hidden = dwu.shape[1]
    cols = width // 4
    piece = 256

    def kernel(out_in, gin_in, vec_ref, dbu_in, csum_ref, dwu_in, dwd_in, gw_in, go_in, *refs):
        (out_o, gin_o, l1g, l1b, wq_o, bq_o, wk_o, wv_o, bv_o, wo_o, bo_o, l2g, l2b, dwu_o, dbu_o, dwd_o, dbd_o) = refs[:17]
        small, wide, same_b, same_f, sems = refs[17:22]
        count = 0

        def pair(src, mid_in, mid_out, dst):
            nonlocal count
            load = pltpu.make_async_copy(src, mid_in, sems.at[count])
            store = pltpu.make_async_copy(mid_out, dst, sems.at[count + 1])
            count += 2
            return load, store

        widen, plain = [], []
        for m, (src, dst) in enumerate(
            ((gw_in.at[0], wq_o), (gw_in.at[1], wk_o), (gw_in.at[2], wv_o), (go_in, wo_o))
        ):
            for n in range(width // piece):
                rows = pl.ds(n * piece, piece)
                at = m * (width // piece) + n
                widen.append((pair(src.at[rows], small.at[at], wide.at[at], dst.at[rows]), at))
        at = 0
        for src, dst, total in ((dwu_in, dwu_o.at[0], width), (dwd_in, dwd_o.at[0], hidden), (gin_in, gin_o.at[0], tok)):
            for n in range(total // piece):
                rows = pl.ds(n * piece, piece)
                plain.append(pair(src.at[rows], same_f.at[at], same_f.at[at], dst.at[rows]))
                at += 1
        plain.append(pair(out_in, same_b, same_b, out_o.at[0]))
        order = []
        for n in range(max(len(widen), len(plain))):
            order += widen[n : n + 1] + [(c, None) for c in plain[n : n + 1]]
        for (load, _), _ in order:
            load.start()
        for n, ref in enumerate((l1g, l1b, bq_o, bv_o, bo_o, l2g, l2b)):
            ref[...] = vec_ref[n : n + 1, :].reshape(width)
        dbu_o[...] = dbu_in[...]
        first = pl.multiple_of(lax.axis_index("seq") * cols, cols)
        dbd_o[...] = csum_ref[:, pl.ds(first, cols)]
        for (load, store), at in order:
            load.wait()
            if at is not None:
                wide[at] = small[at].astype(F32)
            store.start()
        for (_, store), _ in order:
            store.wait()

    vmem = pl.BlockSpec(memory_space=pltpu.VMEM)
    hbm = pl.BlockSpec(memory_space=pl.ANY)
    shape = jax.ShapeDtypeStruct
    row, square = shape((width,), F32), shape((width, width), F32)
    n_widen = 4 * (width // piece)
    n_plain = (width + hidden + tok) // piece
    return pl.pallas_call(
        kernel,
        out_shape=[
            shape((1, tok, width), BF16), shape((1, tok, width), F32), row, row, square, row, square, square, row,
            square, row, row, row, shape((1, width, hidden), F32), shape((1, hidden), F32),
            shape((1, hidden, width), F32), shape((1, cols), F32),
        ],
        in_specs=[hbm, hbm, vmem, vmem, vmem, hbm, hbm, hbm, hbm],
        out_specs=[hbm, hbm, vmem, vmem, hbm, vmem, hbm, hbm, vmem, hbm, vmem, vmem, vmem, hbm, vmem, hbm, vmem],
        scratch_shapes=[
            pltpu.VMEM((n_widen, piece, width), BF16),
            pltpu.VMEM((n_widen, piece, width), F32),
            pltpu.VMEM((tok, width), BF16),
            pltpu.VMEM((n_plain, piece, width), F32),
            pltpu.SemaphoreType.DMA((2 * (n_widen + n_plain + 1),)),
        ],
        compiler_params=pltpu.CompilerParams(vmem_limit_bytes=VMEM_LIMIT),
        name="finish",
    )(output, input_grad, vec, dbu, csum, dwu, dwd, gw, go)


def shards(
    tokens, lengths, expert_ids, ln1_gain, ln1_bias, w_query, b_query, w_key, w_value, b_value, w_out, b_out,
    ln2_gain, ln2_bias, w_up, b_up, w_down, b_down, cotangent,
):
    output, *parts = layer(
        tokens[0], expert_ids[0, :, 0][None], cotangent[0], lengths, (ln1_gain, ln1_bias),
        (w_query, w_key, w_value), b_query, b_value, w_out, b_out, (ln2_gain, ln2_bias), w_up[0], b_up, w_down[0],
        b_down, lax.axis_size("exp"), 0,
    )
    return tuple(finish(output.reshape(tokens.shape[1:]), *parts))


def norm_layer(values_in, gain_vec, shift_vec):
    center = values_in - jnp.mean(values_in, axis=-1, keepdims=True)
    inv_std = lax.rsqrt(jnp.mean(center * center, axis=-1, keepdims=True) + EPSILON)
    return center * inv_std * gain_vec + shift_vec


def segment_ids(positions, seq_ends):
    return jnp.sum((positions[:, None] >= seq_ends[None, :]).astype(jnp.int32), axis=1)


def visible_pairs(query_pos, query_seg, key_pos, key_seg):
    return ((query_seg[:, None] == key_seg[None, :]) & (key_pos[None, :] <= query_pos[:, None]))[
        None
    ]


def project(left_op, right_op):
    return jnp.dot(left_op, right_op, preferred_element_type=jnp.float32)


def shards_any(
    tokens,
    lengths,
    expert_ids,
    ln1_gain,
    ln1_bias,
    w_query,
    b_query,
    w_key,
    w_value,
    b_value,
    w_out,
    b_out,
    ln2_gain,
    ln2_bias,
    w_up,
    b_up,
    w_down,
    b_down,
    cotangent,
):
    tok_rows = tokens.shape[1]
    width = tokens.shape[2]
    seq_size = lax.axis_size("seq")
    exp_size = lax.axis_size("exp")
    seq_rank = lax.axis_index("seq")
    seq_ends = jnp.cumsum(lengths[0])
    own_pos = seq_rank * tok_rows + jnp.arange(tok_rows, dtype=jnp.int32)
    own_seg = segment_ids(own_pos, seq_ends)
    inputs = tokens[0].astype(jnp.float32)
    gain_one = ln1_gain.astype(jnp.float32)
    bias_one = ln1_bias.astype(jnp.float32)
    gain_two = ln2_gain.astype(jnp.float32)
    bias_two = ln2_bias.astype(jnp.float32)
    normed_one_low = norm_layer(inputs, gain_one, bias_one).astype(jnp.bfloat16)
    query_low = (project(normed_one_low, w_query) + b_query.astype(jnp.float32)).astype(
        jnp.bfloat16
    )
    keys_low = project(normed_one_low, w_key).astype(jnp.bfloat16)
    values_low = (project(normed_one_low, w_value) + b_value.astype(jnp.float32)).astype(
        jnp.bfloat16
    )
    query_heads = query_low.reshape(tok_rows, HEADS, HEAD_DIM)
    initial = (
        jnp.full((HEADS, tok_rows), MASKED_SCORE, jnp.float32),
        jnp.zeros((HEADS, tok_rows), jnp.float32),
        jnp.zeros((HEADS, tok_rows, HEAD_DIM), jnp.float32),
    )
    key_piece = lax.all_gather(keys_low, "seq", axis=0, tiled=True)
    value_piece = lax.all_gather(values_low, "seq", axis=0, tiled=True)
    piece_len = key_piece.shape[0]
    fold_block_len = math.gcd(piece_len, 512)
    block_count = piece_len // fold_block_len
    key_blocks = key_piece.reshape(block_count, fold_block_len, HEADS, HEAD_DIM)
    value_blocks = value_piece.reshape(block_count, fold_block_len, HEADS, HEAD_DIM)
    offsets = jnp.arange(block_count, dtype=jnp.int32) * fold_block_len

    def block_step(state_now, packed):
        row_max, row_total, accumulated = state_now
        key_blk, value_blk, offset = packed
        key_pos = offset + jnp.arange(fold_block_len, dtype=jnp.int32)
        allowed = visible_pairs(own_pos, own_seg, key_pos, segment_ids(key_pos, seq_ends))
        scores = (
            jnp.einsum("qhd,khd->hqk", query_heads, key_blk, preferred_element_type=jnp.float32)
            * SCORE_SCALE
        )
        masked = jnp.where(allowed, scores, MASKED_SCORE)
        new_max = jnp.maximum(row_max, jnp.max(masked, axis=-1))
        weights = jnp.where(allowed, jnp.exp(masked - new_max[..., None]), 0.0)
        factor = jnp.exp(row_max - new_max)
        row_total = row_total * factor + jnp.sum(weights, axis=-1)
        accumulated = accumulated * factor[..., None] + jnp.einsum(
            "hqk,khd->hqd",
            weights.astype(jnp.bfloat16),
            value_blk,
            preferred_element_type=jnp.float32,
        )
        return ((new_max, row_total, accumulated), None)

    result, _ = lax.scan(block_step, initial, (key_blocks, value_blocks, offsets))
    row_max, row_total, accumulated = result
    attn_heads = accumulated / row_total[..., None]
    attn_low = jnp.transpose(attn_heads, (1, 0, 2)).reshape(tok_rows, width).astype(jnp.bfloat16)
    resid = inputs + project(attn_low, w_out) + b_out.astype(jnp.float32)
    normed_two_low = norm_layer(resid, gain_two, bias_two).astype(jnp.bfloat16)
    experts = exp_size * w_up.shape[0]
    capacity = 2 * tok_rows // experts
    expert_of = expert_ids[0, :, 0]
    onehot = (expert_of[:, None] == jnp.arange(experts, dtype=jnp.int32)[None, :]).astype(jnp.int32)
    slot_of = jnp.sum(onehot * (jnp.cumsum(onehot, axis=0) - onehot), axis=1)
    send_rows = (
        jnp.zeros((experts, capacity, width), jnp.bfloat16)
        .at[expert_of, slot_of]
        .set(normed_two_low)
    )
    received = lax.all_to_all(send_rows, "exp", split_axis=0, concat_axis=0, tiled=True)
    recv_count = experts * capacity
    recv_rows = received.reshape(recv_count, width)
    up_weight = w_up[0]
    up_bias = b_up[0]
    down_weight = w_down[0]
    down_bias = b_down[0].astype(jnp.float32)
    piece_width = width // seq_size
    grad_send = (
        jnp.zeros((experts, capacity, width), jnp.bfloat16).at[expert_of, slot_of].set(cotangent[0])
    )
    gathered = lax.all_gather(recv_rows, "seq", axis=0, tiled=True)
    preact = project(gathered, up_weight) + up_bias.astype(jnp.float32)
    act_low = jax.nn.gelu(preact).astype(jnp.bfloat16)
    part = act_low
    expert_out = (
        lax.psum_scatter(
            project(part, down_weight).astype(jnp.bfloat16), "seq", scatter_dimension=0, tiled=True
        ).astype(jnp.float32)
        + down_bias
    )
    returned = lax.all_to_all(
        expert_out.astype(jnp.bfloat16).reshape(experts, capacity, width),
        "exp",
        split_axis=0,
        concat_axis=0,
        tiled=True,
    )
    grad_recv = lax.all_to_all(grad_send, "exp", split_axis=0, concat_axis=0, tiled=True).reshape(
        recv_count, width
    )
    grad_all = lax.all_gather(grad_recv, "seq", axis=0, tiled=True)
    bias_full = jnp.sum(grad_all.astype(jnp.float32), axis=0)
    grad_b_down = lax.dynamic_slice_in_dim(bias_full, seq_rank * piece_width, piece_width, 0)
    grad_act = jnp.einsum("rd,fd->rf", grad_all, down_weight, preferred_element_type=jnp.float32)
    grad_pre = jax.vjp(jax.nn.gelu, preact)[1](grad_act)[0].astype(jnp.bfloat16)
    grad_w_down = jnp.einsum("rf,rd->fd", act_low, grad_all, preferred_element_type=jnp.float32)
    grad_w_up = jnp.einsum("rd,rf->df", gathered, grad_pre, preferred_element_type=jnp.float32)
    grad_b_up = jnp.sum(grad_pre.astype(jnp.float32), axis=0)
    part = grad_pre
    grad_home = lax.psum_scatter(
        jnp.einsum("rf,df->rd", part, up_weight, preferred_element_type=jnp.float32).astype(
            jnp.bfloat16
        ),
        "seq",
        scatter_dimension=0,
        tiled=True,
    )
    ffn_rows = returned[expert_of, slot_of].astype(jnp.float32)
    output = (resid + ffn_rows).astype(jnp.bfloat16)
    grad_back = lax.all_to_all(
        grad_home.reshape(experts, capacity, width), "exp", split_axis=0, concat_axis=0, tiled=True
    )
    grad_normed_two = grad_back[expert_of, slot_of].astype(jnp.float32)
    _, norm_two_back = jax.vjp(norm_layer, resid, gain_two, bias_two)
    grad_resid_norm, grad_gain_two, grad_bias_two = norm_two_back(grad_normed_two)
    grad_resid = cotangent[0].astype(jnp.float32) + grad_resid_norm
    grad_out_low = grad_resid.astype(jnp.bfloat16)
    grad_w_out = jnp.einsum("qa,qd->ad", attn_low, grad_out_low, preferred_element_type=jnp.float32)
    grad_b_out = jnp.sum(grad_out_low.astype(jnp.float32), axis=0)
    grad_attn_low = jnp.einsum(
        "qd,ad->qa", grad_out_low, w_out, preferred_element_type=jnp.float32
    ).astype(jnp.bfloat16)
    grad_attn_heads = grad_attn_low.reshape(tok_rows, HEADS, HEAD_DIM)
    delta = jnp.sum(
        jnp.transpose(grad_attn_heads.astype(jnp.float32), (1, 0, 2)) * attn_heads, axis=-1
    )
    whole_keys, whole_values = (
        lax.all_gather(keys_low, "seq", axis=0, tiled=True),
        lax.all_gather(values_low, "seq", axis=0, tiled=True),
    )
    group_len = whole_keys.shape[0]
    block_len = math.gcd(group_len, 512)
    block_count = group_len // block_len

    def back_step(grad_query, packed):
        key_blk, value_blk, offset = packed
        key_pos = offset + jnp.arange(block_len, dtype=jnp.int32)
        allowed = visible_pairs(own_pos, own_seg, key_pos, segment_ids(key_pos, seq_ends))
        scores = (
            jnp.einsum("qhd,khd->hqk", query_heads, key_blk, preferred_element_type=jnp.float32)
            * SCORE_SCALE
        )
        masked = jnp.where(allowed, scores, MASKED_SCORE)
        probabilities = (
            jnp.where(allowed, jnp.exp(masked - row_max[..., None]), 0.0) / row_total[..., None]
        )
        probs_low = probabilities.astype(jnp.bfloat16)
        grad_probs = jnp.einsum(
            "qhd,khd->hqk", grad_attn_heads, value_blk, preferred_element_type=jnp.float32
        )
        grad_scores = (probabilities * (grad_probs - delta[..., None])).astype(jnp.bfloat16)
        grad_query = (
            grad_query
            + jnp.einsum("hqk,khd->qhd", grad_scores, key_blk, preferred_element_type=jnp.float32)
            * SCORE_SCALE
        )
        grad_key_blk = (
            jnp.einsum("hqk,qhd->khd", grad_scores, query_heads, preferred_element_type=jnp.float32)
            * SCORE_SCALE
        )
        grad_value_blk = jnp.einsum(
            "hqk,qhd->khd", probs_low, grad_attn_heads, preferred_element_type=jnp.float32
        )
        return (grad_query, (grad_key_blk, grad_value_blk))

    block_offsets = jnp.arange(block_count, dtype=jnp.int32) * block_len
    grad_query, key_value_parts = lax.scan(
        back_step,
        jnp.zeros((tok_rows, HEADS, HEAD_DIM), jnp.float32),
        (
            whole_keys.reshape(block_count, block_len, HEADS, HEAD_DIM),
            whole_values.reshape(block_count, block_len, HEADS, HEAD_DIM),
            block_offsets,
        ),
    )
    grad_keys, grad_values = (
        lax.psum_scatter(
            key_value_parts[0].reshape(group_len, width).astype(jnp.bfloat16),
            "seq",
            scatter_dimension=0,
            tiled=True,
        ).astype(jnp.float32),
        lax.psum_scatter(
            key_value_parts[1].reshape(group_len, width).astype(jnp.bfloat16),
            "seq",
            scatter_dimension=0,
            tiled=True,
        ).astype(jnp.float32),
    )
    grad_query_low = grad_query.reshape(tok_rows, width).astype(jnp.bfloat16)
    grad_keys_low = grad_keys.astype(jnp.bfloat16)
    grad_values_low = grad_values.astype(jnp.bfloat16)
    grad_w_query = jnp.einsum(
        "qa,qd->ad", normed_one_low, grad_query_low, preferred_element_type=jnp.float32
    )
    grad_b_query = jnp.sum(grad_query_low.astype(jnp.float32), axis=0)
    grad_w_key = jnp.einsum(
        "qa,qd->ad", normed_one_low, grad_keys_low, preferred_element_type=jnp.float32
    )
    grad_w_value = jnp.einsum(
        "qa,qd->ad", normed_one_low, grad_values_low, preferred_element_type=jnp.float32
    )
    grad_b_value = jnp.sum(grad_values_low.astype(jnp.float32), axis=0)
    grad_normed_one = (
        (
            jnp.einsum("qd,ad->qa", grad_query_low, w_query, preferred_element_type=jnp.float32)
            + jnp.einsum("qd,ad->qa", grad_keys_low, w_key, preferred_element_type=jnp.float32)
            + jnp.einsum("qd,ad->qa", grad_values_low, w_value, preferred_element_type=jnp.float32)
        )
        .astype(jnp.bfloat16)
        .astype(jnp.float32)
    )
    _, norm_one_back = jax.vjp(norm_layer, inputs, gain_one, bias_one)
    grad_in_norm, grad_gain_one, grad_bias_one = norm_one_back(grad_normed_one)
    input_grad = grad_resid + grad_in_norm
    summed = lax.psum(
        (
            grad_gain_one,
            grad_bias_one,
            grad_w_query,
            grad_b_query,
            grad_w_key,
            grad_w_value,
            grad_b_value,
            grad_w_out,
            grad_b_out,
            grad_gain_two,
            grad_bias_two,
        ),
        ("seq", "exp"),
    )
    return (
        output[None],
        input_grad[None],
        summed[0],
        summed[1],
        summed[2],
        summed[3],
        summed[4],
        summed[5],
        summed[6],
        summed[7],
        summed[8],
        summed[9],
        summed[10],
        grad_w_up[None],
        grad_b_up[None],
        grad_w_down[None],
        grad_b_down[None],
    )


def solution(mesh):
    placed = (
        P("exp", "seq", None),
        P("exp", None),
        P("exp", "seq", None),
        P(),
        P(),
        P(),
        P(),
        P(),
        P(),
        P(),
        P(),
        P(),
        P(),
        P(),
        P("exp", None, "seq"),
        P("exp", "seq"),
        P("exp", "seq", None),
        P("exp", None),
        P("exp", "seq", None),
    )
    plane = mesh.shape["seq"] == 4 and mesh.shape["exp"] == 8
    return jax.shard_map(
        shards if plane else shards_any,
        mesh=mesh,
        in_specs=placed,
        out_specs=(
            P("exp", "seq", None),
            P("exp", "seq", None),
            P(),
            P(),
            P(),
            P(),
            P(),
            P(),
            P(),
            P(),
            P(),
            P(),
            P(),
            P("exp", None, "seq"),
            P("exp", "seq"),
            P("exp", "seq", None),
            P("exp", "seq"),
        ),
        check_vma=False,
    )
```

```python
import functools
import math

import jax
import jax.numpy as jnp
from jax import lax
from jax.experimental import pallas as pl
from jax.experimental.pallas import tpu as pltpu
from jax.sharding import PartitionSpec as P

MESH = pl.DeviceIdType.MESH
F32 = jnp.float32
BF16 = jnp.bfloat16
VMEM_LIMIT = 63 * 2**20


def dot(a, b, dims=((1,), (0,))):
    return lax.dot_general(a, b, (dims, ((), ())), preferred_element_type=F32)


class Place:
    def __init__(self, n_exp):
        self.n_exp = n_exp
        self.s = lax.axis_index("seq")
        self.e = lax.axis_index("exp")
        low = lax.rem(self.s, 2)
        high = lax.div(self.s, 2)
        self.near = high * 2 + (1 - low)
        self.far = (1 - high) * 2 + low
        self.diag = (1 - high) * 2 + (1 - low)
        self.core = lax.rem(self.e, 2)
        self.chip = lax.div(self.e, 2)

    def peer(self, step, way):
        chips = self.n_exp // 2
        hop = lax.div(step, 2)
        if chips == 4:
            hop = hop + lax.div(hop, 2) * (5 - 2 * hop)
        chip = lax.rem(self.chip + way * hop + chips, chips)
        return chip * 2 + lax.rem(self.core + step, 2)

    def greet(self, diag=False):
        barrier = pltpu.get_barrier_semaphore()
        others = (self.near, self.far, self.diag) if diag else (self.near, self.far)
        for other in others:
            pl.semaphore_signal(barrier, inc=1, device_id=(other, self.e), device_id_type=MESH)

        def tell(step, carry):
            pl.semaphore_signal(
                barrier, inc=1, device_id=(self.s, self.peer(step, 1)), device_id_type=MESH
            )
            return carry

        lax.fori_loop(1, self.n_exp, tell, 0)
        pl.semaphore_wait(barrier, len(others) + self.n_exp - 1)

    def to_seq(self, src, dst, send_sem, recv_sem, other):
        return pltpu.make_async_remote_copy(
            src_ref=src, dst_ref=dst, send_sem=send_sem, recv_sem=recv_sem,
            device_id=(other, self.e), device_id_type=MESH,
        )

    def to_exp(self, src, dst, send_sem, recv_sem, other):
        return pltpu.make_async_remote_copy(
            src_ref=src, dst_ref=dst, send_sem=send_sem, recv_sem=recv_sem,
            device_id=(self.s, other), device_id_type=MESH,
        )


class Dispatch:
    def __init__(self, place, send, held, exp_sems, seq_sems):
        self.place, self.send, self.held = place, send, held
        self.exp_send, self.exp_recv = exp_sems
        self.seq_send, self.seq_recv = seq_sems
        self.cap = send.shape[1]

    @staticmethod
    def scratch(n_exp):
        return [
            pltpu.SemaphoreType.DMA((n_exp,)),
            pltpu.SemaphoreType.DMA((n_exp,)),
            pltpu.SemaphoreType.DMA((n_exp, 6)),
            pltpu.SemaphoreType.DMA((n_exp, 6)),
        ]

    def _exp(self, step):
        p = self.place
        other = p.peer(step, -1)
        return p.to_exp(
            self.send.at[other], self.held.at[step, p.s], self.exp_send.at[step], self.exp_recv.at[step], other
        )

    def _seq(self, step, owner, half, lane, other):
        p = self.place
        rows = pl.ds(half * (self.cap // 2), self.cap // 2)
        part = self.held.at[step, owner, rows]
        return p.to_seq(part, part, self.seq_send.at[step, lane], self.seq_recv.at[step, lane], other)

    def copies(self, step, lanes=range(6)):
        p = self.place
        spec = (
            (p.s, 0, p.near),
            (p.s, 1, p.far),
            (p.s, 1, p.near),
            (p.s, 0, p.far),
            (p.near, 0, p.far),
            (p.far, 1, p.near),
        )
        return [self._seq(step, spec[n][0], spec[n][1], n, spec[n][2]) for n in lanes]

    def start_exp(self, step):
        self._exp(step).start()

    def own(self):
        p = self.place
        self.held[0, p.s] = self.send[p.e]

    def start_seq(self, step):
        @pl.when(step > 0)
        def _():
            self._exp(step).wait_recv()

        for c in self.copies(step, range(4)):
            c.start()

    def relay(self, step):
        for c, out in zip(self.copies(step, (0, 1)), self.copies(step, (4, 5))):
            c.wait_recv()
            out.start()

    def arrived(self, step):
        for c in self.copies(step, range(2, 6)):
            c.wait_recv()

    def sent(self, step):
        for c in self.copies(step):
            c.wait_send()

    def drain(self, seq=True):
        def body(step, carry):
            if seq:
                self.sent(step)

            @pl.when(step > 0)
            def _():
                self._exp(step).wait_send()

            return carry

        lax.fori_loop(0, self.place.n_exp, body, 0)


class Combine:
    def __init__(self, place, part, passing, landing, total, back, seq_sems, exp_sems, slots):
        self.place, self.part, self.passing, self.landing = place, part, passing, landing
        self.total, self.back, self.slots = total, back, slots
        self.seq_send, self.seq_recv = seq_sems
        self.exp_send, self.exp_recv = exp_sems
        self.half = part.shape[2] // 2

    @staticmethod
    def scratch(n_exp, cap, width):
        return [
            pltpu.VMEM((n_exp, 2, cap // 2, width), BF16),
            pltpu.VMEM((n_exp, 4, cap // 2, width), BF16),
            pltpu.VMEM((n_exp, cap, width), BF16),
            pltpu.SemaphoreType.DMA((n_exp, 6)),
            pltpu.SemaphoreType.DMA((n_exp, 6)),
            pltpu.SemaphoreType.DMA((n_exp,)),
            pltpu.SemaphoreType.DMA((n_exp,)),
        ]

    def _slot(self, step):
        return lax.rem(step, self.slots)

    def _piece(self, step, owner, half):
        return self.part.at[self._slot(step), owner, pl.ds(half * self.half, self.half)]

    def _seq(self, src, dst, step, lane, other):
        return self.place.to_seq(
            src, dst, self.seq_send.at[step, lane], self.seq_recv.at[step, lane], other
        )

    def copies(self, step, lanes=range(6)):
        p = self.place
        spec = (
            (p.diag, 0, self.passing, 0, p.near),
            (p.diag, 1, self.passing, 1, p.far),
            (p.near, 0, self.landing, 0, p.near),
            (p.far, 1, self.landing, 3, p.far),
            (p.far, 0, self.landing, 2, p.far),
            (p.near, 1, self.landing, 1, p.near),
        )
        made = []
        for n in lanes:
            owner, half, buffer, at, other = spec[n]
            made.append(self._seq(self._piece(step, owner, half), buffer.at[step, at], step, n, other))
        return made

    def start(self, step):
        for c in self.copies(step, range(4)):
            c.start()

    def pass_on(self, step):
        p = self.place
        slot = self._slot(step)
        came, out = self.copies(step, (0, 1)), self.copies(step, (4, 5))
        for n, owner in enumerate((p.far, p.near)):
            rows = pl.ds(n * self.half, self.half)
            came[n].wait_recv()
            self.part[slot, owner, rows] = (
                self.part[slot, owner, rows].astype(F32) + self.passing[step, n].astype(F32)
            ).astype(BF16)
            out[n].start()

    def _whole(self, step):
        if self.total is None:
            return self.part.at[self._slot(step), self.place.s]
        return self.total.at[step]

    def _exp(self, step):
        p = self.place
        other = p.peer(step, 1)
        return p.to_exp(
            self._whole(step), self.back.at[p.e], self.exp_send.at[step], self.exp_recv.at[step], other
        )

    def arrived(self, step):
        copies = self.copies(step)
        for c in copies[2:]:
            c.wait_recv()
        for c in copies:
            c.wait_send()

    def summed(self, step, half):
        rows = pl.ds(half * self.half, self.half)
        return (
            self.part[self._slot(step), self.place.s, rows].astype(F32)
            + self.landing[step, half].astype(F32)
            + self.landing[step, 2 + half].astype(F32)
        )

    def finish(self, step, bias=None):
        p = self.place
        self.arrived(step)
        for half in range(2):
            value = self.summed(step, half)
            if bias is not None:
                value = value + bias
            rows = pl.ds(half * self.half, self.half)
            if self.total is None:
                self.part[self._slot(step), p.s, rows] = value.astype(BF16)
            else:
                self.total[step, rows] = value.astype(BF16)

        @pl.when(step > 0)
        def _():
            self._exp(step).start()

        @pl.when(step == 0)
        def _():
            self.back[p.e] = self._whole(0)[...]

    def drain(self):
        p = self.place

        def body(step, carry):
            c = self._exp(step)
            c.wait_send()
            c.wait_recv()
            return carry

        lax.fori_loop(1, p.n_exp, body, 0)


GELU_A = math.sqrt(2.0 / math.pi)
GELU_B = 0.044715


EPSILON = 1e-05
SCORE_SCALE = 0.125
MASKED_SCORE = -1e30
HEAD_DIM = 64
HEADS = 16


class Gather:
    def __init__(self, place, held, send_sems, recv_sems):
        self.place, self.held = place, held
        self.send_sems, self.recv_sems = send_sems, recv_sems
        self.half = held.shape[1] // 2

    @staticmethod
    def scratch():
        return [pltpu.SemaphoreType.DMA((6,)), pltpu.SemaphoreType.DMA((6,))]

    def copies(self, lanes=range(6)):
        p = self.place
        spec = (
            (p.s, 0, p.near),
            (p.s, 1, p.far),
            (p.s, 1, p.near),
            (p.s, 0, p.far),
            (p.near, 0, p.far),
            (p.far, 1, p.near),
        )
        made = []
        for n in lanes:
            owner, half, other = spec[n]
            part = self.held.at[owner, pl.ds(half * self.half, self.half)]
            made.append(p.to_seq(part, part, self.send_sems.at[n], self.recv_sems.at[n], other))
        return made

    def start(self):
        for c in self.copies(range(4)):
            c.start()

    def relay(self):
        for c, out in zip(self.copies((0, 1)), self.copies((4, 5))):
            c.wait_recv()
            out.start()

    def wait(self, lanes):
        for c in self.copies(lanes):
            c.wait_recv()

    def drain(self):
        for c in self.copies():
            c.wait_send()


def layer_norm(values, gain, shift):
    center = values - jnp.mean(values, axis=-1, keepdims=True)
    inv_std = lax.rsqrt(jnp.mean(center * center, axis=-1, keepdims=True) + EPSILON)
    xhat = center * inv_std
    return xhat * gain + shift, xhat, inv_std


def norm_back(grad, xhat, inv_std, gain):
    d = grad * gain
    return (
        d - jnp.mean(d, axis=-1, keepdims=True) - xhat * jnp.mean(d * xhat, axis=-1, keepdims=True)
    ) * inv_std


def row_choice(ids, n_exp, cap):
    tokens = ids.shape[1]
    named = (ids == lax.broadcasted_iota(jnp.int32, (128, tokens), 0)).astype(BF16)
    before = (
        lax.broadcasted_iota(jnp.int32, (tokens, tokens), 0)
        < lax.broadcasted_iota(jnp.int32, (tokens, tokens), 1)
    ).astype(BF16)
    earlier = dot(named, before) * named.astype(F32)
    slot = jnp.sum(earlier, axis=0, keepdims=True).astype(jnp.int32) + ids * cap
    return (slot == lax.broadcasted_iota(jnp.int32, (n_exp * cap, tokens), 0)).astype(BF16)


def segment_of(position, lengths):
    end = jnp.int32(0)
    count = jnp.zeros_like(position)
    for n in range(lengths.shape[1]):
        end = end + lengths[0, n]
        count = count + (position >= end).astype(jnp.int32)
    return count


def head_mask(rows, width, head):
    lane = lax.broadcasted_iota(jnp.int32, (rows, width), 1)
    return (lane >= head * HEAD_DIM) & (lane < (head + 1) * HEAD_DIM)


class SumAll:
    def __init__(self, place, src, core_in, mine, chip_in, res, where, local_sem, sems):
        self.place, self.src, self.core_in, self.mine = place, src, core_in, mine
        self.chip_in, self.res, self.where, self.local_sem = chip_in, res, where, local_sem
        (self.core_sems, self.rs_send, self.rs_recv, self.ag_send, self.ag_recv,
         self.seq_send, self.seq_recv, self.pair_send, self.pair_recv) = sems
        self.chips = place.n_exp // 2
        p = place
        self.sibling = p.chip * 2 + (1 - p.core)

    @staticmethod
    def scratch(n_exp, *piece):
        chips = n_exp // 2
        dma = pltpu.SemaphoreType.DMA
        return [
            pltpu.VMEM((2, chips, *piece), BF16),
            pltpu.VMEM((chips, *piece), BF16),
            pltpu.VMEM((chips, *piece), BF16),
            pltpu.VMEM((chips, *piece), BF16),
            pltpu.VMEM(piece, BF16),
            dma((1,)),
            dma((2,)),
            dma((chips,)),
            dma((chips,)),
            dma((chips,)),
            dma((chips,)),
            dma((chips, 6)),
            dma((chips, 6)),
            dma((chips, 4)),
            dma((chips, 4)),
        ]

    def chip(self, hop):
        return lax.rem(self.place.chip + hop, self.chips)

    def exp(self, hop):
        return self.chip(hop) * 2 + self.place.core

    def _core(self):
        p = self.place
        return p.to_exp(
            self.src.at[1 - p.core], self.core_in, self.core_sems.at[0], self.core_sems.at[1], self.sibling
        )

    def start(self):
        self._core().start()

    def _spread(self, hop):
        p = self.place
        to = self.chip(hop)
        return p.to_exp(
            self.mine.at[to], self.chip_in.at[p.chip], self.rs_send.at[to], self.rs_recv.at[p.chip], self.exp(hop)
        )

    def _spread_from(self, hop):
        p = self.place
        at = self.chip(hop)
        return p.to_exp(
            self.mine.at[at], self.chip_in.at[at], self.rs_send.at[at], self.rs_recv.at[at], self.exp(hop)
        )

    def spread(self):
        p = self.place
        self._core().wait_recv()
        for n in range(self.chips):
            self.mine[n] = (self.src[p.core, n].astype(F32) + self.core_in[n].astype(F32)).astype(BF16)
        for hop in range(1, self.chips):
            self._spread(hop).start()

    def _local(self):
        p = self.place
        return pltpu.make_async_copy(self.res, self.where(p.s, p.e), self.local_sem.at[0])

    def _share(self, hop):
        p = self.place
        to = self.chip(hop)
        return p.to_exp(
            self.res, self.where(p.s, p.e), self.ag_send.at[to], self.ag_recv.at[p.chip], self.exp(hop)
        )

    def _share_from(self, hop):
        p = self.place
        at = self.chip(hop)
        return p.to_exp(
            self.res, self.where(p.s, self.exp(hop)), self.ag_send.at[at], self.ag_recv.at[at], self.exp(hop)
        )

    def copies(self, hop, lanes=range(6)):
        p = self.place
        spec = (
            (p.s, 0, p.near),
            (p.s, 1, p.far),
            (p.s, 1, p.near),
            (p.s, 0, p.far),
            (p.near, 0, p.far),
            (p.far, 1, p.near),
        )
        made = []
        for n in lanes:
            owner, half, other = spec[n]
            part = self.where(owner, self.exp(hop), half)
            made.append(p.to_seq(part, part, self.seq_send.at[hop, n], self.seq_recv.at[hop, n], other))
        return made

    def _pair(self, hop, n):
        p = self.place
        part = self.where((p.s, p.near, p.far, p.diag)[n], self.exp(hop))
        return p.to_exp(part, part, self.pair_send.at[hop, n], self.pair_recv.at[hop, n], self.sibling)

    def _pair_from(self, hop, n):
        p = self.place
        owner = (p.s, p.near, p.far, p.diag)[n]
        part = self.where(owner, self.chip(hop) * 2 + (1 - p.core))
        return p.to_exp(part, part, self.pair_send.at[hop, n], self.pair_recv.at[hop, n], self.sibling)

    def reduce(self):
        p = self.place
        for hop in range(1, self.chips):
            self._spread_from(hop).wait_recv()
        total = self.mine[p.chip].astype(F32)
        for hop in range(1, self.chips):
            total = total + self.chip_in[self.chip(hop)].astype(F32)
        self.res[...] = total.astype(BF16)
        self._local().start()
        for hop in range(1, self.chips):
            self._share(hop).start()
        self._local().wait()

    def forward(self, hop):
        if hop > 0:
            self._share_from(hop).wait_recv()
        for c in self.copies(hop, range(4)):
            c.start()
        self._pair(hop, 0).start()

    def relay(self, hop):
        for c, out in zip(self.copies(hop, (0, 1)), self.copies(hop, (4, 5))):
            c.wait_recv()
            out.start()

    def arrived(self, hop):
        for c in self.copies(hop, (2, 3)):
            c.wait_recv()
        self._pair(hop, 1).start()
        self._pair(hop, 2).start()
        for c in self.copies(hop, (4, 5)):
            c.wait_recv()
        self._pair(hop, 3).start()

    def drain(self):
        self._core().wait_send()
        for hop in range(1, self.chips):
            self._spread(hop).wait_send()
            self._share(hop).wait_send()
        for hop in range(self.chips):
            for c in self.copies(hop):
                c.wait_send()
            for n in range(4):
                self._pair(hop, n).wait_send()
                self._pair_from(hop, n).wait_recv()


def layer(
    tokens, ids, cotangent, lengths, ln1, w_qkv, b_query, b_value, w_out, b_out, ln2, w_up, b_up, w_down, b_down,
    n_exp, collective_id,
):
    tok, width = tokens.shape
    hidden = w_up.shape[1]
    n_seq = 4
    total = n_seq * tok
    cols = width // n_seq
    heads = cols // HEAD_DIM
    cap = 2 * tok // n_exp
    q_block = 256
    chips = n_exp // 2
    rows_w, rows_o = width // n_exp, cols // n_exp
    pairs = cols // 128
    per_pair = 128 // HEAD_DIM
    routed = n_seq * cap
    block = min(256, hidden)
    slots = 2
    ahead = 5

    vm = pltpu.VMEM
    dma = pltpu.SemaphoreType.DMA
    table = dict(
        xall=vm((1, n_seq, tok, width), BF16),
        n1=vm((width, total), BF16),
        q=vm((total, cols), BF16),
        k=vm((total, cols), BF16),
        v=vm((total, cols), BF16),
        attn=vm((total, cols), F32),
        lse=vm((8, total), F32),
        resid=vm((tok, width), F32),
        pick=vm((n_exp * cap, tok), BF16),
        w_all=vm((width, 3 * cols), BF16),
        w_o=vm((width, width), BF16),
        send_c=vm((n_exp, cap, width), BF16),
        send_n=vm((n_exp, cap, width), BF16),
        back=vm((n_exp, cap, width), BF16),
        ret=vm((n_exp, cap, width), BF16),
        attn_out=vm((n_seq, tok, cols), BF16),
        attn_in=vm((n_seq, tok, cols), BF16),
        cot=vm((n_exp, n_seq, cap, width), BF16),
        held=vm((n_exp, n_seq, cap, width), BF16),
        wu=vm((width, hidden), BF16),
        wd=vm((hidden, width), BF16),
        part=vm((slots, n_seq, cap, width), BF16),
        dwu=vm((width, hidden), F32),
        dwd=vm((hidden, width), F32),
        dqkv=vm((total, 3 * cols), BF16),
        vec_own=vm((8, width), F32),
        vec_seq=vm((n_seq, 8, width), F32),
        vec_exp=vm((n_exp, 8, width), F32),
        local_sems=dma((8,)),
        load_sems=dma((3 * pairs,)),
        dq=vm((tok, cols), F32),
        a2a_send=dma((n_seq,)),
        a2a_recv=dma((n_seq,)),
        vs_send=dma((n_seq,)),
        vs_recv=dma((n_seq,)),
        ve_send=dma((n_exp,)),
        ve_recv=dma((n_exp,)),
    )
    groups = dict(
        gather1=Gather.scratch(),
        gather2=Gather.scratch(),
        disp_c=Dispatch.scratch(n_exp),
        disp_n=Dispatch.scratch(n_exp),
        comb_g=Combine.scratch(n_exp, cap, width),
        comb_f=Combine.scratch(n_exp, cap, width)[:2] + Combine.scratch(n_exp, cap, width)[3:],
        red=[
            vm((1, 2, tok // 2, width), BF16),
            vm((1, 4, tok // 2, width), BF16),
            dma((1, 6)),
            dma((1, 6)),
        ],
        sum_o=SumAll.scratch(n_exp, rows_o, width),
        **{f"sum_{j}": SumAll.scratch(n_exp, 3, rows_w, 128) for j in range(pairs)},
    )
    scratch = list(table.values()) + [ref for group in groups.values() for ref in group]

    def kernel(tok_ref, ids_ref, cot_ref, len_ref, g1_ref, c1_ref, wq_in, wk_in, wv_in, bq_ref, bv_ref, wo_in, bo_ref,
               g2_ref, c2_ref, wu_in, bu_ref, wd_in, bd_ref,
               out_out, gin_out, vec_ref, dbu_ref, csum_ref, dwu_out, dwd_out, gw_out, go_out, *refs):
        r = dict(zip(table, refs))
        at = len(table)
        g = {}
        for name, group in groups.items():
            g[name] = refs[at : at + len(group)]
            at += len(group)
        xall, n1, q_all, k_all, v_all = r["xall"], r["n1"], r["q"], r["k"], r["v"]
        attn, lse_all, resid, pick = r["attn"], r["lse"], r["resid"], r["pick"]
        w_all, w_o, wu, wd = r["w_all"], r["w_o"], r["wu"], r["wd"]
        send_c, send_n, back, ret = r["send_c"], r["send_n"], r["back"], r["ret"]
        attn_out, attn_in, cot, held, part = r["attn_out"], r["attn_in"], r["cot"], r["held"], r["part"]
        dwu, dwd, dqkv = r["dwu"], r["dwd"], r["dqkv"]
        gattn = attn_out
        gin_ref = dwd.at[0:tok, :]
        dk, dv = dwu.at[0:total, 0:cols], dwu.at[0:total, cols : 2 * cols]
        vec_own, vec_seq, vec_exp = r["vec_own"], r["vec_seq"], r["vec_exp"]
        local_sems, load_sems, dq = r["local_sems"], r["load_sems"], r["dq"]

        p = Place(n_exp)
        mine = pl.ds(pl.multiple_of(p.s * cols, cols), cols)

        tile = 32

        def tile_rows(n):
            return pl.ds(pl.multiple_of(n * tile, tile), tile)

        def row_of(ref):
            return ref[...].astype(F32).reshape(1, ref.shape[-1])

        loads = [
            pltpu.make_async_copy(
                src.at[:, pl.ds(pl.multiple_of(p.s * cols + j * 128, 128), 128)],
                w_all.at[:, pl.ds((3 * j + m) * 128, 128)],
                load_sems.at[3 * j + m],
            )
            for m, src in enumerate((wq_in, wk_in, wv_in))
            for j in range(pairs)
        ]
        load_o = pltpu.make_async_copy(wo_in, w_o, local_sems.at[3])
        load_ffn = [
            pltpu.make_async_copy(wu_in, wu, local_sems.at[4]),
            pltpu.make_async_copy(wd_in, wd, local_sems.at[5]),
        ]
        for c in loads + [load_o] + load_ffn:
            c.start()

        xall[0, p.s] = tok_ref[...]
        p.greet(diag=True)
        gather1 = Gather(p, xall.at[0], *g["gather1"])
        gather1.start()
        pick[...] = row_choice(ids_ref[...], n_exp, cap)

        def lay_out(send, rows_ref):
            for e in range(0, n_exp, 2):
                laid = dot(pick[e * cap : (e + 2) * cap, :], rows_ref[...])
                send[e : e + 2] = laid.astype(BF16).reshape(2, cap, width)

        lay_out(send_c, cot_ref)
        disp_c = Dispatch(p, send_c, cot, g["disp_c"][0:2], g["disp_c"][2:4])
        for step in range(1, n_exp):
            disp_c.start_exp(step)
        disp_c.own()
        gain1, bias1 = row_of(g1_ref), row_of(c1_ref)
        gain2, bias2 = row_of(g2_ref), row_of(c2_ref)
        bq = bq_ref[mine].astype(F32).reshape(1, cols)
        bv = bv_ref[mine].astype(F32).reshape(1, cols)

        def project(owner):
            rows = pl.ds(pl.multiple_of(owner * tok, tok), tok)

            def norm_tile(n, carry):
                x = xall[0, owner, tile_rows(n), :].astype(F32)
                per = cap // tile
                rows = pl.ds(pl.multiple_of(lax.rem(n, per) * tile, tile), tile)
                part[0, lax.div(n, per), rows, :] = layer_norm(x, gain1, bias1)[0].astype(BF16)
                return carry

            lax.fori_loop(0, tok // tile, norm_tile, 0)
            normed = part[0].reshape(tok, width)
            n1[:, rows] = jnp.transpose(normed)
            out = dot(normed, w_all[...])
            for j in range(pairs):
                at, first = slice(j * 128, (j + 1) * 128), 3 * j * 128
                q = (out[:, first : first + 128] + bq[:, at]).astype(BF16)
                q_all[rows, at] = (q.astype(F32) * SCORE_SCALE).astype(BF16)
                k_all[rows, at] = out[:, first + 128 : first + 256].astype(BF16)
                v_all[rows, at] = (out[:, first + 256 : first + 384] + bv[:, at]).astype(BF16)

        for c in loads:
            c.wait()
        project(p.s)
        gather1.relay()
        gather1.wait((2, 3))
        project(p.near)
        project(p.far)
        gather1.wait((4, 5))
        disp_c.start_seq(0)
        disp_c.start_seq(1)
        project(p.diag)

        def a2a(owner):
            return p.to_seq(
                attn_out.at[owner], attn_in.at[p.s], r["a2a_send"].at[owner], r["a2a_recv"].at[p.s], owner
            )

        def a2a_from(owner):
            return p.to_seq(
                attn_out.at[owner], attn_in.at[owner], r["a2a_send"].at[owner], r["a2a_recv"].at[owner], owner
            )

        blocks = total // q_block
        for n in reversed(range(blocks)):
            seen = (n + 1) * q_block
            rows = pl.ds(n * q_block, q_block)
            q_pos = lax.broadcasted_iota(jnp.int32, (q_block, 1), 0) + n * q_block
            k_pos = lax.broadcasted_iota(jnp.int32, (1, seen), 1)
            allowed = (segment_of(q_pos, len_ref) == segment_of(k_pos, len_ref)) & (k_pos <= q_pos)
            q_rows = q_all[rows, :]
            acc = jnp.zeros((q_block, cols), F32)
            lse = jnp.zeros((q_block, 128), F32)
            lane = lax.broadcasted_iota(jnp.int32, (q_block, 128), 1)
            for head in range(heads):
                own = head_mask(q_block, cols, head)
                scores = dot(jnp.where(own, q_rows, jnp.zeros_like(q_rows)), k_all[0:seen, :], ((1,), (1,)))
                scores = jnp.where(allowed, scores, MASKED_SCORE)
                top = jnp.max(scores, axis=1, keepdims=True)
                weights = jnp.exp(scores - top)
                sums = jnp.sum(weights, axis=1, keepdims=True)
                out = dot(weights.astype(BF16), v_all[0:seen, :]) / sums
                acc = jnp.where(own, out, acc)
                lse = jnp.where(lane == head, top + jnp.log(sums), lse)
            attn[rows, :] = acc
            lse_all[:, rows] = jnp.transpose(lse)[0:8, :]
            owner, first = (n * q_block) // tok, (n * q_block) % tok
            attn_out[owner, pl.ds(first, q_block)] = acc.astype(BF16)
            if first == 0:

                @pl.when(p.s != owner)
                def _(owner=owner):
                    a2a(owner).start()

                @pl.when(p.s == owner)
                def _(owner=owner):
                    attn_in[owner] = attn_out[owner]

        disp_c.start_seq(2)
        disp_c.relay(0)
        disp_c.relay(1)
        load_o.wait()
        sums = tok_ref[...].astype(F32) + row_of(bo_ref)
        for owner in range(n_seq):

            @pl.when(p.s != owner)
            def _(owner=owner):
                a2a_from(owner).wait_recv()

            sums = sums + dot(attn_in[owner], w_o[pl.ds(owner * cols, cols), :])
        resid[...] = sums
        disp_c.start_seq(3)
        disp_c.relay(2)

        gather1.drain()
        for owner in range(n_seq):

            @pl.when(p.s != owner)
            def _(owner=owner):
                a2a(owner).wait_send()

        gout = xall.at[0]
        low = gout.at[p.s]

        def norm_two_tile(n, carry):
            low[tile_rows(n), :] = layer_norm(resid[tile_rows(n), :], gain2, bias2)[0].astype(BF16)
            return carry

        lax.fori_loop(0, tok // tile, norm_two_tile, 0)
        lay_out(send_n, low)

        disp_n = Dispatch(p, send_n, held, g["disp_n"][0:2], g["disp_n"][2:4])
        comb_g = Combine(p, part, *g["comb_g"][0:3], back, g["comb_g"][3:5], g["comb_g"][5:7], slots)
        comb_f = Combine(p, held, *g["comb_f"][0:2], None, ret, g["comb_f"][2:4], g["comb_f"][4:6], n_exp)
        disp_n.own()
        disp_n.start_seq(0)
        for step in range(1, n_exp):
            disp_n.start_exp(step)
        disp_c.start_seq(4)
        disp_c.relay(3)
        dwu[...] = jnp.zeros_like(dwu)
        dwd[...] = jnp.zeros_like(dwd)
        dbu_ref[...] = jnp.zeros_like(dbu_ref)
        csum_ref[...] = jnp.zeros_like(csum_ref)
        bias_down = bd_ref[...].astype(F32)
        for c in load_ffn:
            c.wait()

        def ffn_start(*steps):
            for step in steps:
                comb_f.start(step)

        def ffn_pass(*steps):
            for step in steps:
                comb_f.pass_on(step)

        def ffn_finish(*steps):
            for step in steps:
                comb_f.finish(step, bias_down)

        def compute(step):
            x = held[step].reshape(routed, width)
            gr = cot[step].reshape(routed, width)
            ones = jnp.ones((8, routed), BF16)
            csum_ref[...] += dot(ones, gr)[0:1, :]
            y = jnp.zeros((routed, width), F32)
            gx = jnp.zeros((routed, width), F32)
            for b in range(hidden // block):
                at = pl.ds(b * block, block)
                wu_b, wd_b = wu[:, at], wd[at, :]
                pre = dot(x, wu_b) + bu_ref[:, at].astype(F32)
                g_act = dot(gr, wd_b, ((1,), (1,)))
                sq = pre * pre
                th = jnp.tanh(GELU_A * pre * (1.0 + GELU_B * sq))
                half = 0.5 * (1.0 + th)
                act = (pre * half).astype(BF16)
                slope = half + 0.5 * pre * (1.0 - th * th) * (GELU_A * (1.0 + 3.0 * GELU_B * sq))
                g_pre = (g_act * slope).astype(BF16)
                dbu_ref[:, at] += dot(ones, g_pre)[0:1, :]
                y = y + dot(act, wd_b)
                gx = gx + dot(g_pre, wu_b, ((1,), (1,)))
                dwu[:, at] += dot(x, g_pre, ((0,), (0,)))
                dwd[at, :] += dot(act, gr, ((0,), (0,)))
            part[lax.rem(step, slots)] = gx.astype(BF16).reshape(n_seq, cap, width)
            disp_n.sent(step)
            held[step] = y.astype(BF16).reshape(n_seq, cap, width)

        stores = [
            pltpu.make_async_copy(dwu, dwu_out, local_sems.at[6]),
            pltpu.make_async_copy(dwd, dwd_out, local_sems.at[7]),
        ]

        def loop(t, carry):
            @pl.when(t + ahead - 1 < n_exp)
            def _():
                disp_c.start_seq(t + ahead - 1)

            @pl.when(t + ahead - 2 < n_exp)
            def _():
                disp_c.relay(t + ahead - 2)

            @pl.when(t <= n_exp)
            def _():
                disp_n.relay(t - 1)

            @pl.when(t < n_exp)
            def _():
                disp_n.start_seq(t)

            @pl.when((t >= 3) & (t <= n_exp + 2))
            def _():
                comb_g.pass_on(t - 3)

            @pl.when(t >= 4)
            def _():
                comb_g.finish(t - 4)

            @pl.when(t == n_exp + 1)
            def _():
                ffn_start(0)

            @pl.when((t >= 2) & (t <= n_exp + 1))
            def _():
                disp_c.arrived(t - 2)
                disp_n.arrived(t - 2)
                compute(t - 2)
                comb_g.start(t - 2)

            @pl.when(t == n_exp + 1)
            def _():
                for c in stores:
                    c.start()
                ffn_start(1)

            @pl.when(t == n_exp + 2)
            def _():
                ffn_start(2)

            @pl.when(t == n_exp + 3)
            def _():
                ffn_start(3)

            return carry

        lax.fori_loop(1, n_exp + 4, loop, 0)
        comb_g.drain()

        for c in stores:
            c.wait()
        gin_ref[...] = dot(pick[...], back[...].reshape(n_exp * cap, width), ((0,), (0,)))

        def norm_two_back(n, carry):
            at = tile_rows(n)
            g_two = gin_ref[at, :]
            _, xhat, inv_std = layer_norm(resid[at, :], gain2, 0.0)
            g_resid = cot_ref[at, :].astype(F32) + norm_back(g_two, xhat, inv_std, gain2)
            gin_ref[at, :] = g_resid
            g_low = g_resid.astype(BF16)
            gout[p.s, at, :] = g_low
            new = (g_low.astype(F32), g_two * xhat, g_two)
            return tuple(old + jnp.sum(v, axis=0, keepdims=True) for old, v in zip(carry, new))

        zero_row = jnp.zeros((1, width), F32)
        sums2 = lax.fori_loop(0, tok // tile, norm_two_back, (zero_row,) * 3)
        gather2 = Gather(p, gout, *g["gather2"])
        gather2.start()
        vec_own[...] = jnp.zeros_like(vec_own)
        for n in range(3):
            vec_own[4 + n : 5 + n, :] = sums2[n]
        wo_mine = w_o.at[mine, :]

        def grad_attn(owner):
            gattn[owner] = dot(gout[owner], wo_mine[...], ((1,), (1,))).astype(BF16)

        dwu[0:total, 0 : 2 * cols] = jnp.zeros((total, 2 * cols), F32)

        head_rows = lax.broadcasted_iota(jnp.int32, (8, cols), 0)
        head_lane = lax.broadcasted_iota(jnp.int32, (8, cols), 1)
        per_head = (lax.div(head_lane, HEAD_DIM) == head_rows).astype(F32)

        def attn_back(owner, some_heads):
            rows = pl.ds(pl.multiple_of(owner * tok, tok), tok)
            q_pos = lax.broadcasted_iota(jnp.int32, (1, tok), 1) + owner * tok
            q_seg = segment_of(q_pos, len_ref)
            q_rows, g_rows = q_all[rows, :], gattn[owner]
            delta = lax.dot_general(
                per_head, g_rows.astype(F32) * attn[rows, :], (((1,), (1,)), ((), ())),
                precision=lax.Precision.HIGHEST, preferred_element_type=F32,
            )
            masks = [head_mask(tok, cols, head) for head in some_heads]
            zero = jnp.zeros_like(q_rows)
            q_owns = [jnp.where(own, q_rows, zero) for own in masks]
            g_owns = [jnp.where(own, g_rows, zero) for own in masks]
            dq[...] = jnp.zeros_like(dq)

            def key_block(n, carry):
                keys = pl.ds(pl.multiple_of(n * tok, tok), tok)
                k_pos = lax.broadcasted_iota(jnp.int32, (tok, 1), 0) + n * tok
                allowed = (q_seg == segment_of(k_pos, len_ref)) & (k_pos <= q_pos)
                k_rows, v_rows = k_all[keys, :], v_all[keys, :]
                dq_new = jnp.zeros((tok, cols), F32)
                dk_new = jnp.zeros((tok, cols), F32)
                dv_new = jnp.zeros((tok, cols), F32)
                for head, own, q_own, g_own in zip(some_heads, masks, q_owns, g_owns):
                    scores = dot(k_rows, q_own, ((1,), (1,)))
                    probs = jnp.where(allowed, jnp.exp(scores - lse_all[head : head + 1, rows]), 0.0)
                    g_probs = dot(v_rows, g_own, ((1,), (1,)))
                    g_scores = (probs * (g_probs - delta[head : head + 1, :])).astype(BF16)
                    dk_new = dk_new + dot(g_scores, q_own)
                    dv_new = dv_new + dot(probs.astype(BF16), g_own)
                    dq_new = dq_new + jnp.where(own, dot(g_scores, k_rows, ((0,), (0,))), 0.0)
                dk[keys, :] += dk_new
                dv[keys, :] += dv_new
                dq[...] += dq_new
                return carry

            lax.fori_loop(0, owner + 1, key_block, 0)
            low_dq = (dq[...] * SCORE_SCALE).astype(BF16)
            for j in sorted({head // per_pair for head in some_heads}):
                dqkv[rows, pl.ds(3 * j * 128, 128)] = low_dq[:, j * 128 : (j + 1) * 128]

        every = range(heads)
        grad_attn(p.s)
        gather2.relay()
        ffn_pass(0, 1, 2, 3)
        attn_back(p.s, every)
        gather2.wait((2, 3))
        grad_attn(p.near)
        attn_back(p.near, every)
        grad_attn(p.far)
        attn_back(p.far, every)
        ffn_finish(0, 1, 2, 3)
        gather2.wait((4, 5))
        ffn_start(4, 5, 6, 7)
        grad_attn(p.diag)

        def place_w(j, owner, e, half=None):
            rows = rows_w if half is None else rows_w // 2
            first = e * rows_w + (0 if half is None else half * rows)
            return gw_out.at[
                :, pl.ds(pl.multiple_of(first, rows), rows), pl.ds(pl.multiple_of(owner * cols + j * 128, 128), 128)
            ]

        def place_o(owner, e, half=None):
            rows = pl.ds(pl.multiple_of(owner * cols + e * rows_o, rows_o), rows_o)
            if half is None:
                return go_out.at[rows, :]
            return go_out.at[rows, pl.ds(half * (width // 2), width // 2)]

        def summing(name, place):
            return SumAll(p, *g[name][0:5], place, g[name][5], g[name][6:])

        sum_w = [summing(f"sum_{j}", functools.partial(place_w, j)) for j in range(pairs)]
        sum_o = summing("sum_o", place_o)

        for b in range(cols // 128):
            a_low = attn[:, b * 128 : (b + 1) * 128].astype(BF16)
            got = dot(a_low, gout[...].reshape(total, width), ((0,), (0,))).astype(BF16)
            for n in range(128 // rows_o):
                e = b * (128 // rows_o) + n
                sum_o.src[e % 2, e // 2] = got[n * rows_o : (n + 1) * rows_o]
        sum_o.start()
        for j in range(pairs):
            attn_back(p.diag, range(j * per_pair, (j + 1) * per_pair))
            first = 3 * j * 128
            at = slice(j * 128, (j + 1) * 128)
            dqkv[:, first + 128 : first + 256] = dk[:, at].astype(BF16)
            dqkv[:, first + 256 : first + 384] = dv[:, at].astype(BF16)
            src = sum_w[j].src
            for b in range(width // 256):
                got = dot(n1[b * 256 : (b + 1) * 256, :], dqkv[:, first : first + 384]).astype(BF16)
                for n in range(256 // rows_w):
                    e = b * (256 // rows_w) + n
                    for m in range(3):
                        src[e % 2, e // 2, m] = got[n * rows_w : (n + 1) * rows_w, m * 128 : (m + 1) * 128]
            sum_w[j].start()
            if j == 0:
                sum_o.spread()
            if j > 0:
                sum_w[j - 1].spread()
        sum_o.reduce()
        sum_o.forward(0)
        sum_w[pairs - 1].spread()
        gather2.drain()
        red = Combine(p, xall, *g["red"][0:2], None, None, g["red"][2:4], (None, None), 1)
        for owner in range(n_seq):
            piece = dqkv[pl.ds(owner * tok, tok), :]
            xall[0, owner] = dot(piece, w_all[...], ((1,), (1,))).astype(BF16)
        red.start(0)
        d_sums = dot(jnp.ones((8, total), BF16), dqkv[...])
        for j in range(pairs):
            at = pl.ds(pl.multiple_of(p.s * cols + j * 128, 128), 128)
            first = 3 * j * 128
            vec_own[2:3, at] = d_sums[0:1, first : first + 128]
            vec_own[3:4, at] = d_sums[0:1, first + 256 : first + 384]
        sums = [sum_o] + sum_w
        ffn_pass(4, 5, 6, 7)
        red.pass_on(0)
        for n in range(1, len(sums)):
            sums[n].reduce()
            sums[n].forward(0)
            sums[n - 1].relay(0)
        red.arrived(0)
        half_tok = tok // 2
        for n in range(2):
            gout[p.s, pl.ds(n * half_tok, half_tok), :] = red.summed(0, n).astype(BF16)

        def norm_one_back(n, carry):
            at = tile_rows(n)
            g_one = gout[p.s, at, :].astype(F32)
            _, xhat, inv_std = layer_norm(tok_ref[at, :].astype(F32), gain1, 0.0)
            gin_ref[at, :] += norm_back(g_one, xhat, inv_std, gain1)
            new = (g_one * xhat, g_one)
            return tuple(old + jnp.sum(v, axis=0, keepdims=True) for old, v in zip(carry, new))

        sums1 = lax.fori_loop(0, tok // tile, norm_one_back, (zero_row,) * 2)
        store_gin = pltpu.make_async_copy(gin_ref, gin_out, local_sems.at[0])
        store_gin.start()
        for n in range(2):
            vec_own[n : n + 1, :] = sums1[n]
        vec_seq[p.s] = vec_own[...]

        def tell(other):
            return p.to_seq(vec_own, vec_seq.at[p.s], r["vs_send"].at[other], r["vs_recv"].at[p.s], other)

        def told(other):
            return p.to_seq(vec_own, vec_seq.at[other], r["vs_send"].at[other], r["vs_recv"].at[other], other)

        others = (p.near, p.far, p.diag)
        for other in others:
            tell(other).start()
        for hop in range(1, chips):
            ffn_finish(*range(4 + 4 * (hop - 1) // (chips - 1), 4 + 4 * hop // (chips - 1)))
            for one in sums:
                one.forward(hop)
                if hop > 1 or one is sums[-1]:
                    one.relay(hop - 1)
        for other in others:
            told(other).wait_recv()
        for other in others:
            tell(other).wait_send()
        vec = vec_seq[0]
        for n in range(1, n_seq):
            vec = vec + vec_seq[n]
        vec_own[...] = vec
        vec_exp[p.e] = vec

        def show(step):
            other = p.peer(step, -1)
            return p.to_exp(vec_own, vec_exp.at[p.e], r["ve_send"].at[step], r["ve_recv"].at[step], other)

        def shown(step):
            other = p.peer(step, 1)
            return p.to_exp(vec_own, vec_exp.at[other], r["ve_send"].at[step], r["ve_recv"].at[step], other)

        for step in range(1, n_exp):
            show(step).start()
        for one in sums:
            one.relay(chips - 1)
        comb_f.drain()
        out_ref = part.at[0]
        for n in range(tok // 128):
            at = slice(n * 128, (n + 1) * 128)
            rows_back = dot(pick[:, at], ret[...].reshape(n_exp * cap, width), ((0,), (0,)))
            out_ref[n * 128 // cap : (n + 1) * 128 // cap] = (
                (resid[at, :] + rows_back).astype(BF16).reshape(128 // cap, cap, width)
            )
        store_out = pltpu.make_async_copy(out_ref, out_out, local_sems.at[1])
        store_out.start()
        for hop in range(chips):
            for one in sums:
                one.arrived(hop)
        for step in range(1, n_exp):
            shown(step).wait_recv()
            show(step).wait_send()
        vec = vec_exp[0]
        for n in range(1, n_exp):
            vec = vec + vec_exp[n]
        vec_ref[...] = vec
        disp_c.drain()
        disp_n.drain(seq=False)
        for one in sums:
            one.drain()
        store_gin.wait()
        store_out.wait()

    vmem = pl.BlockSpec(memory_space=pltpu.VMEM)
    hbm = pl.BlockSpec(memory_space=pl.ANY)
    smem = pl.BlockSpec(memory_space=pltpu.SMEM)
    shape = jax.ShapeDtypeStruct
    return pl.pallas_call(
        kernel,
        out_shape=[
            shape((n_seq, cap, width), BF16),
            shape((tok, width), F32),
            shape((8, width), F32),
            shape((1, hidden), F32),
            shape((1, width), F32),
            shape((width, hidden), F32),
            shape((hidden, width), F32),
            shape((3, width, width), BF16),
            shape((width, width), BF16),
        ],
        in_specs=[vmem] * 3 + [smem] + [vmem] * 2 + [hbm] * 3 + [vmem] * 2 + [hbm] + [vmem] * 3
        + [hbm, vmem, hbm, vmem],
        out_specs=[hbm, hbm] + [vmem] * 3 + [hbm] * 4,
        scratch_shapes=scratch,
        compiler_params=pltpu.CompilerParams(
            collective_id=collective_id, has_side_effects=True, vmem_limit_bytes=VMEM_LIMIT
        ),
        name="layer",
    )(tokens, ids, cotangent, lengths, *ln1, *w_qkv, b_query, b_value, w_out, b_out, *ln2, w_up, b_up, w_down, b_down)


def finish(output, input_grad, vec, dbu, csum, dwu, dwd, gw, go):
    tok, width = output.shape
    hidden = dwu.shape[1]
    cols = width // 4
    piece = 256

    def kernel(out_in, gin_in, vec_ref, dbu_in, csum_ref, dwu_in, dwd_in, gw_in, go_in, *refs):
        (out_o, gin_o, l1g, l1b, wq_o, bq_o, wk_o, wv_o, bv_o, wo_o, bo_o, l2g, l2b, dwu_o, dbu_o, dwd_o, dbd_o) = refs[:17]
        small, wide, same_b, same_f, sems = refs[17:22]
        count = 0

        def pair(src, mid_in, mid_out, dst):
            nonlocal count
            load = pltpu.make_async_copy(src, mid_in, sems.at[count])
            store = pltpu.make_async_copy(mid_out, dst, sems.at[count + 1])
            count += 2
            return load, store

        widen, plain = [], []
        for m, (src, dst) in enumerate(
            ((gw_in.at[0], wq_o), (gw_in.at[1], wk_o), (gw_in.at[2], wv_o), (go_in, wo_o))
        ):
            for n in range(width // piece):
                rows = pl.ds(n * piece, piece)
                at = m * (width // piece) + n
                widen.append((pair(src.at[rows], small.at[at], wide.at[at], dst.at[rows]), at))
        at = 0
        for src, dst, total in ((dwu_in, dwu_o.at[0], width), (dwd_in, dwd_o.at[0], hidden), (gin_in, gin_o.at[0], tok)):
            for n in range(total // piece):
                rows = pl.ds(n * piece, piece)
                plain.append(pair(src.at[rows], same_f.at[at], same_f.at[at], dst.at[rows]))
                at += 1
        plain.append(pair(out_in, same_b, same_b, out_o.at[0]))
        order = []
        for n in range(max(len(widen), len(plain))):
            order += widen[n : n + 1] + [(c, None) for c in plain[n : n + 1]]
        for (load, _), _ in order:
            load.start()
        for n, ref in enumerate((l1g, l1b, bq_o, bv_o, bo_o, l2g, l2b)):
            ref[...] = vec_ref[n : n + 1, :].reshape(width)
        dbu_o[...] = dbu_in[...]
        first = pl.multiple_of(lax.axis_index("seq") * cols, cols)
        dbd_o[...] = csum_ref[:, pl.ds(first, cols)]
        for (load, store), at in order:
            load.wait()
            if at is not None:
                wide[at] = small[at].astype(F32)
            store.start()
        for (_, store), _ in order:
            store.wait()

    vmem = pl.BlockSpec(memory_space=pltpu.VMEM)
    hbm = pl.BlockSpec(memory_space=pl.ANY)
    shape = jax.ShapeDtypeStruct
    row, square = shape((width,), F32), shape((width, width), F32)
    n_widen = 4 * (width // piece)
    n_plain = (width + hidden + tok) // piece
    return pl.pallas_call(
        kernel,
        out_shape=[
            shape((1, tok, width), BF16), shape((1, tok, width), F32), row, row, square, row, square, square, row,
            square, row, row, row, shape((1, width, hidden), F32), shape((1, hidden), F32),
            shape((1, hidden, width), F32), shape((1, cols), F32),
        ],
        in_specs=[hbm, hbm, vmem, vmem, vmem, hbm, hbm, hbm, hbm],
        out_specs=[hbm, hbm, vmem, vmem, hbm, vmem, hbm, hbm, vmem, hbm, vmem, vmem, vmem, hbm, vmem, hbm, vmem],
        scratch_shapes=[
            pltpu.VMEM((n_widen, piece, width), BF16),
            pltpu.VMEM((n_widen, piece, width), F32),
            pltpu.VMEM((tok, width), BF16),
            pltpu.VMEM((n_plain, piece, width), F32),
            pltpu.SemaphoreType.DMA((2 * (n_widen + n_plain + 1),)),
        ],
        compiler_params=pltpu.CompilerParams(vmem_limit_bytes=VMEM_LIMIT),
        name="finish",
    )(output, input_grad, vec, dbu, csum, dwu, dwd, gw, go)


def shards(
    tokens, lengths, expert_ids, ln1_gain, ln1_bias, w_query, b_query, w_key, w_value, b_value, w_out, b_out,
    ln2_gain, ln2_bias, w_up, b_up, w_down, b_down, cotangent,
):
    output, *parts = layer(
        tokens[0], expert_ids[0, :, 0][None], cotangent[0], lengths, (ln1_gain, ln1_bias),
        (w_query, w_key, w_value), b_query, b_value, w_out, b_out, (ln2_gain, ln2_bias), w_up[0], b_up, w_down[0],
        b_down, lax.axis_size("exp"), 0,
    )
    return tuple(finish(output.reshape(tokens.shape[1:]), *parts))


def norm_layer(values_in, gain_vec, shift_vec):
    center = values_in - jnp.mean(values_in, axis=-1, keepdims=True)
    inv_std = lax.rsqrt(jnp.mean(center * center, axis=-1, keepdims=True) + EPSILON)
    return center * inv_std * gain_vec + shift_vec


def segment_ids(positions, seq_ends):
    return jnp.sum((positions[:, None] >= seq_ends[None, :]).astype(jnp.int32), axis=1)


def visible_pairs(query_pos, query_seg, key_pos, key_seg):
    return ((query_seg[:, None] == key_seg[None, :]) & (key_pos[None, :] <= query_pos[:, None]))[
        None
    ]


def project(left_op, right_op):
    return jnp.dot(left_op, right_op, preferred_element_type=jnp.float32)


def shards_any(
    tokens,
    lengths,
    expert_ids,
    ln1_gain,
    ln1_bias,
    w_query,
    b_query,
    w_key,
    w_value,
    b_value,
    w_out,
    b_out,
    ln2_gain,
    ln2_bias,
    w_up,
    b_up,
    w_down,
    b_down,
    cotangent,
):
    tok_rows = tokens.shape[1]
    width = tokens.shape[2]
    seq_size = lax.axis_size("seq")
    exp_size = lax.axis_size("exp")
    seq_rank = lax.axis_index("seq")
    seq_ends = jnp.cumsum(lengths[0])
    own_pos = seq_rank * tok_rows + jnp.arange(tok_rows, dtype=jnp.int32)
    own_seg = segment_ids(own_pos, seq_ends)
    inputs = tokens[0].astype(jnp.float32)
    gain_one = ln1_gain.astype(jnp.float32)
    bias_one = ln1_bias.astype(jnp.float32)
    gain_two = ln2_gain.astype(jnp.float32)
    bias_two = ln2_bias.astype(jnp.float32)
    normed_one_low = norm_layer(inputs, gain_one, bias_one).astype(jnp.bfloat16)
    query_low = (project(normed_one_low, w_query) + b_query.astype(jnp.float32)).astype(
        jnp.bfloat16
    )
    keys_low = project(normed_one_low, w_key).astype(jnp.bfloat16)
    values_low = (project(normed_one_low, w_value) + b_value.astype(jnp.float32)).astype(
        jnp.bfloat16
    )
    query_heads = query_low.reshape(tok_rows, HEADS, HEAD_DIM)
    initial = (
        jnp.full((HEADS, tok_rows), MASKED_SCORE, jnp.float32),
        jnp.zeros((HEADS, tok_rows), jnp.float32),
        jnp.zeros((HEADS, tok_rows, HEAD_DIM), jnp.float32),
    )
    key_piece = lax.all_gather(keys_low, "seq", axis=0, tiled=True)
    value_piece = lax.all_gather(values_low, "seq", axis=0, tiled=True)
    piece_len = key_piece.shape[0]
    fold_block_len = math.gcd(piece_len, 512)
    block_count = piece_len // fold_block_len
    key_blocks = key_piece.reshape(block_count, fold_block_len, HEADS, HEAD_DIM)
    value_blocks = value_piece.reshape(block_count, fold_block_len, HEADS, HEAD_DIM)
    offsets = jnp.arange(block_count, dtype=jnp.int32) * fold_block_len

    def block_step(state_now, packed):
        row_max, row_total, accumulated = state_now
        key_blk, value_blk, offset = packed
        key_pos = offset + jnp.arange(fold_block_len, dtype=jnp.int32)
        allowed = visible_pairs(own_pos, own_seg, key_pos, segment_ids(key_pos, seq_ends))
        scores = (
            jnp.einsum("qhd,khd->hqk", query_heads, key_blk, preferred_element_type=jnp.float32)
            * SCORE_SCALE
        )
        masked = jnp.where(allowed, scores, MASKED_SCORE)
        new_max = jnp.maximum(row_max, jnp.max(masked, axis=-1))
        weights = jnp.where(allowed, jnp.exp(masked - new_max[..., None]), 0.0)
        factor = jnp.exp(row_max - new_max)
        row_total = row_total * factor + jnp.sum(weights, axis=-1)
        accumulated = accumulated * factor[..., None] + jnp.einsum(
            "hqk,khd->hqd",
            weights.astype(jnp.bfloat16),
            value_blk,
            preferred_element_type=jnp.float32,
        )
        return ((new_max, row_total, accumulated), None)

    result, _ = lax.scan(block_step, initial, (key_blocks, value_blocks, offsets))
    row_max, row_total, accumulated = result
    attn_heads = accumulated / row_total[..., None]
    attn_low = jnp.transpose(attn_heads, (1, 0, 2)).reshape(tok_rows, width).astype(jnp.bfloat16)
    resid = inputs + project(attn_low, w_out) + b_out.astype(jnp.float32)
    normed_two_low = norm_layer(resid, gain_two, bias_two).astype(jnp.bfloat16)
    experts = exp_size * w_up.shape[0]
    capacity = 2 * tok_rows // experts
    expert_of = expert_ids[0, :, 0]
    onehot = (expert_of[:, None] == jnp.arange(experts, dtype=jnp.int32)[None, :]).astype(jnp.int32)
    slot_of = jnp.sum(onehot * (jnp.cumsum(onehot, axis=0) - onehot), axis=1)
    send_rows = (
        jnp.zeros((experts, capacity, width), jnp.bfloat16)
        .at[expert_of, slot_of]
        .set(normed_two_low)
    )
    received = lax.all_to_all(send_rows, "exp", split_axis=0, concat_axis=0, tiled=True)
    recv_count = experts * capacity
    recv_rows = received.reshape(recv_count, width)
    up_weight = w_up[0]
    up_bias = b_up[0]
    down_weight = w_down[0]
    down_bias = b_down[0].astype(jnp.float32)
    piece_width = width // seq_size
    grad_send = (
        jnp.zeros((experts, capacity, width), jnp.bfloat16).at[expert_of, slot_of].set(cotangent[0])
    )
    gathered = lax.all_gather(recv_rows, "seq", axis=0, tiled=True)
    preact = project(gathered, up_weight) + up_bias.astype(jnp.float32)
    act_low = jax.nn.gelu(preact).astype(jnp.bfloat16)
    part = act_low
    expert_out = (
        lax.psum_scatter(
            project(part, down_weight).astype(jnp.bfloat16), "seq", scatter_dimension=0, tiled=True
        ).astype(jnp.float32)
        + down_bias
    )
    returned = lax.all_to_all(
        expert_out.astype(jnp.bfloat16).reshape(experts, capacity, width),
        "exp",
        split_axis=0,
        concat_axis=0,
        tiled=True,
    )
    grad_recv = lax.all_to_all(grad_send, "exp", split_axis=0, concat_axis=0, tiled=True).reshape(
        recv_count, width
    )
    grad_all = lax.all_gather(grad_recv, "seq", axis=0, tiled=True)
    bias_full = jnp.sum(grad_all.astype(jnp.float32), axis=0)
    grad_b_down = lax.dynamic_slice_in_dim(bias_full, seq_rank * piece_width, piece_width, 0)
    grad_act = jnp.einsum("rd,fd->rf", grad_all, down_weight, preferred_element_type=jnp.float32)
    grad_pre = jax.vjp(jax.nn.gelu, preact)[1](grad_act)[0].astype(jnp.bfloat16)
    grad_w_down = jnp.einsum("rf,rd->fd", act_low, grad_all, preferred_element_type=jnp.float32)
    grad_w_up = jnp.einsum("rd,rf->df", gathered, grad_pre, preferred_element_type=jnp.float32)
    grad_b_up = jnp.sum(grad_pre.astype(jnp.float32), axis=0)
    part = grad_pre
    grad_home = lax.psum_scatter(
        jnp.einsum("rf,df->rd", part, up_weight, preferred_element_type=jnp.float32).astype(
            jnp.bfloat16
        ),
        "seq",
        scatter_dimension=0,
        tiled=True,
    )
    ffn_rows = returned[expert_of, slot_of].astype(jnp.float32)
    output = (resid + ffn_rows).astype(jnp.bfloat16)
    grad_back = lax.all_to_all(
        grad_home.reshape(experts, capacity, width), "exp", split_axis=0, concat_axis=0, tiled=True
    )
    grad_normed_two = grad_back[expert_of, slot_of].astype(jnp.float32)
    _, norm_two_back = jax.vjp(norm_layer, resid, gain_two, bias_two)
    grad_resid_norm, grad_gain_two, grad_bias_two = norm_two_back(grad_normed_two)
    grad_resid = cotangent[0].astype(jnp.float32) + grad_resid_norm
    grad_out_low = grad_resid.astype(jnp.bfloat16)
    grad_w_out = jnp.einsum("qa,qd->ad", attn_low, grad_out_low, preferred_element_type=jnp.float32)
    grad_b_out = jnp.sum(grad_out_low.astype(jnp.float32), axis=0)
    grad_attn_low = jnp.einsum(
        "qd,ad->qa", grad_out_low, w_out, preferred_element_type=jnp.float32
    ).astype(jnp.bfloat16)
    grad_attn_heads = grad_attn_low.reshape(tok_rows, HEADS, HEAD_DIM)
    delta = jnp.sum(
        jnp.transpose(grad_attn_heads.astype(jnp.float32), (1, 0, 2)) * attn_heads, axis=-1
    )
    whole_keys, whole_values = (
        lax.all_gather(keys_low, "seq", axis=0, tiled=True),
        lax.all_gather(values_low, "seq", axis=0, tiled=True),
    )
    group_len = whole_keys.shape[0]
    block_len = math.gcd(group_len, 512)
    block_count = group_len // block_len

    def back_step(grad_query, packed):
        key_blk, value_blk, offset = packed
        key_pos = offset + jnp.arange(block_len, dtype=jnp.int32)
        allowed = visible_pairs(own_pos, own_seg, key_pos, segment_ids(key_pos, seq_ends))
        scores = (
            jnp.einsum("qhd,khd->hqk", query_heads, key_blk, preferred_element_type=jnp.float32)
            * SCORE_SCALE
        )
        masked = jnp.where(allowed, scores, MASKED_SCORE)
        probabilities = (
            jnp.where(allowed, jnp.exp(masked - row_max[..., None]), 0.0) / row_total[..., None]
        )
        probs_low = probabilities.astype(jnp.bfloat16)
        grad_probs = jnp.einsum(
            "qhd,khd->hqk", grad_attn_heads, value_blk, preferred_element_type=jnp.float32
        )
        grad_scores = (probabilities * (grad_probs - delta[..., None])).astype(jnp.bfloat16)
        grad_query = (
            grad_query
            + jnp.einsum("hqk,khd->qhd", grad_scores, key_blk, preferred_element_type=jnp.float32)
            * SCORE_SCALE
        )
        grad_key_blk = (
            jnp.einsum("hqk,qhd->khd", grad_scores, query_heads, preferred_element_type=jnp.float32)
            * SCORE_SCALE
        )
        grad_value_blk = jnp.einsum(
            "hqk,qhd->khd", probs_low, grad_attn_heads, preferred_element_type=jnp.float32
        )
        return (grad_query, (grad_key_blk, grad_value_blk))

    block_offsets = jnp.arange(block_count, dtype=jnp.int32) * block_len
    grad_query, key_value_parts = lax.scan(
        back_step,
        jnp.zeros((tok_rows, HEADS, HEAD_DIM), jnp.float32),
        (
            whole_keys.reshape(block_count, block_len, HEADS, HEAD_DIM),
            whole_values.reshape(block_count, block_len, HEADS, HEAD_DIM),
            block_offsets,
        ),
    )
    grad_keys, grad_values = (
        lax.psum_scatter(
            key_value_parts[0].reshape(group_len, width).astype(jnp.bfloat16),
            "seq",
            scatter_dimension=0,
            tiled=True,
        ).astype(jnp.float32),
        lax.psum_scatter(
            key_value_parts[1].reshape(group_len, width).astype(jnp.bfloat16),
            "seq",
            scatter_dimension=0,
            tiled=True,
        ).astype(jnp.float32),
    )
    grad_query_low = grad_query.reshape(tok_rows, width).astype(jnp.bfloat16)
    grad_keys_low = grad_keys.astype(jnp.bfloat16)
    grad_values_low = grad_values.astype(jnp.bfloat16)
    grad_w_query = jnp.einsum(
        "qa,qd->ad", normed_one_low, grad_query_low, preferred_element_type=jnp.float32
    )
    grad_b_query = jnp.sum(grad_query_low.astype(jnp.float32), axis=0)
    grad_w_key = jnp.einsum(
        "qa,qd->ad", normed_one_low, grad_keys_low, preferred_element_type=jnp.float32
    )
    grad_w_value = jnp.einsum(
        "qa,qd->ad", normed_one_low, grad_values_low, preferred_element_type=jnp.float32
    )
    grad_b_value = jnp.sum(grad_values_low.astype(jnp.float32), axis=0)
    grad_normed_one = (
        (
            jnp.einsum("qd,ad->qa", grad_query_low, w_query, preferred_element_type=jnp.float32)
            + jnp.einsum("qd,ad->qa", grad_keys_low, w_key, preferred_element_type=jnp.float32)
            + jnp.einsum("qd,ad->qa", grad_values_low, w_value, preferred_element_type=jnp.float32)
        )
        .astype(jnp.bfloat16)
        .astype(jnp.float32)
    )
    _, norm_one_back = jax.vjp(norm_layer, inputs, gain_one, bias_one)
    grad_in_norm, grad_gain_one, grad_bias_one = norm_one_back(grad_normed_one)
    input_grad = grad_resid + grad_in_norm
    summed = lax.psum(
        (
            grad_gain_one,
            grad_bias_one,
            grad_w_query,
            grad_b_query,
            grad_w_key,
            grad_w_value,
            grad_b_value,
            grad_w_out,
            grad_b_out,
            grad_gain_two,
            grad_bias_two,
        ),
        ("seq", "exp"),
    )
    return (
        output[None],
        input_grad[None],
        summed[0],
        summed[1],
        summed[2],
        summed[3],
        summed[4],
        summed[5],
        summed[6],
        summed[7],
        summed[8],
        summed[9],
        summed[10],
        grad_w_up[None],
        grad_b_up[None],
        grad_w_down[None],
        grad_b_down[None],
    )


def solution(mesh):
    placed = (
        P("exp", "seq", None),
        P("exp", None),
        P("exp", "seq", None),
        P(),
        P(),
        P(),
        P(),
        P(),
        P(),
        P(),
        P(),
        P(),
        P(),
        P(),
        P("exp", None, "seq"),
        P("exp", "seq"),
        P("exp", "seq", None),
        P("exp", None),
        P("exp", "seq", None),
    )
    plane = mesh.shape["seq"] == 4 and mesh.shape["exp"] == 8
    return jax.shard_map(
        shards if plane else shards_any,
        mesh=mesh,
        in_specs=placed,
        out_specs=(
            P("exp", "seq", None),
            P("exp", "seq", None),
            P(),
            P(),
            P(),
            P(),
            P(),
            P(),
            P(),
            P(),
            P(),
            P(),
            P(),
            P("exp", None, "seq"),
            P("exp", "seq"),
            P("exp", "seq", None),
            P("exp", "seq"),
        ),
        check_vma=False,
    )
```

```python
import functools
import math

import jax
import jax.numpy as jnp
from jax import lax
from jax.experimental import pallas as pl
from jax.experimental.pallas import tpu as pltpu
from jax.sharding import PartitionSpec as P

MESH = pl.DeviceIdType.MESH
F32 = jnp.float32
BF16 = jnp.bfloat16
VMEM_LIMIT = 63 * 2**20


def dot(a, b, dims=((1,), (0,))):
    return lax.dot_general(a, b, (dims, ((), ())), preferred_element_type=F32)


class Place:
    def __init__(self, n_exp):
        self.n_exp = n_exp
        self.s = lax.axis_index("seq")
        self.e = lax.axis_index("exp")
        low = lax.rem(self.s, 2)
        high = lax.div(self.s, 2)
        self.near = high * 2 + (1 - low)
        self.far = (1 - high) * 2 + low
        self.diag = (1 - high) * 2 + (1 - low)
        self.core = lax.rem(self.e, 2)
        self.chip = lax.div(self.e, 2)

    def peer(self, step, way):
        chips = self.n_exp // 2
        hop = lax.div(step, 2)
        if chips == 4:
            hop = hop + lax.div(hop, 2) * (5 - 2 * hop)
        chip = lax.rem(self.chip + way * hop + chips, chips)
        return chip * 2 + lax.rem(self.core + step, 2)

    def greet(self, diag=False):
        barrier = pltpu.get_barrier_semaphore()
        others = (self.near, self.far, self.diag) if diag else (self.near, self.far)
        for other in others:
            pl.semaphore_signal(barrier, inc=1, device_id=(other, self.e), device_id_type=MESH)

        def tell(step, carry):
            pl.semaphore_signal(
                barrier, inc=1, device_id=(self.s, self.peer(step, 1)), device_id_type=MESH
            )
            return carry

        lax.fori_loop(1, self.n_exp, tell, 0)
        pl.semaphore_wait(barrier, len(others) + self.n_exp - 1)

    def to_seq(self, src, dst, send_sem, recv_sem, other):
        return pltpu.make_async_remote_copy(
            src_ref=src, dst_ref=dst, send_sem=send_sem, recv_sem=recv_sem,
            device_id=(other, self.e), device_id_type=MESH,
        )

    def to_exp(self, src, dst, send_sem, recv_sem, other):
        return pltpu.make_async_remote_copy(
            src_ref=src, dst_ref=dst, send_sem=send_sem, recv_sem=recv_sem,
            device_id=(self.s, other), device_id_type=MESH,
        )


class Dispatch:
    def __init__(self, place, send, held, exp_sems, seq_sems):
        self.place, self.send, self.held = place, send, held
        self.exp_send, self.exp_recv = exp_sems
        self.seq_send, self.seq_recv = seq_sems
        self.cap = send.shape[1]

    @staticmethod
    def scratch(n_exp):
        return [
            pltpu.SemaphoreType.DMA((n_exp,)),
            pltpu.SemaphoreType.DMA((n_exp,)),
            pltpu.SemaphoreType.DMA((n_exp, 6)),
            pltpu.SemaphoreType.DMA((n_exp, 6)),
        ]

    def _exp(self, step):
        p = self.place
        other = p.peer(step, -1)
        return p.to_exp(
            self.send.at[other], self.held.at[step, p.s], self.exp_send.at[step], self.exp_recv.at[step], other
        )

    def _seq(self, step, owner, half, lane, other):
        p = self.place
        rows = pl.ds(half * (self.cap // 2), self.cap // 2)
        part = self.held.at[step, owner, rows]
        return p.to_seq(part, part, self.seq_send.at[step, lane], self.seq_recv.at[step, lane], other)

    def copies(self, step, lanes=range(6)):
        p = self.place
        spec = (
            (p.s, 0, p.near),
            (p.s, 1, p.far),
            (p.s, 1, p.near),
            (p.s, 0, p.far),
            (p.near, 0, p.far),
            (p.far, 1, p.near),
        )
        return [self._seq(step, spec[n][0], spec[n][1], n, spec[n][2]) for n in lanes]

    def start_exp(self, step):
        self._exp(step).start()

    def own(self):
        p = self.place
        self.held[0, p.s] = self.send[p.e]

    def start_seq(self, step):
        @pl.when(step > 0)
        def _():
            self._exp(step).wait_recv()

        for c in self.copies(step, range(4)):
            c.start()

    def relay(self, step):
        for c, out in zip(self.copies(step, (0, 1)), self.copies(step, (4, 5))):
            c.wait_recv()
            out.start()

    def arrived(self, step):
        for c in self.copies(step, range(2, 6)):
            c.wait_recv()

    def sent(self, step):
        for c in self.copies(step):
            c.wait_send()

    def drain(self, seq=True):
        def body(step, carry):
            if seq:
                self.sent(step)

            @pl.when(step > 0)
            def _():
                self._exp(step).wait_send()

            return carry

        lax.fori_loop(0, self.place.n_exp, body, 0)


class Combine:
    def __init__(self, place, part, passing, landing, total, back, seq_sems, exp_sems, slots):
        self.place, self.part, self.passing, self.landing = place, part, passing, landing
        self.total, self.back, self.slots = total, back, slots
        self.seq_send, self.seq_recv = seq_sems
        self.exp_send, self.exp_recv = exp_sems
        self.half = part.shape[2] // 2

    @staticmethod
    def scratch(n_exp, cap, width):
        return [
            pltpu.VMEM((n_exp, 2, cap // 2, width), BF16),
            pltpu.VMEM((n_exp, 4, cap // 2, width), BF16),
            pltpu.VMEM((n_exp, cap, width), BF16),
            pltpu.SemaphoreType.DMA((n_exp, 6)),
            pltpu.SemaphoreType.DMA((n_exp, 6)),
            pltpu.SemaphoreType.DMA((n_exp,)),
            pltpu.SemaphoreType.DMA((n_exp,)),
        ]

    def _slot(self, step):
        return lax.rem(step, self.slots)

    def _piece(self, step, owner, half):
        return self.part.at[self._slot(step), owner, pl.ds(half * self.half, self.half)]

    def _seq(self, src, dst, step, lane, other):
        return self.place.to_seq(
            src, dst, self.seq_send.at[step, lane], self.seq_recv.at[step, lane], other
        )

    def copies(self, step, lanes=range(6)):
        p = self.place
        spec = (
            (p.diag, 0, self.passing, 0, p.near),
            (p.diag, 1, self.passing, 1, p.far),
            (p.near, 0, self.landing, 0, p.near),
            (p.far, 1, self.landing, 3, p.far),
            (p.far, 0, self.landing, 2, p.far),
            (p.near, 1, self.landing, 1, p.near),
        )
        made = []
        for n in lanes:
            owner, half, buffer, at, other = spec[n]
            made.append(self._seq(self._piece(step, owner, half), buffer.at[step, at], step, n, other))
        return made

    def start(self, step):
        for c in self.copies(step, range(4)):
            c.start()

    def pass_on(self, step):
        p = self.place
        slot = self._slot(step)
        came, out = self.copies(step, (0, 1)), self.copies(step, (4, 5))
        for n, owner in enumerate((p.far, p.near)):
            rows = pl.ds(n * self.half, self.half)
            came[n].wait_recv()
            self.part[slot, owner, rows] = (
                self.part[slot, owner, rows].astype(F32) + self.passing[step, n].astype(F32)
            ).astype(BF16)
            out[n].start()

    def _whole(self, step):
        if self.total is None:
            return self.part.at[self._slot(step), self.place.s]
        return self.total.at[step]

    def _exp(self, step):
        p = self.place
        other = p.peer(step, 1)
        return p.to_exp(
            self._whole(step), self.back.at[p.e], self.exp_send.at[step], self.exp_recv.at[step], other
        )

    def arrived(self, step):
        copies = self.copies(step)
        for c in copies[2:]:
            c.wait_recv()
        for c in copies:
            c.wait_send()

    def summed(self, step, half):
        rows = pl.ds(half * self.half, self.half)
        return (
            self.part[self._slot(step), self.place.s, rows].astype(F32)
            + self.landing[step, half].astype(F32)
            + self.landing[step, 2 + half].astype(F32)
        )

    def finish(self, step, bias=None):
        p = self.place
        self.arrived(step)
        for half in range(2):
            value = self.summed(step, half)
            if bias is not None:
                value = value + bias
            rows = pl.ds(half * self.half, self.half)
            if self.total is None:
                self.part[self._slot(step), p.s, rows] = value.astype(BF16)
            else:
                self.total[step, rows] = value.astype(BF16)

        @pl.when(step > 0)
        def _():
            self._exp(step).start()

        @pl.when(step == 0)
        def _():
            self.back[p.e] = self._whole(0)[...]

    def drain(self):
        p = self.place

        def body(step, carry):
            c = self._exp(step)
            c.wait_send()
            c.wait_recv()
            return carry

        lax.fori_loop(1, p.n_exp, body, 0)


GELU_A = math.sqrt(2.0 / math.pi)
GELU_B = 0.044715


EPSILON = 1e-05
SCORE_SCALE = 0.125
MASKED_SCORE = -1e30
HEAD_DIM = 64
HEADS = 16


class Gather:
    def __init__(self, place, held, send_sems, recv_sems):
        self.place, self.held = place, held
        self.send_sems, self.recv_sems = send_sems, recv_sems
        self.half = held.shape[1] // 2

    @staticmethod
    def scratch():
        return [pltpu.SemaphoreType.DMA((6,)), pltpu.SemaphoreType.DMA((6,))]

    def copies(self, lanes=range(6)):
        p = self.place
        spec = (
            (p.s, 0, p.near),
            (p.s, 1, p.far),
            (p.s, 1, p.near),
            (p.s, 0, p.far),
            (p.near, 0, p.far),
            (p.far, 1, p.near),
        )
        made = []
        for n in lanes:
            owner, half, other = spec[n]
            part = self.held.at[owner, pl.ds(half * self.half, self.half)]
            made.append(p.to_seq(part, part, self.send_sems.at[n], self.recv_sems.at[n], other))
        return made

    def start(self):
        for c in self.copies(range(4)):
            c.start()

    def relay(self):
        for c, out in zip(self.copies((0, 1)), self.copies((4, 5))):
            c.wait_recv()
            out.start()

    def wait(self, lanes):
        for c in self.copies(lanes):
            c.wait_recv()

    def drain(self):
        for c in self.copies():
            c.wait_send()


def layer_norm(values, gain, shift):
    center = values - jnp.mean(values, axis=-1, keepdims=True)
    inv_std = lax.rsqrt(jnp.mean(center * center, axis=-1, keepdims=True) + EPSILON)
    xhat = center * inv_std
    return xhat * gain + shift, xhat, inv_std


def norm_back(grad, xhat, inv_std, gain):
    d = grad * gain
    return (
        d - jnp.mean(d, axis=-1, keepdims=True) - xhat * jnp.mean(d * xhat, axis=-1, keepdims=True)
    ) * inv_std


def row_choice(ids, n_exp, cap):
    tokens = ids.shape[1]
    named = (ids == lax.broadcasted_iota(jnp.int32, (128, tokens), 0)).astype(BF16)
    before = (
        lax.broadcasted_iota(jnp.int32, (tokens, tokens), 0)
        < lax.broadcasted_iota(jnp.int32, (tokens, tokens), 1)
    ).astype(BF16)
    earlier = dot(named, before) * named.astype(F32)
    slot = jnp.sum(earlier, axis=0, keepdims=True).astype(jnp.int32) + ids * cap
    return (slot == lax.broadcasted_iota(jnp.int32, (n_exp * cap, tokens), 0)).astype(BF16)


def segment_of(position, lengths):
    end = jnp.int32(0)
    count = jnp.zeros_like(position)
    for n in range(lengths.shape[1]):
        end = end + lengths[0, n]
        count = count + (position >= end).astype(jnp.int32)
    return count


def head_mask(rows, width, head):
    lane = lax.broadcasted_iota(jnp.int32, (rows, width), 1)
    return (lane >= head * HEAD_DIM) & (lane < (head + 1) * HEAD_DIM)


class SumAll:
    def __init__(self, place, src, core_in, mine, chip_in, res, where, local_sem, sems):
        self.place, self.src, self.core_in, self.mine = place, src, core_in, mine
        self.chip_in, self.res, self.where, self.local_sem = chip_in, res, where, local_sem
        (self.core_sems, self.rs_send, self.rs_recv, self.ag_send, self.ag_recv,
         self.seq_send, self.seq_recv, self.pair_send, self.pair_recv) = sems
        self.chips = place.n_exp // 2
        p = place
        self.sibling = p.chip * 2 + (1 - p.core)

    @staticmethod
    def scratch(n_exp, *piece):
        chips = n_exp // 2
        dma = pltpu.SemaphoreType.DMA
        return [
            pltpu.VMEM((2, chips, *piece), BF16),
            pltpu.VMEM((chips, *piece), BF16),
            pltpu.VMEM((chips, *piece), BF16),
            pltpu.VMEM((chips, *piece), BF16),
            pltpu.VMEM(piece, BF16),
            dma((1,)),
            dma((2,)),
            dma((chips,)),
            dma((chips,)),
            dma((chips,)),
            dma((chips,)),
            dma((chips, 6)),
            dma((chips, 6)),
            dma((chips, 4)),
            dma((chips, 4)),
        ]

    def chip(self, hop):
        return lax.rem(self.place.chip + hop, self.chips)

    def exp(self, hop):
        return self.chip(hop) * 2 + self.place.core

    def _core(self):
        p = self.place
        return p.to_exp(
            self.src.at[1 - p.core], self.core_in, self.core_sems.at[0], self.core_sems.at[1], self.sibling
        )

    def start(self):
        self._core().start()

    def _spread(self, hop):
        p = self.place
        to = self.chip(hop)
        return p.to_exp(
            self.mine.at[to], self.chip_in.at[p.chip], self.rs_send.at[to], self.rs_recv.at[p.chip], self.exp(hop)
        )

    def _spread_from(self, hop):
        p = self.place
        at = self.chip(hop)
        return p.to_exp(
            self.mine.at[at], self.chip_in.at[at], self.rs_send.at[at], self.rs_recv.at[at], self.exp(hop)
        )

    def spread(self):
        p = self.place
        self._core().wait_recv()
        for n in range(self.chips):
            self.mine[n] = (self.src[p.core, n].astype(F32) + self.core_in[n].astype(F32)).astype(BF16)
        for hop in range(1, self.chips):
            self._spread(hop).start()

    def _local(self):
        p = self.place
        return pltpu.make_async_copy(self.res, self.where(p.s, p.e), self.local_sem.at[0])

    def _share(self, hop):
        p = self.place
        to = self.chip(hop)
        return p.to_exp(
            self.res, self.where(p.s, p.e), self.ag_send.at[to], self.ag_recv.at[p.chip], self.exp(hop)
        )

    def _share_from(self, hop):
        p = self.place
        at = self.chip(hop)
        return p.to_exp(
            self.res, self.where(p.s, self.exp(hop)), self.ag_send.at[at], self.ag_recv.at[at], self.exp(hop)
        )

    def copies(self, hop, lanes=range(6)):
        p = self.place
        spec = (
            (p.s, 0, p.near),
            (p.s, 1, p.far),
            (p.s, 1, p.near),
            (p.s, 0, p.far),
            (p.near, 0, p.far),
            (p.far, 1, p.near),
        )
        made = []
        for n in lanes:
            owner, half, other = spec[n]
            part = self.where(owner, self.exp(hop), half)
            made.append(p.to_seq(part, part, self.seq_send.at[hop, n], self.seq_recv.at[hop, n], other))
        return made

    def _pair(self, hop, n):
        p = self.place
        part = self.where((p.s, p.near, p.far, p.diag)[n], self.exp(hop))
        return p.to_exp(part, part, self.pair_send.at[hop, n], self.pair_recv.at[hop, n], self.sibling)

    def _pair_from(self, hop, n):
        p = self.place
        owner = (p.s, p.near, p.far, p.diag)[n]
        part = self.where(owner, self.chip(hop) * 2 + (1 - p.core))
        return p.to_exp(part, part, self.pair_send.at[hop, n], self.pair_recv.at[hop, n], self.sibling)

    def reduce(self):
        p = self.place
        for hop in range(1, self.chips):
            self._spread_from(hop).wait_recv()
        total = self.mine[p.chip].astype(F32)
        for hop in range(1, self.chips):
            total = total + self.chip_in[self.chip(hop)].astype(F32)
        self.res[...] = total.astype(BF16)
        self._local().start()
        for hop in range(1, self.chips):
            self._share(hop).start()
        self._local().wait()

    def forward(self, hop):
        if hop > 0:
            self._share_from(hop).wait_recv()
        for c in self.copies(hop, range(4)):
            c.start()
        self._pair(hop, 0).start()

    def relay(self, hop):
        for c, out in zip(self.copies(hop, (0, 1)), self.copies(hop, (4, 5))):
            c.wait_recv()
            out.start()

    def arrived(self, hop):
        for c in self.copies(hop, (2, 3)):
            c.wait_recv()
        self._pair(hop, 1).start()
        self._pair(hop, 2).start()
        for c in self.copies(hop, (4, 5)):
            c.wait_recv()
        self._pair(hop, 3).start()

    def drain(self):
        self._core().wait_send()
        for hop in range(1, self.chips):
            self._spread(hop).wait_send()
            self._share(hop).wait_send()
        for hop in range(self.chips):
            for c in self.copies(hop):
                c.wait_send()
            for n in range(4):
                self._pair(hop, n).wait_send()
                self._pair_from(hop, n).wait_recv()


def layer(
    tokens, ids, cotangent, lengths, ln1, w_qkv, b_query, b_value, w_out, b_out, ln2, w_up, b_up, w_down, b_down,
    n_exp, collective_id,
):
    tok, width = tokens.shape
    hidden = w_up.shape[1]
    n_seq = 4
    total = n_seq * tok
    cols = width // n_seq
    heads = cols // HEAD_DIM
    cap = 2 * tok // n_exp
    q_block = 256
    chips = n_exp // 2
    rows_w, rows_o = width // n_exp, cols // n_exp
    pairs = cols // 128
    per_pair = 128 // HEAD_DIM
    routed = n_seq * cap
    block = min(256, hidden)
    slots = 2
    ahead = 5

    vm = pltpu.VMEM
    dma = pltpu.SemaphoreType.DMA
    table = dict(
        xall=vm((1, n_seq, tok, width), BF16),
        n1=vm((width, total), BF16),
        q=vm((total, cols), BF16),
        k=vm((total, cols), BF16),
        v=vm((total, cols), BF16),
        attn=vm((total, cols), F32),
        lse=vm((8, total), F32),
        resid=vm((tok, width), F32),
        pick=vm((n_exp * cap, tok), BF16),
        w_all=vm((width, 3 * cols), BF16),
        w_o=vm((width, width), BF16),
        send_c=vm((n_exp, cap, width), BF16),
        send_n=vm((n_exp, cap, width), BF16),
        back=vm((n_exp, cap, width), BF16),
        ret=vm((n_exp, cap, width), BF16),
        attn_out=vm((n_seq, tok, cols), BF16),
        attn_in=vm((n_seq, tok, cols), BF16),
        cot=vm((n_exp, n_seq, cap, width), BF16),
        held=vm((n_exp, n_seq, cap, width), BF16),
        wu=vm((width, hidden), BF16),
        wd=vm((hidden, width), BF16),
        part=vm((slots, n_seq, cap, width), BF16),
        dwu=vm((width, hidden), F32),
        dwd=vm((hidden, width), F32),
        dqkv=vm((total, 3 * cols), BF16),
        vec_own=vm((8, width), F32),
        vec_seq=vm((n_seq, 8, width), F32),
        vec_exp=vm((n_exp, 8, width), F32),
        local_sems=dma((8,)),
        load_sems=dma((3 * pairs,)),
        dq=vm((tok, cols), F32),
        a2a_send=dma((n_seq,)),
        a2a_recv=dma((n_seq,)),
        vs_send=dma((n_seq,)),
        vs_recv=dma((n_seq,)),
        ve_send=dma((n_exp,)),
        ve_recv=dma((n_exp,)),
    )
    groups = dict(
        gather1=Gather.scratch(),
        gather2=Gather.scratch(),
        disp_c=Dispatch.scratch(n_exp),
        disp_n=Dispatch.scratch(n_exp),
        comb_g=Combine.scratch(n_exp, cap, width),
        comb_f=Combine.scratch(n_exp, cap, width)[:2] + Combine.scratch(n_exp, cap, width)[3:],
        red=[
            vm((1, 2, tok // 2, width), BF16),
            vm((1, 4, tok // 2, width), BF16),
            dma((1, 6)),
            dma((1, 6)),
        ],
        sum_o=SumAll.scratch(n_exp, rows_o, width),
        **{f"sum_{j}": SumAll.scratch(n_exp, 3, rows_w, 128) for j in range(pairs)},
    )
    scratch = list(table.values()) + [ref for group in groups.values() for ref in group]

    def kernel(tok_ref, ids_ref, cot_ref, len_ref, g1_ref, c1_ref, wq_in, wk_in, wv_in, bq_ref, bv_ref, wo_in, bo_ref,
               g2_ref, c2_ref, wu_in, bu_ref, wd_in, bd_ref,
               out_out, gin_out, vec_ref, dbu_ref, csum_ref, dwu_out, dwd_out, gw_out, go_out, *refs):
        r = dict(zip(table, refs))
        at = len(table)
        g = {}
        for name, group in groups.items():
            g[name] = refs[at : at + len(group)]
            at += len(group)
        xall, n1, q_all, k_all, v_all = r["xall"], r["n1"], r["q"], r["k"], r["v"]
        attn, lse_all, resid, pick = r["attn"], r["lse"], r["resid"], r["pick"]
        w_all, w_o, wu, wd = r["w_all"], r["w_o"], r["wu"], r["wd"]
        send_c, send_n, back, ret = r["send_c"], r["send_n"], r["back"], r["ret"]
        attn_out, attn_in, cot, held, part = r["attn_out"], r["attn_in"], r["cot"], r["held"], r["part"]
        dwu, dwd, dqkv = r["dwu"], r["dwd"], r["dqkv"]
        gattn = attn_out
        gin_ref = dwd.at[0:tok, :]
        dk, dv = dwu.at[0:total, 0:cols], dwu.at[0:total, cols : 2 * cols]
        vec_own, vec_seq, vec_exp = r["vec_own"], r["vec_seq"], r["vec_exp"]
        local_sems, load_sems, dq = r["local_sems"], r["load_sems"], r["dq"]

        p = Place(n_exp)
        mine = pl.ds(pl.multiple_of(p.s * cols, cols), cols)

        tile = 32

        def tile_rows(n):
            return pl.ds(pl.multiple_of(n * tile, tile), tile)

        def row_of(ref):
            return ref[...].astype(F32).reshape(1, ref.shape[-1])

        loads = [
            pltpu.make_async_copy(
                src.at[:, pl.ds(pl.multiple_of(p.s * cols + j * 128, 128), 128)],
                w_all.at[:, pl.ds((3 * j + m) * 128, 128)],
                load_sems.at[3 * j + m],
            )
            for m, src in enumerate((wq_in, wk_in, wv_in))
            for j in range(pairs)
        ]
        load_o = pltpu.make_async_copy(wo_in, w_o, local_sems.at[3])
        load_ffn = [
            pltpu.make_async_copy(wu_in, wu, local_sems.at[4]),
            pltpu.make_async_copy(wd_in, wd, local_sems.at[5]),
        ]
        for c in loads + [load_o] + load_ffn:
            c.start()

        xall[0, p.s] = tok_ref[...]
        p.greet(diag=True)
        gather1 = Gather(p, xall.at[0], *g["gather1"])
        gather1.start()
        pick[...] = row_choice(ids_ref[...], n_exp, cap)

        def lay_out(send, rows_ref):
            for e in range(0, n_exp, 2):
                laid = dot(pick[e * cap : (e + 2) * cap, :], rows_ref[...])
                send[e : e + 2] = laid.astype(BF16).reshape(2, cap, width)

        lay_out(send_c, cot_ref)
        disp_c = Dispatch(p, send_c, cot, g["disp_c"][0:2], g["disp_c"][2:4])
        for step in range(1, n_exp):
            disp_c.start_exp(step)
        disp_c.own()
        gain1, bias1 = row_of(g1_ref), row_of(c1_ref)
        gain2, bias2 = row_of(g2_ref), row_of(c2_ref)
        bq = bq_ref[mine].astype(F32).reshape(1, cols)
        bv = bv_ref[mine].astype(F32).reshape(1, cols)

        def project(owner):
            rows = pl.ds(pl.multiple_of(owner * tok, tok), tok)

            def norm_tile(n, carry):
                x = xall[0, owner, tile_rows(n), :].astype(F32)
                per = cap // tile
                rows = pl.ds(pl.multiple_of(lax.rem(n, per) * tile, tile), tile)
                part[0, lax.div(n, per), rows, :] = layer_norm(x, gain1, bias1)[0].astype(BF16)
                return carry

            lax.fori_loop(0, tok // tile, norm_tile, 0)
            normed = part[0].reshape(tok, width)
            n1[:, rows] = jnp.transpose(normed)
            out = dot(normed, w_all[...])
            for j in range(pairs):
                at, first = slice(j * 128, (j + 1) * 128), 3 * j * 128
                q = (out[:, first : first + 128] + bq[:, at]).astype(BF16)
                q_all[rows, at] = (q.astype(F32) * SCORE_SCALE).astype(BF16)
                k_all[rows, at] = out[:, first + 128 : first + 256].astype(BF16)
                v_all[rows, at] = (out[:, first + 256 : first + 384] + bv[:, at]).astype(BF16)

        for c in loads:
            c.wait()
        project(p.s)
        gather1.relay()
        gather1.wait((2, 3))
        project(p.near)
        project(p.far)
        gather1.wait((4, 5))
        disp_c.start_seq(0)
        disp_c.start_seq(1)
        project(p.diag)

        def a2a(owner):
            return p.to_seq(
                attn_out.at[owner], attn_in.at[p.s], r["a2a_send"].at[owner], r["a2a_recv"].at[p.s], owner
            )

        def a2a_from(owner):
            return p.to_seq(
                attn_out.at[owner], attn_in.at[owner], r["a2a_send"].at[owner], r["a2a_recv"].at[owner], owner
            )

        blocks = total // q_block
        for n in reversed(range(blocks)):
            seen = (n + 1) * q_block
            rows = pl.ds(n * q_block, q_block)
            q_pos = lax.broadcasted_iota(jnp.int32, (q_block, 1), 0) + n * q_block
            k_pos = lax.broadcasted_iota(jnp.int32, (1, seen), 1)
            allowed = (segment_of(q_pos, len_ref) == segment_of(k_pos, len_ref)) & (k_pos <= q_pos)
            q_rows = q_all[rows, :]
            acc = jnp.zeros((q_block, cols), F32)
            lse = jnp.zeros((q_block, 128), F32)
            lane = lax.broadcasted_iota(jnp.int32, (q_block, 128), 1)
            for head in range(heads):
                own = head_mask(q_block, cols, head)
                scores = dot(jnp.where(own, q_rows, jnp.zeros_like(q_rows)), k_all[0:seen, :], ((1,), (1,)))
                scores = jnp.where(allowed, scores, MASKED_SCORE)
                top = jnp.max(scores, axis=1, keepdims=True)
                weights = jnp.exp(scores - top)
                sums = jnp.sum(weights, axis=1, keepdims=True)
                out = dot(weights.astype(BF16), v_all[0:seen, :]) / sums
                acc = jnp.where(own, out, acc)
                lse = jnp.where(lane == head, top + jnp.log(sums), lse)
            attn[rows, :] = acc
            lse_all[:, rows] = jnp.transpose(lse)[0:8, :]
            owner, first = (n * q_block) // tok, (n * q_block) % tok
            attn_out[owner, pl.ds(first, q_block)] = acc.astype(BF16)
            if first == 0:

                @pl.when(p.s != owner)
                def _(owner=owner):
                    a2a(owner).start()

                @pl.when(p.s == owner)
                def _(owner=owner):
                    attn_in[owner] = attn_out[owner]

        disp_c.start_seq(2)
        disp_c.relay(0)
        disp_c.relay(1)
        load_o.wait()
        sums = tok_ref[...].astype(F32) + row_of(bo_ref)
        for owner in range(n_seq):

            @pl.when(p.s != owner)
            def _(owner=owner):
                a2a_from(owner).wait_recv()

            sums = sums + dot(attn_in[owner], w_o[pl.ds(owner * cols, cols), :])
        resid[...] = sums
        disp_c.start_seq(3)
        disp_c.relay(2)

        gather1.drain()
        for owner in range(n_seq):

            @pl.when(p.s != owner)
            def _(owner=owner):
                a2a(owner).wait_send()

        gout = xall.at[0]
        low = gout.at[p.s]

        def norm_two_tile(n, carry):
            low[tile_rows(n), :] = layer_norm(resid[tile_rows(n), :], gain2, bias2)[0].astype(BF16)
            return carry

        lax.fori_loop(0, tok // tile, norm_two_tile, 0)
        lay_out(send_n, low)

        disp_n = Dispatch(p, send_n, held, g["disp_n"][0:2], g["disp_n"][2:4])
        comb_g = Combine(p, part, *g["comb_g"][0:3], back, g["comb_g"][3:5], g["comb_g"][5:7], slots)
        comb_f = Combine(p, held, *g["comb_f"][0:2], None, ret, g["comb_f"][2:4], g["comb_f"][4:6], n_exp)
        disp_n.own()
        disp_n.start_seq(0)
        for step in range(1, n_exp):
            disp_n.start_exp(step)
        disp_c.start_seq(4)
        disp_c.relay(3)
        dwu[...] = jnp.zeros_like(dwu)
        dwd[...] = jnp.zeros_like(dwd)
        dbu_ref[...] = jnp.zeros_like(dbu_ref)
        csum_ref[...] = jnp.zeros_like(csum_ref)
        bias_down = bd_ref[...].astype(F32)
        for c in load_ffn:
            c.wait()

        def ffn_start(*steps):
            for step in steps:
                comb_f.start(step)

        def ffn_pass(*steps):
            for step in steps:
                comb_f.pass_on(step)

        def ffn_finish(*steps):
            for step in steps:
                comb_f.finish(step, bias_down)

        disp_c.drain(seq=False)
        keep_act, keep_grad = send_c.at[0:n_seq], send_c.at[n_seq : 2 * n_seq]

        def compute(step):
            x = held[step].reshape(routed, width)
            gr = cot[step].reshape(routed, width)
            ones = jnp.ones((8, routed), BF16)
            csum_ref[...] += dot(ones, gr)[0:1, :]
            gx = jnp.zeros((routed, width), F32)
            for b in range(hidden // block):
                at = pl.ds(b * block, block)
                wu_b, wd_b = wu[:, at], wd[at, :]
                pre = dot(x, wu_b) + bu_ref[:, at].astype(F32)
                g_act = dot(gr, wd_b, ((1,), (1,)))
                sq = pre * pre
                th = jnp.tanh(GELU_A * pre * (1.0 + GELU_B * sq))
                half = 0.5 * (1.0 + th)
                slope = half + 0.5 * pre * (1.0 - th * th) * (GELU_A * (1.0 + 3.0 * GELU_B * sq))
                g_pre = (g_act * slope).astype(BF16)
                keep_act[:, :, at] = (pre * half).astype(BF16).reshape(n_seq, cap, block)
                keep_grad[:, :, at] = g_pre.reshape(n_seq, cap, block)
                gx = gx + dot(g_pre, wu_b, ((1,), (1,)))
            part[lax.rem(step, slots)] = gx.astype(BF16).reshape(n_seq, cap, width)
            comb_g.start(step)
            y = jnp.zeros((routed, width), F32)
            for b in range(hidden // block):
                at = pl.ds(b * block, block)
                act = keep_act[:, :, at].reshape(routed, block)
                g_pre = keep_grad[:, :, at].reshape(routed, block)
                dbu_ref[:, at] += dot(ones, g_pre)[0:1, :]
                y = y + dot(act, wd[at, :])
                dwu[:, at] += dot(x, g_pre, ((0,), (0,)))
                dwd[at, :] += dot(act, gr, ((0,), (0,)))
            disp_n.sent(step)
            held[step] = y.astype(BF16).reshape(n_seq, cap, width)

        stores = [
            pltpu.make_async_copy(dwu, dwu_out, local_sems.at[6]),
            pltpu.make_async_copy(dwd, dwd_out, local_sems.at[7]),
        ]

        def loop(t, carry):
            @pl.when(t + ahead - 1 < n_exp)
            def _():
                disp_c.start_seq(t + ahead - 1)

            @pl.when(t + ahead - 2 < n_exp)
            def _():
                disp_c.relay(t + ahead - 2)

            @pl.when(t <= n_exp)
            def _():
                disp_n.relay(t - 1)

            @pl.when(t < n_exp)
            def _():
                disp_n.start_seq(t)

            @pl.when((t >= 3) & (t <= n_exp + 2))
            def _():
                comb_g.pass_on(t - 3)

            @pl.when(t >= 4)
            def _():
                comb_g.finish(t - 4)

            @pl.when(t == n_exp + 1)
            def _():
                ffn_start(0)

            @pl.when((t >= 2) & (t <= n_exp + 1))
            def _():
                disp_c.arrived(t - 2)
                disp_n.arrived(t - 2)
                compute(t - 2)

            @pl.when(t == n_exp + 1)
            def _():
                for c in stores:
                    c.start()
                ffn_start(1)

            @pl.when(t == n_exp + 2)
            def _():
                ffn_start(2)

            @pl.when(t == n_exp + 3)
            def _():
                ffn_start(3)

            return carry

        lax.fori_loop(1, n_exp + 4, loop, 0)
        comb_g.drain()

        for c in stores:
            c.wait()
        gin_ref[...] = dot(pick[...], back[...].reshape(n_exp * cap, width), ((0,), (0,)))

        def norm_two_back(n, carry):
            at = tile_rows(n)
            g_two = gin_ref[at, :]
            _, xhat, inv_std = layer_norm(resid[at, :], gain2, 0.0)
            g_resid = cot_ref[at, :].astype(F32) + norm_back(g_two, xhat, inv_std, gain2)
            gin_ref[at, :] = g_resid
            g_low = g_resid.astype(BF16)
            gout[p.s, at, :] = g_low
            new = (g_low.astype(F32), g_two * xhat, g_two)
            return tuple(old + jnp.sum(v, axis=0, keepdims=True) for old, v in zip(carry, new))

        zero_row = jnp.zeros((1, width), F32)
        sums2 = lax.fori_loop(0, tok // tile, norm_two_back, (zero_row,) * 3)
        gather2 = Gather(p, gout, *g["gather2"])
        gather2.start()
        vec_own[...] = jnp.zeros_like(vec_own)
        for n in range(3):
            vec_own[4 + n : 5 + n, :] = sums2[n]
        wo_mine = w_o.at[mine, :]

        def grad_attn(owner):
            gattn[owner] = dot(gout[owner], wo_mine[...], ((1,), (1,))).astype(BF16)

        dwu[0:total, 0 : 2 * cols] = jnp.zeros((total, 2 * cols), F32)

        head_rows = lax.broadcasted_iota(jnp.int32, (8, cols), 0)
        head_lane = lax.broadcasted_iota(jnp.int32, (8, cols), 1)
        per_head = (lax.div(head_lane, HEAD_DIM) == head_rows).astype(F32)

        def attn_back(owner, some_heads):
            rows = pl.ds(pl.multiple_of(owner * tok, tok), tok)
            q_pos = lax.broadcasted_iota(jnp.int32, (1, tok), 1) + owner * tok
            q_seg = segment_of(q_pos, len_ref)
            q_rows, g_rows = q_all[rows, :], gattn[owner]
            delta = lax.dot_general(
                per_head, g_rows.astype(F32) * attn[rows, :], (((1,), (1,)), ((), ())),
                precision=lax.Precision.HIGHEST, preferred_element_type=F32,
            )
            masks = [head_mask(tok, cols, head) for head in some_heads]
            zero = jnp.zeros_like(q_rows)
            q_owns = [jnp.where(own, q_rows, zero) for own in masks]
            g_owns = [jnp.where(own, g_rows, zero) for own in masks]
            dq[...] = jnp.zeros_like(dq)

            def key_block(n, carry):
                keys = pl.ds(pl.multiple_of(n * tok, tok), tok)
                k_pos = lax.broadcasted_iota(jnp.int32, (tok, 1), 0) + n * tok
                allowed = (q_seg == segment_of(k_pos, len_ref)) & (k_pos <= q_pos)
                k_rows, v_rows = k_all[keys, :], v_all[keys, :]
                dq_new = jnp.zeros((tok, cols), F32)
                dk_new = jnp.zeros((tok, cols), F32)
                dv_new = jnp.zeros((tok, cols), F32)
                for head, own, q_own, g_own in zip(some_heads, masks, q_owns, g_owns):
                    scores = dot(k_rows, q_own, ((1,), (1,)))
                    probs = jnp.where(allowed, jnp.exp(scores - lse_all[head : head + 1, rows]), 0.0)
                    g_probs = dot(v_rows, g_own, ((1,), (1,)))
                    g_scores = (probs * (g_probs - delta[head : head + 1, :])).astype(BF16)
                    dk_new = dk_new + dot(g_scores, q_own)
                    dv_new = dv_new + dot(probs.astype(BF16), g_own)
                    dq_new = dq_new + jnp.where(own, dot(g_scores, k_rows, ((0,), (0,))), 0.0)
                dk[keys, :] += dk_new
                dv[keys, :] += dv_new
                dq[...] += dq_new
                return carry

            lax.fori_loop(0, owner + 1, key_block, 0)
            low_dq = (dq[...] * SCORE_SCALE).astype(BF16)
            for j in sorted({head // per_pair for head in some_heads}):
                dqkv[rows, pl.ds(3 * j * 128, 128)] = low_dq[:, j * 128 : (j + 1) * 128]

        every = range(heads)
        grad_attn(p.s)
        gather2.relay()
        ffn_pass(0, 1, 2, 3)
        attn_back(p.s, every)
        gather2.wait((2, 3))
        grad_attn(p.near)
        attn_back(p.near, every)
        grad_attn(p.far)
        attn_back(p.far, every)
        ffn_finish(0, 1, 2, 3)
        gather2.wait((4, 5))
        ffn_start(4, 5, 6, 7)
        grad_attn(p.diag)

        def place_w(j, owner, e, half=None):
            rows = rows_w if half is None else rows_w // 2
            first = e * rows_w + (0 if half is None else half * rows)
            return gw_out.at[
                :, pl.ds(pl.multiple_of(first, rows), rows), pl.ds(pl.multiple_of(owner * cols + j * 128, 128), 128)
            ]

        def place_o(owner, e, half=None):
            rows = pl.ds(pl.multiple_of(owner * cols + e * rows_o, rows_o), rows_o)
            if half is None:
                return go_out.at[rows, :]
            return go_out.at[rows, pl.ds(half * (width // 2), width // 2)]

        def summing(name, place):
            return SumAll(p, *g[name][0:5], place, g[name][5], g[name][6:])

        sum_w = [summing(f"sum_{j}", functools.partial(place_w, j)) for j in range(pairs)]
        sum_o = summing("sum_o", place_o)

        for b in range(cols // 128):
            a_low = attn[:, b * 128 : (b + 1) * 128].astype(BF16)
            got = dot(a_low, gout[...].reshape(total, width), ((0,), (0,))).astype(BF16)
            for n in range(128 // rows_o):
                e = b * (128 // rows_o) + n
                sum_o.src[e % 2, e // 2] = got[n * rows_o : (n + 1) * rows_o]
        sum_o.start()
        for j in range(pairs):
            attn_back(p.diag, range(j * per_pair, (j + 1) * per_pair))
            first = 3 * j * 128
            at = slice(j * 128, (j + 1) * 128)
            dqkv[:, first + 128 : first + 256] = dk[:, at].astype(BF16)
            dqkv[:, first + 256 : first + 384] = dv[:, at].astype(BF16)
            src = sum_w[j].src
            for b in range(width // 256):
                got = dot(n1[b * 256 : (b + 1) * 256, :], dqkv[:, first : first + 384]).astype(BF16)
                for n in range(256 // rows_w):
                    e = b * (256 // rows_w) + n
                    for m in range(3):
                        src[e % 2, e // 2, m] = got[n * rows_w : (n + 1) * rows_w, m * 128 : (m + 1) * 128]
            sum_w[j].start()
            if j == 0:
                sum_o.spread()
            if j > 0:
                sum_w[j - 1].spread()
        sum_w[pairs - 1].spread()
        sum_o.reduce()
        sum_o.forward(0)
        gather2.drain()
        red = Combine(p, xall, *g["red"][0:2], None, None, g["red"][2:4], (None, None), 1)
        for owner in range(n_seq):
            piece = dqkv[pl.ds(owner * tok, tok), :]
            xall[0, owner] = dot(piece, w_all[...], ((1,), (1,))).astype(BF16)
        red.start(0)
        d_sums = dot(jnp.ones((8, total), BF16), dqkv[...])
        for j in range(pairs):
            at = pl.ds(pl.multiple_of(p.s * cols + j * 128, 128), 128)
            first = 3 * j * 128
            vec_own[2:3, at] = d_sums[0:1, first : first + 128]
            vec_own[3:4, at] = d_sums[0:1, first + 256 : first + 384]
        sums = [sum_o] + sum_w
        ffn_pass(4, 5, 6, 7)
        red.pass_on(0)
        for n in range(1, len(sums)):
            sums[n].reduce()
            sums[n].forward(0)
            sums[n - 1].relay(0)
        red.arrived(0)
        half_tok = tok // 2
        for n in range(2):
            gout[p.s, pl.ds(n * half_tok, half_tok), :] = red.summed(0, n).astype(BF16)

        def norm_one_back(n, carry):
            at = tile_rows(n)
            g_one = gout[p.s, at, :].astype(F32)
            _, xhat, inv_std = layer_norm(tok_ref[at, :].astype(F32), gain1, 0.0)
            gin_ref[at, :] += norm_back(g_one, xhat, inv_std, gain1)
            new = (g_one * xhat, g_one)
            return tuple(old + jnp.sum(v, axis=0, keepdims=True) for old, v in zip(carry, new))

        sums1 = lax.fori_loop(0, tok // tile, norm_one_back, (zero_row,) * 2)
        store_gin = pltpu.make_async_copy(gin_ref, gin_out, local_sems.at[0])
        store_gin.start()
        for n in range(2):
            vec_own[n : n + 1, :] = sums1[n]
        vec_seq[p.s] = vec_own[...]

        def tell(other):
            return p.to_seq(vec_own, vec_seq.at[p.s], r["vs_send"].at[other], r["vs_recv"].at[p.s], other)

        def told(other):
            return p.to_seq(vec_own, vec_seq.at[other], r["vs_send"].at[other], r["vs_recv"].at[other], other)

        others = (p.near, p.far, p.diag)
        for other in others:
            tell(other).start()
        for hop in range(1, chips):
            ffn_finish(*range(4 + 4 * (hop - 1) // (chips - 1), 4 + 4 * hop // (chips - 1)))
            for one in sums:
                one.forward(hop)
                if hop > 1 or one is sums[-1]:
                    one.relay(hop - 1)
            if hop > 1:
                for one in sums:
                    one.arrived(hop - 2)
        for other in others:
            told(other).wait_recv()
        for other in others:
            tell(other).wait_send()
        vec = vec_seq[0]
        for n in range(1, n_seq):
            vec = vec + vec_seq[n]
        vec_own[...] = vec
        vec_exp[p.e] = vec

        def show(step):
            other = p.peer(step, -1)
            return p.to_exp(vec_own, vec_exp.at[p.e], r["ve_send"].at[step], r["ve_recv"].at[step], other)

        def shown(step):
            other = p.peer(step, 1)
            return p.to_exp(vec_own, vec_exp.at[other], r["ve_send"].at[step], r["ve_recv"].at[step], other)

        for step in range(1, n_exp):
            show(step).start()
        for one in sums:
            one.relay(chips - 1)
        comb_f.drain()
        out_ref = part.at[0]
        for n in range(tok // 128):
            at = slice(n * 128, (n + 1) * 128)
            rows_back = dot(pick[:, at], ret[...].reshape(n_exp * cap, width), ((0,), (0,)))
            out_ref[n * 128 // cap : (n + 1) * 128 // cap] = (
                (resid[at, :] + rows_back).astype(BF16).reshape(128 // cap, cap, width)
            )
        store_out = pltpu.make_async_copy(out_ref, out_out, local_sems.at[1])
        store_out.start()
        for hop in range(chips - 2, chips):
            for one in sums:
                one.arrived(hop)
        for step in range(1, n_exp):
            shown(step).wait_recv()
            show(step).wait_send()
        vec = vec_exp[0]
        for n in range(1, n_exp):
            vec = vec + vec_exp[n]
        vec_ref[...] = vec
        for step in range(n_exp):
            disp_c.sent(step)
        disp_n.drain(seq=False)
        for one in sums:
            one.drain()
        store_gin.wait()
        store_out.wait()

    vmem = pl.BlockSpec(memory_space=pltpu.VMEM)
    hbm = pl.BlockSpec(memory_space=pl.ANY)
    smem = pl.BlockSpec(memory_space=pltpu.SMEM)
    shape = jax.ShapeDtypeStruct
    return pl.pallas_call(
        kernel,
        out_shape=[
            shape((n_seq, cap, width), BF16),
            shape((tok, width), F32),
            shape((8, width), F32),
            shape((1, hidden), F32),
            shape((1, width), F32),
            shape((width, hidden), F32),
            shape((hidden, width), F32),
            shape((3, width, width), BF16),
            shape((width, width), BF16),
        ],
        in_specs=[vmem] * 3 + [smem] + [vmem] * 2 + [hbm] * 3 + [vmem] * 2 + [hbm] + [vmem] * 3
        + [hbm, vmem, hbm, vmem],
        out_specs=[hbm, hbm] + [vmem] * 3 + [hbm] * 4,
        scratch_shapes=scratch,
        compiler_params=pltpu.CompilerParams(
            collective_id=collective_id, has_side_effects=True, vmem_limit_bytes=VMEM_LIMIT
        ),
        name="layer",
    )(tokens, ids, cotangent, lengths, *ln1, *w_qkv, b_query, b_value, w_out, b_out, *ln2, w_up, b_up, w_down, b_down)


def finish(output, input_grad, vec, dbu, csum, dwu, dwd, gw, go):
    tok, width = output.shape
    hidden = dwu.shape[1]
    cols = width // 4
    piece = 256

    def kernel(out_in, gin_in, vec_ref, dbu_in, csum_ref, dwu_in, dwd_in, gw_in, go_in, *refs):
        (out_o, gin_o, l1g, l1b, wq_o, bq_o, wk_o, wv_o, bv_o, wo_o, bo_o, l2g, l2b, dwu_o, dbu_o, dwd_o, dbd_o) = refs[:17]
        small, wide, same_b, same_f, sems = refs[17:22]
        count = 0

        def pair(src, mid_in, mid_out, dst):
            nonlocal count
            load = pltpu.make_async_copy(src, mid_in, sems.at[count])
            store = pltpu.make_async_copy(mid_out, dst, sems.at[count + 1])
            count += 2
            return load, store

        widen, plain = [], []
        for m, (src, dst) in enumerate(
            ((gw_in.at[0], wq_o), (gw_in.at[1], wk_o), (gw_in.at[2], wv_o), (go_in, wo_o))
        ):
            for n in range(width // piece):
                rows = pl.ds(n * piece, piece)
                at = m * (width // piece) + n
                widen.append((pair(src.at[rows], small.at[at], wide.at[at], dst.at[rows]), at))
        at = 0
        for src, dst, total in ((dwu_in, dwu_o.at[0], width), (dwd_in, dwd_o.at[0], hidden), (gin_in, gin_o.at[0], tok)):
            for n in range(total // piece):
                rows = pl.ds(n * piece, piece)
                plain.append(pair(src.at[rows], same_f.at[at], same_f.at[at], dst.at[rows]))
                at += 1
        plain.append(pair(out_in, same_b, same_b, out_o.at[0]))
        order = []
        for n in range(max(len(widen), len(plain))):
            order += widen[n : n + 1] + [(c, None) for c in plain[n : n + 1]]
        for (load, _), _ in order:
            load.start()
        for n, ref in enumerate((l1g, l1b, bq_o, bv_o, bo_o, l2g, l2b)):
            ref[...] = vec_ref[n : n + 1, :].reshape(width)
        dbu_o[...] = dbu_in[...]
        first = pl.multiple_of(lax.axis_index("seq") * cols, cols)
        dbd_o[...] = csum_ref[:, pl.ds(first, cols)]
        for (load, store), at in order:
            load.wait()
            if at is not None:
                wide[at] = small[at].astype(F32)
            store.start()
        for (_, store), _ in order:
            store.wait()

    vmem = pl.BlockSpec(memory_space=pltpu.VMEM)
    hbm = pl.BlockSpec(memory_space=pl.ANY)
    shape = jax.ShapeDtypeStruct
    row, square = shape((width,), F32), shape((width, width), F32)
    n_widen = 4 * (width // piece)
    n_plain = (width + hidden + tok) // piece
    return pl.pallas_call(
        kernel,
        out_shape=[
            shape((1, tok, width), BF16), shape((1, tok, width), F32), row, row, square, row, square, square, row,
            square, row, row, row, shape((1, width, hidden), F32), shape((1, hidden), F32),
            shape((1, hidden, width), F32), shape((1, cols), F32),
        ],
        in_specs=[hbm, hbm, vmem, vmem, vmem, hbm, hbm, hbm, hbm],
        out_specs=[hbm, hbm, vmem, vmem, hbm, vmem, hbm, hbm, vmem, hbm, vmem, vmem, vmem, hbm, vmem, hbm, vmem],
        scratch_shapes=[
            pltpu.VMEM((n_widen, piece, width), BF16),
            pltpu.VMEM((n_widen, piece, width), F32),
            pltpu.VMEM((tok, width), BF16),
            pltpu.VMEM((n_plain, piece, width), F32),
            pltpu.SemaphoreType.DMA((2 * (n_widen + n_plain + 1),)),
        ],
        compiler_params=pltpu.CompilerParams(vmem_limit_bytes=VMEM_LIMIT),
        name="finish",
    )(output, input_grad, vec, dbu, csum, dwu, dwd, gw, go)


def shards(
    tokens, lengths, expert_ids, ln1_gain, ln1_bias, w_query, b_query, w_key, w_value, b_value, w_out, b_out,
    ln2_gain, ln2_bias, w_up, b_up, w_down, b_down, cotangent,
):
    output, *parts = layer(
        tokens[0], expert_ids[0, :, 0][None], cotangent[0], lengths, (ln1_gain, ln1_bias),
        (w_query, w_key, w_value), b_query, b_value, w_out, b_out, (ln2_gain, ln2_bias), w_up[0], b_up, w_down[0],
        b_down, lax.axis_size("exp"), 0,
    )
    return tuple(finish(output.reshape(tokens.shape[1:]), *parts))


def norm_layer(values_in, gain_vec, shift_vec):
    center = values_in - jnp.mean(values_in, axis=-1, keepdims=True)
    inv_std = lax.rsqrt(jnp.mean(center * center, axis=-1, keepdims=True) + EPSILON)
    return center * inv_std * gain_vec + shift_vec


def segment_ids(positions, seq_ends):
    return jnp.sum((positions[:, None] >= seq_ends[None, :]).astype(jnp.int32), axis=1)


def visible_pairs(query_pos, query_seg, key_pos, key_seg):
    return ((query_seg[:, None] == key_seg[None, :]) & (key_pos[None, :] <= query_pos[:, None]))[
        None
    ]


def project(left_op, right_op):
    return jnp.dot(left_op, right_op, preferred_element_type=jnp.float32)


def shards_any(
    tokens,
    lengths,
    expert_ids,
    ln1_gain,
    ln1_bias,
    w_query,
    b_query,
    w_key,
    w_value,
    b_value,
    w_out,
    b_out,
    ln2_gain,
    ln2_bias,
    w_up,
    b_up,
    w_down,
    b_down,
    cotangent,
):
    tok_rows = tokens.shape[1]
    width = tokens.shape[2]
    seq_size = lax.axis_size("seq")
    exp_size = lax.axis_size("exp")
    seq_rank = lax.axis_index("seq")
    seq_ends = jnp.cumsum(lengths[0])
    own_pos = seq_rank * tok_rows + jnp.arange(tok_rows, dtype=jnp.int32)
    own_seg = segment_ids(own_pos, seq_ends)
    inputs = tokens[0].astype(jnp.float32)
    gain_one = ln1_gain.astype(jnp.float32)
    bias_one = ln1_bias.astype(jnp.float32)
    gain_two = ln2_gain.astype(jnp.float32)
    bias_two = ln2_bias.astype(jnp.float32)
    normed_one_low = norm_layer(inputs, gain_one, bias_one).astype(jnp.bfloat16)
    query_low = (project(normed_one_low, w_query) + b_query.astype(jnp.float32)).astype(
        jnp.bfloat16
    )
    keys_low = project(normed_one_low, w_key).astype(jnp.bfloat16)
    values_low = (project(normed_one_low, w_value) + b_value.astype(jnp.float32)).astype(
        jnp.bfloat16
    )
    query_heads = query_low.reshape(tok_rows, HEADS, HEAD_DIM)
    initial = (
        jnp.full((HEADS, tok_rows), MASKED_SCORE, jnp.float32),
        jnp.zeros((HEADS, tok_rows), jnp.float32),
        jnp.zeros((HEADS, tok_rows, HEAD_DIM), jnp.float32),
    )
    key_piece = lax.all_gather(keys_low, "seq", axis=0, tiled=True)
    value_piece = lax.all_gather(values_low, "seq", axis=0, tiled=True)
    piece_len = key_piece.shape[0]
    fold_block_len = math.gcd(piece_len, 512)
    block_count = piece_len // fold_block_len
    key_blocks = key_piece.reshape(block_count, fold_block_len, HEADS, HEAD_DIM)
    value_blocks = value_piece.reshape(block_count, fold_block_len, HEADS, HEAD_DIM)
    offsets = jnp.arange(block_count, dtype=jnp.int32) * fold_block_len

    def block_step(state_now, packed):
        row_max, row_total, accumulated = state_now
        key_blk, value_blk, offset = packed
        key_pos = offset + jnp.arange(fold_block_len, dtype=jnp.int32)
        allowed = visible_pairs(own_pos, own_seg, key_pos, segment_ids(key_pos, seq_ends))
        scores = (
            jnp.einsum("qhd,khd->hqk", query_heads, key_blk, preferred_element_type=jnp.float32)
            * SCORE_SCALE
        )
        masked = jnp.where(allowed, scores, MASKED_SCORE)
        new_max = jnp.maximum(row_max, jnp.max(masked, axis=-1))
        weights = jnp.where(allowed, jnp.exp(masked - new_max[..., None]), 0.0)
        factor = jnp.exp(row_max - new_max)
        row_total = row_total * factor + jnp.sum(weights, axis=-1)
        accumulated = accumulated * factor[..., None] + jnp.einsum(
            "hqk,khd->hqd",
            weights.astype(jnp.bfloat16),
            value_blk,
            preferred_element_type=jnp.float32,
        )
        return ((new_max, row_total, accumulated), None)

    result, _ = lax.scan(block_step, initial, (key_blocks, value_blocks, offsets))
    row_max, row_total, accumulated = result
    attn_heads = accumulated / row_total[..., None]
    attn_low = jnp.transpose(attn_heads, (1, 0, 2)).reshape(tok_rows, width).astype(jnp.bfloat16)
    resid = inputs + project(attn_low, w_out) + b_out.astype(jnp.float32)
    normed_two_low = norm_layer(resid, gain_two, bias_two).astype(jnp.bfloat16)
    experts = exp_size * w_up.shape[0]
    capacity = 2 * tok_rows // experts
    expert_of = expert_ids[0, :, 0]
    onehot = (expert_of[:, None] == jnp.arange(experts, dtype=jnp.int32)[None, :]).astype(jnp.int32)
    slot_of = jnp.sum(onehot * (jnp.cumsum(onehot, axis=0) - onehot), axis=1)
    send_rows = (
        jnp.zeros((experts, capacity, width), jnp.bfloat16)
        .at[expert_of, slot_of]
        .set(normed_two_low)
    )
    received = lax.all_to_all(send_rows, "exp", split_axis=0, concat_axis=0, tiled=True)
    recv_count = experts * capacity
    recv_rows = received.reshape(recv_count, width)
    up_weight = w_up[0]
    up_bias = b_up[0]
    down_weight = w_down[0]
    down_bias = b_down[0].astype(jnp.float32)
    piece_width = width // seq_size
    grad_send = (
        jnp.zeros((experts, capacity, width), jnp.bfloat16).at[expert_of, slot_of].set(cotangent[0])
    )
    gathered = lax.all_gather(recv_rows, "seq", axis=0, tiled=True)
    preact = project(gathered, up_weight) + up_bias.astype(jnp.float32)
    act_low = jax.nn.gelu(preact).astype(jnp.bfloat16)
    part = act_low
    expert_out = (
        lax.psum_scatter(
            project(part, down_weight).astype(jnp.bfloat16), "seq", scatter_dimension=0, tiled=True
        ).astype(jnp.float32)
        + down_bias
    )
    returned = lax.all_to_all(
        expert_out.astype(jnp.bfloat16).reshape(experts, capacity, width),
        "exp",
        split_axis=0,
        concat_axis=0,
        tiled=True,
    )
    grad_recv = lax.all_to_all(grad_send, "exp", split_axis=0, concat_axis=0, tiled=True).reshape(
        recv_count, width
    )
    grad_all = lax.all_gather(grad_recv, "seq", axis=0, tiled=True)
    bias_full = jnp.sum(grad_all.astype(jnp.float32), axis=0)
    grad_b_down = lax.dynamic_slice_in_dim(bias_full, seq_rank * piece_width, piece_width, 0)
    grad_act = jnp.einsum("rd,fd->rf", grad_all, down_weight, preferred_element_type=jnp.float32)
    grad_pre = jax.vjp(jax.nn.gelu, preact)[1](grad_act)[0].astype(jnp.bfloat16)
    grad_w_down = jnp.einsum("rf,rd->fd", act_low, grad_all, preferred_element_type=jnp.float32)
    grad_w_up = jnp.einsum("rd,rf->df", gathered, grad_pre, preferred_element_type=jnp.float32)
    grad_b_up = jnp.sum(grad_pre.astype(jnp.float32), axis=0)
    part = grad_pre
    grad_home = lax.psum_scatter(
        jnp.einsum("rf,df->rd", part, up_weight, preferred_element_type=jnp.float32).astype(
            jnp.bfloat16
        ),
        "seq",
        scatter_dimension=0,
        tiled=True,
    )
    ffn_rows = returned[expert_of, slot_of].astype(jnp.float32)
    output = (resid + ffn_rows).astype(jnp.bfloat16)
    grad_back = lax.all_to_all(
        grad_home.reshape(experts, capacity, width), "exp", split_axis=0, concat_axis=0, tiled=True
    )
    grad_normed_two = grad_back[expert_of, slot_of].astype(jnp.float32)
    _, norm_two_back = jax.vjp(norm_layer, resid, gain_two, bias_two)
    grad_resid_norm, grad_gain_two, grad_bias_two = norm_two_back(grad_normed_two)
    grad_resid = cotangent[0].astype(jnp.float32) + grad_resid_norm
    grad_out_low = grad_resid.astype(jnp.bfloat16)
    grad_w_out = jnp.einsum("qa,qd->ad", attn_low, grad_out_low, preferred_element_type=jnp.float32)
    grad_b_out = jnp.sum(grad_out_low.astype(jnp.float32), axis=0)
    grad_attn_low = jnp.einsum(
        "qd,ad->qa", grad_out_low, w_out, preferred_element_type=jnp.float32
    ).astype(jnp.bfloat16)
    grad_attn_heads = grad_attn_low.reshape(tok_rows, HEADS, HEAD_DIM)
    delta = jnp.sum(
        jnp.transpose(grad_attn_heads.astype(jnp.float32), (1, 0, 2)) * attn_heads, axis=-1
    )
    whole_keys, whole_values = (
        lax.all_gather(keys_low, "seq", axis=0, tiled=True),
        lax.all_gather(values_low, "seq", axis=0, tiled=True),
    )
    group_len = whole_keys.shape[0]
    block_len = math.gcd(group_len, 512)
    block_count = group_len // block_len

    def back_step(grad_query, packed):
        key_blk, value_blk, offset = packed
        key_pos = offset + jnp.arange(block_len, dtype=jnp.int32)
        allowed = visible_pairs(own_pos, own_seg, key_pos, segment_ids(key_pos, seq_ends))
        scores = (
            jnp.einsum("qhd,khd->hqk", query_heads, key_blk, preferred_element_type=jnp.float32)
            * SCORE_SCALE
        )
        masked = jnp.where(allowed, scores, MASKED_SCORE)
        probabilities = (
            jnp.where(allowed, jnp.exp(masked - row_max[..., None]), 0.0) / row_total[..., None]
        )
        probs_low = probabilities.astype(jnp.bfloat16)
        grad_probs = jnp.einsum(
            "qhd,khd->hqk", grad_attn_heads, value_blk, preferred_element_type=jnp.float32
        )
        grad_scores = (probabilities * (grad_probs - delta[..., None])).astype(jnp.bfloat16)
        grad_query = (
            grad_query
            + jnp.einsum("hqk,khd->qhd", grad_scores, key_blk, preferred_element_type=jnp.float32)
            * SCORE_SCALE
        )
        grad_key_blk = (
            jnp.einsum("hqk,qhd->khd", grad_scores, query_heads, preferred_element_type=jnp.float32)
            * SCORE_SCALE
        )
        grad_value_blk = jnp.einsum(
            "hqk,qhd->khd", probs_low, grad_attn_heads, preferred_element_type=jnp.float32
        )
        return (grad_query, (grad_key_blk, grad_value_blk))

    block_offsets = jnp.arange(block_count, dtype=jnp.int32) * block_len
    grad_query, key_value_parts = lax.scan(
        back_step,
        jnp.zeros((tok_rows, HEADS, HEAD_DIM), jnp.float32),
        (
            whole_keys.reshape(block_count, block_len, HEADS, HEAD_DIM),
            whole_values.reshape(block_count, block_len, HEADS, HEAD_DIM),
            block_offsets,
        ),
    )
    grad_keys, grad_values = (
        lax.psum_scatter(
            key_value_parts[0].reshape(group_len, width).astype(jnp.bfloat16),
            "seq",
            scatter_dimension=0,
            tiled=True,
        ).astype(jnp.float32),
        lax.psum_scatter(
            key_value_parts[1].reshape(group_len, width).astype(jnp.bfloat16),
            "seq",
            scatter_dimension=0,
            tiled=True,
        ).astype(jnp.float32),
    )
    grad_query_low = grad_query.reshape(tok_rows, width).astype(jnp.bfloat16)
    grad_keys_low = grad_keys.astype(jnp.bfloat16)
    grad_values_low = grad_values.astype(jnp.bfloat16)
    grad_w_query = jnp.einsum(
        "qa,qd->ad", normed_one_low, grad_query_low, preferred_element_type=jnp.float32
    )
    grad_b_query = jnp.sum(grad_query_low.astype(jnp.float32), axis=0)
    grad_w_key = jnp.einsum(
        "qa,qd->ad", normed_one_low, grad_keys_low, preferred_element_type=jnp.float32
    )
    grad_w_value = jnp.einsum(
        "qa,qd->ad", normed_one_low, grad_values_low, preferred_element_type=jnp.float32
    )
    grad_b_value = jnp.sum(grad_values_low.astype(jnp.float32), axis=0)
    grad_normed_one = (
        (
            jnp.einsum("qd,ad->qa", grad_query_low, w_query, preferred_element_type=jnp.float32)
            + jnp.einsum("qd,ad->qa", grad_keys_low, w_key, preferred_element_type=jnp.float32)
            + jnp.einsum("qd,ad->qa", grad_values_low, w_value, preferred_element_type=jnp.float32)
        )
        .astype(jnp.bfloat16)
        .astype(jnp.float32)
    )
    _, norm_one_back = jax.vjp(norm_layer, inputs, gain_one, bias_one)
    grad_in_norm, grad_gain_one, grad_bias_one = norm_one_back(grad_normed_one)
    input_grad = grad_resid + grad_in_norm
    summed = lax.psum(
        (
            grad_gain_one,
            grad_bias_one,
            grad_w_query,
            grad_b_query,
            grad_w_key,
            grad_w_value,
            grad_b_value,
            grad_w_out,
            grad_b_out,
            grad_gain_two,
            grad_bias_two,
        ),
        ("seq", "exp"),
    )
    return (
        output[None],
        input_grad[None],
        summed[0],
        summed[1],
        summed[2],
        summed[3],
        summed[4],
        summed[5],
        summed[6],
        summed[7],
        summed[8],
        summed[9],
        summed[10],
        grad_w_up[None],
        grad_b_up[None],
        grad_w_down[None],
        grad_b_down[None],
    )


def solution(mesh):
    placed = (
        P("exp", "seq", None),
        P("exp", None),
        P("exp", "seq", None),
        P(),
        P(),
        P(),
        P(),
        P(),
        P(),
        P(),
        P(),
        P(),
        P(),
        P(),
        P("exp", None, "seq"),
        P("exp", "seq"),
        P("exp", "seq", None),
        P("exp", None),
        P("exp", "seq", None),
    )
    plane = mesh.shape["seq"] == 4 and mesh.shape["exp"] == 8
    return jax.shard_map(
        shards if plane else shards_any,
        mesh=mesh,
        in_specs=placed,
        out_specs=(
            P("exp", "seq", None),
            P("exp", "seq", None),
            P(),
            P(),
            P(),
            P(),
            P(),
            P(),
            P(),
            P(),
            P(),
            P(),
            P(),
            P("exp", None, "seq"),
            P("exp", "seq"),
            P("exp", "seq", None),
            P("exp", "seq"),
        ),
        check_vma=False,
    )
```

```python
import functools
import math

import jax
import jax.numpy as jnp
from jax import lax
from jax.experimental import pallas as pl
from jax.experimental.pallas import tpu as pltpu
from jax.sharding import PartitionSpec as P

MESH = pl.DeviceIdType.MESH
F32 = jnp.float32
BF16 = jnp.bfloat16
VMEM_LIMIT = 63 * 2**20


def dot(a, b, dims=((1,), (0,))):
    return lax.dot_general(a, b, (dims, ((), ())), preferred_element_type=F32)


class Place:
    def __init__(self, n_exp):
        self.n_exp = n_exp
        self.s = lax.axis_index("seq")
        self.e = lax.axis_index("exp")
        low = lax.rem(self.s, 2)
        high = lax.div(self.s, 2)
        self.near = high * 2 + (1 - low)
        self.far = (1 - high) * 2 + low
        self.diag = (1 - high) * 2 + (1 - low)
        self.core = lax.rem(self.e, 2)
        self.chip = lax.div(self.e, 2)

    def peer(self, step, way):
        chips = self.n_exp // 2
        hop = lax.div(step, 2)
        if chips == 4:
            hop = hop + lax.div(hop, 2) * (5 - 2 * hop)
        chip = lax.rem(self.chip + way * hop + chips, chips)
        return chip * 2 + lax.rem(self.core + step, 2)

    def greet(self, diag=False):
        barrier = pltpu.get_barrier_semaphore()
        others = (self.near, self.far, self.diag) if diag else (self.near, self.far)
        for other in others:
            pl.semaphore_signal(barrier, inc=1, device_id=(other, self.e), device_id_type=MESH)

        def tell(step, carry):
            pl.semaphore_signal(
                barrier, inc=1, device_id=(self.s, self.peer(step, 1)), device_id_type=MESH
            )
            return carry

        lax.fori_loop(1, self.n_exp, tell, 0)
        pl.semaphore_wait(barrier, len(others) + self.n_exp - 1)

    def to_seq(self, src, dst, send_sem, recv_sem, other):
        return pltpu.make_async_remote_copy(
            src_ref=src, dst_ref=dst, send_sem=send_sem, recv_sem=recv_sem,
            device_id=(other, self.e), device_id_type=MESH,
        )

    def to_exp(self, src, dst, send_sem, recv_sem, other):
        return pltpu.make_async_remote_copy(
            src_ref=src, dst_ref=dst, send_sem=send_sem, recv_sem=recv_sem,
            device_id=(self.s, other), device_id_type=MESH,
        )


class Dispatch:
    def __init__(self, place, send, held, exp_sems, seq_sems):
        self.place, self.send, self.held = place, send, held
        self.exp_send, self.exp_recv = exp_sems
        self.seq_send, self.seq_recv = seq_sems
        self.cap = send.shape[1]

    @staticmethod
    def scratch(n_exp):
        return [
            pltpu.SemaphoreType.DMA((n_exp,)),
            pltpu.SemaphoreType.DMA((n_exp,)),
            pltpu.SemaphoreType.DMA((n_exp, 6)),
            pltpu.SemaphoreType.DMA((n_exp, 6)),
        ]

    def _exp(self, step):
        p = self.place
        other = p.peer(step, -1)
        return p.to_exp(
            self.send.at[other], self.held.at[step, p.s], self.exp_send.at[step], self.exp_recv.at[step], other
        )

    def _seq(self, step, owner, half, lane, other):
        p = self.place
        rows = pl.ds(half * (self.cap // 2), self.cap // 2)
        part = self.held.at[step, owner, rows]
        return p.to_seq(part, part, self.seq_send.at[step, lane], self.seq_recv.at[step, lane], other)

    def copies(self, step, lanes=range(6)):
        p = self.place
        spec = (
            (p.s, 0, p.near),
            (p.s, 1, p.far),
            (p.s, 1, p.near),
            (p.s, 0, p.far),
            (p.near, 0, p.far),
            (p.far, 1, p.near),
        )
        return [self._seq(step, spec[n][0], spec[n][1], n, spec[n][2]) for n in lanes]

    def start_exp(self, step):
        self._exp(step).start()

    def own(self):
        p = self.place
        self.held[0, p.s] = self.send[p.e]

    def start_seq(self, step):
        @pl.when(step > 0)
        def _():
            self._exp(step).wait_recv()

        for c in self.copies(step, range(4)):
            c.start()

    def relay(self, step):
        for c, out in zip(self.copies(step, (0, 1)), self.copies(step, (4, 5))):
            c.wait_recv()
            out.start()

    def arrived(self, step):
        for c in self.copies(step, range(2, 6)):
            c.wait_recv()

    def sent(self, step):
        for c in self.copies(step):
            c.wait_send()

    def drain(self, seq=True):
        def body(step, carry):
            if seq:
                self.sent(step)

            @pl.when(step > 0)
            def _():
                self._exp(step).wait_send()

            return carry

        lax.fori_loop(0, self.place.n_exp, body, 0)


class Combine:
    def __init__(self, place, part, passing, landing, total, back, seq_sems, exp_sems, slots):
        self.place, self.part, self.passing, self.landing = place, part, passing, landing
        self.total, self.back, self.slots = total, back, slots
        self.seq_send, self.seq_recv = seq_sems
        self.exp_send, self.exp_recv = exp_sems
        self.half = part.shape[2] // 2

    @staticmethod
    def scratch(n_exp, cap, width):
        return [
            pltpu.VMEM((n_exp, 2, cap // 2, width), BF16),
            pltpu.VMEM((n_exp, 4, cap // 2, width), BF16),
            pltpu.VMEM((n_exp, cap, width), BF16),
            pltpu.SemaphoreType.DMA((n_exp, 6)),
            pltpu.SemaphoreType.DMA((n_exp, 6)),
            pltpu.SemaphoreType.DMA((n_exp,)),
            pltpu.SemaphoreType.DMA((n_exp,)),
        ]

    def _slot(self, step):
        return lax.rem(step, self.slots)

    def _piece(self, step, owner, half):
        return self.part.at[self._slot(step), owner, pl.ds(half * self.half, self.half)]

    def _seq(self, src, dst, step, lane, other):
        return self.place.to_seq(
            src, dst, self.seq_send.at[step, lane], self.seq_recv.at[step, lane], other
        )

    def copies(self, step, lanes=range(6)):
        p = self.place
        spec = (
            (p.diag, 0, self.passing, 0, p.near),
            (p.diag, 1, self.passing, 1, p.far),
            (p.near, 0, self.landing, 0, p.near),
            (p.far, 1, self.landing, 3, p.far),
            (p.far, 0, self.landing, 2, p.far),
            (p.near, 1, self.landing, 1, p.near),
        )
        made = []
        for n in lanes:
            owner, half, buffer, at, other = spec[n]
            made.append(self._seq(self._piece(step, owner, half), buffer.at[step, at], step, n, other))
        return made

    def start(self, step):
        for c in self.copies(step, range(4)):
            c.start()

    def pass_on(self, step):
        p = self.place
        slot = self._slot(step)
        came, out = self.copies(step, (0, 1)), self.copies(step, (4, 5))
        for n, owner in enumerate((p.far, p.near)):
            rows = pl.ds(n * self.half, self.half)
            came[n].wait_recv()
            self.part[slot, owner, rows] = (
                self.part[slot, owner, rows].astype(F32) + self.passing[step, n].astype(F32)
            ).astype(BF16)
            out[n].start()

    def _whole(self, step):
        if self.total is None:
            return self.part.at[self._slot(step), self.place.s]
        return self.total.at[step]

    def _exp(self, step):
        p = self.place
        other = p.peer(step, 1)
        return p.to_exp(
            self._whole(step), self.back.at[p.e], self.exp_send.at[step], self.exp_recv.at[step], other
        )

    def arrived(self, step):
        copies = self.copies(step)
        for c in copies[2:]:
            c.wait_recv()
        for c in copies:
            c.wait_send()

    def summed(self, step, half):
        rows = pl.ds(half * self.half, self.half)
        return (
            self.part[self._slot(step), self.place.s, rows].astype(F32)
            + self.landing[step, half].astype(F32)
            + self.landing[step, 2 + half].astype(F32)
        )

    def finish(self, step, bias=None):
        p = self.place
        self.arrived(step)
        for half in range(2):
            value = self.summed(step, half)
            if bias is not None:
                value = value + bias
            rows = pl.ds(half * self.half, self.half)
            if self.total is None:
                self.part[self._slot(step), p.s, rows] = value.astype(BF16)
            else:
                self.total[step, rows] = value.astype(BF16)

        @pl.when(step > 0)
        def _():
            self._exp(step).start()

        @pl.when(step == 0)
        def _():
            self.back[p.e] = self._whole(0)[...]

    def drain(self):
        p = self.place

        def body(step, carry):
            c = self._exp(step)
            c.wait_send()
            c.wait_recv()
            return carry

        lax.fori_loop(1, p.n_exp, body, 0)


GELU_A = math.sqrt(2.0 / math.pi)
GELU_B = 0.044715


EPSILON = 1e-05
SCORE_SCALE = 0.125
MASKED_SCORE = -1e30
HEAD_DIM = 64
HEADS = 16


class Gather:
    def __init__(self, place, held, send_sems, recv_sems):
        self.place, self.held = place, held
        self.send_sems, self.recv_sems = send_sems, recv_sems
        self.half = held.shape[1] // 2

    @staticmethod
    def scratch():
        return [pltpu.SemaphoreType.DMA((6,)), pltpu.SemaphoreType.DMA((6,))]

    def copies(self, lanes=range(6)):
        p = self.place
        spec = (
            (p.s, 0, p.near),
            (p.s, 1, p.far),
            (p.s, 1, p.near),
            (p.s, 0, p.far),
            (p.near, 0, p.far),
            (p.far, 1, p.near),
        )
        made = []
        for n in lanes:
            owner, half, other = spec[n]
            part = self.held.at[owner, pl.ds(half * self.half, self.half)]
            made.append(p.to_seq(part, part, self.send_sems.at[n], self.recv_sems.at[n], other))
        return made

    def start(self):
        for c in self.copies(range(4)):
            c.start()

    def relay(self):
        for c, out in zip(self.copies((0, 1)), self.copies((4, 5))):
            c.wait_recv()
            out.start()

    def wait(self, lanes):
        for c in self.copies(lanes):
            c.wait_recv()

    def drain(self):
        for c in self.copies():
            c.wait_send()


def layer_norm(values, gain, shift):
    center = values - jnp.mean(values, axis=-1, keepdims=True)
    inv_std = lax.rsqrt(jnp.mean(center * center, axis=-1, keepdims=True) + EPSILON)
    xhat = center * inv_std
    return xhat * gain + shift, xhat, inv_std


def norm_back(grad, xhat, inv_std, gain):
    d = grad * gain
    return (
        d - jnp.mean(d, axis=-1, keepdims=True) - xhat * jnp.mean(d * xhat, axis=-1, keepdims=True)
    ) * inv_std


def row_choice(ids, n_exp, cap):
    tokens = ids.shape[1]
    named = (ids == lax.broadcasted_iota(jnp.int32, (128, tokens), 0)).astype(BF16)
    before = (
        lax.broadcasted_iota(jnp.int32, (tokens, tokens), 0)
        < lax.broadcasted_iota(jnp.int32, (tokens, tokens), 1)
    ).astype(BF16)
    earlier = dot(named, before) * named.astype(F32)
    slot = jnp.sum(earlier, axis=0, keepdims=True).astype(jnp.int32) + ids * cap
    return (slot == lax.broadcasted_iota(jnp.int32, (n_exp * cap, tokens), 0)).astype(BF16)


def segment_of(position, lengths):
    end = jnp.int32(0)
    count = jnp.zeros_like(position)
    for n in range(lengths.shape[1]):
        end = end + lengths[0, n]
        count = count + (position >= end).astype(jnp.int32)
    return count


def head_mask(rows, width, head):
    lane = lax.broadcasted_iota(jnp.int32, (rows, width), 1)
    return (lane >= head * HEAD_DIM) & (lane < (head + 1) * HEAD_DIM)


class SumAll:
    def __init__(self, place, src, core_in, mine, chip_in, res, where, local_sem, sems):
        self.place, self.src, self.core_in, self.mine = place, src, core_in, mine
        self.chip_in, self.res, self.where, self.local_sem = chip_in, res, where, local_sem
        (self.core_sems, self.rs_send, self.rs_recv, self.ag_send, self.ag_recv,
         self.seq_send, self.seq_recv, self.pair_send, self.pair_recv) = sems
        self.chips = place.n_exp // 2
        p = place
        self.sibling = p.chip * 2 + (1 - p.core)

    @staticmethod
    def scratch(n_exp, *piece):
        chips = n_exp // 2
        dma = pltpu.SemaphoreType.DMA
        return [
            pltpu.VMEM((2, chips, *piece), BF16),
            pltpu.VMEM((chips, *piece), BF16),
            pltpu.VMEM((chips, *piece), BF16),
            pltpu.VMEM((chips, *piece), BF16),
            pltpu.VMEM(piece, BF16),
            dma((1,)),
            dma((2,)),
            dma((chips,)),
            dma((chips,)),
            dma((chips,)),
            dma((chips,)),
            dma((chips, 6)),
            dma((chips, 6)),
            dma((chips, 4)),
            dma((chips, 4)),
        ]

    def chip(self, hop):
        return lax.rem(self.place.chip + hop, self.chips)

    def exp(self, hop):
        return self.chip(hop) * 2 + self.place.core

    def _core(self):
        p = self.place
        return p.to_exp(
            self.src.at[1 - p.core], self.core_in, self.core_sems.at[0], self.core_sems.at[1], self.sibling
        )

    def start(self):
        self._core().start()

    def _spread(self, hop):
        p = self.place
        to = self.chip(hop)
        return p.to_exp(
            self.mine.at[to], self.chip_in.at[p.chip], self.rs_send.at[to], self.rs_recv.at[p.chip], self.exp(hop)
        )

    def _spread_from(self, hop):
        p = self.place
        at = self.chip(hop)
        return p.to_exp(
            self.mine.at[at], self.chip_in.at[at], self.rs_send.at[at], self.rs_recv.at[at], self.exp(hop)
        )

    def spread(self):
        p = self.place
        self._core().wait_recv()
        for n in range(self.chips):
            self.mine[n] = (self.src[p.core, n].astype(F32) + self.core_in[n].astype(F32)).astype(BF16)
        for hop in range(1, self.chips):
            self._spread(hop).start()

    def _local(self):
        p = self.place
        return pltpu.make_async_copy(self.res, self.where(p.s, p.e), self.local_sem.at[0])

    def _share(self, hop):
        p = self.place
        to = self.chip(hop)
        return p.to_exp(
            self.res, self.where(p.s, p.e), self.ag_send.at[to], self.ag_recv.at[p.chip], self.exp(hop)
        )

    def _share_from(self, hop):
        p = self.place
        at = self.chip(hop)
        return p.to_exp(
            self.res, self.where(p.s, self.exp(hop)), self.ag_send.at[at], self.ag_recv.at[at], self.exp(hop)
        )

    def copies(self, hop, lanes=range(6)):
        p = self.place
        spec = (
            (p.s, 0, p.near),
            (p.s, 1, p.far),
            (p.s, 1, p.near),
            (p.s, 0, p.far),
            (p.near, 0, p.far),
            (p.far, 1, p.near),
        )
        made = []
        for n in lanes:
            owner, half, other = spec[n]
            part = self.where(owner, self.exp(hop), half)
            made.append(p.to_seq(part, part, self.seq_send.at[hop, n], self.seq_recv.at[hop, n], other))
        return made

    def _pair(self, hop, n):
        p = self.place
        part = self.where((p.s, p.near, p.far, p.diag)[n], self.exp(hop))
        return p.to_exp(part, part, self.pair_send.at[hop, n], self.pair_recv.at[hop, n], self.sibling)

    def _pair_from(self, hop, n):
        p = self.place
        owner = (p.s, p.near, p.far, p.diag)[n]
        part = self.where(owner, self.chip(hop) * 2 + (1 - p.core))
        return p.to_exp(part, part, self.pair_send.at[hop, n], self.pair_recv.at[hop, n], self.sibling)

    def reduce(self):
        p = self.place
        for hop in range(1, self.chips):
            self._spread_from(hop).wait_recv()
        total = self.mine[p.chip].astype(F32)
        for hop in range(1, self.chips):
            total = total + self.chip_in[self.chip(hop)].astype(F32)
        self.res[...] = total.astype(BF16)
        self._local().start()
        for hop in range(1, self.chips):
            self._share(hop).start()
        self._local().wait()

    def forward(self, hop):
        if hop > 0:
            self._share_from(hop).wait_recv()
        for c in self.copies(hop, range(4)):
            c.start()
        self._pair(hop, 0).start()

    def relay(self, hop):
        for c, out in zip(self.copies(hop, (0, 1)), self.copies(hop, (4, 5))):
            c.wait_recv()
            out.start()

    def arrived(self, hop):
        for c in self.copies(hop, (2, 3)):
            c.wait_recv()
        self._pair(hop, 1).start()
        self._pair(hop, 2).start()
        for c in self.copies(hop, (4, 5)):
            c.wait_recv()
        self._pair(hop, 3).start()

    def drain(self):
        self._core().wait_send()
        for hop in range(1, self.chips):
            self._spread(hop).wait_send()
            self._share(hop).wait_send()
        for hop in range(self.chips):
            for c in self.copies(hop):
                c.wait_send()
            for n in range(4):
                self._pair(hop, n).wait_send()
                self._pair_from(hop, n).wait_recv()


def layer(
    tokens, ids, cotangent, lengths, ln1, w_qkv, b_query, b_value, w_out, b_out, ln2, w_up, b_up, w_down, b_down,
    n_exp, collective_id,
):
    tok, width = tokens.shape
    hidden = w_up.shape[1]
    n_seq = 4
    total = n_seq * tok
    cols = width // n_seq
    heads = cols // HEAD_DIM
    cap = 2 * tok // n_exp
    q_block = 256
    chips = n_exp // 2
    rows_w, rows_o = width // n_exp, cols // n_exp
    pairs = cols // 128
    per_pair = 128 // HEAD_DIM
    routed = n_seq * cap
    block = min(256, hidden)
    slots = 2
    ahead = 5

    vm = pltpu.VMEM
    dma = pltpu.SemaphoreType.DMA
    table = dict(
        xall=vm((1, n_seq, tok, width), BF16),
        n1=vm((width, total), BF16),
        q=vm((total, cols), BF16),
        k=vm((total, cols), BF16),
        v=vm((total, cols), BF16),
        attn=vm((total, cols), F32),
        lse=vm((8, total), F32),
        resid=vm((tok, width), F32),
        pick=vm((n_exp * cap, tok), BF16),
        w_all=vm((width, 3 * cols), BF16),
        w_o=vm((width, width), BF16),
        send_c=vm((n_exp, cap, width), BF16),
        send_n=vm((n_exp, cap, width), BF16),
        back=vm((n_exp, cap, width), BF16),
        ret=vm((n_exp, cap, width), BF16),
        attn_out=vm((n_seq, tok, cols), BF16),
        attn_in=vm((n_seq, tok, cols), BF16),
        cot=vm((n_exp, n_seq, cap, width), BF16),
        held=vm((n_exp, n_seq, cap, width), BF16),
        wu=vm((width, hidden), BF16),
        wd=vm((hidden, width), BF16),
        part=vm((slots, n_seq, cap, width), BF16),
        dwu=vm((width, hidden), F32),
        dwd=vm((hidden, width), F32),
        dqkv=vm((total, 3 * cols), BF16),
        vec_own=vm((8, width), F32),
        vec_seq=vm((n_seq, 8, width), F32),
        vec_exp=vm((n_exp, 8, width), F32),
        local_sems=dma((8,)),
        load_sems=dma((3 * pairs,)),
        dq=vm((tok, cols), F32),
        a2a_send=dma((n_seq,)),
        a2a_recv=dma((n_seq,)),
        vs_send=dma((n_seq,)),
        vs_recv=dma((n_seq,)),
        ve_send=dma((n_exp,)),
        ve_recv=dma((n_exp,)),
    )
    groups = dict(
        gather1=Gather.scratch(),
        gather2=Gather.scratch(),
        disp_c=Dispatch.scratch(n_exp),
        disp_n=Dispatch.scratch(n_exp),
        comb_g=Combine.scratch(n_exp, cap, width),
        comb_f=Combine.scratch(n_exp, cap, width)[:2] + Combine.scratch(n_exp, cap, width)[3:],
        red=[
            vm((1, 2, tok // 2, width), BF16),
            vm((1, 4, tok // 2, width), BF16),
            dma((1, 6)),
            dma((1, 6)),
        ],
        sum_o=SumAll.scratch(n_exp, rows_o, width),
        **{f"sum_{j}": SumAll.scratch(n_exp, 3, rows_w, 128) for j in range(pairs)},
    )
    scratch = list(table.values()) + [ref for group in groups.values() for ref in group]

    def kernel(tok_ref, ids_ref, cot_ref, len_ref, g1_ref, c1_ref, wq_in, wk_in, wv_in, bq_ref, bv_ref, wo_in, bo_ref,
               g2_ref, c2_ref, wu_in, bu_ref, wd_in, bd_ref,
               out_out, gin_out, vec_ref, dbu_ref, csum_ref, dwu_out, dwd_out, gw_out, go_out, *refs):
        r = dict(zip(table, refs))
        at = len(table)
        g = {}
        for name, group in groups.items():
            g[name] = refs[at : at + len(group)]
            at += len(group)
        xall, n1, q_all, k_all, v_all = r["xall"], r["n1"], r["q"], r["k"], r["v"]
        attn, lse_all, resid, pick = r["attn"], r["lse"], r["resid"], r["pick"]
        w_all, w_o, wu, wd = r["w_all"], r["w_o"], r["wu"], r["wd"]
        send_c, send_n, back, ret = r["send_c"], r["send_n"], r["back"], r["ret"]
        attn_out, attn_in, cot, held, part = r["attn_out"], r["attn_in"], r["cot"], r["held"], r["part"]
        dwu, dwd, dqkv = r["dwu"], r["dwd"], r["dqkv"]
        gattn = attn_out
        gin_ref = dwd.at[0:tok, :]
        dk, dv = dwu.at[0:total, 0:cols], dwu.at[0:total, cols : 2 * cols]
        vec_own, vec_seq, vec_exp = r["vec_own"], r["vec_seq"], r["vec_exp"]
        local_sems, load_sems, dq = r["local_sems"], r["load_sems"], r["dq"]

        p = Place(n_exp)
        mine = pl.ds(pl.multiple_of(p.s * cols, cols), cols)

        tile = 32

        def tile_rows(n):
            return pl.ds(pl.multiple_of(n * tile, tile), tile)

        def row_of(ref):
            return ref[...].astype(F32).reshape(1, ref.shape[-1])

        loads = [
            pltpu.make_async_copy(
                src.at[:, pl.ds(pl.multiple_of(p.s * cols + j * 128, 128), 128)],
                w_all.at[:, pl.ds((3 * j + m) * 128, 128)],
                load_sems.at[3 * j + m],
            )
            for m, src in enumerate((wq_in, wk_in, wv_in))
            for j in range(pairs)
        ]
        load_o = pltpu.make_async_copy(wo_in, w_o, local_sems.at[3])
        load_ffn = [
            pltpu.make_async_copy(wu_in, wu, local_sems.at[4]),
            pltpu.make_async_copy(wd_in, wd, local_sems.at[5]),
        ]
        for c in loads + [load_o] + load_ffn:
            c.start()

        xall[0, p.s] = tok_ref[...]
        p.greet(diag=True)
        gather1 = Gather(p, xall.at[0], *g["gather1"])
        gather1.start()
        pick[...] = row_choice(ids_ref[...], n_exp, cap)

        def lay_out(send, rows_ref):
            for e in range(0, n_exp, 2):
                laid = dot(pick[e * cap : (e + 2) * cap, :], rows_ref[...])
                send[e : e + 2] = laid.astype(BF16).reshape(2, cap, width)

        lay_out(send_c, cot_ref)
        disp_c = Dispatch(p, send_c, cot, g["disp_c"][0:2], g["disp_c"][2:4])
        for step in range(1, n_exp):
            disp_c.start_exp(step)
        disp_c.own()
        gain1, bias1 = row_of(g1_ref), row_of(c1_ref)
        gain2, bias2 = row_of(g2_ref), row_of(c2_ref)
        bq = bq_ref[mine].astype(F32).reshape(1, cols)
        bv = bv_ref[mine].astype(F32).reshape(1, cols)

        def project(owner):
            rows = pl.ds(pl.multiple_of(owner * tok, tok), tok)

            def norm_tile(n, carry):
                x = xall[0, owner, tile_rows(n), :].astype(F32)
                per = cap // tile
                rows = pl.ds(pl.multiple_of(lax.rem(n, per) * tile, tile), tile)
                part[0, lax.div(n, per), rows, :] = layer_norm(x, gain1, bias1)[0].astype(BF16)
                return carry

            lax.fori_loop(0, tok // tile, norm_tile, 0)
            normed = part[0].reshape(tok, width)
            n1[:, rows] = jnp.transpose(normed)
            out = dot(normed, w_all[...])
            for j in range(pairs):
                at, first = slice(j * 128, (j + 1) * 128), 3 * j * 128
                q = (out[:, first : first + 128] + bq[:, at]).astype(BF16)
                q_all[rows, at] = (q.astype(F32) * SCORE_SCALE).astype(BF16)
                k_all[rows, at] = out[:, first + 128 : first + 256].astype(BF16)
                v_all[rows, at] = (out[:, first + 256 : first + 384] + bv[:, at]).astype(BF16)

        for c in loads:
            c.wait()
        project(p.s)
        gather1.relay()
        gather1.wait((2, 3))
        project(p.near)
        project(p.far)
        gather1.wait((4, 5))
        disp_c.start_seq(0)
        disp_c.start_seq(1)
        project(p.diag)

        def a2a(owner):
            return p.to_seq(
                attn_out.at[owner], attn_in.at[p.s], r["a2a_send"].at[owner], r["a2a_recv"].at[p.s], owner
            )

        def a2a_from(owner):
            return p.to_seq(
                attn_out.at[owner], attn_in.at[owner], r["a2a_send"].at[owner], r["a2a_recv"].at[owner], owner
            )

        blocks = total // q_block
        for n in reversed(range(blocks)):
            seen = (n + 1) * q_block
            rows = pl.ds(n * q_block, q_block)
            q_pos = lax.broadcasted_iota(jnp.int32, (q_block, 1), 0) + n * q_block
            k_pos = lax.broadcasted_iota(jnp.int32, (1, seen), 1)
            allowed = (segment_of(q_pos, len_ref) == segment_of(k_pos, len_ref)) & (k_pos <= q_pos)
            q_rows = q_all[rows, :]
            acc = jnp.zeros((q_block, cols), F32)
            lse = jnp.zeros((q_block, 128), F32)
            lane = lax.broadcasted_iota(jnp.int32, (q_block, 128), 1)
            for head in range(heads):
                own = head_mask(q_block, cols, head)
                scores = dot(jnp.where(own, q_rows, jnp.zeros_like(q_rows)), k_all[0:seen, :], ((1,), (1,)))
                scores = jnp.where(allowed, scores, MASKED_SCORE)
                top = jnp.max(scores, axis=1, keepdims=True)
                weights = jnp.exp(scores - top)
                sums = jnp.sum(weights, axis=1, keepdims=True)
                out = dot(weights.astype(BF16), v_all[0:seen, :]) / sums
                acc = jnp.where(own, out, acc)
                lse = jnp.where(lane == head, top + jnp.log(sums), lse)
            attn[rows, :] = acc
            lse_all[:, rows] = jnp.transpose(lse)[0:8, :]
            owner, first = (n * q_block) // tok, (n * q_block) % tok
            attn_out[owner, pl.ds(first, q_block)] = acc.astype(BF16)
            if first == 0:

                @pl.when(p.s != owner)
                def _(owner=owner):
                    a2a(owner).start()

                @pl.when(p.s == owner)
                def _(owner=owner):
                    attn_in[owner] = attn_out[owner]

        disp_c.start_seq(2)
        disp_c.relay(0)
        disp_c.relay(1)
        load_o.wait()
        sums = tok_ref[...].astype(F32) + row_of(bo_ref)
        for owner in range(n_seq):

            @pl.when(p.s != owner)
            def _(owner=owner):
                a2a_from(owner).wait_recv()

            sums = sums + dot(attn_in[owner], w_o[pl.ds(owner * cols, cols), :])
        resid[...] = sums
        disp_c.start_seq(3)
        disp_c.relay(2)

        gather1.drain()
        for owner in range(n_seq):

            @pl.when(p.s != owner)
            def _(owner=owner):
                a2a(owner).wait_send()

        gout = xall.at[0]
        low = gout.at[p.s]

        def norm_two_tile(n, carry):
            low[tile_rows(n), :] = layer_norm(resid[tile_rows(n), :], gain2, bias2)[0].astype(BF16)
            return carry

        lax.fori_loop(0, tok // tile, norm_two_tile, 0)
        lay_out(send_n, low)

        disp_n = Dispatch(p, send_n, held, g["disp_n"][0:2], g["disp_n"][2:4])
        comb_g = Combine(p, part, *g["comb_g"][0:3], back, g["comb_g"][3:5], g["comb_g"][5:7], slots)
        comb_f = Combine(p, held, *g["comb_f"][0:2], None, ret, g["comb_f"][2:4], g["comb_f"][4:6], n_exp)
        disp_n.own()
        disp_n.start_seq(0)
        for step in range(1, n_exp):
            disp_n.start_exp(step)
        disp_c.start_seq(4)
        disp_c.relay(3)
        dwu[...] = jnp.zeros_like(dwu)
        dwd[...] = jnp.zeros_like(dwd)
        dbu_ref[...] = jnp.zeros_like(dbu_ref)
        csum_ref[...] = jnp.zeros_like(csum_ref)
        bias_down = bd_ref[...].astype(F32)
        for c in load_ffn:
            c.wait()

        def ffn_start(*steps):
            for step in steps:
                comb_f.start(step)

        def ffn_pass(*steps):
            for step in steps:
                comb_f.pass_on(step)

        def ffn_finish(*steps):
            for step in steps:
                comb_f.finish(step, bias_down)

        disp_c.drain(seq=False)
        keep_act, keep_grad = send_c.at[0:n_seq], send_c.at[n_seq : 2 * n_seq]

        def compute(step):
            x = held[step].reshape(routed, width)
            gr = cot[step].reshape(routed, width)
            ones = jnp.ones((8, routed), BF16)
            csum_ref[...] += dot(ones, gr)[0:1, :]
            gx = jnp.zeros((routed, width), F32)
            for b in range(hidden // block):
                at = pl.ds(b * block, block)
                wu_b, wd_b = wu[:, at], wd[at, :]
                pre = dot(x, wu_b) + bu_ref[:, at].astype(F32)
                g_act = dot(gr, wd_b, ((1,), (1,)))
                sq = pre * pre
                th = jnp.tanh(GELU_A * pre * (1.0 + GELU_B * sq))
                half = 0.5 * (1.0 + th)
                slope = half + 0.5 * pre * (1.0 - th * th) * (GELU_A * (1.0 + 3.0 * GELU_B * sq))
                g_pre = (g_act * slope).astype(BF16)
                keep_act[:, :, at] = (pre * half).astype(BF16).reshape(n_seq, cap, block)
                keep_grad[:, :, at] = g_pre.reshape(n_seq, cap, block)
                gx = gx + dot(g_pre, wu_b, ((1,), (1,)))
            part[lax.rem(step, slots)] = gx.astype(BF16).reshape(n_seq, cap, width)
            comb_g.start(step)
            y = jnp.zeros((routed, width), F32)
            for b in range(hidden // block):
                at = pl.ds(b * block, block)
                act = keep_act[:, :, at].reshape(routed, block)
                g_pre = keep_grad[:, :, at].reshape(routed, block)
                dbu_ref[:, at] += dot(ones, g_pre)[0:1, :]
                y = y + dot(act, wd[at, :])
                dwu[:, at] += dot(x, g_pre, ((0,), (0,)))
                dwd[at, :] += dot(act, gr, ((0,), (0,)))
            disp_n.sent(step)
            held[step] = y.astype(BF16).reshape(n_seq, cap, width)

        stores = [
            pltpu.make_async_copy(dwu, dwu_out, local_sems.at[6]),
            pltpu.make_async_copy(dwd, dwd_out, local_sems.at[7]),
        ]

        def loop(t, carry):
            @pl.when(t + ahead - 1 < n_exp)
            def _():
                disp_c.start_seq(t + ahead - 1)

            @pl.when(t + ahead - 2 < n_exp)
            def _():
                disp_c.relay(t + ahead - 2)

            @pl.when(t <= n_exp)
            def _():
                disp_n.relay(t - 1)

            @pl.when(t < n_exp)
            def _():
                disp_n.start_seq(t)

            @pl.when((t >= 3) & (t <= n_exp + 2))
            def _():
                comb_g.pass_on(t - 3)

            @pl.when(t >= 4)
            def _():
                comb_g.finish(t - 4)

            @pl.when(t == n_exp + 1)
            def _():
                ffn_start(0)

            @pl.when((t >= 2) & (t <= n_exp + 1))
            def _():
                disp_c.arrived(t - 2)
                disp_n.arrived(t - 2)
                compute(t - 2)

            @pl.when(t == n_exp + 1)
            def _():
                for c in stores:
                    c.start()
                ffn_start(1)

            @pl.when(t == n_exp + 2)
            def _():
                ffn_start(2)

            @pl.when(t == n_exp + 3)
            def _():
                ffn_start(3)

            return carry

        lax.fori_loop(1, n_exp + 4, loop, 0)
        comb_g.drain()

        for c in stores:
            c.wait()
        gin_ref[...] = dot(pick[...], back[...].reshape(n_exp * cap, width), ((0,), (0,)))

        def norm_two_back(n, carry):
            at = tile_rows(n)
            g_two = gin_ref[at, :]
            _, xhat, inv_std = layer_norm(resid[at, :], gain2, 0.0)
            g_resid = cot_ref[at, :].astype(F32) + norm_back(g_two, xhat, inv_std, gain2)
            gin_ref[at, :] = g_resid
            g_low = g_resid.astype(BF16)
            gout[p.s, at, :] = g_low
            new = (g_low.astype(F32), g_two * xhat, g_two)
            return tuple(old + jnp.sum(v, axis=0, keepdims=True) for old, v in zip(carry, new))

        zero_row = jnp.zeros((1, width), F32)
        sums2 = lax.fori_loop(0, tok // tile, norm_two_back, (zero_row,) * 3)
        gather2 = Gather(p, gout, *g["gather2"])
        gather2.start()
        vec_own[...] = jnp.zeros_like(vec_own)
        for n in range(3):
            vec_own[4 + n : 5 + n, :] = sums2[n]
        wo_mine = w_o.at[mine, :]

        def grad_attn(owner):
            gattn[owner] = dot(gout[owner], wo_mine[...], ((1,), (1,))).astype(BF16)

        dwu[0:total, 0 : 2 * cols] = jnp.zeros((total, 2 * cols), F32)

        head_rows = lax.broadcasted_iota(jnp.int32, (8, cols), 0)
        head_lane = lax.broadcasted_iota(jnp.int32, (8, cols), 1)
        per_head = (lax.div(head_lane, HEAD_DIM) == head_rows).astype(F32)

        def attn_back(owner, some_heads):
            rows = pl.ds(pl.multiple_of(owner * tok, tok), tok)
            q_pos = lax.broadcasted_iota(jnp.int32, (1, tok), 1) + owner * tok
            q_seg = segment_of(q_pos, len_ref)
            q_rows, g_rows = q_all[rows, :], gattn[owner]
            delta = lax.dot_general(
                per_head, g_rows.astype(F32) * attn[rows, :], (((1,), (1,)), ((), ())),
                precision=lax.Precision.HIGHEST, preferred_element_type=F32,
            )
            masks = [head_mask(tok, cols, head) for head in some_heads]
            zero = jnp.zeros_like(q_rows)
            q_owns = [jnp.where(own, q_rows, zero) for own in masks]
            g_owns = [jnp.where(own, g_rows, zero) for own in masks]
            dq[...] = jnp.zeros_like(dq)

            def key_block(n, carry):
                keys = pl.ds(pl.multiple_of(n * tok, tok), tok)
                k_pos = lax.broadcasted_iota(jnp.int32, (tok, 1), 0) + n * tok
                allowed = (q_seg == segment_of(k_pos, len_ref)) & (k_pos <= q_pos)
                k_rows, v_rows = k_all[keys, :], v_all[keys, :]
                dq_new = jnp.zeros((tok, cols), F32)
                dk_new = jnp.zeros((tok, cols), F32)
                dv_new = jnp.zeros((tok, cols), F32)
                for head, own, q_own, g_own in zip(some_heads, masks, q_owns, g_owns):
                    scores = dot(k_rows, q_own, ((1,), (1,)))
                    probs = jnp.where(allowed, jnp.exp(scores - lse_all[head : head + 1, rows]), 0.0)
                    g_probs = dot(v_rows, g_own, ((1,), (1,)))
                    g_scores = (probs * (g_probs - delta[head : head + 1, :])).astype(BF16)
                    dk_new = dk_new + dot(g_scores, q_own)
                    dv_new = dv_new + dot(probs.astype(BF16), g_own)
                    dq_new = dq_new + jnp.where(own, dot(g_scores, k_rows, ((0,), (0,))), 0.0)
                dk[keys, :] += dk_new
                dv[keys, :] += dv_new
                dq[...] += dq_new
                return carry

            lax.fori_loop(0, owner + 1, key_block, 0)
            low_dq = (dq[...] * SCORE_SCALE).astype(BF16)
            for j in sorted({head // per_pair for head in some_heads}):
                dqkv[rows, pl.ds(3 * j * 128, 128)] = low_dq[:, j * 128 : (j + 1) * 128]

        every = range(heads)
        grad_attn(p.s)
        gather2.relay()
        ffn_pass(0, 1, 2, 3)
        attn_back(p.s, every)
        gather2.wait((2, 3))
        grad_attn(p.near)
        attn_back(p.near, every)
        grad_attn(p.far)
        attn_back(p.far, every)
        ffn_finish(0, 1, 2, 3)
        gather2.wait((4, 5))
        ffn_start(4, 5, 6, 7)
        grad_attn(p.diag)

        def place_w(j, owner, e, half=None):
            rows = rows_w if half is None else rows_w // 2
            first = e * rows_w + (0 if half is None else half * rows)
            return gw_out.at[
                :, pl.ds(pl.multiple_of(first, rows), rows), pl.ds(pl.multiple_of(owner * cols + j * 128, 128), 128)
            ]

        def place_o(owner, e, half=None):
            rows = pl.ds(pl.multiple_of(owner * cols + e * rows_o, rows_o), rows_o)
            if half is None:
                return go_out.at[rows, :]
            return go_out.at[rows, pl.ds(half * (width // 2), width // 2)]

        def summing(name, place):
            return SumAll(p, *g[name][0:5], place, g[name][5], g[name][6:])

        sum_w = [summing(f"sum_{j}", functools.partial(place_w, j)) for j in range(pairs)]
        sum_o = summing("sum_o", place_o)

        for b in range(cols // 128):
            a_low = attn[:, b * 128 : (b + 1) * 128].astype(BF16)
            got = dot(a_low, gout[...].reshape(total, width), ((0,), (0,))).astype(BF16)
            for n in range(128 // rows_o):
                e = b * (128 // rows_o) + n
                sum_o.src[e % 2, e // 2] = got[n * rows_o : (n + 1) * rows_o]
        sum_o.start()
        for j in range(pairs):
            attn_back(p.diag, range(j * per_pair, (j + 1) * per_pair))
            first = 3 * j * 128
            at = slice(j * 128, (j + 1) * 128)
            dqkv[:, first + 128 : first + 256] = dk[:, at].astype(BF16)
            dqkv[:, first + 256 : first + 384] = dv[:, at].astype(BF16)
            src = sum_w[j].src
            for b in range(width // 256):
                got = dot(n1[b * 256 : (b + 1) * 256, :], dqkv[:, first : first + 384]).astype(BF16)
                for n in range(256 // rows_w):
                    e = b * (256 // rows_w) + n
                    for m in range(3):
                        src[e % 2, e // 2, m] = got[n * rows_w : (n + 1) * rows_w, m * 128 : (m + 1) * 128]
            sum_w[j].start()
            if j == 0:
                sum_o.spread()
            if j > 0:
                sum_w[j - 1].spread()
        sum_w[pairs - 1].spread()
        sum_o.reduce()
        sum_o.forward(0)
        gather2.drain()
        red = Combine(p, xall, *g["red"][0:2], None, None, g["red"][2:4], (None, None), 1)
        for owner in range(n_seq):
            piece = dqkv[pl.ds(owner * tok, tok), :]
            xall[0, owner] = dot(piece, w_all[...], ((1,), (1,))).astype(BF16)
        red.start(0)
        d_sums = dot(jnp.ones((8, total), BF16), dqkv[...])
        for j in range(pairs):
            at = pl.ds(pl.multiple_of(p.s * cols + j * 128, 128), 128)
            first = 3 * j * 128
            vec_own[2:3, at] = d_sums[0:1, first : first + 128]
            vec_own[3:4, at] = d_sums[0:1, first + 256 : first + 384]
        sums = [sum_o] + sum_w
        ffn_pass(4, 5, 6, 7)
        red.pass_on(0)
        for n in range(1, len(sums)):
            sums[n].reduce()
            sums[n].forward(0)
            sums[n - 1].relay(0)
        sum_o.forward(1)
        red.arrived(0)
        half_tok = tok // 2
        for n in range(2):
            gout[p.s, pl.ds(n * half_tok, half_tok), :] = red.summed(0, n).astype(BF16)

        def norm_one_back(n, carry):
            at = tile_rows(n)
            g_one = gout[p.s, at, :].astype(F32)
            _, xhat, inv_std = layer_norm(tok_ref[at, :].astype(F32), gain1, 0.0)
            gin_ref[at, :] += norm_back(g_one, xhat, inv_std, gain1)
            new = (g_one * xhat, g_one)
            return tuple(old + jnp.sum(v, axis=0, keepdims=True) for old, v in zip(carry, new))

        sums1 = lax.fori_loop(0, tok // tile, norm_one_back, (zero_row,) * 2)
        store_gin = pltpu.make_async_copy(gin_ref, gin_out, local_sems.at[0])
        store_gin.start()
        for n in range(2):
            vec_own[n : n + 1, :] = sums1[n]
        for one in sum_w:
            one.forward(1)
        vec_seq[p.s] = vec_own[...]

        def tell(other):
            return p.to_seq(vec_own, vec_seq.at[p.s], r["vs_send"].at[other], r["vs_recv"].at[p.s], other)

        def told(other):
            return p.to_seq(vec_own, vec_seq.at[other], r["vs_send"].at[other], r["vs_recv"].at[other], other)

        others = (p.near, p.far, p.diag)
        for other in others:
            tell(other).start()
        for hop in range(1, chips):
            ffn_finish(*range(4 + 4 * (hop - 1) // (chips - 1), 4 + 4 * hop // (chips - 1)))
            for one in sums:
                if hop > 1:
                    one.forward(hop)
                if hop > 1 or one is sums[-1]:
                    one.relay(hop - 1)
            if hop > 1:
                for one in sums:
                    one.arrived(hop - 2)
        for other in others:
            told(other).wait_recv()
        for other in others:
            tell(other).wait_send()
        vec = vec_seq[0]
        for n in range(1, n_seq):
            vec = vec + vec_seq[n]
        vec_own[...] = vec
        vec_exp[p.e] = vec

        def show(step):
            other = p.peer(step, -1)
            return p.to_exp(vec_own, vec_exp.at[p.e], r["ve_send"].at[step], r["ve_recv"].at[step], other)

        def shown(step):
            other = p.peer(step, 1)
            return p.to_exp(vec_own, vec_exp.at[other], r["ve_send"].at[step], r["ve_recv"].at[step], other)

        for step in range(1, n_exp):
            show(step).start()
        for one in sums:
            one.relay(chips - 1)
        comb_f.drain()
        out_ref = part.at[0]
        for n in range(tok // 128):
            at = slice(n * 128, (n + 1) * 128)
            rows_back = dot(pick[:, at], ret[...].reshape(n_exp * cap, width), ((0,), (0,)))
            out_ref[n * 128 // cap : (n + 1) * 128 // cap] = (
                (resid[at, :] + rows_back).astype(BF16).reshape(128 // cap, cap, width)
            )
        store_out = pltpu.make_async_copy(out_ref, out_out, local_sems.at[1])
        store_out.start()
        for hop in range(chips - 2, chips):
            for one in sums:
                one.arrived(hop)
        for step in range(1, n_exp):
            shown(step).wait_recv()
            show(step).wait_send()
        vec = vec_exp[0]
        for n in range(1, n_exp):
            vec = vec + vec_exp[n]
        vec_ref[...] = vec
        for step in range(n_exp):
            disp_c.sent(step)
        disp_n.drain(seq=False)
        for one in sums:
            one.drain()
        store_gin.wait()
        store_out.wait()

    vmem = pl.BlockSpec(memory_space=pltpu.VMEM)
    hbm = pl.BlockSpec(memory_space=pl.ANY)
    smem = pl.BlockSpec(memory_space=pltpu.SMEM)
    shape = jax.ShapeDtypeStruct
    return pl.pallas_call(
        kernel,
        out_shape=[
            shape((n_seq, cap, width), BF16),
            shape((tok, width), F32),
            shape((8, width), F32),
            shape((1, hidden), F32),
            shape((1, width), F32),
            shape((width, hidden), F32),
            shape((hidden, width), F32),
            shape((3, width, width), BF16),
            shape((width, width), BF16),
        ],
        in_specs=[vmem] * 3 + [smem] + [vmem] * 2 + [hbm] * 3 + [vmem] * 2 + [hbm] + [vmem] * 3
        + [hbm, vmem, hbm, vmem],
        out_specs=[hbm, hbm] + [vmem] * 3 + [hbm] * 4,
        scratch_shapes=scratch,
        compiler_params=pltpu.CompilerParams(
            collective_id=collective_id, has_side_effects=True, vmem_limit_bytes=VMEM_LIMIT
        ),
        name="layer",
    )(tokens, ids, cotangent, lengths, *ln1, *w_qkv, b_query, b_value, w_out, b_out, *ln2, w_up, b_up, w_down, b_down)


def finish(output, input_grad, vec, dbu, csum, dwu, dwd, gw, go):
    tok, width = output.shape
    hidden = dwu.shape[1]
    cols = width // 4
    piece = 256

    def kernel(out_in, gin_in, vec_ref, dbu_in, csum_ref, dwu_in, dwd_in, gw_in, go_in, *refs):
        (out_o, gin_o, l1g, l1b, wq_o, bq_o, wk_o, wv_o, bv_o, wo_o, bo_o, l2g, l2b, dwu_o, dbu_o, dwd_o, dbd_o) = refs[:17]
        small, wide, same_b, same_f, sems = refs[17:22]
        count = 0

        def pair(src, mid_in, mid_out, dst):
            nonlocal count
            load = pltpu.make_async_copy(src, mid_in, sems.at[count])
            store = pltpu.make_async_copy(mid_out, dst, sems.at[count + 1])
            count += 2
            return load, store

        widen, plain = [], []
        for m, (src, dst) in enumerate(
            ((gw_in.at[0], wq_o), (gw_in.at[1], wk_o), (gw_in.at[2], wv_o), (go_in, wo_o))
        ):
            for n in range(width // piece):
                rows = pl.ds(n * piece, piece)
                at = m * (width // piece) + n
                widen.append((pair(src.at[rows], small.at[at], wide.at[at], dst.at[rows]), at))
        at = 0
        for src, dst, total in ((dwu_in, dwu_o.at[0], width), (dwd_in, dwd_o.at[0], hidden), (gin_in, gin_o.at[0], tok)):
            for n in range(total // piece):
                rows = pl.ds(n * piece, piece)
                plain.append(pair(src.at[rows], same_f.at[at], same_f.at[at], dst.at[rows]))
                at += 1
        plain.append(pair(out_in, same_b, same_b, out_o.at[0]))
        order = []
        for n in range(max(len(widen), len(plain))):
            order += widen[n : n + 1] + [(c, None) for c in plain[n : n + 1]]
        for (load, _), _ in order:
            load.start()
        for n, ref in enumerate((l1g, l1b, bq_o, bv_o, bo_o, l2g, l2b)):
            ref[...] = vec_ref[n : n + 1, :].reshape(width)
        dbu_o[...] = dbu_in[...]
        first = pl.multiple_of(lax.axis_index("seq") * cols, cols)
        dbd_o[...] = csum_ref[:, pl.ds(first, cols)]
        for (load, store), at in order:
            load.wait()
            if at is not None:
                wide[at] = small[at].astype(F32)
            store.start()
        for (_, store), _ in order:
            store.wait()

    vmem = pl.BlockSpec(memory_space=pltpu.VMEM)
    hbm = pl.BlockSpec(memory_space=pl.ANY)
    shape = jax.ShapeDtypeStruct
    row, square = shape((width,), F32), shape((width, width), F32)
    n_widen = 4 * (width // piece)
    n_plain = (width + hidden + tok) // piece
    return pl.pallas_call(
        kernel,
        out_shape=[
            shape((1, tok, width), BF16), shape((1, tok, width), F32), row, row, square, row, square, square, row,
            square, row, row, row, shape((1, width, hidden), F32), shape((1, hidden), F32),
            shape((1, hidden, width), F32), shape((1, cols), F32),
        ],
        in_specs=[hbm, hbm, vmem, vmem, vmem, hbm, hbm, hbm, hbm],
        out_specs=[hbm, hbm, vmem, vmem, hbm, vmem, hbm, hbm, vmem, hbm, vmem, vmem, vmem, hbm, vmem, hbm, vmem],
        scratch_shapes=[
            pltpu.VMEM((n_widen, piece, width), BF16),
            pltpu.VMEM((n_widen, piece, width), F32),
            pltpu.VMEM((tok, width), BF16),
            pltpu.VMEM((n_plain, piece, width), F32),
            pltpu.SemaphoreType.DMA((2 * (n_widen + n_plain + 1),)),
        ],
        compiler_params=pltpu.CompilerParams(vmem_limit_bytes=VMEM_LIMIT),
        name="finish",
    )(output, input_grad, vec, dbu, csum, dwu, dwd, gw, go)


def shards(
    tokens, lengths, expert_ids, ln1_gain, ln1_bias, w_query, b_query, w_key, w_value, b_value, w_out, b_out,
    ln2_gain, ln2_bias, w_up, b_up, w_down, b_down, cotangent,
):
    output, *parts = layer(
        tokens[0], expert_ids[0, :, 0][None], cotangent[0], lengths, (ln1_gain, ln1_bias),
        (w_query, w_key, w_value), b_query, b_value, w_out, b_out, (ln2_gain, ln2_bias), w_up[0], b_up, w_down[0],
        b_down, lax.axis_size("exp"), 0,
    )
    return tuple(finish(output.reshape(tokens.shape[1:]), *parts))


def norm_layer(values_in, gain_vec, shift_vec):
    center = values_in - jnp.mean(values_in, axis=-1, keepdims=True)
    inv_std = lax.rsqrt(jnp.mean(center * center, axis=-1, keepdims=True) + EPSILON)
    return center * inv_std * gain_vec + shift_vec


def segment_ids(positions, seq_ends):
    return jnp.sum((positions[:, None] >= seq_ends[None, :]).astype(jnp.int32), axis=1)


def visible_pairs(query_pos, query_seg, key_pos, key_seg):
    return ((query_seg[:, None] == key_seg[None, :]) & (key_pos[None, :] <= query_pos[:, None]))[
        None
    ]


def project(left_op, right_op):
    return jnp.dot(left_op, right_op, preferred_element_type=jnp.float32)


def shards_any(
    tokens,
    lengths,
    expert_ids,
    ln1_gain,
    ln1_bias,
    w_query,
    b_query,
    w_key,
    w_value,
    b_value,
    w_out,
    b_out,
    ln2_gain,
    ln2_bias,
    w_up,
    b_up,
    w_down,
    b_down,
    cotangent,
):
    tok_rows = tokens.shape[1]
    width = tokens.shape[2]
    seq_size = lax.axis_size("seq")
    exp_size = lax.axis_size("exp")
    seq_rank = lax.axis_index("seq")
    seq_ends = jnp.cumsum(lengths[0])
    own_pos = seq_rank * tok_rows + jnp.arange(tok_rows, dtype=jnp.int32)
    own_seg = segment_ids(own_pos, seq_ends)
    inputs = tokens[0].astype(jnp.float32)
    gain_one = ln1_gain.astype(jnp.float32)
    bias_one = ln1_bias.astype(jnp.float32)
    gain_two = ln2_gain.astype(jnp.float32)
    bias_two = ln2_bias.astype(jnp.float32)
    normed_one_low = norm_layer(inputs, gain_one, bias_one).astype(jnp.bfloat16)
    query_low = (project(normed_one_low, w_query) + b_query.astype(jnp.float32)).astype(
        jnp.bfloat16
    )
    keys_low = project(normed_one_low, w_key).astype(jnp.bfloat16)
    values_low = (project(normed_one_low, w_value) + b_value.astype(jnp.float32)).astype(
        jnp.bfloat16
    )
    query_heads = query_low.reshape(tok_rows, HEADS, HEAD_DIM)
    initial = (
        jnp.full((HEADS, tok_rows), MASKED_SCORE, jnp.float32),
        jnp.zeros((HEADS, tok_rows), jnp.float32),
        jnp.zeros((HEADS, tok_rows, HEAD_DIM), jnp.float32),
    )
    key_piece = lax.all_gather(keys_low, "seq", axis=0, tiled=True)
    value_piece = lax.all_gather(values_low, "seq", axis=0, tiled=True)
    piece_len = key_piece.shape[0]
    fold_block_len = math.gcd(piece_len, 512)
    block_count = piece_len // fold_block_len
    key_blocks = key_piece.reshape(block_count, fold_block_len, HEADS, HEAD_DIM)
    value_blocks = value_piece.reshape(block_count, fold_block_len, HEADS, HEAD_DIM)
    offsets = jnp.arange(block_count, dtype=jnp.int32) * fold_block_len

    def block_step(state_now, packed):
        row_max, row_total, accumulated = state_now
        key_blk, value_blk, offset = packed
        key_pos = offset + jnp.arange(fold_block_len, dtype=jnp.int32)
        allowed = visible_pairs(own_pos, own_seg, key_pos, segment_ids(key_pos, seq_ends))
        scores = (
            jnp.einsum("qhd,khd->hqk", query_heads, key_blk, preferred_element_type=jnp.float32)
            * SCORE_SCALE
        )
        masked = jnp.where(allowed, scores, MASKED_SCORE)
        new_max = jnp.maximum(row_max, jnp.max(masked, axis=-1))
        weights = jnp.where(allowed, jnp.exp(masked - new_max[..., None]), 0.0)
        factor = jnp.exp(row_max - new_max)
        row_total = row_total * factor + jnp.sum(weights, axis=-1)
        accumulated = accumulated * factor[..., None] + jnp.einsum(
            "hqk,khd->hqd",
            weights.astype(jnp.bfloat16),
            value_blk,
            preferred_element_type=jnp.float32,
        )
        return ((new_max, row_total, accumulated), None)

    result, _ = lax.scan(block_step, initial, (key_blocks, value_blocks, offsets))
    row_max, row_total, accumulated = result
    attn_heads = accumulated / row_total[..., None]
    attn_low = jnp.transpose(attn_heads, (1, 0, 2)).reshape(tok_rows, width).astype(jnp.bfloat16)
    resid = inputs + project(attn_low, w_out) + b_out.astype(jnp.float32)
    normed_two_low = norm_layer(resid, gain_two, bias_two).astype(jnp.bfloat16)
    experts = exp_size * w_up.shape[0]
    capacity = 2 * tok_rows // experts
    expert_of = expert_ids[0, :, 0]
    onehot = (expert_of[:, None] == jnp.arange(experts, dtype=jnp.int32)[None, :]).astype(jnp.int32)
    slot_of = jnp.sum(onehot * (jnp.cumsum(onehot, axis=0) - onehot), axis=1)
    send_rows = (
        jnp.zeros((experts, capacity, width), jnp.bfloat16)
        .at[expert_of, slot_of]
        .set(normed_two_low)
    )
    received = lax.all_to_all(send_rows, "exp", split_axis=0, concat_axis=0, tiled=True)
    recv_count = experts * capacity
    recv_rows = received.reshape(recv_count, width)
    up_weight = w_up[0]
    up_bias = b_up[0]
    down_weight = w_down[0]
    down_bias = b_down[0].astype(jnp.float32)
    piece_width = width // seq_size
    grad_send = (
        jnp.zeros((experts, capacity, width), jnp.bfloat16).at[expert_of, slot_of].set(cotangent[0])
    )
    gathered = lax.all_gather(recv_rows, "seq", axis=0, tiled=True)
    preact = project(gathered, up_weight) + up_bias.astype(jnp.float32)
    act_low = jax.nn.gelu(preact).astype(jnp.bfloat16)
    part = act_low
    expert_out = (
        lax.psum_scatter(
            project(part, down_weight).astype(jnp.bfloat16), "seq", scatter_dimension=0, tiled=True
        ).astype(jnp.float32)
        + down_bias
    )
    returned = lax.all_to_all(
        expert_out.astype(jnp.bfloat16).reshape(experts, capacity, width),
        "exp",
        split_axis=0,
        concat_axis=0,
        tiled=True,
    )
    grad_recv = lax.all_to_all(grad_send, "exp", split_axis=0, concat_axis=0, tiled=True).reshape(
        recv_count, width
    )
    grad_all = lax.all_gather(grad_recv, "seq", axis=0, tiled=True)
    bias_full = jnp.sum(grad_all.astype(jnp.float32), axis=0)
    grad_b_down = lax.dynamic_slice_in_dim(bias_full, seq_rank * piece_width, piece_width, 0)
    grad_act = jnp.einsum("rd,fd->rf", grad_all, down_weight, preferred_element_type=jnp.float32)
    grad_pre = jax.vjp(jax.nn.gelu, preact)[1](grad_act)[0].astype(jnp.bfloat16)
    grad_w_down = jnp.einsum("rf,rd->fd", act_low, grad_all, preferred_element_type=jnp.float32)
    grad_w_up = jnp.einsum("rd,rf->df", gathered, grad_pre, preferred_element_type=jnp.float32)
    grad_b_up = jnp.sum(grad_pre.astype(jnp.float32), axis=0)
    part = grad_pre
    grad_home = lax.psum_scatter(
        jnp.einsum("rf,df->rd", part, up_weight, preferred_element_type=jnp.float32).astype(
            jnp.bfloat16
        ),
        "seq",
        scatter_dimension=0,
        tiled=True,
    )
    ffn_rows = returned[expert_of, slot_of].astype(jnp.float32)
    output = (resid + ffn_rows).astype(jnp.bfloat16)
    grad_back = lax.all_to_all(
        grad_home.reshape(experts, capacity, width), "exp", split_axis=0, concat_axis=0, tiled=True
    )
    grad_normed_two = grad_back[expert_of, slot_of].astype(jnp.float32)
    _, norm_two_back = jax.vjp(norm_layer, resid, gain_two, bias_two)
    grad_resid_norm, grad_gain_two, grad_bias_two = norm_two_back(grad_normed_two)
    grad_resid = cotangent[0].astype(jnp.float32) + grad_resid_norm
    grad_out_low = grad_resid.astype(jnp.bfloat16)
    grad_w_out = jnp.einsum("qa,qd->ad", attn_low, grad_out_low, preferred_element_type=jnp.float32)
    grad_b_out = jnp.sum(grad_out_low.astype(jnp.float32), axis=0)
    grad_attn_low = jnp.einsum(
        "qd,ad->qa", grad_out_low, w_out, preferred_element_type=jnp.float32
    ).astype(jnp.bfloat16)
    grad_attn_heads = grad_attn_low.reshape(tok_rows, HEADS, HEAD_DIM)
    delta = jnp.sum(
        jnp.transpose(grad_attn_heads.astype(jnp.float32), (1, 0, 2)) * attn_heads, axis=-1
    )
    whole_keys, whole_values = (
        lax.all_gather(keys_low, "seq", axis=0, tiled=True),
        lax.all_gather(values_low, "seq", axis=0, tiled=True),
    )
    group_len = whole_keys.shape[0]
    block_len = math.gcd(group_len, 512)
    block_count = group_len // block_len

    def back_step(grad_query, packed):
        key_blk, value_blk, offset = packed
        key_pos = offset + jnp.arange(block_len, dtype=jnp.int32)
        allowed = visible_pairs(own_pos, own_seg, key_pos, segment_ids(key_pos, seq_ends))
        scores = (
            jnp.einsum("qhd,khd->hqk", query_heads, key_blk, preferred_element_type=jnp.float32)
            * SCORE_SCALE
        )
        masked = jnp.where(allowed, scores, MASKED_SCORE)
        probabilities = (
            jnp.where(allowed, jnp.exp(masked - row_max[..., None]), 0.0) / row_total[..., None]
        )
        probs_low = probabilities.astype(jnp.bfloat16)
        grad_probs = jnp.einsum(
            "qhd,khd->hqk", grad_attn_heads, value_blk, preferred_element_type=jnp.float32
        )
        grad_scores = (probabilities * (grad_probs - delta[..., None])).astype(jnp.bfloat16)
        grad_query = (
            grad_query
            + jnp.einsum("hqk,khd->qhd", grad_scores, key_blk, preferred_element_type=jnp.float32)
            * SCORE_SCALE
        )
        grad_key_blk = (
            jnp.einsum("hqk,qhd->khd", grad_scores, query_heads, preferred_element_type=jnp.float32)
            * SCORE_SCALE
        )
        grad_value_blk = jnp.einsum(
            "hqk,qhd->khd", probs_low, grad_attn_heads, preferred_element_type=jnp.float32
        )
        return (grad_query, (grad_key_blk, grad_value_blk))

    block_offsets = jnp.arange(block_count, dtype=jnp.int32) * block_len
    grad_query, key_value_parts = lax.scan(
        back_step,
        jnp.zeros((tok_rows, HEADS, HEAD_DIM), jnp.float32),
        (
            whole_keys.reshape(block_count, block_len, HEADS, HEAD_DIM),
            whole_values.reshape(block_count, block_len, HEADS, HEAD_DIM),
            block_offsets,
        ),
    )
    grad_keys, grad_values = (
        lax.psum_scatter(
            key_value_parts[0].reshape(group_len, width).astype(jnp.bfloat16),
            "seq",
            scatter_dimension=0,
            tiled=True,
        ).astype(jnp.float32),
        lax.psum_scatter(
            key_value_parts[1].reshape(group_len, width).astype(jnp.bfloat16),
            "seq",
            scatter_dimension=0,
            tiled=True,
        ).astype(jnp.float32),
    )
    grad_query_low = grad_query.reshape(tok_rows, width).astype(jnp.bfloat16)
    grad_keys_low = grad_keys.astype(jnp.bfloat16)
    grad_values_low = grad_values.astype(jnp.bfloat16)
    grad_w_query = jnp.einsum(
        "qa,qd->ad", normed_one_low, grad_query_low, preferred_element_type=jnp.float32
    )
    grad_b_query = jnp.sum(grad_query_low.astype(jnp.float32), axis=0)
    grad_w_key = jnp.einsum(
        "qa,qd->ad", normed_one_low, grad_keys_low, preferred_element_type=jnp.float32
    )
    grad_w_value = jnp.einsum(
        "qa,qd->ad", normed_one_low, grad_values_low, preferred_element_type=jnp.float32
    )
    grad_b_value = jnp.sum(grad_values_low.astype(jnp.float32), axis=0)
    grad_normed_one = (
        (
            jnp.einsum("qd,ad->qa", grad_query_low, w_query, preferred_element_type=jnp.float32)
            + jnp.einsum("qd,ad->qa", grad_keys_low, w_key, preferred_element_type=jnp.float32)
            + jnp.einsum("qd,ad->qa", grad_values_low, w_value, preferred_element_type=jnp.float32)
        )
        .astype(jnp.bfloat16)
        .astype(jnp.float32)
    )
    _, norm_one_back = jax.vjp(norm_layer, inputs, gain_one, bias_one)
    grad_in_norm, grad_gain_one, grad_bias_one = norm_one_back(grad_normed_one)
    input_grad = grad_resid + grad_in_norm
    summed = lax.psum(
        (
            grad_gain_one,
            grad_bias_one,
            grad_w_query,
            grad_b_query,
            grad_w_key,
            grad_w_value,
            grad_b_value,
            grad_w_out,
            grad_b_out,
            grad_gain_two,
            grad_bias_two,
        ),
        ("seq", "exp"),
    )
    return (
        output[None],
        input_grad[None],
        summed[0],
        summed[1],
        summed[2],
        summed[3],
        summed[4],
        summed[5],
        summed[6],
        summed[7],
        summed[8],
        summed[9],
        summed[10],
        grad_w_up[None],
        grad_b_up[None],
        grad_w_down[None],
        grad_b_down[None],
    )


def solution(mesh):
    placed = (
        P("exp", "seq", None),
        P("exp", None),
        P("exp", "seq", None),
        P(),
        P(),
        P(),
        P(),
        P(),
        P(),
        P(),
        P(),
        P(),
        P(),
        P(),
        P("exp", None, "seq"),
        P("exp", "seq"),
        P("exp", "seq", None),
        P("exp", None),
        P("exp", "seq", None),
    )
    plane = mesh.shape["seq"] == 4 and mesh.shape["exp"] == 8
    return jax.shard_map(
        shards if plane else shards_any,
        mesh=mesh,
        in_specs=placed,
        out_specs=(
            P("exp", "seq", None),
            P("exp", "seq", None),
            P(),
            P(),
            P(),
            P(),
            P(),
            P(),
            P(),
            P(),
            P(),
            P(),
            P(),
            P("exp", None, "seq"),
            P("exp", "seq"),
            P("exp", "seq", None),
            P("exp", "seq"),
        ),
        check_vma=False,
    )
```
